32 devices in a mesh: batch: 2 (over x), row: 4 (over z), col: 4 (over y, core).
Axes of the slice: x: 2, y: 2, z: 4, core: 2. Of those that a mesh axis runs over, the one named last changes fastest.
Arguments:
- low_map: bfloat16 [8, 64, 64, 64], P('batch', 'row', 'col')
- skip_map: bfloat16 [8, 128, 128, 64], P('batch', 'row', 'col')
- conv_first: bfloat16 [3, 3, 64, 64], replicated, may hold values from -0.25 to 0.25
- gain_first: float32 [64], replicated, may hold values from 0.5 to 1.5
- shift_first: float32 [64], replicated, may hold values from -0.5 to 0.5
- conv_second: bfloat16 [3, 3, 64, 64], replicated, may hold values from -0.25 to 0.25
- gain_second: float32 [64], replicated, may hold values from 0.5 to 1.5
- shift_second: float32 [64], replicated, may hold values from -0.5 to 0.5
- head_conv: bfloat16 [3, 3, 64, 768], replicated, may hold values from -0.25 to 0.25
- head_bias: float32 [768], replicated, may hold values from -3 to 3
- heat_weight: bfloat16 [256, 80], replicated, may hold values from -0.375 to 0.375
- heat_bias: float32 [80], replicated, may hold values from -3 to -1.4
- box_weight: bfloat16 [2, 256, 2], replicated, may hold values from -0.375 to 0.375
- box_bias: float32 [2, 2], replicated, may hold values from -3 to 3
- heat_target: bfloat16 [8, 128, 128, 80], P('batch', 'row', 'col'), as said below
- box_target: float32 [8, 128, 4], P('batch'), may hold values from -6 to 6
- obj_index: int32 [8, 128], P('batch'), may hold values from 0 to 16383, as said below
- obj_count: int32 [8], P('batch'), may hold values from 0 to 128, as said below
Outputs:
- heat_map: float32 [8, 128, 128, 80], P('batch', 'row', 'col')
- box_map: float32 [8, 128, 128, 4], P('batch', 'row', 'col')
- grad_low: float32 [8, 64, 64, 64], P('batch', 'row', 'col')
- grad_skip: float32 [8, 128, 128, 64], P('batch', 'row', 'col')
- grad_conv_first: float32 [3, 3, 64, 64], replicated
- grad_gain_first: float32 [64], replicated
- grad_shift_first: float32 [64], replicated
- grad_conv_second: float32 [3, 3, 64, 64], replicated
- grad_gain_second: float32 [64], replicated
- grad_shift_second: float32 [64], replicated
- grad_head_conv: float32 [3, 3, 64, 768], replicated
- grad_head_bias: float32 [768], replicated
- grad_heat_weight: float32 [256, 80], replicated
- grad_heat_bias: float32 [80], replicated
- grad_box_weight: float32 [2, 256, 2], replicated
- grad_box_bias: float32 [2, 2], replicated
The draws below stay inside these ranges and needn't reach their ends.
Inputs may be any that keep to these rules, and one draw needn't show every extreme that they name: `obj_index`: for image b the first obj_count[b] entries are distinct cells row * 128 + column; the other entries are 0. `obj_count`: some image has 128 objects and some other image has none. `heat_target`: at least one entry equals 1; every other entry is below 0.96.
All inputs are finite; a program needn't handle non-finite values.
Results may differ from the reference program's by a relative error of at most 0.015.
Values may be sent and summed in bfloat16 or wider, within the bound.
A program may use at most 128 MiB of HBM per device.

```python
import jax
import jax.numpy as jnp
from jax import lax

IMAGES = 8
MAP = 128
LOW = 64
CH = 64
HEAD = 256
CLS = 80
MAXOBJ = 128


def ramp_scale(side):
    image_ramp = 1.0 + jnp.arange(IMAGES, dtype=jnp.float32) / IMAGES
    side_ramp = 1.0 + jnp.arange(side, dtype=jnp.float32) / side
    return image_ramp[:, None, None, None] * side_ramp[None, :, None, None] * side_ramp[None, None, :, None]


def draw_low_map(key, part):
    key = jax.random.fold_in(key, 11)
    keys = jax.random.split(key, 3)
    noise = jnp.clip(jax.random.normal(keys[0], (IMAGES, LOW, LOW, CH), jnp.float32), -4.0, 4.0)
    channel = jnp.exp(jax.random.uniform(keys[1], (CH,), jnp.float32, -0.7, 0.7))
    centre = jnp.clip(0.5 * jax.random.normal(keys[2], (CH,), jnp.float32), -1.5, 1.5)
    return (ramp_scale(LOW) * channel * (centre + noise)).astype(jnp.bfloat16)


def draw_skip_map(key, part):
    key = jax.random.fold_in(key, 12)
    keys = jax.random.split(key, 3)
    noise = jnp.clip(jax.random.normal(keys[0], (IMAGES, MAP, MAP, CH), jnp.float32), -4.0, 4.0)
    channel = jnp.exp(jax.random.uniform(keys[1], (CH,), jnp.float32, -0.7, 0.7))
    centre = jnp.clip(0.5 * jax.random.normal(keys[2], (CH,), jnp.float32), -1.5, 1.5)
    return (ramp_scale(MAP) * channel * (centre + noise)).astype(jnp.bfloat16)


def draw_heat_target(key, part):
    key = jax.random.fold_in(key, 13)
    keys = jax.random.split(key, 2)
    shape = (IMAGES, MAP, MAP, CLS)
    base = jax.random.uniform(keys[0], shape, jnp.float32)
    values = 0.95 * base * base * base
    row_ramp = 1.0 + 2.0 * jnp.arange(MAP, dtype=jnp.float32) / MAP
    centres = jax.random.uniform(keys[1], shape, jnp.float32) * 1024.0 < row_ramp[None, :, None, None]
    values = jnp.where(centres, 1.0, values)
    values = values.at[0, 0, 0, 0].set(1.0)
    return values.astype(jnp.bfloat16)


def object_layout(key):
    key = jax.random.fold_in(key, 17)
    keys = jax.random.split(key, 4)
    counts = jax.random.randint(keys[0], (IMAGES,), 0, MAXOBJ + 1)
    full_image = jax.random.randint(keys[1], (), 0, IMAGES)
    empty_image = (full_image + 1 + jax.random.randint(keys[2], (), 0, IMAGES - 1)) % IMAGES
    counts = counts.at[full_image].set(MAXOBJ).at[empty_image].set(0)
    image_keys = jax.random.split(keys[3], IMAGES)
    last_cell = MAP * MAP - 1

    def choose_cells(image_key, is_full):
        order = jax.random.permutation(image_key, MAP * MAP)
        where_last = jnp.argmax((order == last_cell).astype(jnp.int32)).astype(jnp.int32)
        rolled = jnp.roll(order, -where_last)
        return jnp.where(is_full, rolled, order)[:MAXOBJ]
    full_flags = jnp.arange(IMAGES) == full_image
    chosen = jax.vmap(choose_cells)(image_keys, full_flags)
    slot_ids = jnp.arange(MAXOBJ)
    indices = jnp.where(slot_ids[None, :] < counts[:, None], chosen, 0)
    return (indices.astype(jnp.int32), counts.astype(jnp.int32))


def draw_obj_index(key, part):
    return object_layout(key)[0]


def draw_obj_count(key, part):
    return object_layout(key)[1]


def block_levels(key, extent, cuts, least, high):
    factor_of = 1.0
    for dim, blocks in cuts:
        draws = jax.random.uniform(jax.random.fold_in(jax.random.fold_in(key, 6), dim), (blocks,), jnp.float32, least / len(cuts), high / len(cuts))
        factor_of = factor_of * jnp.repeat(jnp.exp(draws), extent[dim] // blocks).reshape((-1,) + (1,) * (len(extent) - 1 - dim))
    return factor_of


def centred(stream_key, extent, deviation, most, shards=(), held_as=jnp.bfloat16):
    drawn = deviation * jax.random.normal(stream_key, extent, jnp.float32)
    if shards:
        drawn = drawn * block_levels(stream_key, extent, shards, -0.22, 0.18)
    return jnp.clip(drawn, -most, most).astype(held_as)


def setup_inputs(seed: int = 0) -> dict:
    key_list = jax.random.split(jax.random.key(seed), 19)
    return {
        "low_map": draw_low_map(jax.random.fold_in(key_list[18], 71), 0),
        "skip_map": draw_skip_map(jax.random.fold_in(key_list[18], 71), 0),
        "conv_first": centred(key_list[2], (3, 3, CH, CH), (9 * CH) ** -0.5, 0.25),
        "gain_first": jnp.clip(1.0 + 0.1 * jax.random.normal(key_list[3], (CH,), jnp.float32), 0.5, 1.5),
        "shift_first": jnp.clip(jax.random.uniform(key_list[4], (CH,), jnp.float32, -0.5, 0.5), -0.5, 0.5),
        "conv_second": centred(key_list[5], (3, 3, CH, CH), (9 * CH) ** -0.5, 0.25),
        "gain_second": jnp.clip(1.0 + 0.1 * jax.random.normal(key_list[6], (CH,), jnp.float32), 0.5, 1.5),
        "shift_second": jnp.clip(jax.random.uniform(key_list[7], (CH,), jnp.float32, -0.5, 0.5), -0.5, 0.5),
        "head_conv": centred(key_list[8], (3, 3, CH, 3 * HEAD), (9 * CH) ** -0.5, 0.25),
        "head_bias": centred(key_list[9], (3 * HEAD,), 0.5, 3.0, (), jnp.float32),
        "heat_weight": centred(key_list[10], (HEAD, CLS), HEAD ** -0.5, 0.375),
        "heat_bias": jnp.clip(jax.random.uniform(key_list[11], (CLS,), jnp.float32, -3.0, -1.4), -3.0, -1.4),
        "box_weight": centred(key_list[12], (2, HEAD, 2), HEAD ** -0.5, 0.375),
        "box_bias": centred(key_list[13], (2, 2), 1.0, 3.0, (), jnp.float32),
        "heat_target": draw_heat_target(jax.random.fold_in(key_list[18], 71), 0),
        "box_target": centred(key_list[15], (IMAGES, MAXOBJ, 4), 1.5, 6.0, ((0, 2),), jnp.float32),
        "obj_index": draw_obj_index(jax.random.fold_in(key_list[18], 71), 0),
        "obj_count": draw_obj_count(jax.random.fold_in(key_list[18], 71), 0),
    }


EPSILON = 1e-05
HIGHEST = lax.Precision.HIGHEST

@jax.custom_vjp
def low(v):
    return lax.optimization_barrier(v.astype(jnp.bfloat16)).astype(jnp.float32)

@jax.custom_vjp
def low_back(v):
    return v

def low_keep(v):
    return (low(v), None)

def low_pass(kept, grad):
    return (grad,)

def back_keep(v):
    return (v, None)

def back_low(kept, grad):
    return (low(grad),)
low.defvjp(low_keep, low_pass)
low_back.defvjp(back_keep, back_low)

def convolve(values, kernel):
    return lax.conv_general_dilated(values, kernel, (1, 1), ((1, 1), (1, 1)), dimension_numbers=('NHWC', 'HWIO', 'NHWC'), precision=HIGHEST)

def upsample(padded, axis):
    length = padded.shape[axis] - 2
    before = lax.slice_in_dim(padded, 0, length, axis=axis)
    middle = lax.slice_in_dim(padded, 1, length + 1, axis=axis)
    behind = lax.slice_in_dim(padded, 2, length + 2, axis=axis)
    even_rows = 0.75 * middle + 0.25 * before
    odd_rows = 0.75 * middle + 0.25 * behind
    stacked = jnp.stack([even_rows, odd_rows], axis=axis + 1)
    new_shape = list(middle.shape)
    new_shape[axis] = 2 * length
    return stacked.reshape(new_shape)

def spread(values):
    padded = jnp.pad(values, ((0, 0), (1, 1), (1, 1), (0, 0)))
    return upsample(upsample(padded, 1), 2)

def batch_norm(values, gain, shift):
    centre = lax.optimization_barrier(jnp.mean(values, axis=(0, 1, 2)))
    second = lax.optimization_barrier(jnp.mean(values * values, axis=(0, 1, 2))) - centre * centre
    return (values - centre) * lax.rsqrt(second + EPSILON) * gain + shift

def smooth_gap(values):
    return jnp.sqrt(values * values + 1.0) - 1.0

def reference(low_map, skip_map, conv_first, gain_first, shift_first, conv_second, gain_second, shift_second, head_conv, head_bias, heat_weight, heat_bias, box_weight, box_bias, heat_target, box_target, obj_index, obj_count):
    targets_all = heat_target.astype(jnp.float32)
    positives = jnp.sum((targets_all == 1.0).astype(jnp.float32))
    objects = jnp.sum(obj_count).astype(jnp.float32)
    group_size = 4 if IMAGES % 4 == 0 else 1
    group_count = IMAGES // group_size
    slot_ids = jnp.arange(MAXOBJ)

    def forward(low_in, skip_in, conv_one, gain_one, shift_one, conv_two, gain_two, shift_two, head_kernel, head_shift, heat_kernel, heat_shift, box_kernel, box_shift):
        y_one = low_back(convolve(low_in, conv_one))
        act_one = low(jax.nn.silu(batch_norm(y_one, gain_one, shift_one)))
        merged = low(low_back(spread(act_one)) + skip_in)
        y_two = low_back(convolve(merged, conv_two))
        feature = low(jax.nn.silu(batch_norm(y_two, gain_two, shift_two)))

        def head_block(pieces):
            features, targets, indices, counts, box_goal = pieces
            hidden = low_back(convolve(features, head_kernel) + head_shift)
            active = low(jax.nn.silu(hidden))
            logit = low_back(jnp.einsum('brch,hk->brck', active[..., :HEAD], heat_kernel, precision=HIGHEST) + heat_shift)
            size_part = jnp.einsum('brch,hk->brck', active[..., HEAD:2 * HEAD], box_kernel[0], precision=HIGHEST) + box_shift[0]
            offset_part = jnp.einsum('brch,hk->brck', active[..., 2 * HEAD:], box_kernel[1], precision=HIGHEST) + box_shift[1]
            boxes_out = low_back(jnp.concatenate([size_part, offset_part], axis=-1))
            probability = jax.nn.sigmoid(logit)
            focal_term = jnp.where(targets == 1.0, (1.0 - probability) ** 2 * jax.nn.softplus(-logit), (1.0 - targets) ** 4 * probability ** 2 * jax.nn.softplus(logit))
            flat_boxes = boxes_out.reshape(group_size, MAP * MAP, 4)
            picked = flat_boxes[jnp.arange(group_size)[:, None], indices]
            valid = (slot_ids[None, :] < counts[:, None]).astype(jnp.float32)[..., None]
            distance = smooth_gap(picked - box_goal) * valid
            part_loss = jnp.sum(focal_term) / positives + (0.1 * jnp.sum(distance[..., :2]) + jnp.sum(distance[..., 2:])) / (2.0 * objects)
            return (probability, boxes_out, part_loss)
        heat_all, boxes_all, losses = lax.map(jax.checkpoint(head_block), (feature.reshape(group_count, group_size, MAP, MAP, CH), targets_all.reshape(group_count, group_size, MAP, MAP, CLS), obj_index.reshape(group_count, group_size, MAXOBJ), obj_count.reshape(group_count, group_size), box_target.astype(jnp.float32).reshape(group_count, group_size, MAXOBJ, 4)))
        return (jnp.sum(losses), (heat_all.reshape(IMAGES, MAP, MAP, CLS), boxes_all.reshape(IMAGES, MAP, MAP, 4)))
    loss_value, pullback, outputs_aux = jax.vjp(forward, low_map.astype(jnp.float32), skip_map.astype(jnp.float32), conv_first.astype(jnp.float32), gain_first.astype(jnp.float32), shift_first.astype(jnp.float32), conv_second.astype(jnp.float32), gain_second.astype(jnp.float32), shift_second.astype(jnp.float32), head_conv.astype(jnp.float32), head_bias.astype(jnp.float32), heat_weight.astype(jnp.float32), heat_bias.astype(jnp.float32), box_weight.astype(jnp.float32), box_bias.astype(jnp.float32), has_aux=True)
    gradients = pullback(jnp.ones_like(loss_value))
    return (outputs_aux[0], outputs_aux[1], gradients[0], gradients[1], gradients[2], gradients[3], gradients[4], gradients[5], gradients[6], gradients[7], gradients[8], gradients[9], gradients[10], gradients[11], gradients[12], gradients[13])
```

```python
import functools

import jax
import jax.numpy as jnp
from jax import lax
from jax.experimental import pallas as pl
from jax.experimental.pallas import tpu as pltpu
from jax.sharding import PartitionSpec as P

EPSILON = 1e-05
F32 = jnp.float32
BF16 = jnp.bfloat16
KEEP = (((1,), (1,)), ((), ()))
LEFT = (((0,), (0,)), ((), ()))
MIB = 1024 * 1024


def dot(left, right):
    return jnp.dot(left, right, preferred_element_type=F32)


def dot_keep(left, right):
    return lax.dot_general(left, right, KEEP, preferred_element_type=F32)


def dot_left(left, right):
    return lax.dot_general(left, right, LEFT, preferred_element_type=F32)


def three_parts(values):
    high = values.astype(BF16)
    rest = values - high.astype(F32)
    mid = rest.astype(BF16)
    return high, mid, (rest - mid.astype(F32)).astype(BF16)


def tile_count(devices):
    return -(-230 // (2 * devices)) * 2 * devices


def heads_body(
    chunks,
    map_side,
    y_two_ref,
    target_ref,
    spot_ref,
    goal_ref,
    stat_ref,
    conv_ref,
    bias_ref,
    heat_w_ref,
    heat_b_ref,
    box_w_ref,
    box_b_ref,
    heat_out,
    box_out,
    spread_out,
    load_out,
    small_out,
    feat_s,
    taps_ref,
    kernel_s,
    back_s,
    box_s,
    goal_s,
    wide_s,
    grad_s,
    heat_grad_s,
    box_grad_s,
    heat_sum_s,
    box_sum_s,
):
    image = pl.program_id(0)
    chunk = pl.program_id(1)
    rows, breadth = target_ref.shape[1], target_ref.shape[2]
    cells = rows * breadth
    units = 256

    @pl.when(jnp.logical_and(image == 0, chunk == 0))
    def _():
        for tap in range(3):
            kernel_s[tap, 0:192, :] = (0.5 * conv_ref[tap].astype(F32)).astype(BF16)
            kernel_s[tap, 192:256, :] = jnp.zeros((64, 768), BF16)
        parts = three_parts(0.5 * bias_ref[...].reshape(1, 768))
        which = lax.broadcasted_iota(jnp.int32, (16, 768), 0)
        filled = jnp.zeros((16, 768), F32)
        for place in range(3):
            filled = jnp.where(which == place, parts[place].astype(F32), filled)
        kernel_s[1, 192:208, :] = filled.astype(BF16)
        for tap in range(3):
            for block in range(3):
                span = slice(256 * block, 256 * block + 256)
                back_s[span, 256 * tap : 256 * tap + 256] = (
                    kernel_s[tap, :, span].astype(F32).T.astype(BF16)
                )
        empty = jnp.zeros((2, 256), F32)
        for part in range(2):
            pieces = [empty, empty]
            pieces[part] = box_w_ref[part].astype(F32)
            box_s[part] = jnp.concatenate(pieces, axis=0).astype(BF16)
        grad_s[...] = jnp.zeros_like(grad_s)
        heat_grad_s[...] = jnp.zeros_like(heat_grad_s)
        box_grad_s[...] = jnp.zeros_like(box_grad_s)
        heat_sum_s[...] = jnp.zeros_like(heat_sum_s)
        box_sum_s[...] = jnp.zeros_like(box_sum_s)

    @pl.when(chunk == 0)
    def _():
        wide_s[...] = jnp.zeros_like(wide_s)
        ext, wide = taps_ref.shape[0], breadth + 16
        normed = (y_two_ref[0, 1 : ext + 1] - stat_ref[2:3, :]) * stat_ref[3:4, :]
        feature, _ = silu_parts(normed * stat_ref[8:9, :] + stat_ref[9:10, :])
        column = lax.broadcasted_iota(jnp.int32, (wide, 128), 0)
        keep = jnp.where(column < 8, stat_ref[12:13, :], 1.0)
        keep = jnp.where(column >= 8 + breadth, stat_ref[13:14, :], keep)
        feat_s[0:PAD, :] = jnp.zeros((PAD, 128), F32)
        feat_s[PAD : PAD + ext * wide, :] = (feature * keep).reshape(ext * wide, 128)
        feat_s[PAD + ext * wide :, :] = jnp.zeros((PAD, 128), F32)
        for line, row in ((PAD, 10), (PAD + (ext - 1) * wide, 11)):
            feat_s[line : line + wide, :] = feat_s[line : line + wide, :] * stat_ref[row : row + 1]
        pairs = tap_pairs(feat_s, PAD, ext * wide, 1.0)
        taps_ref[...] = pairs.reshape(ext, wide, 256)[:, 8 : 8 + breadth].astype(BF16)
        for place, part in enumerate(three_parts(goal_ref[0])):
            goal_s[place] = part

    first = chunk * rows
    taps = jnp.concatenate(
        [taps_ref[pl.ds(first + tap, rows)].reshape(cells, 256) for tap in range(3)], axis=1
    )
    active, slope = [], []
    for block in range(3):
        weight = kernel_s[:, :, block * units : (block + 1) * units].reshape(768, units)
        hidden = dot(taps, weight)
        turn = jnp.tanh(hidden)
        above = 1.0 + turn
        product = hidden * above
        active.append(product.astype(BF16))
        slope.append(above + product * (1.0 - turn))

    logit = dot_keep(active[0], heat_w_ref[...]) + heat_b_ref[...]
    decay = jnp.exp(-jnp.abs(logit))
    large = 1.0 / (1.0 + decay)
    small = decay * large
    above = logit >= 0.0
    chance = jnp.where(above, large, small)
    heat_out[0] = chance.reshape(rows, breadth, 80)
    target = target_ref[0].reshape(cells, 80).astype(F32)
    positive = target == 1.0
    side = jnp.where(positive, jnp.where(above, small, large), chance)
    value = jnp.where(positive, -logit, logit)
    soft = jnp.maximum(value, 0.0) + jnp.log(1.0 + decay)
    slant = side * side * (2.0 * (1.0 - side) * soft + side)
    gap = 1.0 - target
    gap = gap * gap
    weighting = jnp.where(positive, -1.0, gap * gap) * stat_ref[4:5, 0:80]
    logit_grad = weighting * slant
    logit_low = logit_grad.astype(BF16)

    box_bias = jnp.concatenate([box_b_ref[0:1, :], box_b_ref[1:2, :]], axis=1)
    boxes = dot_keep(active[1], box_s[0]) + dot_keep(active[2], box_s[1]) + box_bias
    box_out[0] = jnp.swapaxes(boxes.reshape(rows, breadth, 4), 1, 2)
    shape = (rows, breadth, 128)
    cell = (first + lax.broadcasted_iota(jnp.int32, shape, 0)) * map_side
    cell = (cell + lax.broadcasted_iota(jnp.int32, shape, 1)).reshape(cells, 128)
    chosen = (cell == spot_ref[pl.ds(image, 1), :]).astype(F32).astype(BF16)
    goals = dot_keep(chosen, goal_s[0]) + dot_keep(chosen, goal_s[1])
    goals = goals + dot_keep(chosen, goal_s[2])
    hit = dot(chosen, jnp.ones((128, 4), BF16))
    miss = boxes - goals
    lane = lax.broadcasted_iota(jnp.int32, (1, 4), 1)
    factor = jnp.where(lane < 2, 0.1, 1.0) * stat_ref[5:6, 0:4]
    box_grad = hit * factor * miss * lax.rsqrt(miss * miss + 1.0)
    box_low = box_grad.astype(BF16)

    heat_sum_s[...] += jnp.sum(logit_low.astype(F32).reshape(cells // 8, 8, 80), axis=0)
    box_sum_s[...] += jnp.sum(box_low.astype(F32).reshape(cells // 8, 8, 4), axis=0)
    heat_grad_s[...] += dot_left(logit_low, active[0])
    for part in range(2):
        box_grad_s[part] += dot_left(box_low, active[1 + part])

    back = [
        dot(logit_low, heat_w_ref[...]),
        dot(box_low, box_s[0]),
        dot(box_low, box_s[1]),
    ]
    grad_hidden = jnp.concatenate(
        [(back[block] * slope[block]).astype(BF16) for block in range(3)], axis=1
    )
    spread = []
    for tap in range(3):
        part = dot(grad_hidden, back_s[:, 256 * tap : 256 * tap + 256])
        spread.append(part.reshape(rows, breadth, 256))
    inner = slice(16, 16 + breadth)
    wide_s[pl.ds(first, 1), inner, :] += spread[0][0:1]
    wide_s[pl.ds(first + 1, 1), inner, :] += spread[0][1:2] + spread[1][0:1]
    wide_s[pl.ds(first + 2, rows - 2), inner, :] = (
        spread[0][2:] + spread[1][1:-1] + spread[2][:-2]
    )
    wide_s[pl.ds(first + rows, 1), inner, :] = spread[1][-1:] + spread[2][-2:-1]
    wide_s[pl.ds(first + rows + 1, 1), inner, :] = spread[2][-1:]
    for tap in range(3):
        grad_s[tap] += dot_left(taps[:, 256 * tap : 256 * tap + 256], grad_hidden)

    @pl.when(chunk == chunks - 1)
    def _():
        reach = breadth + 16
        centre = pltpu.roll(wide_s[:, 8 : 8 + reach, 0:128], 64, 2)
        total = wide_s[:, 9 : 9 + reach, 0:128] + centre + wide_s[:, 7 : 7 + reach, 128:256]
        lanes = lax.broadcasted_iota(jnp.int32, total.shape, 2)
        spread_out[0] = jnp.where(lanes < 64, total, pltpu.roll(total, 64, 2))

    @pl.when(jnp.logical_and(image == pl.num_programs(0) - 1, chunk == chunks - 1))
    def _():
        for column in range(6):
            span = slice(128 * column, 128 * column + 128)
            for tap in range(3):
                start = 36 * column + 12 * tap
                load_out[start : start + 12] = (
                    (0.5 * grad_s[tap, 0:192, span]).reshape(12, 16, 128).astype(BF16)
                )
            small_out[column : column + 1, :] = 0.5 * grad_s[1, 192:193, span]
        for half in range(2):
            span = slice(128 * half, 128 * half + 128)
            start = 216 + 5 * half
            load_out[start : start + 5] = heat_grad_s[:, span].reshape(5, 16, 128).astype(BF16)
            for part in range(2):
                padded = jnp.concatenate(
                    [box_grad_s[part, :, span], jnp.zeros((12, 128), F32)], axis=0
                )
                load_out[226 + 2 * part + half] = padded.astype(BF16)
        load_out[230:] = jnp.zeros((load_out.shape[0] - 230, 16, 128), BF16)
        small_out[6:8, :] = jnp.zeros((2, 128), F32)
        small_out[6:7, 0:80] = jnp.sum(heat_sum_s[...], axis=0, keepdims=True)
        small_out[7:8, 0:4] = jnp.sum(box_sum_s[...], axis=0, keepdims=True)


def heads(
    taps, target, spot, goal, stats, conv, bias, heat_w, heat_b, box_w, box_b, devices
):
    images, height, breadth, classes = target.shape
    rows = height
    chunks = height // rows
    tiles = tile_count(devices)
    whole = lambda *shape: pl.BlockSpec(shape, lambda b, c: (0,) * len(shape))
    cells = images * height * breadth
    return pl.pallas_call(
        functools.partial(heads_body, chunks, breadth * lax.axis_size("col")),
        grid=(images, chunks),
        in_specs=[
            pl.BlockSpec((1, height + 4, breadth + 16, 128), lambda b, c: (b, 0, 0, 0)),
            pl.BlockSpec((1, rows, breadth, classes), lambda b, c: (b, c, 0, 0)),
            whole(8, 128),
            pl.BlockSpec((1, 4, 128), lambda b, c: (b, 0, 0)),
            whole(24, 128),
            whole(3, 192, 768),
            whole(768),
            whole(80, 256),
            whole(1, 80),
            whole(2, 2, 256),
            whole(2, 2),
        ],
        out_specs=[
            pl.BlockSpec((1, rows, breadth, classes), lambda b, c: (b, c, 0, 0)),
            pl.BlockSpec((1, rows, 4, breadth), lambda b, c: (b, c, 0, 0)),
            pl.BlockSpec((1, height + 2, breadth + 16, 128), lambda b, c: (b, 0, 0, 0)),
            whole(tiles, 16, 128),
            whole(8, 128),
        ],
        out_shape=[
            jax.ShapeDtypeStruct((images, height, breadth, classes), F32),
            jax.ShapeDtypeStruct((images, height, 4, breadth), F32),
            jax.ShapeDtypeStruct((images, height + 2, breadth + 16, 128), F32),
            jax.ShapeDtypeStruct((tiles, 16, 128), BF16),
            jax.ShapeDtypeStruct((8, 128), F32),
        ],
        scratch_shapes=[
            pltpu.VMEM((2 * PAD + (height + 2) * (breadth + 16), 128), F32),
            pltpu.VMEM((height + 2, breadth, 256), BF16),
            pltpu.VMEM((3, 256, 768), BF16),
            pltpu.VMEM((768, 768), BF16),
            pltpu.VMEM((2, 4, 256), BF16),
            pltpu.VMEM((3, 4, 128), BF16),
            pltpu.VMEM((height + 2, breadth + 32, 256), F32),
            pltpu.VMEM((3, 256, 768), F32),
            pltpu.VMEM((80, 256), F32),
            pltpu.VMEM((2, 4, 256), F32),
            pltpu.VMEM((8, 80), F32),
            pltpu.VMEM((8, 4), F32),
        ],
        compiler_params=pltpu.CompilerParams(vmem_limit_bytes=60 * MIB),
        cost_estimate=pl.CostEstimate(
            flops=cells * 576 * 768 * 6, bytes_accessed=12 * MIB, transcendentals=cells * 768
        ),
        name="heads",
    )(taps, target, spot, goal, stats, conv, bias, heat_w, heat_b, box_w, box_b)


MESH = pl.DeviceIdType.MESH


def rounded_up(value, step):
    return -(-value // step) * step


def place():
    return lax.axis_index("batch"), lax.axis_index("row"), lax.axis_index("col")


def extents():
    return lax.axis_size("batch"), lax.axis_size("row"), lax.axis_size("col")


def plane_partners():
    batch, row, col = place()
    batches, _, cols = extents()
    partners = []
    for over in range(batches):
        for along in range(cols):
            if over or along:
                partners.append(
                    (lax.rem(batch + over, batches), row, lax.rem(col + along, cols))
                )
    return partners


def row_partners():
    batch, row, col = place()
    rows = lax.axis_size("row")
    return [(batch, lax.rem(row + over, rows), col) for over in range(1, rows)]


def flat():
    batches, rows, cols = extents()
    return batches * rows * cols <= 8


def all_partners():
    batch, row, col = place()
    batches, rows, cols = extents()
    partners = []
    for over in range(batches):
        for up in range(rows):
            for along in range(cols):
                if over or up or along:
                    partners.append(
                        (
                            lax.rem(batch + over, batches),
                            lax.rem(row + up, rows),
                            lax.rem(col + along, cols),
                        )
                    )
    return partners


def greet():
    barrier = pltpu.get_barrier_semaphore()
    partners = all_partners() if flat() else plane_partners() + row_partners()
    for partner in partners:
        pl.semaphore_signal(barrier, inc=1, device_id=partner, device_id_type=MESH)
    batch, row, col = place()
    _, rows, cols = extents()
    expected = len(partners)
    for up in (-1, 1):
        for along in (-1, 1):
            fits = jnp.logical_and(row + up >= 0, row + up < rows)
            fits = jnp.logical_and(fits, jnp.logical_and(col + along >= 0, col + along < cols))
            expected = expected + fits.astype(jnp.int32)

            @pl.when(fits)
            def _(up=up, along=along):
                pl.semaphore_signal(
                    barrier,
                    inc=1,
                    device_id=(batch, row + up, col + along),
                    device_id_type=MESH,
                )

    pl.semaphore_wait(barrier, expected)


def remote(source, target, send, recv, device):
    return pltpu.make_async_remote_copy(
        src_ref=source,
        dst_ref=target,
        send_sem=send,
        recv_sem=recv,
        device_id=device,
        device_id_type=MESH,
    )


def start_all(copies):
    for copy in copies:
        copy.start()


def wait_all(copies):
    for copy in copies:
        copy.wait()


def slot_sum(slots):
    total = slots[0]
    for k in range(1, slots.shape[0]):
        total = total + slots[k]
    return total


class Total:
    def __init__(self, source, slots, mid, row_slots, sems):
        self.source, self.slots, self.mid = source, slots, mid
        self.row_slots, self.sems = row_slots, sems

    def send(self, source, slots, mine, partners, step):
        self.copies = [
            remote(
                source,
                slots.at[mine],
                self.sems.at[step, 0, k],
                self.sems.at[step, 1, k],
                partner,
            )
            for k, partner in enumerate(partners)
        ]
        start_all(self.copies)
        slots[mine] = source[...]

    def begin(self):
        batch, row, col = place()
        _, rows, cols = extents()
        if flat():
            mine, partners = (batch * rows + row) * cols + col, all_partners()
        else:
            mine, partners = batch * cols + col, plane_partners()
        self.send(self.source, self.slots, mine, partners, 0)

    def middle(self):
        if not flat():
            wait_all(self.copies)
            self.mid[...] = slot_sum(self.slots)
            self.send(self.mid, self.row_slots, place()[1], row_partners(), 1)

    def end(self):
        wait_all(self.copies)
        return slot_sum(self.slots if flat() else self.row_slots)


def total_scratch(lines):
    batches, rows, cols = extents()
    slots = batches * cols * (rows if flat() else 1)
    return [
        pltpu.VMEM((lines, 128), F32),
        pltpu.VMEM((slots, lines, 128), F32),
        pltpu.VMEM((lines, 128), F32),
        pltpu.VMEM((rows, lines, 128), F32),
        pltpu.SemaphoreType.DMA((2, 2, max(slots, rows) - 1)),
    ]


AROUND = ((-1, 0), (1, 0), (0, -1), (0, 1), (-1, -1), (-1, 1), (1, -1), (1, 1))


class Around:
    def __init__(self, pieces, slots, sems):
        batch, row, col = place()
        _, rows, cols = extents()

        def exists(up, along):
            fits = jnp.logical_and(row + up >= 0, row + up < rows)
            return jnp.logical_and(fits, jnp.logical_and(col + along >= 0, col + along < cols))

        self.sends = [exists(up, along) for up, along in AROUND]
        self.comes = [exists(-up, -along) for up, along in AROUND]
        self.copies = [
            remote(pieces[k], slots[k], sems.at[0, k], sems.at[1, k], (batch, row + up, col + along))
            for k, (up, along) in enumerate(AROUND)
        ]

    def start(self, which=range(8)):
        for k in which:
            pl.when(self.sends[k])(self.copies[k].start)

    def wait(self, which=range(8)):
        for k in which:
            pl.when(self.comes[k])(self.copies[k].wait_recv)
            pl.when(self.sends[k])(self.copies[k].wait_send)

    def each(self, use, which=range(8)):
        for k in which:
            pl.when(self.comes[k])(functools.partial(use, k))


def twice(values):
    return jnp.concatenate([values, values], axis=-1)


def lower_half(shape):
    return lax.broadcasted_iota(jnp.int32, shape, len(shape) - 1) < 64


def swapped(values):
    return pltpu.roll(values, 64, len(values.shape) - 1)


def widened(values):
    rows, cols = values.shape[0], values.shape[1]
    side = jnp.zeros((rows, 8, 128), F32)
    return jnp.concatenate([side, twice(values.astype(F32)), side], axis=1)


def tap_pairs(buffer, start, count, fill):
    low = lower_half((1, 128))
    first = jnp.where(low, buffer[pl.ds(start - 1, count), :], buffer[pl.ds(start, count), :])
    second = jnp.where(low, buffer[pl.ds(start + 1, count), :], fill)
    return jnp.concatenate([first, second], axis=1)


def silu_parts(values):
    logistic = 0.5 * jnp.tanh(0.5 * values) + 0.5
    return values * logistic, logistic


PAD = 16


def row_loop(total, step, body, init):
    return lax.fori_loop(0, total // step, lambda k, carry: body(k * step, carry), init)


def fold_sum(values):
    return jnp.sum(values.reshape(-1, 8, 128), axis=0)


def clear(buffer, start, rows, pitch, tops, bottoms, lefts, rights):
    _, row_at, col_at = place()
    count = rounded_up(rows, 8)

    def clear_rows(span):
        first, last = span
        size = (last - first) * pitch
        buffer[pl.ds(start + first * pitch, size), :] = jnp.zeros((size, 128), F32)

    def clear_columns(span):
        for column in range(*span):
            buffer[pl.ds(start + column, count, stride=pitch), :] = jnp.zeros((count, 128), F32)

    pl.when(row_at == 0)(lambda: clear_rows(tops))
    pl.when(row_at == lax.axis_size("row") - 1)(lambda: clear_rows(bottoms))
    pl.when(col_at == 0)(lambda: clear_columns(lefts))
    pl.when(col_at == lax.axis_size("col") - 1)(lambda: clear_columns(rights))


def stack_weight(target, source):
    for tap in range(3):
        target[256 * tap : 256 * tap + 192, :] = twice(source[tap].astype(F32)).astype(BF16)
        target[256 * tap + 192 : 256 * tap + 256, :] = jnp.zeros((64, 128), BF16)


def unpacked(packed, image, images):
    low = lower_half((1, 128))
    keep = low if image < images // 2 else jnp.logical_not(low)
    return jnp.where(keep, packed, swapped(packed))


def pack_columns(buffer, target, images, rows, pitch, first_row, first, depth):
    low = lower_half((1, 128))
    half = images // 2
    count = target.shape[1]
    for pair in range(half):
        for j in range(depth):
            parts = [
                buffer[
                    pl.ds(
                        PAD + (image * rows + first_row) * pitch + first + j, count, stride=pitch
                    ),
                    :,
                ]
                for image in (pair, pair + half)
            ]
            target[depth * pair + j] = jnp.where(low, parts[0], parts[1]).astype(target.dtype)


def pack_corner(buffer, target, images, rows, pitch, first_row, first, depth):
    low = lower_half((1, 128))
    half = images // 2
    count = target.shape[1] // 8
    for pair in range(half):
        pieces = []
        for row in range(count):
            if row < depth:
                starts = [
                    PAD + (image * rows + first_row + row) * pitch + first
                    for image in (pair, pair + half)
                ]
                pieces.append(
                    jnp.where(
                        low,
                        buffer[starts[0] : starts[0] + 8, :],
                        buffer[starts[1] : starts[1] + 8, :],
                    )
                )
            else:
                pieces.append(jnp.zeros((8, 128), F32))
        target[pair] = jnp.concatenate(pieces, axis=0).astype(target.dtype)


def unpack_columns(buffer, source, images, rows, pitch, first_row, first, depth, lines, add):
    half = images // 2
    count = rounded_up(lines, 8)
    valid = lax.broadcasted_iota(jnp.int32, (count, 128), 0) < lines
    for image in range(images):
        for j in range(depth):
            packed = source[depth * (image % half) + j].astype(F32)
            values = unpacked(packed, image, images)[:count]
            spots = pl.ds(
                PAD + (image * rows + first_row) * pitch + first + j, count, stride=pitch
            )
            if add:
                values = buffer[spots, :] + jnp.where(valid, values, 0.0)
            elif count > lines:
                values = jnp.where(valid, values, buffer[spots, :])
            buffer[spots, :] = values


def unpack_corner(buffer, source, images, rows, pitch, first_row, first, depth, add):
    half = images // 2
    valid = lax.broadcasted_iota(jnp.int32, (8, 128), 0) < depth
    for image in range(images):
        packed = unpacked(source[image % half].astype(F32), image, images)
        for row in range(depth):
            start = PAD + (image * rows + first_row + row) * pitch + first
            old = buffer[start : start + 8, :]
            values = packed[8 * row : 8 * row + 8]
            if add:
                values = old + jnp.where(valid, values, 0.0)
            else:
                values = jnp.where(valid, values, old)
            buffer[start : start + 8, :] = values


def rise_body(
    low_ref,
    skip_ref,
    target_ref,
    conv_one_ref,
    conv_two_ref,
    gain_one_ref,
    shift_one_ref,
    gain_two_ref,
    shift_two_ref,
    index_ref,
    count_ref,
    y_two_out,
    y_one_out,
    merged_out,
    low_out,
    stat_out,
    spot_out,
    tiles_out,
    low_in,
    skip_in,
    target_in,
    conv_one_in,
    conv_two_in,
    param_in,
    index_in,
    y_two_s,
    y_one_s,
    merged_s,
    low_s,
    low_x,
    skip_x,
    act_s,
    row_s,
    up_s,
    w_one,
    w_two,
    g_low,
    own_low,
    low_rows,
    skip_rows,
    low_send,
    low_recv,
    low_corner,
    skip_send,
    skip_recv,
    skip_corner,
    first_scratch,
    second_scratch,
    in_sems,
    out_sems,
    strip_sems,
):
    images, h, w, _ = low_ref.shape
    height, breadth = skip_ref.shape[1], skip_ref.shape[2]
    batch_at, row_at, col_at = place()
    batches, row_count, col_count = extents()
    pitch, wide = w + 16, breadth + 16
    low_r, y_one_r = h + 6, h + 4
    skip_r, y_two_r = height + 6, height + 4
    cells_low = float(images * batches * h * row_count * w * col_count)
    cells_high = 4.0 * cells_low

    loads = [
        pltpu.make_async_copy(source, target, in_sems.at[k])
        for k, (source, target) in enumerate(
            (
                (low_ref, low_in),
                (conv_one_ref, conv_one_in),
                (skip_ref, skip_in),
                (index_ref, index_in),
                (target_ref, target_in),
                (gain_one_ref, param_in.at[0]),
                (shift_one_ref, param_in.at[1]),
                (gain_two_ref, param_in.at[2]),
                (shift_two_ref, param_in.at[3]),
                (conv_two_ref, conv_two_in),
            )
        )
    ]
    for load in loads:
        load.start()
    greet()
    low_around = Around(
        [low_ref.at[:, 0:3], low_ref.at[:, h - 3 : h]]
        + [low_send.at[k] for k in range(2)]
        + [low_corner.at[0, k] for k in range(4)],
        [low_rows.at[0], low_rows.at[1]]
        + [low_recv.at[k] for k in range(2)]
        + [low_corner.at[1, k] for k in range(4)],
        strip_sems.at[0],
    )
    skip_around = Around(
        [skip_ref.at[:, 0:3], skip_ref.at[:, height - 3 : height]]
        + [skip_send.at[k] for k in range(2)]
        + [skip_corner.at[0, k] for k in range(4)],
        [skip_rows.at[0], skip_rows.at[1]]
        + [skip_recv.at[k] for k in range(2)]
        + [skip_corner.at[1, k] for k in range(4)],
        strip_sems.at[1],
    )
    low_around.start(range(2))

    def place_low(b, carry):
        start = PAD + b * low_r * pitch
        low_x[pl.ds(start, 3 * pitch), :] = jnp.zeros((3 * pitch, 128), F32)
        low_x[pl.ds(start + 3 * pitch, h * pitch), :] = widened(low_in[b]).reshape(h * pitch, 128)
        low_x[pl.ds(start + (h + 3) * pitch, 3 * pitch), :] = jnp.zeros((3 * pitch, 128), F32)
        return carry

    low_x[0:PAD, :] = jnp.zeros((PAD, 128), F32)
    tail = low_x.shape[0] - PAD - images * low_r * pitch
    low_x[PAD + images * low_r * pitch :, :] = jnp.zeros((tail, 128), F32)
    loads[0].wait()
    lax.fori_loop(0, images, place_low, 0)
    loads[1].wait()
    stack_weight(w_one, conv_one_in)

    def pack(buffer, sends, corners, rows, step, line, across):
        for side, first in enumerate((8, 5 + across)):
            pack_columns(buffer, sends.at[side], images, rows, line, 3, first, 3)
        for k, (up, along) in enumerate(AROUND[4:]):
            pack_corner(
                buffer,
                corners.at[0, k],
                images,
                rows,
                line,
                3 if up < 0 else step,
                8 if along < 0 else 5 + across,
                3,
            )

    def unpack(around, buffer, strips, columns, corners, rows, step, line, across):
        def use(k):
            up, along = AROUND[k]
            row = step + 3 if up < 0 else 0
            column = 8 + across if along < 0 else 5
            if k < 2:

                def body(b, carry):
                    start = PAD + (b * rows + row) * line
                    buffer[pl.ds(start, 3 * line), :] = widened(strips[k, b]).reshape(
                        3 * line, 128
                    )
                    return carry

                lax.fori_loop(0, images, body, 0)
            elif k < 4:
                unpack_columns(
                    buffer, columns.at[k - 2], images, rows, line, 3, column, 3, step, False
                )
            else:
                unpack_corner(
                    buffer, corners.at[1, k - 4], images, rows, line, row, column, 3, False
                )

        around.each(use)

    pack(low_x, low_send, low_corner, low_r, h, pitch, w)
    low_around.start(range(2, 8))
    skip_around.start(range(2))

    def place_skip(b, carry):
        start = PAD + b * skip_r * wide
        edge = jnp.zeros((3 * wide, 128), F32)
        skip_x[pl.ds(start, 3 * wide), :] = edge
        skip_x[pl.ds(start + 3 * wide, height * wide), :] = widened(skip_in[b]).reshape(
            height * wide, 128
        )
        skip_x[pl.ds(start + (height + 3) * wide, 3 * wide), :] = edge
        return carry

    skip_x[0:PAD, :] = jnp.zeros((PAD, 128), F32)
    skip_tail = skip_x.shape[0] - PAD - images * skip_r * wide
    skip_x[PAD + images * skip_r * wide :, :] = jnp.zeros((skip_tail, 128), F32)
    loads[2].wait()
    lax.fori_loop(0, images, place_skip, 0)
    pack(skip_x, skip_send, skip_corner, skip_r, height, wide, breadth)
    skip_around.start(range(2, 8))
    low_around.wait()
    unpack(low_around, low_x, low_rows, low_recv, low_corner, low_r, h, pitch, w)

    def conv_one(b, sums):
        pairs = tap_pairs(low_x, PAD + b * low_r * pitch, low_r * pitch, 0.0)
        own = pairs.reshape(low_r, pitch, 256)[2 : h + 4, 8 : 8 + w]
        low_s[b] = own.astype(BF16)
        lines = jnp.sum(own.astype(BF16).astype(F32), axis=1)
        tap_sums = [
            sums[2 + tap] + jnp.sum(lines[tap : tap + h], axis=0, keepdims=True)
            for tap in range(3)
        ]
        pairs = pairs.astype(BF16)
        count = y_one_r * pitch
        taps = jnp.concatenate([pairs[pitch * a : pitch * a + count] for a in range(3)], axis=1)
        value = dot(taps, w_one[...]).reshape(y_one_r, pitch, 128)
        y_one_s[b] = value
        own = value[2 : h + 2, 8 : 8 + w].reshape(h * w, 128)
        return (
            sums[0] + jnp.sum(own, axis=0, keepdims=True),
            sums[1] + jnp.sum(own * own, axis=0, keepdims=True),
            *tap_sums,
        )

    def count_ones(b, total):
        ones = (target_in[b].reshape(height * breadth, 80).astype(F32) == 1.0).astype(F32)
        return total + jnp.sum(ones, axis=0, keepdims=True)

    nothing = jnp.zeros((1, 128), F32)
    tap_none = jnp.zeros((1, 256), F32)
    sums = lax.fori_loop(0, images, conv_one, (nothing, nothing, tap_none, tap_none, tap_none))
    tap_sums = sums[2:]
    for k in (3, 4):
        loads[k].wait()
    ones = lax.fori_loop(0, images, count_ones, jnp.zeros((1, 80), F32))
    base = row_at * (height * breadth * col_count) + col_at * breadth
    slot = lax.broadcasted_iota(jnp.int32, (1, 128), 1)
    objects = 0
    spot_out[...] = jnp.full((8, 128), -(2**30), jnp.int32)
    for b in range(images):
        amount = count_ref[b]
        objects = objects + amount
        spot_out[b : b + 1, :] = jnp.where(
            slot < amount, index_in[b : b + 1, :] - base, -(2**30)
        )
    leading = jnp.logical_and(row_at == 0, col_at == 0).astype(F32)
    sum_src = first_scratch[0]
    sum_src[...] = jnp.zeros((8, 128), F32)
    sum_src[0:1, :] = sums[0]
    sum_src[1:2, :] = sums[1]
    sum_src[2:3, 0:80] = ones
    sum_src[3:4, :] = jnp.full((1, 128), objects.astype(F32) * leading)
    first_total = Total(*first_scratch)
    first_total.begin()
    stores = [
        pltpu.make_async_copy(y_one_s, y_one_out, out_sems.at[0, 0]),
        pltpu.make_async_copy(low_s, low_out, out_sems.at[0, 1]),
    ]
    for store in stores:
        store.start()

    loads[9].wait()
    stack_weight(w_two, conv_two_in)
    skip_around.wait()
    unpack(
        skip_around, skip_x, skip_rows, skip_recv, skip_corner, skip_r, height, wide, breadth
    )
    first_total.middle()
    for k in range(5, 9):
        loads[k].wait()
    totals = first_total.end()
    mean_one = totals[0:1] / cells_low
    scale_one = lax.rsqrt(totals[1:2] / cells_low - mean_one * mean_one + EPSILON)
    gain_one, shift_one = twice(param_in[0]), twice(param_in[1])
    gain_two, shift_two = twice(param_in[2]), twice(param_in[3])
    stat_out[...] = jnp.zeros((24, 128), F32)
    stat_out[0:1, :] = mean_one
    stat_out[1:2, :] = scale_one
    positives = jnp.sum(totals[2:3, 0:80], axis=1, keepdims=True)
    stat_out[4:5, :] = jnp.broadcast_to(1.0 / positives, (1, 128))
    stat_out[5:6, :] = 0.5 / totals[3:4]
    stat_out[6:7, :] = gain_one
    stat_out[7:8, :] = shift_one
    stat_out[8:9, :] = gain_two
    stat_out[9:10, :] = shift_two
    ends = (row_at > 0, row_at < row_count - 1, col_at > 0, col_at < col_count - 1)
    for k, inner in enumerate(ends):
        stat_out[10 + k : 11 + k, :] = jnp.full((1, 128), inner.astype(F32))

    def conv_two(b, sums):
        normed = (y_one_s[b] - mean_one) * scale_one
        value, _ = silu_parts(normed * gain_one + shift_one)
        act_s[0 : y_one_r * pitch, :] = value.astype(BF16).astype(F32).reshape(
            y_one_r * pitch, 128
        )
        clear(
            act_s, 0, y_one_r, pitch, (0, 2), (h + 2, h + 4), (6, 8), (8 + w, 10 + w)
        )
        act = act_s[0 : y_one_r * pitch, :].reshape(y_one_r, pitch, 128)
        odd = 0.75 * act[:-1] + 0.25 * act[1:]
        even = 0.75 * act[1:] + 0.25 * act[:-1]
        tall = jnp.stack([odd, even], axis=1).reshape(skip_r * pitch, 128)
        row_s[PAD : PAD + skip_r * pitch, :] = tall
        count = skip_r * pitch
        before = row_s[PAD - 1 : PAD - 1 + count, :]
        behind = row_s[PAD + 1 : PAD + 1 + count, :]
        up_s[pl.ds(0, count, stride=2), :] = 0.75 * tall + 0.25 * before
        up_s[pl.ds(1, count, stride=2), :] = 0.75 * tall + 0.25 * behind
        start = PAD + b * skip_r * wide
        whole = pl.ds(start, skip_r * wide)
        up = up_s[...].reshape(skip_r, 2 * pitch, 128)[:, 8 : 8 + wide]
        merged = up + skip_x[whole, :].reshape(skip_r, wide, 128)
        skip_x[whole, :] = merged.astype(BF16).astype(F32).reshape(skip_r * wide, 128)
        clear(
            skip_x,
            start,
            skip_r,
            wide,
            (0, 3),
            (height + 3, height + 6),
            (5, 8),
            (8 + breadth, 11 + breadth),
        )
        pairs = tap_pairs(skip_x, start, skip_r * wide, 0.0)
        merged_s[b] = pairs.reshape(skip_r, wide, 256)[2 : height + 4, 8 : 8 + breadth].astype(
            BF16
        )
        pltpu.make_async_copy(merged_s.at[b], merged_out.at[b], out_sems.at[1, b]).start()
        pairs = pairs.astype(BF16)
        count = y_two_r * wide
        taps = jnp.concatenate([pairs[wide * a : wide * a + count] for a in range(3)], axis=1)
        value = dot(taps, w_two[...]).reshape(y_two_r, wide, 128)
        y_two_s[b] = value
        pltpu.make_async_copy(y_two_s.at[b], y_two_out.at[b], out_sems.at[2, b]).start()
        own = value[2 : height + 2, 8 : 8 + breadth].reshape(height * breadth, 128)
        return (
            sums[0] + jnp.sum(own, axis=0, keepdims=True),
            sums[1] + jnp.sum(own * own, axis=0, keepdims=True),
        )

    row_s[0:PAD, :] = jnp.zeros((PAD, 128), F32)
    row_s[PAD + skip_r * pitch :, :] = jnp.zeros((PAD, 128), F32)
    sums = lax.fori_loop(0, images, conv_two, (nothing, nothing))
    sum_src = second_scratch[0]
    sum_src[...] = jnp.zeros((8, 128), F32)
    sum_src[0:1, :] = sums[0]
    sum_src[1:2, :] = sums[1]
    for tap in range(3):
        for part in range(2):
            line = 2 + 2 * tap + part
            sum_src[line : line + 1, :] = tap_sums[tap][:, 128 * part : 128 * part + 128]
    second_total = Total(*second_scratch)
    second_total.begin()
    g_low[...] = jnp.zeros_like(g_low)
    own_low[...] = jnp.zeros_like(own_low)

    def normed_taps(b, carry):
        normed = (y_one_s[b, 2 : h + 2] - mean_one) * scale_one
        own_low[2 * w : (h + 2) * w, :] = normed[:, 8 : 8 + w].reshape(h * w, 128)
        g_low[...] += product_of_parts(
            low_s[b].reshape((h + 2) * w, 256), shifted_taps(own_low, h, w)
        )
        return carry

    lax.fori_loop(0, images, normed_taps, 0)
    fold(tiles_out, 0, g_low)
    second_total.middle()
    totals = second_total.end()
    mean_two = totals[0:1] / cells_high
    scale_two = lax.rsqrt(totals[1:2] / cells_high - mean_two * mean_two + EPSILON)
    stat_out[2:3, :] = mean_two
    stat_out[3:4, :] = scale_two
    stat_out[16:22, :] = totals[2:8]

    for store in stores:
        store.wait()
    for b in range(images):
        pltpu.make_async_copy(merged_s.at[b], merged_out.at[b], out_sems.at[1, b]).wait()
        pltpu.make_async_copy(y_two_s.at[b], y_two_out.at[b], out_sems.at[2, b]).wait()


def rise(
    low_map,
    skip_map,
    target,
    conv_one,
    conv_two,
    gain_one,
    shift_one,
    gain_two,
    shift_two,
    index,
    count,
):
    images, h, w, _ = low_map.shape
    _, height, breadth, _ = skip_map.shape
    pitch, wide = w + 16, breadth + 16
    low_r, skip_r = h + 6, height + 6
    half = images // 2
    vmem = pl.BlockSpec(memory_space=pltpu.VMEM)
    hbm = pl.BlockSpec(memory_space=pl.ANY)
    kept = [
        jax.ShapeDtypeStruct((images, height + 4, wide, 128), F32),
        jax.ShapeDtypeStruct((images, h + 4, pitch, 128), F32),
        jax.ShapeDtypeStruct((images, height + 2, breadth, 256), BF16),
        jax.ShapeDtypeStruct((images, h + 2, w, 256), BF16),
    ]
    return pl.pallas_call(
        rise_body,
        in_specs=[hbm] * 10 + [pl.BlockSpec(memory_space=pltpu.SMEM)],
        out_specs=[hbm] * 4 + [vmem] * 3,
        out_shape=kept
        + [jax.ShapeDtypeStruct((24, 128), F32), jax.ShapeDtypeStruct((8, 128), jnp.int32)]
        + [jax.ShapeDtypeStruct((conv_tiles(36), 8, 128), F32)],
        scratch_shapes=[
            pltpu.VMEM(low_map.shape, BF16),
            pltpu.VMEM(skip_map.shape, BF16),
            pltpu.VMEM(target.shape, BF16),
            pltpu.VMEM((3, 192, 64), BF16),
            pltpu.VMEM((3, 192, 64), BF16),
            pltpu.VMEM((4, 1, 64), F32),
            pltpu.VMEM(index.shape, jnp.int32),
        ]
        + [pltpu.VMEM(array.shape, array.dtype) for array in kept]
        + [
            pltpu.VMEM((2 * PAD + (images * low_r + 8) * pitch, 128), F32),
            pltpu.VMEM((2 * PAD + (images * skip_r + 8) * wide, 128), F32),
            pltpu.VMEM((rounded_up(h + 4, 8) * pitch, 128), F32),
            pltpu.VMEM((2 * PAD + skip_r * pitch, 128), F32),
            pltpu.VMEM((2 * skip_r * pitch, 128), F32),
            pltpu.VMEM((768, 128), BF16),
            pltpu.VMEM((768, 128), BF16),
            pltpu.VMEM((256, 256), F32),
            pltpu.VMEM(((h + 4) * w, 128), F32),
            pltpu.VMEM((2, images, 3, w, 64), BF16),
            pltpu.VMEM((2, images, 3, breadth, 64), BF16),
            pltpu.VMEM((2, 3 * half, rounded_up(h, 16), 128), BF16),
            pltpu.VMEM((2, 3 * half, rounded_up(h, 16), 128), BF16),
            pltpu.VMEM((2, 4, half, 32, 128), BF16),
            pltpu.VMEM((2, 3 * half, rounded_up(height, 16), 128), BF16),
            pltpu.VMEM((2, 3 * half, rounded_up(height, 16), 128), BF16),
            pltpu.VMEM((2, 4, half, 32, 128), BF16),
            total_scratch(8),
            total_scratch(8),
            pltpu.SemaphoreType.DMA((10,)),
            pltpu.SemaphoreType.DMA((4, max(images, 2))),
            pltpu.SemaphoreType.DMA((2, 2, 8)),
        ],
        compiler_params=pltpu.CompilerParams(
            collective_id=1, has_side_effects=True, vmem_limit_bytes=60 * MIB
        ),
        name="rise",
    )(
        low_map,
        skip_map,
        target,
        conv_one,
        conv_two,
        gain_one,
        shift_one,
        gain_two,
        shift_two,
        index,
        count,
    )


def levels_of(tiles):
    batch, row, col = place()
    batches, rows, cols = extents()
    pairs = 2 if cols % 2 == 0 else 1
    outer = cols // pairs
    levels = []

    def add(count, mine, device_of):
        left = (levels[-1][3] if levels else tiles) // count
        partners = []
        for over in range(1, count):
            other = lax.rem(mine + over, count)
            partners.append((other, device_of(other)))
        levels.append((count, mine, partners, left))

    low = lax.rem(col, pairs)
    add(pairs, low, lambda k: (batch, row, col - low + k))
    add(
        outer * batches,
        lax.div(col, pairs) * batches + batch,
        lambda k: (lax.rem(k, batches), row, lax.div(k, batches) * pairs + low),
    )
    add(rows, row, lambda k: (batch, k, col))
    return levels


def level_sizes(tiles):
    batches, rows, cols = extents()
    pairs = 2 if cols % 2 == 0 else 1
    sizes = []
    for count in (pairs, cols // pairs * batches, rows):
        tiles = tiles // count
        sizes.append((count, tiles))
    return sizes


class Scatter:
    def __init__(self, source, mids, slots, sems):
        self.parts = [source, *mids]
        self.slots, self.sems = slots, sems
        self.levels = levels_of(source.shape[0])

    def begin(self, level):
        _, _, partners, left = self.levels[level]
        self.copies = [
            remote(
                self.parts[level].at[pl.ds(other * left, left)],
                self.slots[level].at[k],
                self.sems.at[level, 0, k],
                self.sems.at[level, 1, k],
                device,
            )
            for k, (other, device) in enumerate(partners)
        ]
        start_all(self.copies)

    def end(self, level):
        _, mine, partners, left = self.levels[level]
        wait_all(self.copies)
        total = self.parts[level][pl.ds(mine * left, left)].astype(F32)
        for k in range(len(partners)):
            total = total + self.slots[level][k].astype(F32)
        self.parts[level + 1][...] = total.astype(BF16)


class Gather:
    def __init__(self, full, sems):
        self.full, self.sems = full, sems
        self.levels = levels_of(full.shape[0])

    def span(self, level):
        base = 0
        for _, mine, _, left in self.levels[: level + 1]:
            base = base + mine * left
        return pl.ds(base, self.levels[level][3])

    def begin(self, level):
        part = self.full.at[self.span(level)]
        self.copies = [
            remote(part, part, self.sems.at[level, 0, k], self.sems.at[level, 1, k], device)
            for k, (_, device) in enumerate(self.levels[level][2])
        ]
        start_all(self.copies)

    def end(self):
        wait_all(self.copies)


def scatter_scratch(tiles):
    sizes = level_sizes(tiles)
    return (
        tuple(pltpu.VMEM((left, 16, 128), BF16) for _, left in sizes[:-1]),
        tuple(pltpu.VMEM((count - 1, left, 16, 128), BF16) for count, left in sizes),
        level_sems(),
    )


def level_sems():
    return pltpu.SemaphoreType.DMA((3, 2, max(count for count, _ in level_sizes(1)) - 1))


class PlaneReducer:
    def __init__(self, source, slots, mid, row_slots, full, sems):
        batch, row, col = place()
        batches, rows, cols = extents()
        self.source, self.slots, self.mid = source, slots, mid
        self.row_slots, self.full, self.sems = row_slots, full, sems
        self.share = mid.shape[0]
        self.mine = batch * cols + col
        self.row = row

    def begin(self):
        _, _, cols = extents()
        self.copies = []
        for k, (batch, row, col) in enumerate(plane_partners()):
            other = batch * cols + col
            part = self.source.at[pl.ds(other * self.share, self.share)]
            self.copies.append(
                remote(
                    part, self.slots.at[k], self.sems.at[0, 0, k], self.sems.at[0, 1, k],
                    (batch, row, col),
                )
            )
        start_all(self.copies)

    def middle(self):
        wait_all(self.copies)
        total = self.source[pl.ds(self.mine * self.share, self.share)]
        for k in range(self.slots.shape[0]):
            total = total + self.slots[k]
        self.mid[...] = total
        self.copies = [
            remote(
                self.mid, self.row_slots.at[self.row], self.sems.at[1, 0, k],
                self.sems.at[1, 1, k], partner,
            )
            for k, partner in enumerate(row_partners())
        ]
        start_all(self.copies)
        self.row_slots[self.row] = total

    def last(self):
        wait_all(self.copies)
        self.full[pl.ds(self.mine * self.share, self.share)] = slot_sum(self.row_slots)
        part = self.full.at[pl.ds(self.mine * self.share, self.share)]
        self.copies = [
            remote(part, part, self.sems.at[2, 0, k], self.sems.at[2, 1, k], partner)
            for k, partner in enumerate(plane_partners())
        ]
        start_all(self.copies)

    def end(self):
        wait_all(self.copies)


def plane_scratch(tiles):
    batches, rows, cols = extents()
    planes = batches * cols
    share = tiles // planes
    most = max(planes, rows) - 1
    return [
        pltpu.VMEM((tiles, 8, 128), F32),
        pltpu.VMEM((planes - 1, share, 8, 128), F32),
        pltpu.VMEM((share, 8, 128), F32),
        pltpu.VMEM((rows, share, 8, 128), F32),
        pltpu.SemaphoreType.DMA((3, 2, most)),
    ]


def conv_tiles(tiles):
    batches, _, cols = extents()
    planes = batches * cols
    return -(-tiles // planes) * planes


def fold(target, first, grads):
    low = lower_half((1, 128))
    last = grads[0:192, 128:256]
    target[first : first + 24] = grads[0:192, 0:128].reshape(24, 8, 128)
    target[first + 24 : first + 36] = jnp.where(low, last[0:96], swapped(last[96:192])).reshape(
        12, 8, 128
    )
    if target.shape[0] > first + 36:
        target[first + 36 :] = jnp.zeros((target.shape[0] - first - 36, 8, 128), F32)


def unfold(source, first):
    pairs = source[first : first + 24].reshape(192, 128)
    last = source[first + 24 : first + 36].reshape(96, 128)
    return [
        pairs[:, 0:64],
        swapped(pairs)[:, 0:64],
        jnp.concatenate([last[:, 0:64], swapped(last)[:, 0:64]], axis=0),
    ]


def shifted_taps(buffer, rows, line):
    count = (rows + 2) * line
    views = [buffer[(2 - tap) * line : (2 - tap) * line + count, :] for tap in range(3)]
    low = lower_half((1, 128))
    return jnp.concatenate(
        [jnp.where(low, views[0], views[1]), jnp.where(low, views[2], 0.0)], axis=1
    )


def product_of_parts(left, right):
    high = right.astype(BF16)
    rest = (right - high.astype(F32)).astype(BF16)
    return dot_left(left, high) + dot_left(left, rest)


def stack_back(target, source):
    for tap in range(3):
        for e in range(3):
            block = source[tap, 64 * e : 64 * e + 64, :].astype(F32)
            start = 256 * tap + 64 * e
            target[start : start + 64, :] = twice(block.T).astype(BF16)
        target[256 * tap + 192 : 256 * tap + 256, :] = jnp.zeros((64, 128), BF16)


def back_pairs(buffer, start, count):
    low = lower_half((1, 128))
    first = jnp.where(low, buffer[pl.ds(start + 1, count), :], buffer[pl.ds(start, count), :])
    second = jnp.where(low, buffer[pl.ds(start - 1, count), :], 0.0)
    return jnp.concatenate([first, second], axis=1).astype(BF16)


def slope_of(values):
    logistic = 0.5 * jnp.tanh(0.5 * values) + 0.5
    return logistic * (1.0 + values * (1.0 - logistic))


def fall_body(
    spread_ref,
    y_two_ref,
    stat_ref,
    load_ref,
    small_ref,
    tiles_ref,
    y_one_ref,
    merged_ref,
    low_ref,
    conv_ref,
    conv_one_ref,
    skip_out,
    zed_out,
    load_out,
    conv_out,
    conv_x_out,
    sums_out,
    last_out,
    weight_out,
    y_two_s,
    slope_s,
    y_one_s,
    merged_s,
    low_s,
    conv_s,
    load_s,
    skip_s,
    share_s,
    grad_x,
    zed_x,
    own_s,
    own_low_s,
    pair_s,
    narrow_s,
    w_two,
    g_two,
    g_one,
    total_s,
    strip_send,
    strip_recv,
    side_send,
    side_recv,
    corners,
    zed_send,
    zed_recv,
    edge_send,
    edge_recv,
    zed_corners,
    third_scratch,
    fourth_scratch,
    load_scratch,
    conv_x_scratch,
    conv_scratch,
    gather_sems,
    in_sems,
    map_sems,
    out_sems,
    strip_sems,
    zed_sems,
):
    images, rows, wide, _ = y_two_ref.shape
    height, breadth = rows - 4, wide - 16
    h, w = height // 2, breadth // 2
    pitch, ext = w + 16, height + 2
    zed_rows = h + 2
    half = images // 2
    _, row_at, col_at = place()
    batches, row_count, col_count = extents()
    cells_high = float(images * batches * height * row_count * breadth * col_count)
    low_half = lower_half((1, 128))
    mean_one, scale_one = stat_ref[0:1, :], stat_ref[1:2, :]
    mean_two, scale_two = stat_ref[2:3, :], stat_ref[3:4, :]
    gain_one, shift_one = stat_ref[6:7, :], stat_ref[7:8, :]
    gain_two, shift_two = stat_ref[8:9, :], stat_ref[9:10, :]
    top, bottom = stat_ref[10:11, :], stat_ref[11:12, :]
    left, right = stat_ref[12:13, :], stat_ref[13:14, :]

    def spread_load(b):
        start = PAD + (b * rows + 1) * wide
        return pltpu.make_async_copy(
            spread_ref.at[b], grad_x.at[pl.ds(start, ext * wide)], map_sems.at[0, b]
        )

    def y_two_load(b):
        return pltpu.make_async_copy(y_two_ref.at[b], y_two_s.at[b], map_sems.at[1, b])

    loads = [
        pltpu.make_async_copy(source, target, in_sems.at[k])
        for k, (source, target) in enumerate(
            (
                (load_ref, load_s),
                (tiles_ref, conv_x_scratch[0]),
                (conv_ref, conv_s.at[0]),
                (conv_one_ref, conv_s.at[1]),
                (merged_ref, merged_s),
                (y_one_ref, y_one_s),
                (low_ref, low_s),
            )
        )
    ]
    for b in range(images):
        spread_load(b).start()
    for b in range(images):
        y_two_load(b).start()
    for load in loads:
        load.start()
    grad_x[0:PAD, :] = jnp.zeros((PAD, 128), F32)
    tail = PAD + images * rows * wide
    grad_x[tail:, :] = jnp.zeros((grad_x.shape[0] - tail, 128), F32)
    for b in range(images):
        for line in (0, ext + 1):
            start = PAD + (b * rows + line) * wide
            grad_x[start : start + wide, :] = jnp.zeros((wide, 128), F32)
    greet()
    for b in range(images):
        spread_load(b).wait()
    for pair in range(half):
        for side, first in enumerate((1, ext - 2)):
            parts = []
            for image in (pair, pair + half):
                start = PAD + (image * rows + first) * wide
                parts.append(grad_x[start : start + 3 * wide, :])
            strip_send[side, pair] = jnp.where(low_half, parts[0], parts[1]).astype(BF16)
    around = Around(
        [strip_send.at[k] for k in range(2)]
        + [side_send.at[k] for k in range(2)]
        + [corners.at[0, k] for k in range(4)],
        [strip_recv.at[k] for k in range(2)]
        + [side_recv.at[k] for k in range(2)]
        + [corners.at[1, k] for k in range(4)],
        strip_sems,
    )
    around.start(range(2))
    for side, first in enumerate((7, 6 + breadth)):
        pack_columns(grad_x, side_send.at[side], images, rows, wide, 1, first, 3)
    for k, (up, along) in enumerate(AROUND[4:]):
        pack_corner(
            grad_x,
            corners.at[0, k],
            images,
            rows,
            wide,
            1 if up < 0 else height,
            7 if along < 0 else 6 + breadth,
            3,
        )
    around.start(range(2, 8))
    loads[0].wait()
    load_sum = Scatter(load_s, (*load_scratch[0], share_s), load_scratch[1], load_scratch[2])
    load_sum.begin(0)

    def begin(b, sums):
        y_two_load(b).wait()
        start = PAD + b * rows * wide
        clear(
            grad_x,
            start,
            rows,
            wide,
            (1, 2),
            (ext, ext + 1),
            (7, 8),
            (8 + breadth, 9 + breadth),
        )
        normed = (y_two_s[b] - mean_two) * scale_two
        slope = slope_of(normed * gain_two + shift_two)
        slope_s[b] = slope
        part = grad_x[pl.ds(start, rows * wide), :].reshape(rows, wide, 128)
        weighted = part * slope
        return sums[0] + fold_sum(weighted), sums[1] + fold_sum(weighted * normed)

    nothing = jnp.zeros((8, 128), F32)
    sums = lax.fori_loop(0, images, begin, (nothing, nothing))
    sum_src = third_scratch[0]
    sum_src[...] = jnp.zeros((16, 128), F32)
    sum_src[0:8, :] = small_ref[...]
    sum_src[8:9, :] = jnp.sum(sums[0], axis=0, keepdims=True)
    sum_src[9:10, :] = jnp.sum(sums[1], axis=0, keepdims=True)
    third_total = Total(*third_scratch)
    third_total.begin()
    load_sum.end(0)
    load_sum.begin(1)
    loads[2].wait()
    stack_back(w_two, conv_s.at[0])
    loads[3].wait()
    stack_back(weight_out, conv_s.at[1])
    g_two[...] = jnp.zeros_like(g_two)
    g_one[...] = jnp.zeros_like(g_one)
    own_s[...] = jnp.zeros_like(own_s)
    own_low_s[...] = jnp.zeros_like(own_low_s)
    narrow_s[...] = jnp.zeros_like(narrow_s)
    zed_x[...] = jnp.zeros_like(zed_x)
    third_total.middle()
    around.wait()

    def use(k):
        up, along = AROUND[k]
        row = height + 1 if up < 0 else 0
        column = 7 + breadth if along < 0 else 6
        if k < 2:
            for image in range(images):
                values = unpacked(strip_recv[k, image % half].astype(F32), image, images)
                start = PAD + (image * rows + row) * wide
                grad_x[start : start + 3 * wide, :] += values
        elif k < 4:
            unpack_columns(
                grad_x, side_recv.at[k - 2], images, rows, wide, 1, column, 3, ext, True
            )
        else:
            unpack_corner(
                grad_x, corners.at[1, k - 4], images, rows, wide, row, column, 3, True
            )

    around.each(use)

    loads[1].wait()
    conv_x_sum = PlaneReducer(*conv_x_scratch[:4], conv_x_out, conv_x_scratch[4])
    totals = third_total.end()
    sums_out[...] = totals
    conv_x_sum.begin()
    load_sum.end(1)
    load_sum.begin(2)
    factor_two = gain_two * scale_two
    shift_part, gain_part = totals[8:9] / cells_high, totals[9:10] / cells_high
    for k in (4, 5, 6):
        loads[k].wait()
    column = lax.broadcasted_iota(jnp.int32, (wide, 128), 0)
    keep = jnp.where(column < 8, left, 1.0)
    keep = jnp.where(column >= 8 + breadth, right, keep)

    def merge(b, sums):
        start = PAD + b * rows * wide
        whole = pl.ds(start, rows * wide)
        normed = (y_two_s[b] - mean_two) * scale_two
        grad_z = grad_x[whole, :].reshape(rows, wide, 128) * slope_s[b]
        grad_y = factor_two * (grad_z - shift_part - normed * gain_part)
        grad_y = (grad_y * keep).astype(BF16).astype(F32)
        grad_x[whole, :] = grad_y.reshape(rows * wide, 128)
        for line, flag in ((0, top), (ext, bottom)):
            span = pl.ds(start + line * wide, 2 * wide)
            grad_x[span, :] = grad_x[span, :] * flag
        own_s[2 * breadth : (height + 2) * breadth, :] = grad_y[
            2 : height + 2, 8 : 8 + breadth
        ].reshape(height * breadth, 128)
        source = merged_s[b].reshape(ext * breadth, 256)
        g_two[...] += dot_left(source, shifted_taps(own_s, height, breadth).astype(BF16))
        pair_s[...] = back_pairs(grad_x, start, rows * wide)
        count = ext * wide
        taps = jnp.concatenate(
            [pair_s[wide * (2 - a) : wide * (2 - a) + count, :] for a in range(3)], axis=1
        )
        merged_grad = dot(taps, w_two[...]).reshape(ext, wide, 128)
        skip_s[b] = merged_grad[1 : height + 1, 8 : 8 + breadth, 0:64]
        pltpu.make_async_copy(skip_s.at[b], skip_out.at[b], out_sems.at[0, b]).start()
        fine = (merged_grad * keep).astype(BF16).astype(F32).reshape(h + 1, 2, wide, 128)
        even, odd = fine[:, 0], fine[:, 1]
        even = jnp.concatenate([even[0:1] * top, even[1:]], axis=0)
        odd = jnp.concatenate([odd[:-1], odd[-1:] * bottom], axis=0)
        short = 0.75 * (odd[:-1] + even[1:]) + 0.25 * (even[:-1] + odd[1:])
        side = jnp.zeros((h, 8, 128), F32)
        count = h * 2 * pitch
        narrow_s[PAD : PAD + count, :] = jnp.concatenate([side, short, side], axis=1).reshape(
            count, 128
        )
        lines = [narrow_s[pl.ds(PAD + k, count // 2, stride=2), :] for k in (-1, 0, 1, 2)]
        act_grad = 0.75 * (lines[1] + lines[2]) + 0.25 * (lines[0] + lines[3])
        act_grad = act_grad.reshape(h, pitch, 128)
        normed = (y_one_s[b, 2 : h + 2] - mean_one) * scale_one
        slope = slope_of(normed * gain_one + shift_one)
        place_at = lax.broadcasted_iota(jnp.int32, (pitch, 128), 0)
        inner = jnp.logical_and(place_at >= 8, place_at < 8 + w)
        grad_z = jnp.where(inner, act_grad * slope, 0.0)
        spot = PAD + (b * zed_rows + 1) * pitch
        zed_x[pl.ds(spot, h * pitch), :] = grad_z.reshape(h * pitch, 128)
        own_low_s[2 * w : (h + 2) * w, :] = grad_z[:, 8 : 8 + w].reshape(h * w, 128)
        g_one[...] += product_of_parts(
            low_s[b].reshape((h + 2) * w, 256), shifted_taps(own_low_s, h, w)
        )
        return sums[0] + fold_sum(grad_z), sums[1] + fold_sum(grad_z * normed)

    sums = lax.fori_loop(0, half, merge, (nothing, nothing))
    gather = Gather(load_out, gather_sems)
    load_sum.end(2)
    load_out[gather.span(2)] = share_s[...]
    gather.begin(2)
    conv_x_sum.middle()
    sums = lax.fori_loop(half, images, merge, sums)
    last_src = fourth_scratch[0]
    last_src[...] = jnp.zeros((8, 128), F32)
    last_src[0:1, :] = jnp.sum(sums[0], axis=0, keepdims=True)
    last_src[1:2, :] = jnp.sum(sums[1], axis=0, keepdims=True)
    fourth_total = Total(*fourth_scratch)
    fourth_total.begin()
    gather.end()
    gather.begin(1)
    fold(conv_scratch[0], 0, g_two)
    fold(conv_scratch[0], 36, g_one)
    conv_sum = PlaneReducer(*conv_scratch[:4], conv_out, conv_scratch[4])
    conv_sum.begin()
    for pair in range(half):
        for side, line in enumerate((1, h)):
            parts = []
            for image in (pair, pair + half):
                start = PAD + (image * zed_rows + line) * pitch
                parts.append(zed_x[start : start + pitch, :])
            zed_send[side, pair] = jnp.where(low_half, parts[0], parts[1])
    for side, column in enumerate((8, 7 + w)):
        pack_columns(zed_x, edge_send.at[side], images, zed_rows, pitch, 1, column, 1)
    for k, (up, along) in enumerate(AROUND[4:]):
        pack_corner(
            zed_x,
            zed_corners.at[0, k],
            images,
            zed_rows,
            pitch,
            1 if up < 0 else h,
            8 if along < 0 else 7 + w,
            1,
        )
    zed_around = Around(
        [zed_send.at[k] for k in range(2)]
        + [edge_send.at[k] for k in range(2)]
        + [zed_corners.at[0, k] for k in range(4)],
        [zed_recv.at[k] for k in range(2)]
        + [edge_recv.at[k] for k in range(2)]
        + [zed_corners.at[1, k] for k in range(4)],
        zed_sems,
    )
    zed_around.start()
    fourth_total.middle()
    conv_x_sum.last()
    conv_sum.middle()
    zed_around.wait()

    def use_zed(k):
        up, along = AROUND[k]
        row = h + 1 if up < 0 else 0
        column = 8 + w if along < 0 else 7
        if k < 2:
            for image in range(images):
                start = PAD + (image * zed_rows + row) * pitch
                zed_x[start : start + pitch, :] = unpacked(
                    zed_recv[k, image % half], image, images
                )
        elif k < 4:
            unpack_columns(
                zed_x, edge_recv.at[k - 2], images, zed_rows, pitch, 1, column, 1, h, False
            )
        else:
            unpack_corner(
                zed_x, zed_corners.at[1, k - 4], images, zed_rows, pitch, row, column, 1, False
            )

    zed_around.each(use_zed)

    def zed_store(b):
        return pltpu.make_async_copy(
            zed_x.at[pl.ds(PAD + b * zed_rows * pitch, zed_rows * pitch)],
            zed_out.at[b],
            out_sems.at[1, b],
        )

    for b in range(images):
        zed_store(b).start()
    last_out[...] = fourth_total.end()
    conv_sum.last()
    gather.end()
    gather.begin(0)
    conv_x_sum.end()
    conv_sum.end()
    gather.end()
    for b in range(images):
        zed_store(b).wait()
        pltpu.make_async_copy(skip_s.at[b], skip_out.at[b], out_sems.at[0, b]).wait()


def fall(
    spread, y_two, stats, load, small, tiles_x, y_one, merged, low, conv_two, conv_one
):
    images, rows, wide, _ = y_two.shape
    height, breadth = rows - 4, wide - 16
    h, w = height // 2, breadth // 2
    pitch, ext, zed_rows = w + 16, height + 2, h + 2
    half = images // 2
    tiles, parts_x, parts = load.shape[0], tiles_x.shape[0], conv_tiles(72)
    vmem = pl.BlockSpec(memory_space=pltpu.VMEM)
    hbm = pl.BlockSpec(memory_space=pl.ANY)
    lines, low_lines = rounded_up(ext, 16), rounded_up(h, 8)
    return pl.pallas_call(
        fall_body,
        in_specs=[hbm] * 2 + [vmem, hbm, vmem] + [hbm] * 6,
        out_specs=[hbm] * 2 + [vmem] * 6,
        out_shape=[
            jax.ShapeDtypeStruct((images, height, breadth, 64), F32),
            jax.ShapeDtypeStruct((images, zed_rows * pitch, 128), F32),
            jax.ShapeDtypeStruct((tiles, 16, 128), BF16),
            jax.ShapeDtypeStruct((parts, 8, 128), F32),
            jax.ShapeDtypeStruct((parts_x, 8, 128), F32),
            jax.ShapeDtypeStruct((16, 128), F32),
            jax.ShapeDtypeStruct((8, 128), F32),
            jax.ShapeDtypeStruct((768, 128), BF16),
        ],
        scratch_shapes=[
            pltpu.VMEM(y_two.shape, F32),
            pltpu.VMEM(y_two.shape, F32),
            pltpu.VMEM(y_one.shape, F32),
            pltpu.VMEM(merged.shape, BF16),
            pltpu.VMEM(low.shape, BF16),
            pltpu.VMEM((2, 3, 192, 64), BF16),
            pltpu.VMEM(load.shape, BF16),
            pltpu.VMEM((images, height, breadth, 64), F32),
            pltpu.VMEM((level_sizes(tiles)[-1][1], 16, 128), BF16),
            pltpu.VMEM((2 * PAD + (images * rows + lines - ext) * wide, 128), F32),
            pltpu.VMEM((2 * PAD + (images * zed_rows + 8) * pitch, 128), F32),
            pltpu.VMEM(((height + 4) * breadth, 128), F32),
            pltpu.VMEM(((h + 4) * w, 128), F32),
            pltpu.VMEM((rows * wide, 256), BF16),
            pltpu.VMEM((2 * PAD + h * 2 * pitch, 128), F32),
            pltpu.VMEM((768, 128), BF16),
            pltpu.VMEM((256, 256), F32),
            pltpu.VMEM((256, 256), F32),
            pltpu.VMEM((2, 8, 128), F32),
            pltpu.VMEM((2, half, 3 * wide, 128), BF16),
            pltpu.VMEM((2, half, 3 * wide, 128), BF16),
            pltpu.VMEM((2, 3 * half, lines, 128), BF16),
            pltpu.VMEM((2, 3 * half, lines, 128), BF16),
            pltpu.VMEM((2, 4, half, 32, 128), BF16),
            pltpu.VMEM((2, half, pitch, 128), F32),
            pltpu.VMEM((2, half, pitch, 128), F32),
            pltpu.VMEM((2, half, low_lines, 128), F32),
            pltpu.VMEM((2, half, low_lines, 128), F32),
            pltpu.VMEM((2, 4, half, 8, 128), F32),
            total_scratch(16),
            total_scratch(8),
            scatter_scratch(tiles),
            plane_scratch(parts_x),
            plane_scratch(parts),
            level_sems(),
            pltpu.SemaphoreType.DMA((7,)),
            pltpu.SemaphoreType.DMA((2, images)),
            pltpu.SemaphoreType.DMA((2, images)),
            pltpu.SemaphoreType.DMA((2, 8)),
            pltpu.SemaphoreType.DMA((2, 8)),
        ],
        compiler_params=pltpu.CompilerParams(
            collective_id=2, has_side_effects=True, vmem_limit_bytes=60 * MIB
        ),
        name="fall",
    )(spread, y_two, stats, load, small, tiles_x, y_one, merged, low, conv_two, conv_one)


def finish_body(
    cells_low,
    load_ref,
    rest_ref,
    conv_ref,
    conv_x_ref,
    sums_ref,
    last_ref,
    stat_ref,
    zed_ref,
    y_one_ref,
    weight_ref,
    skip_ref,
    conv_one_out,
    gain_one_out,
    shift_one_out,
    conv_two_out,
    gain_two_out,
    shift_two_out,
    head_out,
    head_b_out,
    heat_w_out,
    heat_b_out,
    box_w_out,
    box_b_out,
    low_out,
    skip_out,
    zed_x,
):
    step = pl.program_id(0)
    each, h, w, _ = low_out.shape
    pitch = w + 16
    rows = h + 2
    factor = stat_ref[6:7, :] * stat_ref[1:2, :]
    shift_low, gain_low = last_ref[0:1, :] / cells_low, last_ref[1:2, :] / cells_low
    skip_out[...] = skip_ref[...]
    for column in range(head_out.shape[3] // 128):
        block = load_ref[36 * column : 36 * column + 36].astype(F32)
        head_out[:, :, :, 128 * column : 128 * column + 128] = block.reshape(3, 3, 64, 128)

    @pl.when(step == 0)
    def _():
        zed_x[0:PAD, :] = jnp.zeros((PAD, 128), F32)
        zed_x[PAD + rows * pitch :, :] = jnp.zeros((PAD, 128), F32)
        spread = stat_ref[16:24, :].T
        ones = unfold(conv_ref, 36)
        normed = unfold(conv_x_ref, 0)
        for tap, part in enumerate(unfold(conv_ref, 0)):
            conv_two_out[tap] = part.reshape(3, 64, 64)
            count = jnp.concatenate(
                [spread[:, 2 * tap : 2 * tap + 1], spread[0:64, 2 * tap + 1 : 2 * tap + 2]], axis=0
            )
            value = ones[tap] - count * shift_low[:, 0:64] - normed[tap] * gain_low[:, 0:64]
            conv_one_out[tap] = (value * factor[:, 0:64]).reshape(3, 64, 64)
        for column in range(6):
            span = slice(128 * column, 128 * column + 128)
            head_b_out[span] = sums_ref[column : column + 1, :].reshape(128)
        for part in range(2):
            span = slice(128 * part, 128 * part + 128)
            heat_w_out[:, span] = rest_ref[5 * part : 5 * part + 5].astype(F32).reshape(80, 128)
            for box in range(2):
                block = rest_ref[10 + 2 * box + part].astype(F32)
                box_w_out[box, :, span] = block[2 * box : 2 * box + 2, :]
            box_b_out[part : part + 1, :] = sums_ref[7:8, 2 * part : 2 * part + 2]
        heat_b_out[...] = sums_ref[6:7, 0:80]
        shift_two_out[...] = sums_ref[8:9, 0:64]
        gain_two_out[...] = sums_ref[9:10, 0:64]
        shift_one_out[...] = last_ref[0:1, 0:64]
        gain_one_out[...] = last_ref[1:2, 0:64]

    for b in range(each):
        normed = (y_one_ref[b, 1 : h + 3] - stat_ref[0:1, :]) * stat_ref[1:2, :]
        grad_z = zed_ref[b].reshape(rows, pitch, 128)
        grad_y = factor * (grad_z - shift_low - normed * gain_low)
        column = lax.broadcasted_iota(jnp.int32, (pitch, 128), 0)
        keep = jnp.where(column < 8, stat_ref[12:13, :], 1.0)
        keep = jnp.where(column >= 8 + w, stat_ref[13:14, :], keep)
        grad_y = (grad_y * keep).astype(BF16).astype(F32)
        zed_x[PAD : PAD + rows * pitch, :] = grad_y.reshape(rows * pitch, 128)
        for line, row in ((0, 10), (rows - 1, 11)):
            span = slice(PAD + line * pitch, PAD + (line + 1) * pitch)
            zed_x[span, :] = zed_x[span, :] * stat_ref[row : row + 1, :]
        pairs = back_pairs(zed_x, PAD, rows * pitch)
        count = h * pitch
        taps = jnp.concatenate(
            [pairs[pitch * (2 - a) : pitch * (2 - a) + count] for a in range(3)], axis=1
        )
        grad = dot(taps, weight_ref[...]).reshape(h, pitch, 128)
        low_out[b] = grad[:, 8 : 8 + w, 0:64]


def finish(load, conv, conv_x, sums, last, stats, zed, y_one, weight, skip):
    images, y_rows, pitch, _ = y_one.shape
    h, w = y_rows - 4, pitch - 16
    batches, row_count, col_count = extents()
    cells = float(images * batches * h * row_count * w * col_count)
    span = zed.shape[1]
    steps = 2
    each = images // steps
    shapes = [
        (3, 3, 64, 64),
        (1, 64),
        (1, 64),
        (3, 3, 64, 64),
        (1, 64),
        (1, 64),
        (3, 3, 64, 768),
        (768,),
        (80, 256),
        (1, 80),
        (2, 2, 256),
        (2, 2),
        (images, h, w, 64),
        skip.shape,
    ]
    whole = lambda shape: pl.BlockSpec(shape, lambda c: (0,) * len(shape))
    part = lambda shape: pl.BlockSpec(shape, lambda c: (c,) + (0,) * (len(shape) - 1))
    out_specs = [whole(shape) for shape in shapes]
    out_specs[6] = pl.BlockSpec((3, 3, 64, 768 // steps), lambda c: (0, 0, 0, c))
    out_specs[12] = part((each, h, w, 64))
    out_specs[13] = part((each,) + skip.shape[1:])
    return pl.pallas_call(
        functools.partial(finish_body, cells),
        grid=(steps,),
        in_specs=[
            part((216 // steps, 16, 128)),
            pl.BlockSpec((36, 16, 128), lambda c: (6, 0, 0)),
        ]
        + [whole(array.shape) for array in (conv, conv_x, sums, last, stats)]
        + [
            part((each, span, 128)),
            part((each, y_rows, pitch, 128)),
            whole(weight.shape),
            part((each,) + skip.shape[1:]),
        ],
        out_specs=out_specs,
        out_shape=[jax.ShapeDtypeStruct(shape, F32) for shape in shapes],
        scratch_shapes=[
            pltpu.VMEM((2 * PAD + span, 128), F32),
        ],
        compiler_params=pltpu.CompilerParams(vmem_limit_bytes=60 * MIB),
        name="finish",
    )(load, load, conv, conv_x, sums, last, stats, zed, y_one, weight, skip)


def local(
    low_map,
    skip_map,
    conv_first,
    gain_first,
    shift_first,
    conv_second,
    gain_second,
    shift_second,
    head_conv,
    head_bias,
    heat_weight,
    heat_bias,
    box_weight,
    box_bias,
    heat_target,
    box_target,
    obj_index,
    obj_count,
):
    batches, rows, cols = extents()
    devices = batches * rows * cols
    conv_one = conv_first.reshape(3, 192, 64)
    conv_two = conv_second.reshape(3, 192, 64)
    y_two, y_one, merged, low, stats, spot, tiles_x = rise(
        low_map,
        skip_map,
        heat_target,
        conv_one,
        conv_two,
        gain_first.reshape(1, 64),
        shift_first.reshape(1, 64),
        gain_second.reshape(1, 64),
        shift_second.reshape(1, 64),
        obj_index,
        obj_count,
    )
    heat_map, box_map, spread, load, small = heads(
        y_two,
        heat_target,
        spot,
        box_target.transpose(0, 2, 1),
        stats,
        head_conv.reshape(3, 192, 768),
        head_bias,
        heat_weight.T,
        heat_bias.reshape(1, 80),
        box_weight.transpose(0, 2, 1),
        box_bias,
        devices,
    )
    images, ext, wide, _ = spread.shape
    grad_skip, zed, load, conv, conv_x, sums, last, weight = fall(
        spread.reshape(images, ext * wide, 128),
        y_two,
        stats,
        load,
        small,
        tiles_x,
        y_one,
        merged,
        low,
        conv_two,
        conv_one,
    )
    grads = finish(load, conv, conv_x, sums, last, stats, zed, y_one, weight, grad_skip)
    return (
        heat_map,
        box_map.transpose(0, 1, 3, 2),
        grads[12],
        grads[13],
        grads[0],
        grads[1].reshape(64),
        grads[2].reshape(64),
        grads[3],
        grads[4].reshape(64),
        grads[5].reshape(64),
        grads[6],
        grads[7],
        grads[8].T,
        grads[9].reshape(80),
        grads[10].transpose(0, 2, 1),
        grads[11],
    )


def solution(mesh):
    tile = P("batch", "row", "col", None)
    return jax.shard_map(
        local,
        mesh=mesh,
        in_specs=(tile, tile)
        + (P(),) * 12
        + (tile, P("batch", None, None), P("batch", None), P("batch")),
        out_specs=(tile,) * 4 + (P(),) * 12,
        check_vma=False,
    )
```

```python
import functools

import jax
import jax.numpy as jnp
from jax import lax
from jax.experimental import pallas as pl
from jax.experimental.pallas import tpu as pltpu
from jax.sharding import PartitionSpec as P

EPSILON = 1e-05
F32 = jnp.float32
BF16 = jnp.bfloat16
KEEP = (((1,), (1,)), ((), ()))
LEFT = (((0,), (0,)), ((), ()))
MIB = 1024 * 1024


def dot(left, right):
    return jnp.dot(left, right, preferred_element_type=F32)


def dot_keep(left, right):
    return lax.dot_general(left, right, KEEP, preferred_element_type=F32)


def dot_left(left, right):
    return lax.dot_general(left, right, LEFT, preferred_element_type=F32)


def three_parts(values):
    high = values.astype(BF16)
    rest = values - high.astype(F32)
    mid = rest.astype(BF16)
    return high, mid, (rest - mid.astype(F32)).astype(BF16)


def tile_count(devices):
    return -(-230 // (2 * devices)) * 2 * devices


def heads_body(
    map_side,
    y_two_ref,
    target_ref,
    spot_ref,
    goal_ref,
    stat_ref,
    conv_ref,
    bias_ref,
    heat_w_ref,
    heat_b_ref,
    box_w_ref,
    box_b_ref,
    heat_out,
    box_out,
    spread_out,
    load_out,
    small_out,
    feat_s,
    taps_ref,
    kernel_s,
    back_s,
    box_s,
    wide_s,
    grad_s,
    heat_grad_s,
    box_grad_s,
    heat_sum_s,
    box_sum_s,
):
    step = pl.program_id(0)
    each, height, breadth, _ = target_ref.shape
    image_cells = height * breadth
    cells = each * image_cells
    units = 256

    @pl.when(step == 0)
    def _():
        for tap in range(3):
            kernel_s[tap, 0:192, :] = (0.5 * conv_ref[tap].astype(F32)).astype(BF16)
            kernel_s[tap, 192:256, :] = jnp.zeros((64, 768), BF16)
        parts = three_parts(0.5 * bias_ref[...].reshape(1, 768))
        which = lax.broadcasted_iota(jnp.int32, (16, 768), 0)
        filled = jnp.zeros((16, 768), F32)
        for place in range(3):
            filled = jnp.where(which == place, parts[place].astype(F32), filled)
        kernel_s[1, 192:208, :] = filled.astype(BF16)
        for tap in range(3):
            for block in range(3):
                span = slice(256 * block, 256 * block + 256)
                back_s[span, 256 * tap : 256 * tap + 256] = (
                    kernel_s[tap, :, span].astype(F32).T.astype(BF16)
                )
        empty = jnp.zeros((2, 256), F32)
        for part in range(2):
            pieces = [empty, empty]
            pieces[part] = box_w_ref[part].astype(F32)
            box_s[part] = jnp.concatenate(pieces, axis=0).astype(BF16)
        grad_s[...] = jnp.zeros_like(grad_s)
        heat_grad_s[...] = jnp.zeros_like(heat_grad_s)
        box_grad_s[...] = jnp.zeros_like(box_grad_s)
        heat_sum_s[...] = jnp.zeros_like(heat_sum_s)
        box_sum_s[...] = jnp.zeros_like(box_sum_s)
        wide_s[...] = jnp.zeros_like(wide_s)

    ext, wide = height + 2, breadth + 16
    column = lax.broadcasted_iota(jnp.int32, (wide, 128), 0)
    keep = jnp.where(column < 8, stat_ref[12:13, :], 1.0)
    keep = jnp.where(column >= 8 + breadth, stat_ref[13:14, :], keep)
    feat_s[0:PAD, :] = jnp.zeros((PAD, 128), F32)
    feat_s[PAD + ext * wide :, :] = jnp.zeros((PAD, 128), F32)
    for image in range(each):
        normed = (y_two_ref[image, 1 : ext + 1] - stat_ref[2:3, :]) * stat_ref[3:4, :]
        feature, _ = silu_parts(normed * stat_ref[8:9, :] + stat_ref[9:10, :])
        feat_s[PAD : PAD + ext * wide, :] = (feature * keep).reshape(ext * wide, 128)
        for line, row in ((PAD, 10), (PAD + (ext - 1) * wide, 11)):
            feat_s[line : line + wide, :] = feat_s[line : line + wide, :] * stat_ref[row : row + 1]
        pairs = tap_pairs(feat_s, PAD, ext * wide, 1.0)
        taps_ref[image] = pairs.reshape(ext, wide, 256)[:, 8 : 8 + breadth].astype(BF16)

    taps = jnp.concatenate(
        [taps_ref[:, tap : tap + height].reshape(cells, 256) for tap in range(3)], axis=1
    )
    active, slope = [], []
    for block in range(3):
        weight = kernel_s[:, :, block * units : (block + 1) * units].reshape(768, units)
        hidden = dot(taps, weight)
        turn = jnp.tanh(hidden)
        above = 1.0 + turn
        product = hidden * above
        active.append(product.astype(BF16))
        slope.append(above + product * (1.0 - turn))

    logit = dot_keep(active[0], heat_w_ref[...]) + heat_b_ref[...]
    decay = jnp.exp(-jnp.abs(logit))
    large = 1.0 / (1.0 + decay)
    small = decay * large
    above = logit >= 0.0
    chance = jnp.where(above, large, small)
    heat_out[...] = chance.reshape(each, height, breadth, 80)
    target = target_ref[...].reshape(cells, 80).astype(F32)
    positive = target == 1.0
    side = jnp.where(positive, jnp.where(above, small, large), chance)
    value = jnp.where(positive, -logit, logit)
    soft = jnp.maximum(value, 0.0) + jnp.log(1.0 + decay)
    slant = side * side * (2.0 * (1.0 - side) * soft + side)
    gap = 1.0 - target
    gap = gap * gap
    weighting = jnp.where(positive, -1.0, gap * gap) * stat_ref[4:5, 0:80]
    logit_grad = weighting * slant
    logit_low = logit_grad.astype(BF16)

    box_bias = jnp.concatenate([box_b_ref[0:1, :], box_b_ref[1:2, :]], axis=1)
    boxes = dot_keep(active[1], box_s[0]) + dot_keep(active[2], box_s[1]) + box_bias
    turned = jnp.swapaxes(boxes.reshape(each * height, breadth, 4), 1, 2)
    box_out[...] = turned.reshape(each, height, 4, breadth)
    shape = (height, breadth, 128)
    cell = lax.broadcasted_iota(jnp.int32, shape, 0) * map_side
    cell = (cell + lax.broadcasted_iota(jnp.int32, shape, 1)).reshape(image_cells, 128)
    goals, hits = [], []
    for image in range(each):
        spots = spot_ref[pl.ds(step * each + image, 1), :]
        chosen = (cell == spots).astype(F32).astype(BF16)
        goal = jnp.zeros((image_cells, 4), F32)
        for part in three_parts(goal_ref[image]):
            goal = goal + dot_keep(chosen, part)
        goals.append(goal)
        hits.append(dot(chosen, jnp.ones((128, 4), BF16)))
    goals, hit = jnp.concatenate(goals, axis=0), jnp.concatenate(hits, axis=0)
    miss = boxes - goals
    lane = lax.broadcasted_iota(jnp.int32, (1, 4), 1)
    factor = jnp.where(lane < 2, 0.1, 1.0) * stat_ref[5:6, 0:4]
    box_grad = hit * factor * miss * lax.rsqrt(miss * miss + 1.0)
    box_low = box_grad.astype(BF16)

    heat_sum_s[...] += jnp.sum(logit_low.astype(F32).reshape(cells // 8, 8, 80), axis=0)
    box_sum_s[...] += jnp.sum(box_low.astype(F32).reshape(cells // 8, 8, 4), axis=0)
    heat_grad_s[...] += dot_left(logit_low, active[0])
    for part in range(2):
        box_grad_s[part] += dot_left(box_low, active[1 + part])

    back = [
        dot(logit_low, heat_w_ref[...]),
        dot(box_low, box_s[0]),
        dot(box_low, box_s[1]),
    ]
    grad_hidden = jnp.concatenate(
        [(back[block] * slope[block]).astype(BF16) for block in range(3)], axis=1
    )
    spread = []
    for tap in range(3):
        part = dot(grad_hidden, back_s[:, 256 * tap : 256 * tap + 256])
        spread.append(part.reshape(each, height, breadth, 256))
    inner = slice(16, 16 + breadth)
    for image in range(each):
        first, second, third = [part[image] for part in spread]
        wide_s[0:1, inner, :] = first[0:1]
        wide_s[1:2, inner, :] = first[1:2] + second[0:1]
        wide_s[2:height, inner, :] = first[2:] + second[1:-1] + third[:-2]
        wide_s[height : height + 1, inner, :] = second[-1:] + third[-2:-1]
        wide_s[height + 1 :, inner, :] = third[-1:]
        centre = swapped(wide_s[:, 8 : 8 + wide, 0:128])
        total = wide_s[:, 9 : 9 + wide, 0:128] + centre + wide_s[:, 7 : 7 + wide, 128:256]
        lanes = lax.broadcasted_iota(jnp.int32, total.shape, 2)
        spread_out[image] = jnp.where(lanes < 64, total, swapped(total))
    for tap in range(3):
        grad_s[tap] += dot_left(taps[:, 256 * tap : 256 * tap + 256], grad_hidden)

    @pl.when(step == pl.num_programs(0) - 1)
    def _():
        for column in range(6):
            span = slice(128 * column, 128 * column + 128)
            for tap in range(3):
                start = 36 * column + 12 * tap
                load_out[start : start + 12] = (
                    (0.5 * grad_s[tap, 0:192, span]).reshape(12, 16, 128).astype(BF16)
                )
            small_out[column : column + 1, :] = 0.5 * grad_s[1, 192:193, span]
        for half in range(2):
            span = slice(128 * half, 128 * half + 128)
            start = 216 + 5 * half
            load_out[start : start + 5] = heat_grad_s[:, span].reshape(5, 16, 128).astype(BF16)
            for part in range(2):
                padded = jnp.concatenate(
                    [box_grad_s[part, :, span], jnp.zeros((12, 128), F32)], axis=0
                )
                load_out[226 + 2 * part + half] = padded.astype(BF16)
        load_out[230:] = jnp.zeros((load_out.shape[0] - 230, 16, 128), BF16)
        small_out[6:8, :] = jnp.zeros((2, 128), F32)
        small_out[6:7, 0:80] = jnp.sum(heat_sum_s[...], axis=0, keepdims=True)
        small_out[7:8, 0:4] = jnp.sum(box_sum_s[...], axis=0, keepdims=True)


def heads(
    taps, target, spot, goal, stats, conv, bias, heat_w, heat_b, box_w, box_b, devices
):
    images, height, breadth, classes = target.shape
    each = 1
    tiles = tile_count(devices)
    whole = lambda *shape: pl.BlockSpec(shape, lambda b: (0,) * len(shape))
    part = lambda *shape: pl.BlockSpec((each,) + shape, lambda b: (b,) + (0,) * len(shape))
    cells = images * height * breadth
    return pl.pallas_call(
        functools.partial(heads_body, breadth * lax.axis_size("col")),
        grid=(images // each,),
        in_specs=[
            part(height + 4, breadth + 16, 128),
            part(height, breadth, classes),
            whole(8, 128),
            part(4, 128),
            whole(24, 128),
            whole(3, 192, 768),
            whole(768),
            whole(80, 256),
            whole(1, 80),
            whole(2, 2, 256),
            whole(2, 2),
        ],
        out_specs=[
            part(height, breadth, classes),
            part(height, 4, breadth),
            part(height + 2, breadth + 16, 128),
            whole(tiles, 16, 128),
            whole(8, 128),
        ],
        out_shape=[
            jax.ShapeDtypeStruct((images, height, breadth, classes), F32),
            jax.ShapeDtypeStruct((images, height, 4, breadth), F32),
            jax.ShapeDtypeStruct((images, height + 2, breadth + 16, 128), F32),
            jax.ShapeDtypeStruct((tiles, 16, 128), BF16),
            jax.ShapeDtypeStruct((8, 128), F32),
        ],
        scratch_shapes=[
            pltpu.VMEM((2 * PAD + (height + 2) * (breadth + 16), 128), F32),
            pltpu.VMEM((each, height + 2, breadth, 256), BF16),
            pltpu.VMEM((3, 256, 768), BF16),
            pltpu.VMEM((768, 768), BF16),
            pltpu.VMEM((2, 4, 256), BF16),
            pltpu.VMEM((height + 2, breadth + 32, 256), F32),
            pltpu.VMEM((3, 256, 768), F32),
            pltpu.VMEM((80, 256), F32),
            pltpu.VMEM((2, 4, 256), F32),
            pltpu.VMEM((8, 80), F32),
            pltpu.VMEM((8, 4), F32),
        ],
        compiler_params=pltpu.CompilerParams(vmem_limit_bytes=60 * MIB),
        cost_estimate=pl.CostEstimate(
            flops=cells * 576 * 768 * 6, bytes_accessed=12 * MIB, transcendentals=cells * 768
        ),
        name="heads",
    )(taps, target, spot, goal, stats, conv, bias, heat_w, heat_b, box_w, box_b)


MESH = pl.DeviceIdType.MESH


def rounded_up(value, step):
    return -(-value // step) * step


def place():
    return lax.axis_index("batch"), lax.axis_index("row"), lax.axis_index("col")


def extents():
    return lax.axis_size("batch"), lax.axis_size("row"), lax.axis_size("col")


def plane_partners():
    batch, row, col = place()
    batches, _, cols = extents()
    partners = []
    for over in range(batches):
        for along in range(cols):
            if over or along:
                partners.append(
                    (lax.rem(batch + over, batches), row, lax.rem(col + along, cols))
                )
    return partners


def row_partners():
    batch, row, col = place()
    rows = lax.axis_size("row")
    return [(batch, lax.rem(row + over, rows), col) for over in range(1, rows)]


def flat():
    batches, rows, cols = extents()
    return batches * rows * cols <= 8


def all_partners():
    batch, row, col = place()
    batches, rows, cols = extents()
    partners = []
    for over in range(batches):
        for up in range(rows):
            for along in range(cols):
                if over or up or along:
                    partners.append(
                        (
                            lax.rem(batch + over, batches),
                            lax.rem(row + up, rows),
                            lax.rem(col + along, cols),
                        )
                    )
    return partners


def greet():
    barrier = pltpu.get_barrier_semaphore()
    partners = all_partners() if flat() else plane_partners() + row_partners()
    for partner in partners:
        pl.semaphore_signal(barrier, inc=1, device_id=partner, device_id_type=MESH)
    batch, row, col = place()
    _, rows, cols = extents()
    expected = len(partners)
    for up in (-1, 1):
        for along in (-1, 1):
            fits = jnp.logical_and(row + up >= 0, row + up < rows)
            fits = jnp.logical_and(fits, jnp.logical_and(col + along >= 0, col + along < cols))
            expected = expected + fits.astype(jnp.int32)

            @pl.when(fits)
            def _(up=up, along=along):
                pl.semaphore_signal(
                    barrier,
                    inc=1,
                    device_id=(batch, row + up, col + along),
                    device_id_type=MESH,
                )

    return expected


def greeted(expected):
    pl.semaphore_wait(pltpu.get_barrier_semaphore(), expected)


def remote(source, target, send, recv, device):
    return pltpu.make_async_remote_copy(
        src_ref=source,
        dst_ref=target,
        send_sem=send,
        recv_sem=recv,
        device_id=device,
        device_id_type=MESH,
    )


def start_all(copies):
    for copy in copies:
        copy.start()


def wait_all(copies):
    for copy in copies:
        copy.wait()


def slot_sum(slots):
    total = slots[0]
    for k in range(1, slots.shape[0]):
        total = total + slots[k]
    return total


class Total:
    def __init__(self, source, slots, mid, row_slots, sems):
        self.source, self.slots, self.mid = source, slots, mid
        self.row_slots, self.sems = row_slots, sems

    def send(self, source, slots, mine, partners, step):
        self.copies = [
            remote(
                source,
                slots.at[mine],
                self.sems.at[step, 0, k],
                self.sems.at[step, 1, k],
                partner,
            )
            for k, partner in enumerate(partners)
        ]
        start_all(self.copies)
        slots[mine] = source[...]

    def begin(self):
        batch, row, col = place()
        _, rows, cols = extents()
        if flat():
            mine, partners = (batch * rows + row) * cols + col, all_partners()
        else:
            mine, partners = batch * cols + col, plane_partners()
        self.send(self.source, self.slots, mine, partners, 0)

    def middle(self):
        if not flat():
            wait_all(self.copies)
            self.mid[...] = slot_sum(self.slots)
            self.send(self.mid, self.row_slots, place()[1], row_partners(), 1)

    def end(self):
        wait_all(self.copies)
        return slot_sum(self.slots if flat() else self.row_slots)


def total_scratch(lines):
    batches, rows, cols = extents()
    slots = batches * cols * (rows if flat() else 1)
    return [
        pltpu.VMEM((lines, 128), F32),
        pltpu.VMEM((slots, lines, 128), F32),
        pltpu.VMEM((lines, 128), F32),
        pltpu.VMEM((rows, lines, 128), F32),
        pltpu.SemaphoreType.DMA((2, 2, max(slots, rows) - 1)),
    ]


AROUND = ((-1, 0), (1, 0), (0, -1), (0, 1), (-1, -1), (-1, 1), (1, -1), (1, 1))


class Around:
    def __init__(self, pieces, slots, sems):
        batch, row, col = place()
        _, rows, cols = extents()

        def exists(up, along):
            fits = jnp.logical_and(row + up >= 0, row + up < rows)
            return jnp.logical_and(fits, jnp.logical_and(col + along >= 0, col + along < cols))

        self.sends = [exists(up, along) for up, along in AROUND]
        self.comes = [exists(-up, -along) for up, along in AROUND]
        self.copies = [
            remote(pieces[k], slots[k], sems.at[0, k], sems.at[1, k], (batch, row + up, col + along))
            for k, (up, along) in enumerate(AROUND)
        ]

    def start(self, which=range(8)):
        for k in which:
            pl.when(self.sends[k])(self.copies[k].start)

    def wait(self, which=range(8)):
        for k in which:
            pl.when(self.comes[k])(self.copies[k].wait_recv)
            pl.when(self.sends[k])(self.copies[k].wait_send)

    def each(self, use, which=range(8)):
        for k in which:
            pl.when(self.comes[k])(functools.partial(use, k))


def twice(values):
    return jnp.concatenate([values, values], axis=-1)


def lower_half(shape):
    return lax.broadcasted_iota(jnp.int32, shape, len(shape) - 1) < 64


def swapped(values):
    return pltpu.roll(values, 64, len(values.shape) - 1)


def widened(values):
    rows, cols = values.shape[0], values.shape[1]
    side = jnp.zeros((rows, 8, 128), F32)
    return jnp.concatenate([side, twice(values.astype(F32)), side], axis=1)


def tap_pairs(buffer, start, count, fill):
    low = lower_half((1, 128))
    first = jnp.where(low, buffer[pl.ds(start - 1, count), :], buffer[pl.ds(start, count), :])
    second = jnp.where(low, buffer[pl.ds(start + 1, count), :], fill)
    return jnp.concatenate([first, second], axis=1)


def silu_parts(values):
    logistic = 0.5 * jnp.tanh(0.5 * values) + 0.5
    return values * logistic, logistic


PAD = 16


def row_loop(total, step, body, init):
    return lax.fori_loop(0, total // step, lambda k, carry: body(k * step, carry), init)


def fold_sum(values):
    return jnp.sum(values.reshape(-1, 8, 128), axis=0)


def clear(buffer, start, rows, pitch, tops, bottoms, lefts, rights):
    _, row_at, col_at = place()
    count = rounded_up(rows, 8)

    def clear_rows(span):
        first, last = span
        size = (last - first) * pitch
        buffer[pl.ds(start + first * pitch, size), :] = jnp.zeros((size, 128), F32)

    def clear_columns(span):
        for column in range(*span):
            buffer[pl.ds(start + column, count, stride=pitch), :] = jnp.zeros((count, 128), F32)

    pl.when(row_at == 0)(lambda: clear_rows(tops))
    pl.when(row_at == lax.axis_size("row") - 1)(lambda: clear_rows(bottoms))
    pl.when(col_at == 0)(lambda: clear_columns(lefts))
    pl.when(col_at == lax.axis_size("col") - 1)(lambda: clear_columns(rights))


def stack_weight(target, source):
    for tap in range(3):
        target[256 * tap : 256 * tap + 192, :] = twice(source[tap].astype(F32)).astype(BF16)
        target[256 * tap + 192 : 256 * tap + 256, :] = jnp.zeros((64, 128), BF16)


def unpacked(packed, image, images):
    low = lower_half((1, 128))
    keep = low if image < images // 2 else jnp.logical_not(low)
    return jnp.where(keep, packed, swapped(packed))


def pack_columns(buffer, target, images, rows, pitch, first_row, first, depth):
    low = lower_half((1, 128))
    half = images // 2
    count = target.shape[1]
    for pair in range(half):
        for j in range(depth):
            parts = [
                buffer[
                    pl.ds(
                        PAD + (image * rows + first_row) * pitch + first + j, count, stride=pitch
                    ),
                    :,
                ]
                for image in (pair, pair + half)
            ]
            target[depth * pair + j] = jnp.where(low, parts[0], parts[1]).astype(target.dtype)


def pack_corner(buffer, target, images, rows, pitch, first_row, first, depth):
    low = lower_half((1, 128))
    half = images // 2
    count = target.shape[1] // 8
    for pair in range(half):
        pieces = []
        for row in range(count):
            if row < depth:
                starts = [
                    PAD + (image * rows + first_row + row) * pitch + first
                    for image in (pair, pair + half)
                ]
                pieces.append(
                    jnp.where(
                        low,
                        buffer[starts[0] : starts[0] + 8, :],
                        buffer[starts[1] : starts[1] + 8, :],
                    )
                )
            else:
                pieces.append(jnp.zeros((8, 128), F32))
        target[pair] = jnp.concatenate(pieces, axis=0).astype(target.dtype)


def unpack_columns(buffer, source, images, rows, pitch, first_row, first, depth, lines, add):
    half = images // 2
    count = rounded_up(lines, 8)
    valid = lax.broadcasted_iota(jnp.int32, (count, 128), 0) < lines
    for image in range(images):
        for j in range(depth):
            packed = source[depth * (image % half) + j].astype(F32)
            values = unpacked(packed, image, images)[:count]
            spots = pl.ds(
                PAD + (image * rows + first_row) * pitch + first + j, count, stride=pitch
            )
            if add:
                values = buffer[spots, :] + jnp.where(valid, values, 0.0)
            elif count > lines:
                values = jnp.where(valid, values, buffer[spots, :])
            buffer[spots, :] = values


def unpack_corner(buffer, source, images, rows, pitch, first_row, first, depth, add):
    half = images // 2
    valid = lax.broadcasted_iota(jnp.int32, (8, 128), 0) < depth
    for image in range(images):
        packed = unpacked(source[image % half].astype(F32), image, images)
        for row in range(depth):
            start = PAD + (image * rows + first_row + row) * pitch + first
            old = buffer[start : start + 8, :]
            values = packed[8 * row : 8 * row + 8]
            if add:
                values = old + jnp.where(valid, values, 0.0)
            else:
                values = jnp.where(valid, values, old)
            buffer[start : start + 8, :] = values


def rise_body(
    low_ref,
    skip_ref,
    target_ref,
    conv_one_ref,
    conv_two_ref,
    gain_one_ref,
    shift_one_ref,
    gain_two_ref,
    shift_two_ref,
    index_ref,
    count_ref,
    y_two_out,
    y_one_out,
    merged_out,
    low_out,
    stat_out,
    spot_out,
    tiles_out,
    low_in,
    skip_in,
    target_in,
    conv_one_in,
    conv_two_in,
    param_in,
    index_in,
    y_two_s,
    y_one_s,
    merged_s,
    low_s,
    low_x,
    skip_x,
    act_s,
    row_s,
    up_s,
    w_one,
    w_two,
    g_low,
    own_low,
    low_rows,
    skip_rows,
    low_send,
    low_recv,
    low_corner,
    skip_send,
    skip_recv,
    skip_corner,
    first_scratch,
    second_scratch,
    in_sems,
    out_sems,
    strip_sems,
):
    images, h, w, _ = low_ref.shape
    height, breadth = skip_ref.shape[1], skip_ref.shape[2]
    batch_at, row_at, col_at = place()
    batches, row_count, col_count = extents()
    pitch, wide = w + 16, breadth + 16
    low_r, y_one_r = h + 6, h + 4
    skip_r, y_two_r = height + 6, height + 4
    cells_low = float(images * batches * h * row_count * w * col_count)
    cells_high = 4.0 * cells_low

    loads = [
        pltpu.make_async_copy(source, target, in_sems.at[k])
        for k, (source, target) in enumerate(
            (
                (low_ref, low_in),
                (conv_one_ref, conv_one_in),
                (skip_ref, skip_in),
                (index_ref, index_in),
                (target_ref, target_in),
                (gain_one_ref, param_in.at[0]),
                (shift_one_ref, param_in.at[1]),
                (gain_two_ref, param_in.at[2]),
                (shift_two_ref, param_in.at[3]),
                (conv_two_ref, conv_two_in),
            )
        )
    ]
    expected = greet()
    for load in loads:
        load.start()
    low_around = Around(
        [low_ref.at[:, 0:3], low_ref.at[:, h - 3 : h]]
        + [low_send.at[k] for k in range(2)]
        + [low_corner.at[0, k] for k in range(4)],
        [low_rows.at[0], low_rows.at[1]]
        + [low_recv.at[k] for k in range(2)]
        + [low_corner.at[1, k] for k in range(4)],
        strip_sems.at[0],
    )
    skip_around = Around(
        [skip_ref.at[:, 0:3], skip_ref.at[:, height - 3 : height]]
        + [skip_send.at[k] for k in range(2)]
        + [skip_corner.at[0, k] for k in range(4)],
        [skip_rows.at[0], skip_rows.at[1]]
        + [skip_recv.at[k] for k in range(2)]
        + [skip_corner.at[1, k] for k in range(4)],
        strip_sems.at[1],
    )

    def place_low(b, carry):
        start = PAD + b * low_r * pitch
        low_x[pl.ds(start, 3 * pitch), :] = jnp.zeros((3 * pitch, 128), F32)
        low_x[pl.ds(start + 3 * pitch, h * pitch), :] = widened(low_in[b]).reshape(h * pitch, 128)
        low_x[pl.ds(start + (h + 3) * pitch, 3 * pitch), :] = jnp.zeros((3 * pitch, 128), F32)
        return carry

    low_x[0:PAD, :] = jnp.zeros((PAD, 128), F32)
    tail = low_x.shape[0] - PAD - images * low_r * pitch
    low_x[PAD + images * low_r * pitch :, :] = jnp.zeros((tail, 128), F32)
    loads[0].wait()
    lax.fori_loop(0, images, place_low, 0)

    def pack(buffer, sends, corners, rows, step, line, across):
        for side, first in enumerate((8, 5 + across)):
            pack_columns(buffer, sends.at[side], images, rows, line, 3, first, 3)
        for k, (up, along) in enumerate(AROUND[4:]):
            pack_corner(
                buffer,
                corners.at[0, k],
                images,
                rows,
                line,
                3 if up < 0 else step,
                8 if along < 0 else 5 + across,
                3,
            )

    def unpack(around, buffer, strips, columns, corners, rows, step, line, across):
        def use(k):
            up, along = AROUND[k]
            row = step + 3 if up < 0 else 0
            column = 8 + across if along < 0 else 5
            if k < 2:

                def body(b, carry):
                    start = PAD + (b * rows + row) * line
                    buffer[pl.ds(start, 3 * line), :] = widened(strips[k, b]).reshape(
                        3 * line, 128
                    )
                    return carry

                lax.fori_loop(0, images, body, 0)
            elif k < 4:
                unpack_columns(
                    buffer, columns.at[k - 2], images, rows, line, 3, column, 3, step, False
                )
            else:
                unpack_corner(
                    buffer, corners.at[1, k - 4], images, rows, line, row, column, 3, False
                )

        around.each(use)

    pack(low_x, low_send, low_corner, low_r, h, pitch, w)
    greeted(expected)
    low_around.start()
    skip_around.start(range(2))

    def place_skip(b, carry):
        start = PAD + b * skip_r * wide
        edge = jnp.zeros((3 * wide, 128), F32)
        skip_x[pl.ds(start, 3 * wide), :] = edge
        skip_x[pl.ds(start + 3 * wide, height * wide), :] = widened(skip_in[b]).reshape(
            height * wide, 128
        )
        skip_x[pl.ds(start + (height + 3) * wide, 3 * wide), :] = edge
        return carry

    skip_x[0:PAD, :] = jnp.zeros((PAD, 128), F32)
    skip_tail = skip_x.shape[0] - PAD - images * skip_r * wide
    skip_x[PAD + images * skip_r * wide :, :] = jnp.zeros((skip_tail, 128), F32)
    loads[2].wait()
    lax.fori_loop(0, images, place_skip, 0)
    pack(skip_x, skip_send, skip_corner, skip_r, height, wide, breadth)
    skip_around.start(range(2, 8))
    loads[1].wait()
    stack_weight(w_one, conv_one_in)
    low_around.wait()
    unpack(low_around, low_x, low_rows, low_recv, low_corner, low_r, h, pitch, w)

    def conv_one(b, sums):
        pairs = tap_pairs(low_x, PAD + b * low_r * pitch, low_r * pitch, 0.0)
        own = pairs.reshape(low_r, pitch, 256)[2 : h + 4, 8 : 8 + w]
        low_s[b] = own.astype(BF16)
        lines = jnp.sum(own.astype(BF16).astype(F32), axis=1)
        tap_sums = [
            sums[2 + tap] + jnp.sum(lines[tap : tap + h], axis=0, keepdims=True)
            for tap in range(3)
        ]
        pairs = pairs.astype(BF16)
        count = y_one_r * pitch
        taps = jnp.concatenate([pairs[pitch * a : pitch * a + count] for a in range(3)], axis=1)
        value = dot(taps, w_one[...]).reshape(y_one_r, pitch, 128)
        y_one_s[b] = value
        own = value[2 : h + 2, 8 : 8 + w].reshape(h * w, 128)
        return (
            sums[0] + jnp.sum(own, axis=0, keepdims=True),
            sums[1] + jnp.sum(own * own, axis=0, keepdims=True),
            *tap_sums,
        )

    def count_ones(b, total):
        ones = (target_in[b].reshape(height * breadth, 80).astype(F32) == 1.0).astype(F32)
        return total + jnp.sum(ones, axis=0, keepdims=True)

    nothing = jnp.zeros((1, 128), F32)
    tap_none = jnp.zeros((1, 256), F32)
    sums = lax.fori_loop(0, images, conv_one, (nothing, nothing, tap_none, tap_none, tap_none))
    tap_sums = sums[2:]
    for k in (3, 4):
        loads[k].wait()
    ones = lax.fori_loop(0, images, count_ones, jnp.zeros((1, 80), F32))
    base = row_at * (height * breadth * col_count) + col_at * breadth
    slot = lax.broadcasted_iota(jnp.int32, (1, 128), 1)
    objects = 0
    spot_out[...] = jnp.full((8, 128), -(2**30), jnp.int32)
    for b in range(images):
        amount = count_ref[b]
        objects = objects + amount
        spot_out[b : b + 1, :] = jnp.where(
            slot < amount, index_in[b : b + 1, :] - base, -(2**30)
        )
    leading = jnp.logical_and(row_at == 0, col_at == 0).astype(F32)
    sum_src = first_scratch[0]
    sum_src[...] = jnp.zeros((8, 128), F32)
    sum_src[0:1, :] = sums[0]
    sum_src[1:2, :] = sums[1]
    sum_src[2:3, 0:80] = ones
    sum_src[3:4, :] = jnp.full((1, 128), objects.astype(F32) * leading)
    first_total = Total(*first_scratch)
    first_total.begin()
    stores = [
        pltpu.make_async_copy(y_one_s, y_one_out, out_sems.at[0, 0]),
        pltpu.make_async_copy(low_s, low_out, out_sems.at[0, 1]),
    ]
    for store in stores:
        store.start()

    loads[9].wait()
    stack_weight(w_two, conv_two_in)
    skip_around.wait()
    unpack(
        skip_around, skip_x, skip_rows, skip_recv, skip_corner, skip_r, height, wide, breadth
    )
    first_total.middle()
    for k in range(5, 9):
        loads[k].wait()
    totals = first_total.end()
    mean_one = totals[0:1] / cells_low
    scale_one = lax.rsqrt(totals[1:2] / cells_low - mean_one * mean_one + EPSILON)
    gain_one, shift_one = twice(param_in[0]), twice(param_in[1])
    gain_two, shift_two = twice(param_in[2]), twice(param_in[3])
    stat_out[...] = jnp.zeros((24, 128), F32)
    stat_out[0:1, :] = mean_one
    stat_out[1:2, :] = scale_one
    positives = jnp.sum(totals[2:3, 0:80], axis=1, keepdims=True)
    stat_out[4:5, :] = jnp.broadcast_to(1.0 / positives, (1, 128))
    stat_out[5:6, :] = 0.5 / totals[3:4]
    stat_out[6:7, :] = gain_one
    stat_out[7:8, :] = shift_one
    stat_out[8:9, :] = gain_two
    stat_out[9:10, :] = shift_two
    ends = (row_at > 0, row_at < row_count - 1, col_at > 0, col_at < col_count - 1)
    for k, inner in enumerate(ends):
        stat_out[10 + k : 11 + k, :] = jnp.full((1, 128), inner.astype(F32))

    def conv_two(b, sums):
        normed = (y_one_s[b] - mean_one) * scale_one
        value, _ = silu_parts(normed * gain_one + shift_one)
        act_s[0 : y_one_r * pitch, :] = value.astype(BF16).astype(F32).reshape(
            y_one_r * pitch, 128
        )
        clear(
            act_s, 0, y_one_r, pitch, (0, 2), (h + 2, h + 4), (6, 8), (8 + w, 10 + w)
        )
        act = act_s[0 : y_one_r * pitch, :].reshape(y_one_r, pitch, 128)
        odd = 0.75 * act[:-1] + 0.25 * act[1:]
        even = 0.75 * act[1:] + 0.25 * act[:-1]
        tall = jnp.stack([odd, even], axis=1).reshape(skip_r * pitch, 128)
        row_s[PAD : PAD + skip_r * pitch, :] = tall
        count = skip_r * pitch
        before = row_s[PAD - 1 : PAD - 1 + count, :]
        behind = row_s[PAD + 1 : PAD + 1 + count, :]
        up_s[pl.ds(0, count, stride=2), :] = 0.75 * tall + 0.25 * before
        up_s[pl.ds(1, count, stride=2), :] = 0.75 * tall + 0.25 * behind
        start = PAD + b * skip_r * wide
        whole = pl.ds(start, skip_r * wide)
        up = up_s[...].reshape(skip_r, 2 * pitch, 128)[:, 8 : 8 + wide]
        merged = up + skip_x[whole, :].reshape(skip_r, wide, 128)
        skip_x[whole, :] = merged.astype(BF16).astype(F32).reshape(skip_r * wide, 128)
        clear(
            skip_x,
            start,
            skip_r,
            wide,
            (0, 3),
            (height + 3, height + 6),
            (5, 8),
            (8 + breadth, 11 + breadth),
        )
        pairs = tap_pairs(skip_x, start, skip_r * wide, 0.0)
        merged_s[b] = pairs.reshape(skip_r, wide, 256)[2 : height + 4, 8 : 8 + breadth].astype(
            BF16
        )
        pltpu.make_async_copy(merged_s.at[b], merged_out.at[b], out_sems.at[1, b]).start()
        pairs = pairs.astype(BF16)
        count = y_two_r * wide
        taps = jnp.concatenate([pairs[wide * a : wide * a + count] for a in range(3)], axis=1)
        value = dot(taps, w_two[...]).reshape(y_two_r, wide, 128)
        y_two_s[b] = value
        pltpu.make_async_copy(y_two_s.at[b], y_two_out.at[b], out_sems.at[2, b]).start()
        own = value[2 : height + 2, 8 : 8 + breadth].reshape(height * breadth, 128)
        return (
            sums[0] + jnp.sum(own, axis=0, keepdims=True),
            sums[1] + jnp.sum(own * own, axis=0, keepdims=True),
        )

    row_s[0:PAD, :] = jnp.zeros((PAD, 128), F32)
    row_s[PAD + skip_r * pitch :, :] = jnp.zeros((PAD, 128), F32)
    sums = lax.fori_loop(0, images, conv_two, (nothing, nothing))
    sum_src = second_scratch[0]
    sum_src[...] = jnp.zeros((8, 128), F32)
    sum_src[0:1, :] = sums[0]
    sum_src[1:2, :] = sums[1]
    for tap in range(3):
        for part in range(2):
            line = 2 + 2 * tap + part
            sum_src[line : line + 1, :] = tap_sums[tap][:, 128 * part : 128 * part + 128]
    second_total = Total(*second_scratch)
    second_total.begin()
    g_low[...] = jnp.zeros_like(g_low)
    own_low[...] = jnp.zeros_like(own_low)

    def normed_taps(b, carry):
        normed = (y_one_s[b, 2 : h + 2] - mean_one) * scale_one
        own_low[2 * w : (h + 2) * w, :] = normed[:, 8 : 8 + w].reshape(h * w, 128)
        g_low[...] += product_of_parts(
            low_s[b].reshape((h + 2) * w, 256), shifted_taps(own_low, h, w)
        )
        return carry

    lax.fori_loop(0, images, normed_taps, 0)
    tiles_out[36:] = jnp.zeros((tiles_out.shape[0] - 36, 8, 128), F32)
    fold(tiles_out, 0, g_low)
    second_total.middle()
    totals = second_total.end()
    mean_two = totals[0:1] / cells_high
    scale_two = lax.rsqrt(totals[1:2] / cells_high - mean_two * mean_two + EPSILON)
    stat_out[2:3, :] = mean_two
    stat_out[3:4, :] = scale_two
    stat_out[16:22, :] = totals[2:8]

    for store in stores:
        store.wait()
    for b in range(images):
        pltpu.make_async_copy(merged_s.at[b], merged_out.at[b], out_sems.at[1, b]).wait()
        pltpu.make_async_copy(y_two_s.at[b], y_two_out.at[b], out_sems.at[2, b]).wait()


def rise(
    low_map,
    skip_map,
    target,
    conv_one,
    conv_two,
    gain_one,
    shift_one,
    gain_two,
    shift_two,
    index,
    count,
):
    images, h, w, _ = low_map.shape
    _, height, breadth, _ = skip_map.shape
    pitch, wide = w + 16, breadth + 16
    low_r, skip_r = h + 6, height + 6
    half = images // 2
    vmem = pl.BlockSpec(memory_space=pltpu.VMEM)
    hbm = pl.BlockSpec(memory_space=pl.ANY)
    kept = [
        jax.ShapeDtypeStruct((images, height + 4, wide, 128), F32),
        jax.ShapeDtypeStruct((images, h + 4, pitch, 128), F32),
        jax.ShapeDtypeStruct((images, height + 2, breadth, 256), BF16),
        jax.ShapeDtypeStruct((images, h + 2, w, 256), BF16),
    ]
    return pl.pallas_call(
        rise_body,
        in_specs=[hbm] * 10 + [pl.BlockSpec(memory_space=pltpu.SMEM)],
        out_specs=[hbm] * 4 + [vmem] * 3,
        out_shape=kept
        + [jax.ShapeDtypeStruct((24, 128), F32), jax.ShapeDtypeStruct((8, 128), jnp.int32)]
        + [jax.ShapeDtypeStruct((conv_tiles(36), 8, 128), F32)],
        scratch_shapes=[
            pltpu.VMEM(low_map.shape, BF16),
            pltpu.VMEM(skip_map.shape, BF16),
            pltpu.VMEM(target.shape, BF16),
            pltpu.VMEM((3, 192, 64), BF16),
            pltpu.VMEM((3, 192, 64), BF16),
            pltpu.VMEM((4, 1, 64), F32),
            pltpu.VMEM(index.shape, jnp.int32),
        ]
        + [pltpu.VMEM(array.shape, array.dtype) for array in kept]
        + [
            pltpu.VMEM((2 * PAD + (images * low_r + 8) * pitch, 128), F32),
            pltpu.VMEM((2 * PAD + (images * skip_r + 8) * wide, 128), F32),
            pltpu.VMEM((rounded_up(h + 4, 8) * pitch, 128), F32),
            pltpu.VMEM((2 * PAD + skip_r * pitch, 128), F32),
            pltpu.VMEM((2 * skip_r * pitch, 128), F32),
            pltpu.VMEM((768, 128), BF16),
            pltpu.VMEM((768, 128), BF16),
            pltpu.VMEM((256, 256), F32),
            pltpu.VMEM(((h + 4) * w, 128), F32),
            pltpu.VMEM((2, images, 3, w, 64), BF16),
            pltpu.VMEM((2, images, 3, breadth, 64), BF16),
            pltpu.VMEM((2, 3 * half, rounded_up(h, 16), 128), BF16),
            pltpu.VMEM((2, 3 * half, rounded_up(h, 16), 128), BF16),
            pltpu.VMEM((2, 4, half, 32, 128), BF16),
            pltpu.VMEM((2, 3 * half, rounded_up(height, 16), 128), BF16),
            pltpu.VMEM((2, 3 * half, rounded_up(height, 16), 128), BF16),
            pltpu.VMEM((2, 4, half, 32, 128), BF16),
            total_scratch(8),
            total_scratch(8),
            pltpu.SemaphoreType.DMA((10,)),
            pltpu.SemaphoreType.DMA((4, max(images, 2))),
            pltpu.SemaphoreType.DMA((2, 2, 8)),
        ],
        compiler_params=pltpu.CompilerParams(
            collective_id=1, has_side_effects=True, vmem_limit_bytes=60 * MIB
        ),
        name="rise",
    )(
        low_map,
        skip_map,
        target,
        conv_one,
        conv_two,
        gain_one,
        shift_one,
        gain_two,
        shift_two,
        index,
        count,
    )


def levels_of(tiles):
    batch, row, col = place()
    batches, rows, cols = extents()
    pairs = 2 if cols % 2 == 0 else 1
    outer = cols // pairs
    levels = []

    def add(count, mine, device_of):
        left = (levels[-1][3] if levels else tiles) // count
        partners = []
        for over in range(1, count):
            other = lax.rem(mine + over, count)
            partners.append((other, device_of(other)))
        levels.append((count, mine, partners, left))

    low = lax.rem(col, pairs)
    add(pairs, low, lambda k: (batch, row, col - low + k))
    add(
        outer * batches,
        lax.div(col, pairs) * batches + batch,
        lambda k: (lax.rem(k, batches), row, lax.div(k, batches) * pairs + low),
    )
    add(rows, row, lambda k: (batch, k, col))
    return levels


def level_sizes(tiles):
    batches, rows, cols = extents()
    pairs = 2 if cols % 2 == 0 else 1
    sizes = []
    for count in (pairs, cols // pairs * batches, rows):
        tiles = tiles // count
        sizes.append((count, tiles))
    return sizes


class Scatter:
    def __init__(self, source, mids, slots, sems):
        self.parts = [source, *mids]
        self.slots, self.sems = slots, sems
        self.levels = levels_of(source.shape[0])

    def copies(self, level):
        _, _, partners, left = self.levels[level]
        return [
            remote(
                self.parts[level].at[pl.ds(other * left, left)],
                self.slots[level].at[k],
                self.sems.at[level, 0, k],
                self.sems.at[level, 1, k],
                device,
            )
            for k, (other, device) in enumerate(partners)
        ]

    def begin(self, level):
        start_all(self.copies(level))

    def end(self, level):
        _, mine, partners, left = self.levels[level]
        wait_all(self.copies(level))
        total = self.parts[level][pl.ds(mine * left, left)].astype(F32)
        for k in range(len(partners)):
            total = total + self.slots[level][k].astype(F32)
        self.parts[level + 1][...] = total.astype(BF16)


class Gather:
    def __init__(self, full, sems):
        self.full, self.sems = full, sems
        self.levels = levels_of(full.shape[0])

    def span(self, level):
        base = 0
        for _, mine, _, left in self.levels[: level + 1]:
            base = base + mine * left
        return pl.ds(base, self.levels[level][3])

    def copies(self, level):
        part = self.full.at[self.span(level)]
        return [
            remote(part, part, self.sems.at[level, 0, k], self.sems.at[level, 1, k], device)
            for k, (_, device) in enumerate(self.levels[level][2])
        ]

    def begin(self, level):
        start_all(self.copies(level))

    def end(self, level):
        wait_all(self.copies(level))


def scatter_scratch(tiles):
    sizes = level_sizes(tiles)
    return (
        tuple(pltpu.VMEM((left, 16, 128), BF16) for _, left in sizes[:-1]),
        tuple(pltpu.VMEM((count - 1, left, 16, 128), BF16) for count, left in sizes),
        level_sems(),
    )


def level_sems():
    return pltpu.SemaphoreType.DMA((3, 2, max(count for count, _ in level_sizes(1)) - 1))


class PlaneReducer:
    def __init__(self, source, slots, mid, row_slots, full, sems):
        batch, row, col = place()
        batches, rows, cols = extents()
        self.source, self.slots, self.mid = source, slots, mid
        self.row_slots, self.full, self.sems = row_slots, full, sems
        self.share = mid.shape[0]
        self.mine = batch * cols + col
        self.row = row

    def first_copies(self):
        _, _, cols = extents()
        copies = []
        for k, (batch, row, col) in enumerate(plane_partners()):
            other = batch * cols + col
            part = self.source.at[pl.ds(other * self.share, self.share)]
            copies.append(
                remote(
                    part,
                    self.slots.at[k],
                    self.sems.at[0, 0, k],
                    self.sems.at[0, 1, k],
                    (batch, row, col),
                )
            )
        return copies

    def middle_copies(self):
        return [
            remote(
                self.mid,
                self.row_slots.at[self.row],
                self.sems.at[1, 0, k],
                self.sems.at[1, 1, k],
                partner,
            )
            for k, partner in enumerate(row_partners())
        ]

    def last_copies(self):
        part = self.full.at[pl.ds(self.mine * self.share, self.share)]
        return [
            remote(part, part, self.sems.at[2, 0, k], self.sems.at[2, 1, k], partner)
            for k, partner in enumerate(plane_partners())
        ]

    def begin(self):
        start_all(self.first_copies())

    def middle(self):
        wait_all(self.first_copies())
        total = self.source[pl.ds(self.mine * self.share, self.share)]
        for k in range(self.slots.shape[0]):
            total = total + self.slots[k]
        self.mid[...] = total
        start_all(self.middle_copies())
        self.row_slots[self.row] = total

    def last(self):
        wait_all(self.middle_copies())
        self.full[pl.ds(self.mine * self.share, self.share)] = slot_sum(self.row_slots)
        start_all(self.last_copies())

    def end(self):
        wait_all(self.last_copies())


def plane_scratch(tiles):
    batches, rows, cols = extents()
    planes = batches * cols
    share = tiles // planes
    most = max(planes, rows) - 1
    return [
        pltpu.VMEM((tiles, 8, 128), F32),
        pltpu.VMEM((planes - 1, share, 8, 128), F32),
        pltpu.VMEM((share, 8, 128), F32),
        pltpu.VMEM((rows, share, 8, 128), F32),
        pltpu.SemaphoreType.DMA((3, 2, most)),
    ]


def conv_tiles(tiles):
    batches, _, cols = extents()
    planes = batches * cols
    return -(-tiles // planes) * planes


def fold(target, first, grads):
    low = lower_half((1, 128))
    last = grads[0:192, 128:256]
    target[first : first + 24] = grads[0:192, 0:128].reshape(24, 8, 128)
    target[first + 24 : first + 36] = jnp.where(low, last[0:96], swapped(last[96:192])).reshape(
        12, 8, 128
    )


def unfold(source, first):
    pairs = source[first : first + 24].reshape(192, 128)
    last = source[first + 24 : first + 36].reshape(96, 128)
    return [
        pairs[:, 0:64],
        swapped(pairs)[:, 0:64],
        jnp.concatenate([last[:, 0:64], swapped(last)[:, 0:64]], axis=0),
    ]


def shifted_taps(buffer, rows, line):
    count = (rows + 2) * line
    views = [buffer[(2 - tap) * line : (2 - tap) * line + count, :] for tap in range(3)]
    low = lower_half((1, 128))
    return jnp.concatenate(
        [jnp.where(low, views[0], views[1]), jnp.where(low, views[2], 0.0)], axis=1
    )


def product_of_parts(left, right):
    high = right.astype(BF16)
    rest = (right - high.astype(F32)).astype(BF16)
    return dot_left(left, high) + dot_left(left, rest)


def stack_back(target, source):
    for tap in range(3):
        for e in range(3):
            block = source[tap, 64 * e : 64 * e + 64, :].astype(F32)
            start = 256 * tap + 64 * e
            target[start : start + 64, :] = twice(block.T).astype(BF16)
        target[256 * tap + 192 : 256 * tap + 256, :] = jnp.zeros((64, 128), BF16)


def back_pairs(buffer, start, count):
    low = lower_half((1, 128))
    first = jnp.where(low, buffer[pl.ds(start + 1, count), :], buffer[pl.ds(start, count), :])
    second = jnp.where(low, buffer[pl.ds(start - 1, count), :], 0.0)
    return jnp.concatenate([first, second], axis=1).astype(BF16)


def slope_of(values):
    logistic = 0.5 * jnp.tanh(0.5 * values) + 0.5
    return logistic * (1.0 + values * (1.0 - logistic))


def fall_body(
    spread_ref,
    y_two_ref,
    stat_ref,
    load_ref,
    small_ref,
    tiles_ref,
    y_one_ref,
    merged_ref,
    low_ref,
    conv_ref,
    conv_one_ref,
    skip_out,
    zed_out,
    load_out,
    conv_out,
    conv_x_out,
    sums_out,
    weight_out,
    y_two_s,
    slope_s,
    y_one_s,
    merged_s,
    low_s,
    conv_s,
    load_s,
    skip_s,
    share_s,
    grad_x,
    zed_x,
    own_s,
    own_low_s,
    pair_s,
    narrow_s,
    w_two,
    g_two,
    g_one,
    strip_send,
    strip_recv,
    side_send,
    side_recv,
    corners,
    zed_send,
    zed_recv,
    edge_send,
    edge_recv,
    zed_corners,
    third_scratch,
    load_scratch,
    conv_x_scratch,
    conv_scratch,
    gather_sems,
    in_sems,
    map_sems,
    out_sems,
    strip_sems,
    zed_sems,
):
    images, rows, wide, _ = y_two_ref.shape
    height, breadth = rows - 4, wide - 16
    h, w = height // 2, breadth // 2
    pitch, ext = w + 16, height + 2
    zed_rows = h + 2
    half = images // 2
    _, row_at, col_at = place()
    batches, row_count, col_count = extents()
    cells_high = float(images * batches * height * row_count * breadth * col_count)
    low_half = lower_half((1, 128))
    mean_one, scale_one = stat_ref[0:1, :], stat_ref[1:2, :]
    mean_two, scale_two = stat_ref[2:3, :], stat_ref[3:4, :]
    gain_one, shift_one = stat_ref[6:7, :], stat_ref[7:8, :]
    gain_two, shift_two = stat_ref[8:9, :], stat_ref[9:10, :]
    top, bottom = stat_ref[10:11, :], stat_ref[11:12, :]
    left, right = stat_ref[12:13, :], stat_ref[13:14, :]

    def spread_load(b):
        start = PAD + (b * rows + 1) * wide
        return pltpu.make_async_copy(
            spread_ref.at[b], grad_x.at[pl.ds(start, ext * wide)], map_sems.at[0, b]
        )

    def y_two_load(b):
        return pltpu.make_async_copy(y_two_ref.at[b], y_two_s.at[b], map_sems.at[1, b])

    loads = [
        pltpu.make_async_copy(source, target, in_sems.at[k])
        for k, (source, target) in enumerate(
            (
                (load_ref, load_s),
                (tiles_ref, conv_x_scratch[0]),
                (conv_ref, conv_s.at[0]),
                (conv_one_ref, conv_s.at[1]),
                (merged_ref, merged_s),
                (y_one_ref, y_one_s),
                (low_ref, low_s),
            )
        )
    ]
    expected = greet()
    for b in range(images):
        spread_load(b).start()
    for b in range(images):
        y_two_load(b).start()
    for load in loads:
        load.start()
    grad_x[0:PAD, :] = jnp.zeros((PAD, 128), F32)
    tail = PAD + images * rows * wide
    grad_x[tail:, :] = jnp.zeros((grad_x.shape[0] - tail, 128), F32)
    for b in range(images):
        for line in (0, ext + 1):
            start = PAD + (b * rows + line) * wide
            grad_x[start : start + wide, :] = jnp.zeros((wide, 128), F32)
    for b in range(images):
        spread_load(b).wait()

    for pair in range(half):
        for side, first in enumerate((1, ext - 2)):
            parts = []
            for image in (pair, pair + half):
                start = PAD + (image * rows + first) * wide
                parts.append(grad_x[start : start + 3 * wide, :])
            strip_send[side, pair] = jnp.where(low_half, parts[0], parts[1]).astype(BF16)
    around = Around(
        [strip_send.at[k] for k in range(2)]
        + [side_send.at[k] for k in range(2)]
        + [corners.at[0, k] for k in range(4)],
        [strip_recv.at[k] for k in range(2)]
        + [side_recv.at[k] for k in range(2)]
        + [corners.at[1, k] for k in range(4)],
        strip_sems,
    )
    for side, first in enumerate((7, 6 + breadth)):
        pack_columns(grad_x, side_send.at[side], images, rows, wide, 1, first, 3)
    for k, (up, along) in enumerate(AROUND[4:]):
        pack_corner(
            grad_x,
            corners.at[0, k],
            images,
            rows,
            wide,
            1 if up < 0 else height,
            7 if along < 0 else 6 + breadth,
            3,
        )
    greeted(expected)
    around.start()
    loads[0].wait()
    load_sum = Scatter(load_s, (*load_scratch[0], share_s), load_scratch[1], load_scratch[2])
    load_sum.begin(0)

    def begin(b, sums):
        y_two_load(b).wait()
        start = PAD + b * rows * wide
        clear(
            grad_x,
            start,
            rows,
            wide,
            (1, 2),
            (ext, ext + 1),
            (7, 8),
            (8 + breadth, 9 + breadth),
        )
        normed = (y_two_s[b] - mean_two) * scale_two
        slope = slope_of(normed * gain_two + shift_two)
        slope_s[b] = slope
        part = grad_x[pl.ds(start, rows * wide), :].reshape(rows, wide, 128)
        weighted = part * slope
        return sums[0] + fold_sum(weighted), sums[1] + fold_sum(weighted * normed)

    nothing = jnp.zeros((8, 128), F32)
    sums = lax.fori_loop(0, images, begin, (nothing, nothing))
    sum_src = third_scratch[0]
    sum_src[...] = jnp.zeros((16, 128), F32)
    sum_src[0:8, :] = small_ref[...]
    sum_src[8:9, :] = jnp.sum(sums[0], axis=0, keepdims=True)
    sum_src[9:10, :] = jnp.sum(sums[1], axis=0, keepdims=True)
    third_total = Total(*third_scratch)
    third_total.begin()
    load_sum.end(0)
    load_sum.begin(1)
    loads[2].wait()
    stack_back(w_two, conv_s.at[0])
    loads[3].wait()
    stack_back(weight_out, conv_s.at[1])
    g_two[...] = jnp.zeros_like(g_two)
    g_one[...] = jnp.zeros_like(g_one)
    own_s[...] = jnp.zeros_like(own_s)
    own_low_s[...] = jnp.zeros_like(own_low_s)
    narrow_s[...] = jnp.zeros_like(narrow_s)
    zed_x[...] = jnp.zeros_like(zed_x)
    third_total.middle()
    around.wait()

    def use(k):
        up, along = AROUND[k]
        row = height + 1 if up < 0 else 0
        column = 7 + breadth if along < 0 else 6
        if k < 2:
            for image in range(images):
                values = unpacked(strip_recv[k, image % half].astype(F32), image, images)
                start = PAD + (image * rows + row) * wide
                grad_x[start : start + 3 * wide, :] += values
        elif k < 4:
            unpack_columns(
                grad_x, side_recv.at[k - 2], images, rows, wide, 1, column, 3, ext, True
            )
        else:
            unpack_corner(
                grad_x, corners.at[1, k - 4], images, rows, wide, row, column, 3, True
            )

    around.each(use)

    loads[1].wait()
    conv_x_sum = PlaneReducer(*conv_x_scratch[:4], conv_x_out, conv_x_scratch[4])
    totals = third_total.end()
    sums_out[...] = totals
    conv_x_sum.begin()
    factor_two = gain_two * scale_two
    shift_part, gain_part = totals[8:9] / cells_high, totals[9:10] / cells_high
    for k in (4, 5, 6):
        loads[k].wait()
    column = lax.broadcasted_iota(jnp.int32, (wide, 128), 0)
    keep = jnp.where(column < 8, left, 1.0)
    keep = jnp.where(column >= 8 + breadth, right, keep)

    def merge(b, sums):
        start = PAD + b * rows * wide
        whole = pl.ds(start, rows * wide)
        normed = (y_two_s[b] - mean_two) * scale_two
        grad_z = grad_x[whole, :].reshape(rows, wide, 128) * slope_s[b]
        grad_y = factor_two * (grad_z - shift_part - normed * gain_part)
        grad_y = (grad_y * keep).astype(BF16).astype(F32)
        grad_x[whole, :] = grad_y.reshape(rows * wide, 128)
        for line, flag in ((0, top), (ext, bottom)):
            span = pl.ds(start + line * wide, 2 * wide)
            grad_x[span, :] = grad_x[span, :] * flag
        own_s[2 * breadth : (height + 2) * breadth, :] = grad_y[
            2 : height + 2, 8 : 8 + breadth
        ].reshape(height * breadth, 128)
        source = merged_s[b].reshape(ext * breadth, 256)
        g_two[...] += dot_left(source, shifted_taps(own_s, height, breadth).astype(BF16))
        pair_s[...] = back_pairs(grad_x, start, rows * wide)
        count = ext * wide
        taps = jnp.concatenate(
            [pair_s[wide * (2 - a) : wide * (2 - a) + count, :] for a in range(3)], axis=1
        )
        merged_grad = dot(taps, w_two[...]).reshape(ext, wide, 128)
        skip_s[b] = merged_grad[1 : height + 1, 8 : 8 + breadth, 0:64]
        pltpu.make_async_copy(skip_s.at[b], skip_out.at[b], out_sems.at[0, b]).start()
        fine = (merged_grad * keep).astype(BF16).astype(F32).reshape(h + 1, 2, wide, 128)
        even, odd = fine[:, 0], fine[:, 1]
        even = jnp.concatenate([even[0:1] * top, even[1:]], axis=0)
        odd = jnp.concatenate([odd[:-1], odd[-1:] * bottom], axis=0)
        short = 0.75 * (odd[:-1] + even[1:]) + 0.25 * (even[:-1] + odd[1:])
        side = jnp.zeros((h, 8, 128), F32)
        count = h * 2 * pitch
        narrow_s[PAD : PAD + count, :] = jnp.concatenate([side, short, side], axis=1).reshape(
            count, 128
        )
        lines = [narrow_s[pl.ds(PAD + k, count // 2, stride=2), :] for k in (-1, 0, 1, 2)]
        act_grad = 0.75 * (lines[1] + lines[2]) + 0.25 * (lines[0] + lines[3])
        act_grad = act_grad.reshape(h, pitch, 128)
        normed = (y_one_s[b, 2 : h + 2] - mean_one) * scale_one
        slope = slope_of(normed * gain_one + shift_one)
        place_at = lax.broadcasted_iota(jnp.int32, (pitch, 128), 0)
        inner = jnp.logical_and(place_at >= 8, place_at < 8 + w)
        grad_z = jnp.where(inner, act_grad * slope, 0.0)
        spot = PAD + (b * zed_rows + 1) * pitch
        zed_x[pl.ds(spot, h * pitch), :] = grad_z.reshape(h * pitch, 128)
        own_low_s[2 * w : (h + 2) * w, :] = grad_z[:, 8 : 8 + w].reshape(h * w, 128)
        g_one[...] += product_of_parts(
            low_s[b].reshape((h + 2) * w, 256), shifted_taps(own_low_s, h, w)
        )
        return sums[0] + fold_sum(grad_z), sums[1] + fold_sum(grad_z * normed)

    gather = Gather(load_out, gather_sems)

    def merge_and_move(b, sums):
        sums = merge(b, sums)

        @pl.when(b == 0)
        def _():
            load_sum.end(1)
            load_sum.begin(2)

        @pl.when(b == 1)
        def _():
            conv_x_sum.middle()
            load_sum.end(2)
            load_out[gather.span(2)] = share_s[...]
            gather.begin(2)

        @pl.when(b == 2)
        def _():
            gather.end(2)
            gather.begin(1)

        @pl.when(b == 3)
        def _():
            conv_x_sum.last()

        return sums

    sums = lax.fori_loop(0, images, merge_and_move, (nothing, nothing))
    fold(conv_scratch[0], 36, g_one)
    conv_scratch[0][72:] = jnp.zeros((conv_out.shape[0] - 72, 8, 128), F32)
    for k in range(2):
        conv_scratch[0][72, k : k + 1, :] = jnp.sum(sums[k], axis=0, keepdims=True)
    fold(conv_scratch[0], 0, g_two)
    conv_sum = PlaneReducer(*conv_scratch[:4], conv_out, conv_scratch[4])
    conv_sum.begin()
    for pair in range(half):
        for side, line in enumerate((1, h)):
            parts = []
            for image in (pair, pair + half):
                start = PAD + (image * zed_rows + line) * pitch
                parts.append(zed_x[start : start + pitch, :])
            zed_send[side, pair] = jnp.where(low_half, parts[0], parts[1])
    for side, column in enumerate((8, 7 + w)):
        pack_columns(zed_x, edge_send.at[side], images, zed_rows, pitch, 1, column, 1)
    for k, (up, along) in enumerate(AROUND[4:]):
        pack_corner(
            zed_x,
            zed_corners.at[0, k],
            images,
            zed_rows,
            pitch,
            1 if up < 0 else h,
            8 if along < 0 else 7 + w,
            1,
        )
    zed_around = Around(
        [zed_send.at[k] for k in range(2)]
        + [edge_send.at[k] for k in range(2)]
        + [zed_corners.at[0, k] for k in range(4)],
        [zed_recv.at[k] for k in range(2)]
        + [edge_recv.at[k] for k in range(2)]
        + [zed_corners.at[1, k] for k in range(4)],
        zed_sems,
    )
    zed_around.start()
    conv_sum.middle()
    gather.end(1)
    gather.begin(0)
    zed_around.wait()

    def use_zed(k):
        up, along = AROUND[k]
        row = h + 1 if up < 0 else 0
        column = 8 + w if along < 0 else 7
        if k < 2:
            for image in range(images):
                start = PAD + (image * zed_rows + row) * pitch
                zed_x[start : start + pitch, :] = unpacked(
                    zed_recv[k, image % half], image, images
                )
        elif k < 4:
            unpack_columns(
                zed_x, edge_recv.at[k - 2], images, zed_rows, pitch, 1, column, 1, h, False
            )
        else:
            unpack_corner(
                zed_x, zed_corners.at[1, k - 4], images, zed_rows, pitch, row, column, 1, False
            )

    zed_around.each(use_zed)

    def zed_store(b):
        return pltpu.make_async_copy(
            zed_x.at[pl.ds(PAD + b * zed_rows * pitch, zed_rows * pitch)],
            zed_out.at[b],
            out_sems.at[1, b],
        )

    for b in range(images):
        zed_store(b).start()
    conv_sum.last()
    conv_x_sum.end()
    conv_sum.end()
    gather.end(0)
    for b in range(images):
        zed_store(b).wait()
        pltpu.make_async_copy(skip_s.at[b], skip_out.at[b], out_sems.at[0, b]).wait()


def fall(
    spread, y_two, stats, load, small, tiles_x, y_one, merged, low, conv_two, conv_one
):
    images, rows, wide, _ = y_two.shape
    height, breadth = rows - 4, wide - 16
    h, w = height // 2, breadth // 2
    pitch, ext, zed_rows = w + 16, height + 2, h + 2
    half = images // 2
    tiles, parts_x, parts = load.shape[0], tiles_x.shape[0], conv_tiles(73)
    vmem = pl.BlockSpec(memory_space=pltpu.VMEM)
    hbm = pl.BlockSpec(memory_space=pl.ANY)
    lines, low_lines = rounded_up(ext, 16), rounded_up(h, 8)
    return pl.pallas_call(
        fall_body,
        in_specs=[hbm] * 2 + [vmem, hbm, vmem] + [hbm] * 6,
        out_specs=[hbm] * 2 + [vmem] * 5,
        out_shape=[
            jax.ShapeDtypeStruct((images, height, breadth, 64), F32),
            jax.ShapeDtypeStruct((images, zed_rows * pitch, 128), F32),
            jax.ShapeDtypeStruct((tiles, 16, 128), BF16),
            jax.ShapeDtypeStruct((parts, 8, 128), F32),
            jax.ShapeDtypeStruct((parts_x, 8, 128), F32),
            jax.ShapeDtypeStruct((16, 128), F32),
            jax.ShapeDtypeStruct((768, 128), BF16),
        ],
        scratch_shapes=[
            pltpu.VMEM(y_two.shape, F32),
            pltpu.VMEM(y_two.shape, F32),
            pltpu.VMEM(y_one.shape, F32),
            pltpu.VMEM(merged.shape, BF16),
            pltpu.VMEM(low.shape, BF16),
            pltpu.VMEM((2, 3, 192, 64), BF16),
            pltpu.VMEM(load.shape, BF16),
            pltpu.VMEM((images, height, breadth, 64), F32),
            pltpu.VMEM((level_sizes(tiles)[-1][1], 16, 128), BF16),
            pltpu.VMEM((2 * PAD + (images * rows + lines - ext) * wide, 128), F32),
            pltpu.VMEM((2 * PAD + (images * zed_rows + 8) * pitch, 128), F32),
            pltpu.VMEM(((height + 4) * breadth, 128), F32),
            pltpu.VMEM(((h + 4) * w, 128), F32),
            pltpu.VMEM((rows * wide, 256), BF16),
            pltpu.VMEM((2 * PAD + h * 2 * pitch, 128), F32),
            pltpu.VMEM((768, 128), BF16),
            pltpu.VMEM((256, 256), F32),
            pltpu.VMEM((256, 256), F32),
            pltpu.VMEM((2, half, 3 * wide, 128), BF16),
            pltpu.VMEM((2, half, 3 * wide, 128), BF16),
            pltpu.VMEM((2, 3 * half, lines, 128), BF16),
            pltpu.VMEM((2, 3 * half, lines, 128), BF16),
            pltpu.VMEM((2, 4, half, 32, 128), BF16),
            pltpu.VMEM((2, half, pitch, 128), F32),
            pltpu.VMEM((2, half, pitch, 128), F32),
            pltpu.VMEM((2, half, low_lines, 128), F32),
            pltpu.VMEM((2, half, low_lines, 128), F32),
            pltpu.VMEM((2, 4, half, 8, 128), F32),
            total_scratch(16),
            scatter_scratch(tiles),
            plane_scratch(parts_x),
            plane_scratch(parts),
            level_sems(),
            pltpu.SemaphoreType.DMA((7,)),
            pltpu.SemaphoreType.DMA((2, images)),
            pltpu.SemaphoreType.DMA((2, images)),
            pltpu.SemaphoreType.DMA((2, 8)),
            pltpu.SemaphoreType.DMA((2, 8)),
        ],
        compiler_params=pltpu.CompilerParams(
            collective_id=2, has_side_effects=True, vmem_limit_bytes=60 * MIB
        ),
        name="fall",
    )(spread, y_two, stats, load, small, tiles_x, y_one, merged, low, conv_two, conv_one)


def finish_body(
    cells_low,
    load_ref,
    rest_ref,
    conv_ref,
    conv_x_ref,
    sums_ref,
    stat_ref,
    zed_ref,
    y_one_ref,
    weight_ref,
    skip_ref,
    conv_one_out,
    gain_one_out,
    shift_one_out,
    conv_two_out,
    gain_two_out,
    shift_two_out,
    head_out,
    head_b_out,
    heat_w_out,
    heat_b_out,
    box_w_out,
    box_b_out,
    low_out,
    skip_out,
    zed_x,
):
    step = pl.program_id(0)
    each, h, w, _ = low_out.shape
    pitch = w + 16
    rows = h + 2
    factor = stat_ref[6:7, :] * stat_ref[1:2, :]
    shift_low, gain_low = conv_ref[72, 0:1, :] / cells_low, conv_ref[72, 1:2, :] / cells_low
    skip_out[...] = skip_ref[...]
    for column in range(head_out.shape[3] // 128):
        block = load_ref[36 * column : 36 * column + 36].astype(F32)
        head_out[:, :, :, 128 * column : 128 * column + 128] = block.reshape(3, 3, 64, 128)

    @pl.when(step == 0)
    def _():
        zed_x[0:PAD, :] = jnp.zeros((PAD, 128), F32)
        zed_x[PAD + rows * pitch :, :] = jnp.zeros((PAD, 128), F32)
        spread = stat_ref[16:24, :].T
        ones = unfold(conv_ref, 36)
        normed = unfold(conv_x_ref, 0)
        for tap, part in enumerate(unfold(conv_ref, 0)):
            conv_two_out[tap] = part.reshape(3, 64, 64)
            count = jnp.concatenate(
                [spread[:, 2 * tap : 2 * tap + 1], spread[0:64, 2 * tap + 1 : 2 * tap + 2]], axis=0
            )
            value = ones[tap] - count * shift_low[:, 0:64] - normed[tap] * gain_low[:, 0:64]
            conv_one_out[tap] = (value * factor[:, 0:64]).reshape(3, 64, 64)
        for column in range(6):
            span = slice(128 * column, 128 * column + 128)
            head_b_out[span] = sums_ref[column : column + 1, :].reshape(128)
        for part in range(2):
            span = slice(128 * part, 128 * part + 128)
            heat_w_out[:, span] = rest_ref[5 * part : 5 * part + 5].astype(F32).reshape(80, 128)
            for box in range(2):
                block = rest_ref[10 + 2 * box + part].astype(F32)
                box_w_out[box, :, span] = block[2 * box : 2 * box + 2, :]
            box_b_out[part : part + 1, :] = sums_ref[7:8, 2 * part : 2 * part + 2]
        heat_b_out[...] = sums_ref[6:7, 0:80]
        shift_two_out[...] = sums_ref[8:9, 0:64]
        gain_two_out[...] = sums_ref[9:10, 0:64]
        shift_one_out[...] = conv_ref[72, 0:1, 0:64]
        gain_one_out[...] = conv_ref[72, 1:2, 0:64]

    for b in range(each):
        normed = (y_one_ref[b, 1 : h + 3] - stat_ref[0:1, :]) * stat_ref[1:2, :]
        grad_z = zed_ref[b].reshape(rows, pitch, 128)
        grad_y = factor * (grad_z - shift_low - normed * gain_low)
        column = lax.broadcasted_iota(jnp.int32, (pitch, 128), 0)
        keep = jnp.where(column < 8, stat_ref[12:13, :], 1.0)
        keep = jnp.where(column >= 8 + w, stat_ref[13:14, :], keep)
        grad_y = (grad_y * keep).astype(BF16).astype(F32)
        zed_x[PAD : PAD + rows * pitch, :] = grad_y.reshape(rows * pitch, 128)
        for line, row in ((0, 10), (rows - 1, 11)):
            span = slice(PAD + line * pitch, PAD + (line + 1) * pitch)
            zed_x[span, :] = zed_x[span, :] * stat_ref[row : row + 1, :]
        pairs = back_pairs(zed_x, PAD, rows * pitch)
        count = h * pitch
        taps = jnp.concatenate(
            [pairs[pitch * (2 - a) : pitch * (2 - a) + count] for a in range(3)], axis=1
        )
        grad = dot(taps, weight_ref[...]).reshape(h, pitch, 128)
        low_out[b] = grad[:, 8 : 8 + w, 0:64]


def finish(load, conv, conv_x, sums, stats, zed, y_one, weight, skip):
    images, y_rows, pitch, _ = y_one.shape
    h, w = y_rows - 4, pitch - 16
    batches, row_count, col_count = extents()
    cells = float(images * batches * h * row_count * w * col_count)
    span = zed.shape[1]
    steps = 2
    each = images // steps
    shapes = [
        (3, 3, 64, 64),
        (1, 64),
        (1, 64),
        (3, 3, 64, 64),
        (1, 64),
        (1, 64),
        (3, 3, 64, 768),
        (768,),
        (80, 256),
        (1, 80),
        (2, 2, 256),
        (2, 2),
        (images, h, w, 64),
        skip.shape,
    ]
    whole = lambda shape: pl.BlockSpec(shape, lambda c: (0,) * len(shape))
    part = lambda shape: pl.BlockSpec(shape, lambda c: (c,) + (0,) * (len(shape) - 1))
    out_specs = [whole(shape) for shape in shapes]
    out_specs[6] = pl.BlockSpec((3, 3, 64, 768 // steps), lambda c: (0, 0, 0, c))
    out_specs[12] = part((each, h, w, 64))
    out_specs[13] = part((each,) + skip.shape[1:])
    return pl.pallas_call(
        functools.partial(finish_body, cells),
        grid=(steps,),
        in_specs=[
            part((216 // steps, 16, 128)),
            pl.BlockSpec((36, 16, 128), lambda c: (6, 0, 0)),
        ]
        + [whole(array.shape) for array in (conv, conv_x, sums, stats)]
        + [
            part((each, span, 128)),
            part((each, y_rows, pitch, 128)),
            whole(weight.shape),
            part((each,) + skip.shape[1:]),
        ],
        out_specs=out_specs,
        out_shape=[jax.ShapeDtypeStruct(shape, F32) for shape in shapes],
        scratch_shapes=[
            pltpu.VMEM((2 * PAD + span, 128), F32),
        ],
        compiler_params=pltpu.CompilerParams(vmem_limit_bytes=60 * MIB),
        name="finish",
    )(load, load, conv, conv_x, sums, stats, zed, y_one, weight, skip)


def local(
    low_map,
    skip_map,
    conv_first,
    gain_first,
    shift_first,
    conv_second,
    gain_second,
    shift_second,
    head_conv,
    head_bias,
    heat_weight,
    heat_bias,
    box_weight,
    box_bias,
    heat_target,
    box_target,
    obj_index,
    obj_count,
):
    batches, rows, cols = extents()
    devices = batches * rows * cols
    conv_one = conv_first.reshape(3, 192, 64)
    conv_two = conv_second.reshape(3, 192, 64)
    y_two, y_one, merged, low, stats, spot, tiles_x = rise(
        low_map,
        skip_map,
        heat_target,
        conv_one,
        conv_two,
        gain_first.reshape(1, 64),
        shift_first.reshape(1, 64),
        gain_second.reshape(1, 64),
        shift_second.reshape(1, 64),
        obj_index,
        obj_count,
    )
    heat_map, box_map, spread, load, small = heads(
        y_two,
        heat_target,
        spot,
        box_target.transpose(0, 2, 1),
        stats,
        head_conv.reshape(3, 192, 768),
        head_bias,
        heat_weight.T,
        heat_bias.reshape(1, 80),
        box_weight.transpose(0, 2, 1),
        box_bias,
        devices,
    )
    images, ext, wide, _ = spread.shape
    grad_skip, zed, load, conv, conv_x, sums, weight = fall(
        spread.reshape(images, ext * wide, 128),
        y_two,
        stats,
        load,
        small,
        tiles_x,
        y_one,
        merged,
        low,
        conv_two,
        conv_one,
    )
    grads = finish(load, conv, conv_x, sums, stats, zed, y_one, weight, grad_skip)
    return (
        heat_map,
        box_map.transpose(0, 1, 3, 2),
        grads[12],
        grads[13],
        grads[0],
        grads[1].reshape(64),
        grads[2].reshape(64),
        grads[3],
        grads[4].reshape(64),
        grads[5].reshape(64),
        grads[6],
        grads[7],
        grads[8].T,
        grads[9].reshape(80),
        grads[10].transpose(0, 2, 1),
        grads[11],
    )


def solution(mesh):
    tile = P("batch", "row", "col", None)
    return jax.shard_map(
        local,
        mesh=mesh,
        in_specs=(tile, tile)
        + (P(),) * 12
        + (tile, P("batch", None, None), P("batch", None), P("batch")),
        out_specs=(tile,) * 4 + (P(),) * 12,
        check_vma=False,
    )
```

```python
import functools

import jax
import jax.numpy as jnp
from jax import lax
from jax.experimental import pallas as pl
from jax.experimental.pallas import tpu as pltpu
from jax.sharding import PartitionSpec as P

EPSILON = 1e-05
F32 = jnp.float32
BF16 = jnp.bfloat16
KEEP = (((1,), (1,)), ((), ()))
LEFT = (((0,), (0,)), ((), ()))
MIB = 1024 * 1024


def dot(left, right):
    return jnp.dot(left, right, preferred_element_type=F32)


def dot_keep(left, right):
    return lax.dot_general(left, right, KEEP, preferred_element_type=F32)


def dot_left(left, right):
    return lax.dot_general(left, right, LEFT, preferred_element_type=F32)


def three_parts(values):
    high = values.astype(BF16)
    rest = values - high.astype(F32)
    mid = rest.astype(BF16)
    return high, mid, (rest - mid.astype(F32)).astype(BF16)


def tile_count(devices):
    return -(-230 // (2 * devices)) * 2 * devices


def heads_body(
    map_side,
    y_two_ref,
    target_ref,
    spot_ref,
    goal_ref,
    stat_ref,
    conv_ref,
    bias_ref,
    heat_w_ref,
    heat_b_ref,
    box_w_ref,
    box_b_ref,
    heat_out,
    box_out,
    spread_out,
    load_out,
    small_out,
    feat_s,
    taps_ref,
    kernel_s,
    back_s,
    box_s,
    wide_s,
    grad_s,
    heat_grad_s,
    box_grad_s,
    heat_sum_s,
    box_sum_s,
):
    step = pl.program_id(0)
    each, height, breadth, _ = target_ref.shape
    image_cells = height * breadth
    cells = each * image_cells
    units = 256

    @pl.when(step == 0)
    def _():
        for tap in range(3):
            kernel_s[tap, 0:192, :] = (0.5 * conv_ref[tap].astype(F32)).astype(BF16)
            kernel_s[tap, 192:256, :] = jnp.zeros((64, 768), BF16)
        parts = three_parts(0.5 * bias_ref[...].reshape(1, 768))
        which = lax.broadcasted_iota(jnp.int32, (16, 768), 0)
        filled = jnp.zeros((16, 768), F32)
        for place in range(3):
            filled = jnp.where(which == place, parts[place].astype(F32), filled)
        kernel_s[1, 192:208, :] = filled.astype(BF16)
        for tap in range(3):
            for block in range(3):
                span = slice(256 * block, 256 * block + 256)
                back_s[span, 256 * tap : 256 * tap + 256] = (
                    kernel_s[tap, :, span].astype(F32).T.astype(BF16)
                )
        empty = jnp.zeros((2, 256), F32)
        for part in range(2):
            pieces = [empty, empty]
            pieces[part] = box_w_ref[part].astype(F32)
            box_s[part] = jnp.concatenate(pieces, axis=0).astype(BF16)
        grad_s[...] = jnp.zeros_like(grad_s)
        heat_grad_s[...] = jnp.zeros_like(heat_grad_s)
        box_grad_s[...] = jnp.zeros_like(box_grad_s)
        heat_sum_s[...] = jnp.zeros_like(heat_sum_s)
        box_sum_s[...] = jnp.zeros_like(box_sum_s)
        wide_s[...] = jnp.zeros_like(wide_s)

    ext, wide = height + 2, breadth + 16
    column = lax.broadcasted_iota(jnp.int32, (wide, 128), 0)
    keep = jnp.where(column < 8, stat_ref[12:13, :], 1.0)
    keep = jnp.where(column >= 8 + breadth, stat_ref[13:14, :], keep)
    feat_s[0:PAD, :] = jnp.zeros((PAD, 128), F32)
    feat_s[PAD + ext * wide :, :] = jnp.zeros((PAD, 128), F32)
    for image in range(each):
        normed = (y_two_ref[image, 1 : ext + 1] - stat_ref[2:3, :]) * stat_ref[3:4, :]
        feature, _ = silu_parts(normed * stat_ref[8:9, :] + stat_ref[9:10, :])
        feat_s[PAD : PAD + ext * wide, :] = (feature * keep).reshape(ext * wide, 128)
        for line, row in ((PAD, 10), (PAD + (ext - 1) * wide, 11)):
            feat_s[line : line + wide, :] = feat_s[line : line + wide, :] * stat_ref[row : row + 1]
        pairs = tap_pairs(feat_s, PAD, ext * wide, 1.0)
        taps_ref[image] = pairs.reshape(ext, wide, 256)[:, 8 : 8 + breadth].astype(BF16)

    taps = jnp.concatenate(
        [taps_ref[:, tap : tap + height].reshape(cells, 256) for tap in range(3)], axis=1
    )
    active, slope = [], []

    def forward(block):
        weight = kernel_s[:, :, block * units : (block + 1) * units].reshape(768, units)
        hidden = dot(taps, weight)
        turn = jnp.tanh(hidden)
        above = 1.0 + turn
        product = hidden * above
        active.append(product.astype(BF16))
        slope.append(above + product * (1.0 - turn))

    forward(0)
    logit = dot_keep(active[0], heat_w_ref[...]) + heat_b_ref[...]
    decay = jnp.exp(-jnp.abs(logit))
    large = 1.0 / (1.0 + decay)
    small = decay * large
    above = logit >= 0.0
    chance = jnp.where(above, large, small)
    heat_out[...] = chance.reshape(each, height, breadth, 80)
    target = target_ref[...].reshape(cells, 80).astype(F32)
    positive = target == 1.0
    side = jnp.where(positive, jnp.where(above, small, large), chance)
    value = jnp.where(positive, -logit, logit)
    soft = jnp.maximum(value, 0.0) + jnp.log(1.0 + decay)
    slant = side * side * (2.0 * (1.0 - side) * soft + side)
    gap = 1.0 - target
    gap = gap * gap
    weighting = jnp.where(positive, -1.0, gap * gap) * stat_ref[4:5, 0:80]
    logit_grad = weighting * slant
    logit_low = logit_grad.astype(BF16)
    heat_sum_s[...] += jnp.sum(logit_low.astype(F32).reshape(cells // 8, 8, 80), axis=0)
    heat_grad_s[...] += dot_left(logit_low, active[0])
    hidden_low = [(dot(logit_low, heat_w_ref[...]) * slope[0]).astype(BF16)]
    forward(1)
    forward(2)

    box_bias = jnp.concatenate([box_b_ref[0:1, :], box_b_ref[1:2, :]], axis=1)
    boxes = dot_keep(active[1], box_s[0]) + dot_keep(active[2], box_s[1]) + box_bias
    turned = jnp.swapaxes(boxes.reshape(each * height, breadth, 4), 1, 2)
    box_out[...] = turned.reshape(each, height, 4, breadth)
    shape = (height, breadth, 128)
    cell = lax.broadcasted_iota(jnp.int32, shape, 0) * map_side
    cell = (cell + lax.broadcasted_iota(jnp.int32, shape, 1)).reshape(image_cells, 128)
    goals, hits = [], []
    for image in range(each):
        spots = spot_ref[pl.ds(step * each + image, 1), :]
        chosen = (cell == spots).astype(F32).astype(BF16)
        high, mid, least = three_parts(goal_ref[image])
        ends = jnp.concatenate([least.astype(F32), jnp.ones((4, 128), F32)], axis=0).astype(BF16)
        twofold = jnp.concatenate([chosen, chosen], axis=1)
        goal = dot_keep(twofold, jnp.concatenate([high, mid], axis=1))
        both = dot_keep(chosen, ends)
        goals.append(goal + both[:, 0:4])
        hits.append(both[:, 4:8])
    goals, hit = jnp.concatenate(goals, axis=0), jnp.concatenate(hits, axis=0)
    miss = boxes - goals
    lane = lax.broadcasted_iota(jnp.int32, (1, 4), 1)
    factor = jnp.where(lane < 2, 0.1, 1.0) * stat_ref[5:6, 0:4]
    box_grad = hit * factor * miss * lax.rsqrt(miss * miss + 1.0)
    box_low = box_grad.astype(BF16)

    box_sum_s[...] += jnp.sum(box_low.astype(F32).reshape(cells // 8, 8, 4), axis=0)
    for part in range(2):
        box_grad_s[part] += dot_left(box_low, active[1 + part])

    for part in range(2):
        back = dot(box_low, box_s[part])
        hidden_low.append((back * slope[1 + part]).astype(BF16))
    grad_hidden = jnp.concatenate(hidden_low, axis=1)
    spread = []
    for tap in range(3):
        part = dot(grad_hidden, back_s[:, 256 * tap : 256 * tap + 256])
        spread.append(part.reshape(each, height, breadth, 256))
    inner = slice(16, 16 + breadth)
    for image in range(each):
        first, second, third = [part[image] for part in spread]
        wide_s[0:1, inner, :] = first[0:1]
        wide_s[1:2, inner, :] = first[1:2] + second[0:1]
        wide_s[2:height, inner, :] = first[2:] + second[1:-1] + third[:-2]
        wide_s[height : height + 1, inner, :] = second[-1:] + third[-2:-1]
        wide_s[height + 1 :, inner, :] = third[-1:]
        centre = swapped(wide_s[:, 8 : 8 + wide, 0:128])
        total = wide_s[:, 9 : 9 + wide, 0:128] + centre + wide_s[:, 7 : 7 + wide, 128:256]
        lanes = lax.broadcasted_iota(jnp.int32, total.shape, 2)
        spread_out[image] = jnp.where(lanes < 64, total, swapped(total))
    for tap in range(3):
        grad_s[tap] += dot_left(taps[:, 256 * tap : 256 * tap + 256], grad_hidden)

    @pl.when(step == pl.num_programs(0) - 1)
    def _():
        for column in range(6):
            span = slice(128 * column, 128 * column + 128)
            for tap in range(3):
                start = 36 * column + 12 * tap
                load_out[start : start + 12] = (
                    (0.5 * grad_s[tap, 0:192, span]).reshape(12, 16, 128).astype(BF16)
                )
            small_out[column : column + 1, :] = 0.5 * grad_s[1, 192:193, span]
        for half in range(2):
            span = slice(128 * half, 128 * half + 128)
            start = 216 + 5 * half
            load_out[start : start + 5] = heat_grad_s[:, span].reshape(5, 16, 128).astype(BF16)
            for part in range(2):
                padded = jnp.concatenate(
                    [box_grad_s[part, :, span], jnp.zeros((12, 128), F32)], axis=0
                )
                load_out[226 + 2 * part + half] = padded.astype(BF16)
        load_out[230:] = jnp.zeros((load_out.shape[0] - 230, 16, 128), BF16)
        small_out[6:8, :] = jnp.zeros((2, 128), F32)
        small_out[6:7, 0:80] = jnp.sum(heat_sum_s[...], axis=0, keepdims=True)
        small_out[7:8, 0:4] = jnp.sum(box_sum_s[...], axis=0, keepdims=True)


def heads(
    taps, target, spot, goal, stats, conv, bias, heat_w, heat_b, box_w, box_b, devices
):
    images, height, breadth, classes = target.shape
    each = 1
    tiles = tile_count(devices)
    whole = lambda *shape: pl.BlockSpec(shape, lambda b: (0,) * len(shape))
    part = lambda *shape: pl.BlockSpec((each,) + shape, lambda b: (b,) + (0,) * len(shape))
    cells = images * height * breadth
    return pl.pallas_call(
        functools.partial(heads_body, breadth * lax.axis_size("col")),
        grid=(images // each,),
        in_specs=[
            part(height + 4, breadth + 16, 128),
            part(height, breadth, classes),
            whole(8, 128),
            part(4, 128),
            whole(24, 128),
            whole(3, 192, 768),
            whole(768),
            whole(80, 256),
            whole(1, 80),
            whole(2, 2, 256),
            whole(2, 2),
        ],
        out_specs=[
            part(height, breadth, classes),
            part(height, 4, breadth),
            part(height + 2, breadth + 16, 128),
            whole(tiles, 16, 128),
            whole(8, 128),
        ],
        out_shape=[
            jax.ShapeDtypeStruct((images, height, breadth, classes), F32),
            jax.ShapeDtypeStruct((images, height, 4, breadth), F32),
            jax.ShapeDtypeStruct((images, height + 2, breadth + 16, 128), F32),
            jax.ShapeDtypeStruct((tiles, 16, 128), BF16),
            jax.ShapeDtypeStruct((8, 128), F32),
        ],
        scratch_shapes=[
            pltpu.VMEM((2 * PAD + (height + 2) * (breadth + 16), 128), F32),
            pltpu.VMEM((each, height + 2, breadth, 256), BF16),
            pltpu.VMEM((3, 256, 768), BF16),
            pltpu.VMEM((768, 768), BF16),
            pltpu.VMEM((2, 4, 256), BF16),
            pltpu.VMEM((height + 2, breadth + 32, 256), F32),
            pltpu.VMEM((3, 256, 768), F32),
            pltpu.VMEM((80, 256), F32),
            pltpu.VMEM((2, 4, 256), F32),
            pltpu.VMEM((8, 80), F32),
            pltpu.VMEM((8, 4), F32),
        ],
        compiler_params=pltpu.CompilerParams(vmem_limit_bytes=60 * MIB),
        cost_estimate=pl.CostEstimate(
            flops=cells * 576 * 768 * 6, bytes_accessed=12 * MIB, transcendentals=cells * 768
        ),
        name="heads",
    )(taps, target, spot, goal, stats, conv, bias, heat_w, heat_b, box_w, box_b)


MESH = pl.DeviceIdType.MESH


def rounded_up(value, step):
    return -(-value // step) * step


def place():
    return lax.axis_index("batch"), lax.axis_index("row"), lax.axis_index("col")


def extents():
    return lax.axis_size("batch"), lax.axis_size("row"), lax.axis_size("col")


def plane_partners():
    batch, row, col = place()
    batches, _, cols = extents()
    partners = []
    for over in range(batches):
        for along in range(cols):
            if over or along:
                partners.append(
                    (lax.rem(batch + over, batches), row, lax.rem(col + along, cols))
                )
    return partners


def row_partners():
    batch, row, col = place()
    rows = lax.axis_size("row")
    return [(batch, lax.rem(row + over, rows), col) for over in range(1, rows)]


def flat():
    batches, rows, cols = extents()
    return batches * rows * cols <= 8


def all_partners():
    batch, row, col = place()
    batches, rows, cols = extents()
    partners = []
    for over in range(batches):
        for up in range(rows):
            for along in range(cols):
                if over or up or along:
                    partners.append(
                        (
                            lax.rem(batch + over, batches),
                            lax.rem(row + up, rows),
                            lax.rem(col + along, cols),
                        )
                    )
    return partners


def greet():
    barrier = pltpu.get_barrier_semaphore()
    partners = all_partners() if flat() else plane_partners() + row_partners()
    for partner in partners:
        pl.semaphore_signal(barrier, inc=1, device_id=partner, device_id_type=MESH)
    batch, row, col = place()
    _, rows, cols = extents()
    expected = len(partners)
    for up in (-1, 1):
        for along in (-1, 1):
            fits = jnp.logical_and(row + up >= 0, row + up < rows)
            fits = jnp.logical_and(fits, jnp.logical_and(col + along >= 0, col + along < cols))
            expected = expected + fits.astype(jnp.int32)

            @pl.when(fits)
            def _(up=up, along=along):
                pl.semaphore_signal(
                    barrier,
                    inc=1,
                    device_id=(batch, row + up, col + along),
                    device_id_type=MESH,
                )

    return expected


def greeted(expected):
    pl.semaphore_wait(pltpu.get_barrier_semaphore(), expected)


def remote(source, target, send, recv, device):
    return pltpu.make_async_remote_copy(
        src_ref=source,
        dst_ref=target,
        send_sem=send,
        recv_sem=recv,
        device_id=device,
        device_id_type=MESH,
    )


def start_all(copies):
    for copy in copies:
        copy.start()


def wait_all(copies):
    for copy in copies:
        copy.wait()


def slot_sum(slots):
    total = slots[0]
    for k in range(1, slots.shape[0]):
        total = total + slots[k]
    return total


class Total:
    def __init__(self, source, slots, mid, row_slots, sems):
        self.source, self.slots, self.mid = source, slots, mid
        self.row_slots, self.sems = row_slots, sems

    def send(self, source, slots, mine, partners, step):
        self.copies = [
            remote(
                source,
                slots.at[mine],
                self.sems.at[step, 0, k],
                self.sems.at[step, 1, k],
                partner,
            )
            for k, partner in enumerate(partners)
        ]
        start_all(self.copies)
        slots[mine] = source[...]

    def begin(self):
        batch, row, col = place()
        _, rows, cols = extents()
        if flat():
            mine, partners = (batch * rows + row) * cols + col, all_partners()
        else:
            mine, partners = batch * cols + col, plane_partners()
        self.send(self.source, self.slots, mine, partners, 0)

    def middle(self):
        if not flat():
            wait_all(self.copies)
            self.mid[...] = slot_sum(self.slots)
            self.send(self.mid, self.row_slots, place()[1], row_partners(), 1)

    def end(self):
        wait_all(self.copies)
        return slot_sum(self.slots if flat() else self.row_slots)


def total_scratch(lines):
    batches, rows, cols = extents()
    slots = batches * cols * (rows if flat() else 1)
    return [
        pltpu.VMEM((lines, 128), F32),
        pltpu.VMEM((slots, lines, 128), F32),
        pltpu.VMEM((lines, 128), F32),
        pltpu.VMEM((rows, lines, 128), F32),
        pltpu.SemaphoreType.DMA((2, 2, max(slots, rows) - 1)),
    ]


AROUND = ((-1, 0), (1, 0), (0, -1), (0, 1), (-1, -1), (-1, 1), (1, -1), (1, 1))


class Around:
    def __init__(self, pieces, slots, sems):
        batch, row, col = place()
        _, rows, cols = extents()

        def exists(up, along):
            fits = jnp.logical_and(row + up >= 0, row + up < rows)
            return jnp.logical_and(fits, jnp.logical_and(col + along >= 0, col + along < cols))

        self.sends = [exists(up, along) for up, along in AROUND]
        self.comes = [exists(-up, -along) for up, along in AROUND]
        self.copies = [
            remote(pieces[k], slots[k], sems.at[0, k], sems.at[1, k], (batch, row + up, col + along))
            for k, (up, along) in enumerate(AROUND)
        ]

    def start(self, which=range(8)):
        for k in which:
            pl.when(self.sends[k])(self.copies[k].start)

    def wait(self, which=range(8)):
        for k in which:
            pl.when(self.comes[k])(self.copies[k].wait_recv)
            pl.when(self.sends[k])(self.copies[k].wait_send)

    def each(self, use, which=range(8)):
        for k in which:
            pl.when(self.comes[k])(functools.partial(use, k))


def twice(values):
    return jnp.concatenate([values, values], axis=-1)


def lower_half(shape):
    return lax.broadcasted_iota(jnp.int32, shape, len(shape) - 1) < 64


def swapped(values):
    return pltpu.roll(values, 64, len(values.shape) - 1)


def widened(values):
    rows, cols = values.shape[0], values.shape[1]
    side = jnp.zeros((rows, 8, 128), F32)
    return jnp.concatenate([side, twice(values.astype(F32)), side], axis=1)


def tap_pairs(buffer, start, count, fill):
    low = lower_half((1, 128))
    first = jnp.where(low, buffer[pl.ds(start - 1, count), :], buffer[pl.ds(start, count), :])
    second = jnp.where(low, buffer[pl.ds(start + 1, count), :], fill)
    return jnp.concatenate([first, second], axis=1)


def silu_parts(values):
    logistic = 0.5 * jnp.tanh(0.5 * values) + 0.5
    return values * logistic, logistic


PAD = 16


def row_loop(total, step, body, init):
    return lax.fori_loop(0, total // step, lambda k, carry: body(k * step, carry), init)


def fold_sum(values):
    return jnp.sum(values.reshape(-1, 8, 128), axis=0)


def clear(buffer, start, rows, pitch, tops, bottoms, lefts, rights):
    _, row_at, col_at = place()
    count = rounded_up(rows, 8)

    def clear_rows(span):
        first, last = span
        size = (last - first) * pitch
        buffer[pl.ds(start + first * pitch, size), :] = jnp.zeros((size, 128), F32)

    def clear_columns(span):
        for column in range(*span):
            buffer[pl.ds(start + column, count, stride=pitch), :] = jnp.zeros((count, 128), F32)

    pl.when(row_at == 0)(lambda: clear_rows(tops))
    pl.when(row_at == lax.axis_size("row") - 1)(lambda: clear_rows(bottoms))
    pl.when(col_at == 0)(lambda: clear_columns(lefts))
    pl.when(col_at == lax.axis_size("col") - 1)(lambda: clear_columns(rights))


def stack_weight(target, source):
    for tap in range(3):
        target[256 * tap : 256 * tap + 192, :] = twice(source[tap].astype(F32)).astype(BF16)
        target[256 * tap + 192 : 256 * tap + 256, :] = jnp.zeros((64, 128), BF16)


def unpacked(packed, image, images):
    low = lower_half((1, 128))
    keep = low if image < images // 2 else jnp.logical_not(low)
    return jnp.where(keep, packed, swapped(packed))


def pack_columns(buffer, target, images, rows, pitch, first_row, first, depth):
    low = lower_half((1, 128))
    half = images // 2
    count = target.shape[1]
    for pair in range(half):
        for j in range(depth):
            parts = [
                buffer[
                    pl.ds(
                        PAD + (image * rows + first_row) * pitch + first + j, count, stride=pitch
                    ),
                    :,
                ]
                for image in (pair, pair + half)
            ]
            target[depth * pair + j] = jnp.where(low, parts[0], parts[1]).astype(target.dtype)


def pack_corner(buffer, target, images, rows, pitch, first_row, first, depth):
    low = lower_half((1, 128))
    half = images // 2
    count = target.shape[1] // 8
    for pair in range(half):
        pieces = []
        for row in range(count):
            if row < depth:
                starts = [
                    PAD + (image * rows + first_row + row) * pitch + first
                    for image in (pair, pair + half)
                ]
                pieces.append(
                    jnp.where(
                        low,
                        buffer[starts[0] : starts[0] + 8, :],
                        buffer[starts[1] : starts[1] + 8, :],
                    )
                )
            else:
                pieces.append(jnp.zeros((8, 128), F32))
        target[pair] = jnp.concatenate(pieces, axis=0).astype(target.dtype)


def unpack_columns(buffer, source, images, rows, pitch, first_row, first, depth, lines, add):
    half = images // 2
    count = rounded_up(lines, 8)
    valid = lax.broadcasted_iota(jnp.int32, (count, 128), 0) < lines
    for image in range(images):
        for j in range(depth):
            packed = source[depth * (image % half) + j].astype(F32)
            values = unpacked(packed, image, images)[:count]
            spots = pl.ds(
                PAD + (image * rows + first_row) * pitch + first + j, count, stride=pitch
            )
            if add:
                values = buffer[spots, :] + jnp.where(valid, values, 0.0)
            elif count > lines:
                values = jnp.where(valid, values, buffer[spots, :])
            buffer[spots, :] = values


def unpack_corner(buffer, source, images, rows, pitch, first_row, first, depth, add):
    half = images // 2
    valid = lax.broadcasted_iota(jnp.int32, (8, 128), 0) < depth
    for image in range(images):
        packed = unpacked(source[image % half].astype(F32), image, images)
        for row in range(depth):
            start = PAD + (image * rows + first_row + row) * pitch + first
            old = buffer[start : start + 8, :]
            values = packed[8 * row : 8 * row + 8]
            if add:
                values = old + jnp.where(valid, values, 0.0)
            else:
                values = jnp.where(valid, values, old)
            buffer[start : start + 8, :] = values


def rise_body(
    low_ref,
    skip_ref,
    target_ref,
    conv_one_ref,
    conv_two_ref,
    gain_one_ref,
    shift_one_ref,
    gain_two_ref,
    shift_two_ref,
    index_ref,
    count_ref,
    y_two_out,
    y_one_out,
    merged_out,
    low_out,
    stat_out,
    spot_out,
    tiles_out,
    low_in,
    skip_in,
    target_in,
    conv_one_in,
    conv_two_in,
    param_in,
    index_in,
    y_two_s,
    y_one_s,
    merged_s,
    low_s,
    low_x,
    skip_x,
    act_s,
    row_s,
    up_s,
    w_one,
    w_two,
    g_low,
    own_low,
    low_rows,
    skip_rows,
    low_send,
    low_recv,
    low_corner,
    skip_send,
    skip_recv,
    skip_corner,
    first_scratch,
    second_scratch,
    in_sems,
    out_sems,
    strip_sems,
):
    images, h, w, _ = low_ref.shape
    height, breadth = skip_ref.shape[1], skip_ref.shape[2]
    batch_at, row_at, col_at = place()
    batches, row_count, col_count = extents()
    pitch, wide = w + 16, breadth + 16
    low_r, y_one_r = h + 6, h + 4
    skip_r, y_two_r = height + 6, height + 4
    cells_low = float(images * batches * h * row_count * w * col_count)
    cells_high = 4.0 * cells_low

    loads = [
        pltpu.make_async_copy(source, target, in_sems.at[k])
        for k, (source, target) in enumerate(
            (
                (low_ref, low_in),
                (conv_one_ref, conv_one_in),
                (skip_ref, skip_in),
                (index_ref, index_in),
                (target_ref, target_in),
                (gain_one_ref, param_in.at[0]),
                (shift_one_ref, param_in.at[1]),
                (gain_two_ref, param_in.at[2]),
                (shift_two_ref, param_in.at[3]),
                (conv_two_ref, conv_two_in),
            )
        )
    ]
    expected = greet()
    for load in loads:
        load.start()
    low_around = Around(
        [low_ref.at[:, 0:3], low_ref.at[:, h - 3 : h]]
        + [low_send.at[k] for k in range(2)]
        + [low_corner.at[0, k] for k in range(4)],
        [low_rows.at[0], low_rows.at[1]]
        + [low_recv.at[k] for k in range(2)]
        + [low_corner.at[1, k] for k in range(4)],
        strip_sems.at[0],
    )
    skip_around = Around(
        [skip_ref.at[:, 0:3], skip_ref.at[:, height - 3 : height]]
        + [skip_send.at[k] for k in range(2)]
        + [skip_corner.at[0, k] for k in range(4)],
        [skip_rows.at[0], skip_rows.at[1]]
        + [skip_recv.at[k] for k in range(2)]
        + [skip_corner.at[1, k] for k in range(4)],
        strip_sems.at[1],
    )

    def place_low(b, carry):
        start = PAD + b * low_r * pitch
        low_x[pl.ds(start, 3 * pitch), :] = jnp.zeros((3 * pitch, 128), F32)
        low_x[pl.ds(start + 3 * pitch, h * pitch), :] = widened(low_in[b]).reshape(h * pitch, 128)
        low_x[pl.ds(start + (h + 3) * pitch, 3 * pitch), :] = jnp.zeros((3 * pitch, 128), F32)
        return carry

    low_x[0:PAD, :] = jnp.zeros((PAD, 128), F32)
    tail = low_x.shape[0] - PAD - images * low_r * pitch
    low_x[PAD + images * low_r * pitch :, :] = jnp.zeros((tail, 128), F32)
    loads[0].wait()
    lax.fori_loop(0, images, place_low, 0)

    def pack(buffer, sends, corners, rows, step, line, across):
        for side, first in enumerate((8, 5 + across)):
            pack_columns(buffer, sends.at[side], images, rows, line, 3, first, 3)
        for k, (up, along) in enumerate(AROUND[4:]):
            pack_corner(
                buffer,
                corners.at[0, k],
                images,
                rows,
                line,
                3 if up < 0 else step,
                8 if along < 0 else 5 + across,
                3,
            )

    def unpack(around, buffer, strips, columns, corners, rows, step, line, across):
        def use(k):
            up, along = AROUND[k]
            row = step + 3 if up < 0 else 0
            column = 8 + across if along < 0 else 5
            if k < 2:

                def body(b, carry):
                    start = PAD + (b * rows + row) * line
                    buffer[pl.ds(start, 3 * line), :] = widened(strips[k, b]).reshape(
                        3 * line, 128
                    )
                    return carry

                lax.fori_loop(0, images, body, 0)
            elif k < 4:
                unpack_columns(
                    buffer, columns.at[k - 2], images, rows, line, 3, column, 3, step, False
                )
            else:
                unpack_corner(
                    buffer, corners.at[1, k - 4], images, rows, line, row, column, 3, False
                )

        around.each(use)

    pack(low_x, low_send, low_corner, low_r, h, pitch, w)
    greeted(expected)
    low_around.start()
    skip_around.start(range(2))

    def place_skip(b, carry):
        start = PAD + b * skip_r * wide
        edge = jnp.zeros((3 * wide, 128), F32)
        skip_x[pl.ds(start, 3 * wide), :] = edge
        skip_x[pl.ds(start + 3 * wide, height * wide), :] = widened(skip_in[b]).reshape(
            height * wide, 128
        )
        skip_x[pl.ds(start + (height + 3) * wide, 3 * wide), :] = edge
        return carry

    skip_x[0:PAD, :] = jnp.zeros((PAD, 128), F32)
    skip_tail = skip_x.shape[0] - PAD - images * skip_r * wide
    skip_x[PAD + images * skip_r * wide :, :] = jnp.zeros((skip_tail, 128), F32)
    loads[2].wait()
    lax.fori_loop(0, images, place_skip, 0)
    pack(skip_x, skip_send, skip_corner, skip_r, height, wide, breadth)
    skip_around.start(range(2, 8))
    loads[1].wait()
    stack_weight(w_one, conv_one_in)
    low_around.wait()
    unpack(low_around, low_x, low_rows, low_recv, low_corner, low_r, h, pitch, w)

    def conv_one(b, sums):
        pairs = tap_pairs(low_x, PAD + b * low_r * pitch, low_r * pitch, 0.0)
        own = pairs.reshape(low_r, pitch, 256)[2 : h + 4, 8 : 8 + w]
        low_s[b] = own.astype(BF16)
        lines = jnp.sum(own.astype(BF16).astype(F32), axis=1)
        tap_sums = [
            sums[2 + tap] + jnp.sum(lines[tap : tap + h], axis=0, keepdims=True)
            for tap in range(3)
        ]
        pairs = pairs.astype(BF16)
        count = y_one_r * pitch
        taps = jnp.concatenate([pairs[pitch * a : pitch * a + count] for a in range(3)], axis=1)
        value = dot(taps, w_one[...]).reshape(y_one_r, pitch, 128)
        y_one_s[b] = value
        own = value[2 : h + 2, 8 : 8 + w].reshape(h * w, 128)
        return (
            sums[0] + jnp.sum(own, axis=0, keepdims=True),
            sums[1] + jnp.sum(own * own, axis=0, keepdims=True),
            *tap_sums,
        )

    def count_ones(b, total):
        ones = (target_in[b].reshape(height * breadth, 80).astype(F32) == 1.0).astype(F32)
        return total + jnp.sum(ones, axis=0, keepdims=True)

    nothing = jnp.zeros((1, 128), F32)
    tap_none = jnp.zeros((1, 256), F32)
    sums = lax.fori_loop(0, images, conv_one, (nothing, nothing, tap_none, tap_none, tap_none))
    tap_sums = sums[2:]
    for k in (3, 4):
        loads[k].wait()
    ones = lax.fori_loop(0, images, count_ones, jnp.zeros((1, 80), F32))
    base = row_at * (height * breadth * col_count) + col_at * breadth
    slot = lax.broadcasted_iota(jnp.int32, (1, 128), 1)
    objects = 0
    spot_out[...] = jnp.full((8, 128), -(2**30), jnp.int32)
    for b in range(images):
        amount = count_ref[b]
        objects = objects + amount
        spot_out[b : b + 1, :] = jnp.where(
            slot < amount, index_in[b : b + 1, :] - base, -(2**30)
        )
    leading = jnp.logical_and(row_at == 0, col_at == 0).astype(F32)
    sum_src = first_scratch[0]
    sum_src[...] = jnp.zeros((8, 128), F32)
    sum_src[0:1, :] = sums[0]
    sum_src[1:2, :] = sums[1]
    sum_src[2:3, 0:80] = ones
    sum_src[3:4, :] = jnp.full((1, 128), objects.astype(F32) * leading)
    first_total = Total(*first_scratch)
    first_total.begin()
    stores = [
        pltpu.make_async_copy(y_one_s, y_one_out, out_sems.at[0, 0]),
        pltpu.make_async_copy(low_s, low_out, out_sems.at[0, 1]),
    ]
    for store in stores:
        store.start()

    loads[9].wait()
    stack_weight(w_two, conv_two_in)
    skip_around.wait()
    unpack(
        skip_around, skip_x, skip_rows, skip_recv, skip_corner, skip_r, height, wide, breadth
    )
    first_total.middle()
    for k in range(5, 9):
        loads[k].wait()
    totals = first_total.end()
    mean_one = totals[0:1] / cells_low
    scale_one = lax.rsqrt(totals[1:2] / cells_low - mean_one * mean_one + EPSILON)
    gain_one, shift_one = twice(param_in[0]), twice(param_in[1])
    gain_two, shift_two = twice(param_in[2]), twice(param_in[3])
    stat_out[...] = jnp.zeros((24, 128), F32)
    stat_out[0:1, :] = mean_one
    stat_out[1:2, :] = scale_one
    positives = jnp.sum(totals[2:3, 0:80], axis=1, keepdims=True)
    stat_out[4:5, :] = jnp.broadcast_to(1.0 / positives, (1, 128))
    stat_out[5:6, :] = 0.5 / totals[3:4]
    stat_out[6:7, :] = gain_one
    stat_out[7:8, :] = shift_one
    stat_out[8:9, :] = gain_two
    stat_out[9:10, :] = shift_two
    ends = (row_at > 0, row_at < row_count - 1, col_at > 0, col_at < col_count - 1)
    for k, inner in enumerate(ends):
        stat_out[10 + k : 11 + k, :] = jnp.full((1, 128), inner.astype(F32))

    def conv_two(b, sums):
        normed = (y_one_s[b] - mean_one) * scale_one
        value, _ = silu_parts(normed * gain_one + shift_one)
        act_s[0 : y_one_r * pitch, :] = value.astype(BF16).astype(F32).reshape(
            y_one_r * pitch, 128
        )
        clear(
            act_s, 0, y_one_r, pitch, (0, 2), (h + 2, h + 4), (6, 8), (8 + w, 10 + w)
        )
        act = act_s[0 : y_one_r * pitch, :].reshape(y_one_r, pitch, 128)
        odd = 0.75 * act[:-1] + 0.25 * act[1:]
        even = 0.75 * act[1:] + 0.25 * act[:-1]
        tall = jnp.stack([odd, even], axis=1).reshape(skip_r * pitch, 128)
        row_s[PAD : PAD + skip_r * pitch, :] = tall
        count = skip_r * pitch
        before = row_s[PAD - 1 : PAD - 1 + count, :]
        behind = row_s[PAD + 1 : PAD + 1 + count, :]
        up_s[pl.ds(0, count, stride=2), :] = 0.75 * tall + 0.25 * before
        up_s[pl.ds(1, count, stride=2), :] = 0.75 * tall + 0.25 * behind
        start = PAD + b * skip_r * wide
        whole = pl.ds(start, skip_r * wide)
        up = up_s[...].reshape(skip_r, 2 * pitch, 128)[:, 8 : 8 + wide]
        merged = up + skip_x[whole, :].reshape(skip_r, wide, 128)
        skip_x[whole, :] = merged.astype(BF16).astype(F32).reshape(skip_r * wide, 128)
        clear(
            skip_x,
            start,
            skip_r,
            wide,
            (0, 3),
            (height + 3, height + 6),
            (5, 8),
            (8 + breadth, 11 + breadth),
        )
        pairs = tap_pairs(skip_x, start, skip_r * wide, 0.0)
        merged_s[b] = pairs.reshape(skip_r, wide, 256)[2 : height + 4, 8 : 8 + breadth].astype(
            BF16
        )
        pltpu.make_async_copy(merged_s.at[b], merged_out.at[b], out_sems.at[1, b]).start()
        pairs = pairs.astype(BF16)
        count = y_two_r * wide
        taps = jnp.concatenate([pairs[wide * a : wide * a + count] for a in range(3)], axis=1)
        value = dot(taps, w_two[...]).reshape(y_two_r, wide, 128)
        y_two_s[b] = value
        pltpu.make_async_copy(y_two_s.at[b], y_two_out.at[b], out_sems.at[2, b]).start()
        own = value[2 : height + 2, 8 : 8 + breadth].reshape(height * breadth, 128)
        return (
            sums[0] + jnp.sum(own, axis=0, keepdims=True),
            sums[1] + jnp.sum(own * own, axis=0, keepdims=True),
        )

    row_s[0:PAD, :] = jnp.zeros((PAD, 128), F32)
    row_s[PAD + skip_r * pitch :, :] = jnp.zeros((PAD, 128), F32)
    sums = lax.fori_loop(0, images, conv_two, (nothing, nothing))
    sum_src = second_scratch[0]
    sum_src[...] = jnp.zeros((8, 128), F32)
    sum_src[0:1, :] = sums[0]
    sum_src[1:2, :] = sums[1]
    for tap in range(3):
        for part in range(2):
            line = 2 + 2 * tap + part
            sum_src[line : line + 1, :] = tap_sums[tap][:, 128 * part : 128 * part + 128]
    second_total = Total(*second_scratch)
    second_total.begin()
    g_low[...] = jnp.zeros_like(g_low)
    own_low[...] = jnp.zeros_like(own_low)

    def normed_taps(b, carry):
        normed = (y_one_s[b, 2 : h + 2] - mean_one) * scale_one
        own_low[2 * w : (h + 2) * w, :] = normed[:, 8 : 8 + w].reshape(h * w, 128)
        g_low[...] += product_of_parts(
            low_s[b].reshape((h + 2) * w, 256), shifted_taps(own_low, h, w)
        )
        return carry

    lax.fori_loop(0, images, normed_taps, 0)
    tiles_out[36:] = jnp.zeros((tiles_out.shape[0] - 36, 8, 128), F32)
    fold(tiles_out, 0, g_low)
    second_total.middle()
    totals = second_total.end()
    mean_two = totals[0:1] / cells_high
    scale_two = lax.rsqrt(totals[1:2] / cells_high - mean_two * mean_two + EPSILON)
    stat_out[2:3, :] = mean_two
    stat_out[3:4, :] = scale_two
    stat_out[16:22, :] = totals[2:8]

    for store in stores:
        store.wait()
    for b in range(images):
        pltpu.make_async_copy(merged_s.at[b], merged_out.at[b], out_sems.at[1, b]).wait()
        pltpu.make_async_copy(y_two_s.at[b], y_two_out.at[b], out_sems.at[2, b]).wait()


def rise(
    low_map,
    skip_map,
    target,
    conv_one,
    conv_two,
    gain_one,
    shift_one,
    gain_two,
    shift_two,
    index,
    count,
):
    images, h, w, _ = low_map.shape
    _, height, breadth, _ = skip_map.shape
    pitch, wide = w + 16, breadth + 16
    low_r, skip_r = h + 6, height + 6
    half = images // 2
    vmem = pl.BlockSpec(memory_space=pltpu.VMEM)
    hbm = pl.BlockSpec(memory_space=pl.ANY)
    kept = [
        jax.ShapeDtypeStruct((images, height + 4, wide, 128), F32),
        jax.ShapeDtypeStruct((images, h + 4, pitch, 128), F32),
        jax.ShapeDtypeStruct((images, height + 2, breadth, 256), BF16),
        jax.ShapeDtypeStruct((images, h + 2, w, 256), BF16),
    ]
    return pl.pallas_call(
        rise_body,
        in_specs=[hbm] * 10 + [pl.BlockSpec(memory_space=pltpu.SMEM)],
        out_specs=[hbm] * 4 + [vmem] * 3,
        out_shape=kept
        + [jax.ShapeDtypeStruct((24, 128), F32), jax.ShapeDtypeStruct((8, 128), jnp.int32)]
        + [jax.ShapeDtypeStruct((conv_tiles(36), 8, 128), F32)],
        scratch_shapes=[
            pltpu.VMEM(low_map.shape, BF16),
            pltpu.VMEM(skip_map.shape, BF16),
            pltpu.VMEM(target.shape, BF16),
            pltpu.VMEM((3, 192, 64), BF16),
            pltpu.VMEM((3, 192, 64), BF16),
            pltpu.VMEM((4, 1, 64), F32),
            pltpu.VMEM(index.shape, jnp.int32),
        ]
        + [pltpu.VMEM(array.shape, array.dtype) for array in kept]
        + [
            pltpu.VMEM((2 * PAD + (images * low_r + 8) * pitch, 128), F32),
            pltpu.VMEM((2 * PAD + (images * skip_r + 8) * wide, 128), F32),
            pltpu.VMEM((rounded_up(h + 4, 8) * pitch, 128), F32),
            pltpu.VMEM((2 * PAD + skip_r * pitch, 128), F32),
            pltpu.VMEM((2 * skip_r * pitch, 128), F32),
            pltpu.VMEM((768, 128), BF16),
            pltpu.VMEM((768, 128), BF16),
            pltpu.VMEM((256, 256), F32),
            pltpu.VMEM(((h + 4) * w, 128), F32),
            pltpu.VMEM((2, images, 3, w, 64), BF16),
            pltpu.VMEM((2, images, 3, breadth, 64), BF16),
            pltpu.VMEM((2, 3 * half, rounded_up(h, 16), 128), BF16),
            pltpu.VMEM((2, 3 * half, rounded_up(h, 16), 128), BF16),
            pltpu.VMEM((2, 4, half, 32, 128), BF16),
            pltpu.VMEM((2, 3 * half, rounded_up(height, 16), 128), BF16),
            pltpu.VMEM((2, 3 * half, rounded_up(height, 16), 128), BF16),
            pltpu.VMEM((2, 4, half, 32, 128), BF16),
            total_scratch(8),
            total_scratch(8),
            pltpu.SemaphoreType.DMA((10,)),
            pltpu.SemaphoreType.DMA((4, max(images, 2))),
            pltpu.SemaphoreType.DMA((2, 2, 8)),
        ],
        compiler_params=pltpu.CompilerParams(
            collective_id=1, has_side_effects=True, vmem_limit_bytes=60 * MIB
        ),
        name="rise",
    )(
        low_map,
        skip_map,
        target,
        conv_one,
        conv_two,
        gain_one,
        shift_one,
        gain_two,
        shift_two,
        index,
        count,
    )


def levels_of(tiles):
    batch, row, col = place()
    batches, rows, cols = extents()
    pairs = 2 if cols % 2 == 0 else 1
    outer = cols // pairs
    levels = []

    def add(count, mine, device_of):
        left = (levels[-1][3] if levels else tiles) // count
        partners = []
        for over in range(1, count):
            other = lax.rem(mine + over, count)
            partners.append((other, device_of(other)))
        levels.append((count, mine, partners, left))

    low = lax.rem(col, pairs)
    add(pairs, low, lambda k: (batch, row, col - low + k))
    add(
        outer * batches,
        lax.div(col, pairs) * batches + batch,
        lambda k: (lax.rem(k, batches), row, lax.div(k, batches) * pairs + low),
    )
    add(rows, row, lambda k: (batch, k, col))
    return levels


def level_sizes(tiles):
    batches, rows, cols = extents()
    pairs = 2 if cols % 2 == 0 else 1
    sizes = []
    for count in (pairs, cols // pairs * batches, rows):
        tiles = tiles // count
        sizes.append((count, tiles))
    return sizes


class Scatter:
    def __init__(self, source, mids, slots, sems):
        self.parts = [source, *mids]
        self.slots, self.sems = slots, sems
        self.levels = levels_of(source.shape[0])

    def begin(self, level):
        _, _, partners, left = self.levels[level]
        self.copies = [
            remote(
                self.parts[level].at[pl.ds(other * left, left)],
                self.slots[level].at[k],
                self.sems.at[level, 0, k],
                self.sems.at[level, 1, k],
                device,
            )
            for k, (other, device) in enumerate(partners)
        ]
        start_all(self.copies)

    def end(self, level):
        _, mine, partners, left = self.levels[level]
        wait_all(self.copies)
        total = self.parts[level][pl.ds(mine * left, left)].astype(F32)
        for k in range(len(partners)):
            total = total + self.slots[level][k].astype(F32)
        self.parts[level + 1][...] = total.astype(BF16)


class Gather:
    def __init__(self, full, sems):
        self.full, self.sems = full, sems
        self.levels = levels_of(full.shape[0])

    def span(self, level):
        base = 0
        for _, mine, _, left in self.levels[: level + 1]:
            base = base + mine * left
        return pl.ds(base, self.levels[level][3])

    def begin(self, level):
        part = self.full.at[self.span(level)]
        self.copies = [
            remote(part, part, self.sems.at[level, 0, k], self.sems.at[level, 1, k], device)
            for k, (_, device) in enumerate(self.levels[level][2])
        ]
        start_all(self.copies)

    def end(self):
        wait_all(self.copies)


def scatter_scratch(tiles):
    sizes = level_sizes(tiles)
    return (
        tuple(pltpu.VMEM((left, 16, 128), BF16) for _, left in sizes[:-1]),
        tuple(pltpu.VMEM((count - 1, left, 16, 128), BF16) for count, left in sizes),
        level_sems(),
    )


def level_sems():
    return pltpu.SemaphoreType.DMA((3, 2, max(count for count, _ in level_sizes(1)) - 1))


class PlaneReducer:
    def __init__(self, source, slots, mid, row_slots, full, sems):
        batch, row, col = place()
        batches, rows, cols = extents()
        self.source, self.slots, self.mid = source, slots, mid
        self.row_slots, self.full, self.sems = row_slots, full, sems
        self.share = mid.shape[0]
        self.mine = batch * cols + col
        self.row = row

    def begin(self):
        _, _, cols = extents()
        self.copies = []
        for k, (batch, row, col) in enumerate(plane_partners()):
            other = batch * cols + col
            part = self.source.at[pl.ds(other * self.share, self.share)]
            self.copies.append(
                remote(
                    part, self.slots.at[k], self.sems.at[0, 0, k], self.sems.at[0, 1, k],
                    (batch, row, col),
                )
            )
        start_all(self.copies)

    def middle(self):
        wait_all(self.copies)
        total = self.source[pl.ds(self.mine * self.share, self.share)]
        for k in range(self.slots.shape[0]):
            total = total + self.slots[k]
        self.mid[...] = total
        self.copies = [
            remote(
                self.mid, self.row_slots.at[self.row], self.sems.at[1, 0, k],
                self.sems.at[1, 1, k], partner,
            )
            for k, partner in enumerate(row_partners())
        ]
        start_all(self.copies)
        self.row_slots[self.row] = total

    def last(self):
        wait_all(self.copies)
        self.full[pl.ds(self.mine * self.share, self.share)] = slot_sum(self.row_slots)
        part = self.full.at[pl.ds(self.mine * self.share, self.share)]
        self.copies = [
            remote(part, part, self.sems.at[2, 0, k], self.sems.at[2, 1, k], partner)
            for k, partner in enumerate(plane_partners())
        ]
        start_all(self.copies)

    def end(self):
        wait_all(self.copies)


def plane_scratch(tiles):
    batches, rows, cols = extents()
    planes = batches * cols
    share = tiles // planes
    most = max(planes, rows) - 1
    return [
        pltpu.VMEM((tiles, 8, 128), F32),
        pltpu.VMEM((planes - 1, share, 8, 128), F32),
        pltpu.VMEM((share, 8, 128), F32),
        pltpu.VMEM((rows, share, 8, 128), F32),
        pltpu.SemaphoreType.DMA((3, 2, most)),
    ]


def conv_tiles(tiles):
    batches, _, cols = extents()
    planes = batches * cols
    return -(-tiles // planes) * planes


def fold(target, first, grads):
    low = lower_half((1, 128))
    last = grads[0:192, 128:256]
    target[first : first + 24] = grads[0:192, 0:128].reshape(24, 8, 128)
    target[first + 24 : first + 36] = jnp.where(low, last[0:96], swapped(last[96:192])).reshape(
        12, 8, 128
    )


def unfold(source, first):
    pairs = source[first : first + 24].reshape(192, 128)
    last = source[first + 24 : first + 36].reshape(96, 128)
    return [
        pairs[:, 0:64],
        swapped(pairs)[:, 0:64],
        jnp.concatenate([last[:, 0:64], swapped(last)[:, 0:64]], axis=0),
    ]


def shifted_taps(buffer, rows, line):
    count = (rows + 2) * line
    views = [buffer[(2 - tap) * line : (2 - tap) * line + count, :] for tap in range(3)]
    low = lower_half((1, 128))
    return jnp.concatenate(
        [jnp.where(low, views[0], views[1]), jnp.where(low, views[2], 0.0)], axis=1
    )


def product_of_parts(left, right):
    high = right.astype(BF16)
    rest = (right - high.astype(F32)).astype(BF16)
    return dot_left(left, high) + dot_left(left, rest)


def stack_back(target, source):
    for tap in range(3):
        for e in range(3):
            block = source[tap, 64 * e : 64 * e + 64, :].astype(F32)
            start = 256 * tap + 64 * e
            target[start : start + 64, :] = twice(block.T).astype(BF16)
        target[256 * tap + 192 : 256 * tap + 256, :] = jnp.zeros((64, 128), BF16)


def back_pairs(buffer, start, count):
    low = lower_half((1, 128))
    first = jnp.where(low, buffer[pl.ds(start + 1, count), :], buffer[pl.ds(start, count), :])
    second = jnp.where(low, buffer[pl.ds(start - 1, count), :], 0.0)
    return jnp.concatenate([first, second], axis=1).astype(BF16)


def slope_of(values):
    logistic = 0.5 * jnp.tanh(0.5 * values) + 0.5
    return logistic * (1.0 + values * (1.0 - logistic))


def fall_body(
    spread_ref,
    y_two_ref,
    stat_ref,
    load_ref,
    small_ref,
    tiles_ref,
    y_one_ref,
    merged_ref,
    low_ref,
    conv_ref,
    conv_one_ref,
    skip_out,
    zed_out,
    load_out,
    conv_out,
    conv_x_out,
    sums_out,
    weight_out,
    y_two_s,
    slope_s,
    y_one_s,
    merged_s,
    low_s,
    conv_s,
    load_s,
    skip_s,
    share_s,
    grad_x,
    zed_x,
    own_s,
    own_low_s,
    pair_s,
    narrow_s,
    w_two,
    g_two,
    g_one,
    strip_send,
    strip_recv,
    side_send,
    side_recv,
    corners,
    zed_send,
    zed_recv,
    edge_send,
    edge_recv,
    zed_corners,
    third_scratch,
    load_scratch,
    conv_x_scratch,
    conv_scratch,
    gather_sems,
    in_sems,
    map_sems,
    out_sems,
    strip_sems,
    zed_sems,
):
    images, rows, wide, _ = y_two_ref.shape
    height, breadth = rows - 4, wide - 16
    h, w = height // 2, breadth // 2
    pitch, ext = w + 16, height + 2
    zed_rows = h + 2
    half = images // 2
    _, row_at, col_at = place()
    batches, row_count, col_count = extents()
    cells_high = float(images * batches * height * row_count * breadth * col_count)
    low_half = lower_half((1, 128))
    mean_one, scale_one = stat_ref[0:1, :], stat_ref[1:2, :]
    mean_two, scale_two = stat_ref[2:3, :], stat_ref[3:4, :]
    gain_one, shift_one = stat_ref[6:7, :], stat_ref[7:8, :]
    gain_two, shift_two = stat_ref[8:9, :], stat_ref[9:10, :]
    top, bottom = stat_ref[10:11, :], stat_ref[11:12, :]
    left, right = stat_ref[12:13, :], stat_ref[13:14, :]

    def spread_load(b):
        start = PAD + (b * rows + 1) * wide
        return pltpu.make_async_copy(
            spread_ref.at[b], grad_x.at[pl.ds(start, ext * wide)], map_sems.at[0, b]
        )

    def y_two_load(b):
        return pltpu.make_async_copy(y_two_ref.at[b], y_two_s.at[b], map_sems.at[1, b])

    loads = [
        pltpu.make_async_copy(source, target, in_sems.at[k])
        for k, (source, target) in enumerate(
            (
                (load_ref, load_s),
                (tiles_ref, conv_x_scratch[0]),
                (conv_ref, conv_s.at[0]),
                (conv_one_ref, conv_s.at[1]),
                (merged_ref, merged_s),
                (y_one_ref, y_one_s),
                (low_ref, low_s),
            )
        )
    ]
    for b in range(images):
        spread_load(b).start()
    for b in range(images):
        y_two_load(b).start()
    for load in loads:
        load.start()
    grad_x[0:PAD, :] = jnp.zeros((PAD, 128), F32)
    tail = PAD + images * rows * wide
    grad_x[tail:, :] = jnp.zeros((grad_x.shape[0] - tail, 128), F32)
    for b in range(images):
        for line in (0, ext + 1):
            start = PAD + (b * rows + line) * wide
            grad_x[start : start + wide, :] = jnp.zeros((wide, 128), F32)
    greeted(greet())
    for b in range(images):
        spread_load(b).wait()
    for pair in range(half):
        for side, first in enumerate((1, ext - 2)):
            parts = []
            for image in (pair, pair + half):
                start = PAD + (image * rows + first) * wide
                parts.append(grad_x[start : start + 3 * wide, :])
            strip_send[side, pair] = jnp.where(low_half, parts[0], parts[1]).astype(BF16)
    around = Around(
        [strip_send.at[k] for k in range(2)]
        + [side_send.at[k] for k in range(2)]
        + [corners.at[0, k] for k in range(4)],
        [strip_recv.at[k] for k in range(2)]
        + [side_recv.at[k] for k in range(2)]
        + [corners.at[1, k] for k in range(4)],
        strip_sems,
    )
    around.start(range(2))
    for side, first in enumerate((7, 6 + breadth)):
        pack_columns(grad_x, side_send.at[side], images, rows, wide, 1, first, 3)
    for k, (up, along) in enumerate(AROUND[4:]):
        pack_corner(
            grad_x,
            corners.at[0, k],
            images,
            rows,
            wide,
            1 if up < 0 else height,
            7 if along < 0 else 6 + breadth,
            3,
        )
    around.start(range(2, 8))
    loads[0].wait()
    load_sum = Scatter(load_s, (*load_scratch[0], share_s), load_scratch[1], load_scratch[2])
    load_sum.begin(0)

    def begin(b, sums):
        y_two_load(b).wait()
        start = PAD + b * rows * wide
        clear(
            grad_x,
            start,
            rows,
            wide,
            (1, 2),
            (ext, ext + 1),
            (7, 8),
            (8 + breadth, 9 + breadth),
        )
        normed = (y_two_s[b] - mean_two) * scale_two
        slope = slope_of(normed * gain_two + shift_two)
        slope_s[b] = slope
        part = grad_x[pl.ds(start, rows * wide), :].reshape(rows, wide, 128)
        weighted = part * slope
        return sums[0] + fold_sum(weighted), sums[1] + fold_sum(weighted * normed)

    nothing = jnp.zeros((8, 128), F32)
    sums = lax.fori_loop(0, images, begin, (nothing, nothing))
    sum_src = third_scratch[0]
    sum_src[...] = jnp.zeros((16, 128), F32)
    sum_src[0:8, :] = small_ref[...]
    sum_src[8:9, :] = jnp.sum(sums[0], axis=0, keepdims=True)
    sum_src[9:10, :] = jnp.sum(sums[1], axis=0, keepdims=True)
    third_total = Total(*third_scratch)
    third_total.begin()
    load_sum.end(0)
    load_sum.begin(1)
    loads[2].wait()
    stack_back(w_two, conv_s.at[0])
    loads[3].wait()
    stack_back(weight_out, conv_s.at[1])
    g_two[...] = jnp.zeros_like(g_two)
    g_one[...] = jnp.zeros_like(g_one)
    own_s[...] = jnp.zeros_like(own_s)
    own_low_s[...] = jnp.zeros_like(own_low_s)
    narrow_s[...] = jnp.zeros_like(narrow_s)
    zed_x[...] = jnp.zeros_like(zed_x)
    third_total.middle()
    around.wait()

    def use(k):
        up, along = AROUND[k]
        row = height + 1 if up < 0 else 0
        column = 7 + breadth if along < 0 else 6
        if k < 2:
            for image in range(images):
                values = unpacked(strip_recv[k, image % half].astype(F32), image, images)
                start = PAD + (image * rows + row) * wide
                grad_x[start : start + 3 * wide, :] += values
        elif k < 4:
            unpack_columns(
                grad_x, side_recv.at[k - 2], images, rows, wide, 1, column, 3, ext, True
            )
        else:
            unpack_corner(
                grad_x, corners.at[1, k - 4], images, rows, wide, row, column, 3, True
            )

    around.each(use)

    loads[1].wait()
    conv_x_sum = PlaneReducer(*conv_x_scratch[:4], conv_x_out, conv_x_scratch[4])
    totals = third_total.end()
    sums_out[...] = totals
    conv_x_sum.begin()
    load_sum.end(1)
    load_sum.begin(2)
    factor_two = gain_two * scale_two
    shift_part, gain_part = totals[8:9] / cells_high, totals[9:10] / cells_high
    for k in (4, 5, 6):
        loads[k].wait()
    column = lax.broadcasted_iota(jnp.int32, (wide, 128), 0)
    keep = jnp.where(column < 8, left, 1.0)
    keep = jnp.where(column >= 8 + breadth, right, keep)

    def merge(b, sums):
        start = PAD + b * rows * wide
        whole = pl.ds(start, rows * wide)
        normed = (y_two_s[b] - mean_two) * scale_two
        grad_z = grad_x[whole, :].reshape(rows, wide, 128) * slope_s[b]
        grad_y = factor_two * (grad_z - shift_part - normed * gain_part)
        grad_y = (grad_y * keep).astype(BF16).astype(F32)
        grad_x[whole, :] = grad_y.reshape(rows * wide, 128)
        for line, flag in ((0, top), (ext, bottom)):
            span = pl.ds(start + line * wide, 2 * wide)
            grad_x[span, :] = grad_x[span, :] * flag
        own_s[2 * breadth : (height + 2) * breadth, :] = grad_y[
            2 : height + 2, 8 : 8 + breadth
        ].reshape(height * breadth, 128)
        source = merged_s[b].reshape(ext * breadth, 256)
        g_two[...] += dot_left(source, shifted_taps(own_s, height, breadth).astype(BF16))
        pair_s[...] = back_pairs(grad_x, start, rows * wide)
        count = ext * wide
        taps = jnp.concatenate(
            [pair_s[wide * (2 - a) : wide * (2 - a) + count, :] for a in range(3)], axis=1
        )
        merged_grad = dot(taps, w_two[...]).reshape(ext, wide, 128)
        skip_s[b] = merged_grad[1 : height + 1, 8 : 8 + breadth, 0:64]
        pltpu.make_async_copy(skip_s.at[b], skip_out.at[b], out_sems.at[0, b]).start()
        fine = (merged_grad * keep).astype(BF16).astype(F32).reshape(h + 1, 2, wide, 128)
        even, odd = fine[:, 0], fine[:, 1]
        even = jnp.concatenate([even[0:1] * top, even[1:]], axis=0)
        odd = jnp.concatenate([odd[:-1], odd[-1:] * bottom], axis=0)
        short = 0.75 * (odd[:-1] + even[1:]) + 0.25 * (even[:-1] + odd[1:])
        side = jnp.zeros((h, 8, 128), F32)
        count = h * 2 * pitch
        narrow_s[PAD : PAD + count, :] = jnp.concatenate([side, short, side], axis=1).reshape(
            count, 128
        )
        lines = [narrow_s[pl.ds(PAD + k, count // 2, stride=2), :] for k in (-1, 0, 1, 2)]
        act_grad = 0.75 * (lines[1] + lines[2]) + 0.25 * (lines[0] + lines[3])
        act_grad = act_grad.reshape(h, pitch, 128)
        normed = (y_one_s[b, 2 : h + 2] - mean_one) * scale_one
        slope = slope_of(normed * gain_one + shift_one)
        place_at = lax.broadcasted_iota(jnp.int32, (pitch, 128), 0)
        inner = jnp.logical_and(place_at >= 8, place_at < 8 + w)
        grad_z = jnp.where(inner, act_grad * slope, 0.0)
        spot = PAD + (b * zed_rows + 1) * pitch
        zed_x[pl.ds(spot, h * pitch), :] = grad_z.reshape(h * pitch, 128)
        own_low_s[2 * w : (h + 2) * w, :] = grad_z[:, 8 : 8 + w].reshape(h * w, 128)
        g_one[...] += product_of_parts(
            low_s[b].reshape((h + 2) * w, 256), shifted_taps(own_low_s, h, w)
        )
        return sums[0] + fold_sum(grad_z), sums[1] + fold_sum(grad_z * normed)

    sums = lax.fori_loop(0, half, merge, (nothing, nothing))
    gather = Gather(load_out, gather_sems)
    load_sum.end(2)
    load_out[gather.span(2)] = share_s[...]
    gather.begin(2)
    conv_x_sum.middle()
    sums = lax.fori_loop(half, images, merge, sums)
    gather.end()
    gather.begin(1)
    fold(conv_scratch[0], 0, g_two)
    fold(conv_scratch[0], 36, g_one)
    conv_scratch[0][72:] = jnp.zeros((conv_out.shape[0] - 72, 8, 128), F32)
    for k in range(2):
        conv_scratch[0][72, k : k + 1, :] = jnp.sum(sums[k], axis=0, keepdims=True)
    conv_sum = PlaneReducer(*conv_scratch[:4], conv_out, conv_scratch[4])
    conv_sum.begin()
    for pair in range(half):
        for side, line in enumerate((1, h)):
            parts = []
            for image in (pair, pair + half):
                start = PAD + (image * zed_rows + line) * pitch
                parts.append(zed_x[start : start + pitch, :])
            zed_send[side, pair] = jnp.where(low_half, parts[0], parts[1])
    for side, column in enumerate((8, 7 + w)):
        pack_columns(zed_x, edge_send.at[side], images, zed_rows, pitch, 1, column, 1)
    for k, (up, along) in enumerate(AROUND[4:]):
        pack_corner(
            zed_x,
            zed_corners.at[0, k],
            images,
            zed_rows,
            pitch,
            1 if up < 0 else h,
            8 if along < 0 else 7 + w,
            1,
        )
    zed_around = Around(
        [zed_send.at[k] for k in range(2)]
        + [edge_send.at[k] for k in range(2)]
        + [zed_corners.at[0, k] for k in range(4)],
        [zed_recv.at[k] for k in range(2)]
        + [edge_recv.at[k] for k in range(2)]
        + [zed_corners.at[1, k] for k in range(4)],
        zed_sems,
    )
    zed_around.start()
    conv_x_sum.last()
    conv_sum.middle()
    zed_around.wait()

    def use_zed(k):
        up, along = AROUND[k]
        row = h + 1 if up < 0 else 0
        column = 8 + w if along < 0 else 7
        if k < 2:
            for image in range(images):
                start = PAD + (image * zed_rows + row) * pitch
                zed_x[start : start + pitch, :] = unpacked(
                    zed_recv[k, image % half], image, images
                )
        elif k < 4:
            unpack_columns(
                zed_x, edge_recv.at[k - 2], images, zed_rows, pitch, 1, column, 1, h, False
            )
        else:
            unpack_corner(
                zed_x, zed_corners.at[1, k - 4], images, zed_rows, pitch, row, column, 1, False
            )

    zed_around.each(use_zed)

    def zed_store(b):
        return pltpu.make_async_copy(
            zed_x.at[pl.ds(PAD + b * zed_rows * pitch, zed_rows * pitch)],
            zed_out.at[b],
            out_sems.at[1, b],
        )

    for b in range(images):
        zed_store(b).start()
    conv_sum.last()
    gather.end()
    gather.begin(0)
    conv_x_sum.end()
    conv_sum.end()
    gather.end()
    for b in range(images):
        zed_store(b).wait()
        pltpu.make_async_copy(skip_s.at[b], skip_out.at[b], out_sems.at[0, b]).wait()


def fall(
    spread, y_two, stats, load, small, tiles_x, y_one, merged, low, conv_two, conv_one
):
    images, rows, wide, _ = y_two.shape
    height, breadth = rows - 4, wide - 16
    h, w = height // 2, breadth // 2
    pitch, ext, zed_rows = w + 16, height + 2, h + 2
    half = images // 2
    tiles, parts_x, parts = load.shape[0], tiles_x.shape[0], conv_tiles(73)
    vmem = pl.BlockSpec(memory_space=pltpu.VMEM)
    hbm = pl.BlockSpec(memory_space=pl.ANY)
    lines, low_lines = rounded_up(ext, 16), rounded_up(h, 8)
    return pl.pallas_call(
        fall_body,
        in_specs=[hbm] * 2 + [vmem, hbm, vmem] + [hbm] * 6,
        out_specs=[hbm] * 2 + [vmem] * 5,
        out_shape=[
            jax.ShapeDtypeStruct((images, height, breadth, 64), F32),
            jax.ShapeDtypeStruct((images, zed_rows * pitch, 128), F32),
            jax.ShapeDtypeStruct((tiles, 16, 128), BF16),
            jax.ShapeDtypeStruct((parts, 8, 128), F32),
            jax.ShapeDtypeStruct((parts_x, 8, 128), F32),
            jax.ShapeDtypeStruct((16, 128), F32),
            jax.ShapeDtypeStruct((768, 128), BF16),
        ],
        scratch_shapes=[
            pltpu.VMEM(y_two.shape, F32),
            pltpu.VMEM(y_two.shape, F32),
            pltpu.VMEM(y_one.shape, F32),
            pltpu.VMEM(merged.shape, BF16),
            pltpu.VMEM(low.shape, BF16),
            pltpu.VMEM((2, 3, 192, 64), BF16),
            pltpu.VMEM(load.shape, BF16),
            pltpu.VMEM((images, height, breadth, 64), F32),
            pltpu.VMEM((level_sizes(tiles)[-1][1], 16, 128), BF16),
            pltpu.VMEM((2 * PAD + (images * rows + lines - ext) * wide, 128), F32),
            pltpu.VMEM((2 * PAD + (images * zed_rows + 8) * pitch, 128), F32),
            pltpu.VMEM(((height + 4) * breadth, 128), F32),
            pltpu.VMEM(((h + 4) * w, 128), F32),
            pltpu.VMEM((rows * wide, 256), BF16),
            pltpu.VMEM((2 * PAD + h * 2 * pitch, 128), F32),
            pltpu.VMEM((768, 128), BF16),
            pltpu.VMEM((256, 256), F32),
            pltpu.VMEM((256, 256), F32),
            pltpu.VMEM((2, half, 3 * wide, 128), BF16),
            pltpu.VMEM((2, half, 3 * wide, 128), BF16),
            pltpu.VMEM((2, 3 * half, lines, 128), BF16),
            pltpu.VMEM((2, 3 * half, lines, 128), BF16),
            pltpu.VMEM((2, 4, half, 32, 128), BF16),
            pltpu.VMEM((2, half, pitch, 128), F32),
            pltpu.VMEM((2, half, pitch, 128), F32),
            pltpu.VMEM((2, half, low_lines, 128), F32),
            pltpu.VMEM((2, half, low_lines, 128), F32),
            pltpu.VMEM((2, 4, half, 8, 128), F32),
            total_scratch(16),
            scatter_scratch(tiles),
            plane_scratch(parts_x),
            plane_scratch(parts),
            level_sems(),
            pltpu.SemaphoreType.DMA((7,)),
            pltpu.SemaphoreType.DMA((2, images)),
            pltpu.SemaphoreType.DMA((2, images)),
            pltpu.SemaphoreType.DMA((2, 8)),
            pltpu.SemaphoreType.DMA((2, 8)),
        ],
        compiler_params=pltpu.CompilerParams(
            collective_id=2, has_side_effects=True, vmem_limit_bytes=60 * MIB
        ),
        name="fall",
    )(spread, y_two, stats, load, small, tiles_x, y_one, merged, low, conv_two, conv_one)


def finish_body(
    cells_low,
    load_ref,
    rest_ref,
    conv_ref,
    conv_x_ref,
    sums_ref,
    stat_ref,
    zed_ref,
    y_one_ref,
    weight_ref,
    skip_ref,
    conv_one_out,
    gain_one_out,
    shift_one_out,
    conv_two_out,
    gain_two_out,
    shift_two_out,
    head_out,
    head_b_out,
    heat_w_out,
    heat_b_out,
    box_w_out,
    box_b_out,
    low_out,
    skip_out,
    zed_x,
):
    step = pl.program_id(0)
    each, h, w, _ = low_out.shape
    pitch = w + 16
    rows = h + 2
    factor = stat_ref[6:7, :] * stat_ref[1:2, :]
    shift_low, gain_low = conv_ref[72, 0:1, :] / cells_low, conv_ref[72, 1:2, :] / cells_low
    skip_out[...] = skip_ref[...]
    for column in range(head_out.shape[3] // 128):
        block = load_ref[36 * column : 36 * column + 36].astype(F32)
        head_out[:, :, :, 128 * column : 128 * column + 128] = block.reshape(3, 3, 64, 128)

    @pl.when(step == 0)
    def _():
        zed_x[0:PAD, :] = jnp.zeros((PAD, 128), F32)
        zed_x[PAD + rows * pitch :, :] = jnp.zeros((PAD, 128), F32)
        spread = stat_ref[16:24, :].T
        ones = unfold(conv_ref, 36)
        normed = unfold(conv_x_ref, 0)
        for tap, part in enumerate(unfold(conv_ref, 0)):
            conv_two_out[tap] = part.reshape(3, 64, 64)
            count = jnp.concatenate(
                [spread[:, 2 * tap : 2 * tap + 1], spread[0:64, 2 * tap + 1 : 2 * tap + 2]], axis=0
            )
            value = ones[tap] - count * shift_low[:, 0:64] - normed[tap] * gain_low[:, 0:64]
            conv_one_out[tap] = (value * factor[:, 0:64]).reshape(3, 64, 64)
        for column in range(6):
            span = slice(128 * column, 128 * column + 128)
            head_b_out[span] = sums_ref[column : column + 1, :].reshape(128)
        for part in range(2):
            span = slice(128 * part, 128 * part + 128)
            heat_w_out[:, span] = rest_ref[5 * part : 5 * part + 5].astype(F32).reshape(80, 128)
            for box in range(2):
                block = rest_ref[10 + 2 * box + part].astype(F32)
                box_w_out[box, :, span] = block[2 * box : 2 * box + 2, :]
            box_b_out[part : part + 1, :] = sums_ref[7:8, 2 * part : 2 * part + 2]
        heat_b_out[...] = sums_ref[6:7, 0:80]
        shift_two_out[...] = sums_ref[8:9, 0:64]
        gain_two_out[...] = sums_ref[9:10, 0:64]
        shift_one_out[...] = conv_ref[72, 0:1, 0:64]
        gain_one_out[...] = conv_ref[72, 1:2, 0:64]

    for b in range(each):
        normed = (y_one_ref[b, 1 : h + 3] - stat_ref[0:1, :]) * stat_ref[1:2, :]
        grad_z = zed_ref[b].reshape(rows, pitch, 128)
        grad_y = factor * (grad_z - shift_low - normed * gain_low)
        column = lax.broadcasted_iota(jnp.int32, (pitch, 128), 0)
        keep = jnp.where(column < 8, stat_ref[12:13, :], 1.0)
        keep = jnp.where(column >= 8 + w, stat_ref[13:14, :], keep)
        grad_y = (grad_y * keep).astype(BF16).astype(F32)
        zed_x[PAD : PAD + rows * pitch, :] = grad_y.reshape(rows * pitch, 128)
        for line, row in ((0, 10), (rows - 1, 11)):
            span = slice(PAD + line * pitch, PAD + (line + 1) * pitch)
            zed_x[span, :] = zed_x[span, :] * stat_ref[row : row + 1, :]
        pairs = back_pairs(zed_x, PAD, rows * pitch)
        count = h * pitch
        taps = jnp.concatenate(
            [pairs[pitch * (2 - a) : pitch * (2 - a) + count] for a in range(3)], axis=1
        )
        grad = dot(taps, weight_ref[...]).reshape(h, pitch, 128)
        low_out[b] = grad[:, 8 : 8 + w, 0:64]


def finish(load, conv, conv_x, sums, stats, zed, y_one, weight, skip):
    images, y_rows, pitch, _ = y_one.shape
    h, w = y_rows - 4, pitch - 16
    batches, row_count, col_count = extents()
    cells = float(images * batches * h * row_count * w * col_count)
    span = zed.shape[1]
    steps = 2
    each = images // steps
    shapes = [
        (3, 3, 64, 64),
        (1, 64),
        (1, 64),
        (3, 3, 64, 64),
        (1, 64),
        (1, 64),
        (3, 3, 64, 768),
        (768,),
        (80, 256),
        (1, 80),
        (2, 2, 256),
        (2, 2),
        (images, h, w, 64),
        skip.shape,
    ]
    whole = lambda shape: pl.BlockSpec(shape, lambda c: (0,) * len(shape))
    part = lambda shape: pl.BlockSpec(shape, lambda c: (c,) + (0,) * (len(shape) - 1))
    out_specs = [whole(shape) for shape in shapes]
    out_specs[6] = pl.BlockSpec((3, 3, 64, 768 // steps), lambda c: (0, 0, 0, c))
    out_specs[12] = part((each, h, w, 64))
    out_specs[13] = part((each,) + skip.shape[1:])
    return pl.pallas_call(
        functools.partial(finish_body, cells),
        grid=(steps,),
        in_specs=[
            part((216 // steps, 16, 128)),
            pl.BlockSpec((36, 16, 128), lambda c: (6, 0, 0)),
        ]
        + [whole(array.shape) for array in (conv, conv_x, sums, stats)]
        + [
            part((each, span, 128)),
            part((each, y_rows, pitch, 128)),
            whole(weight.shape),
            part((each,) + skip.shape[1:]),
        ],
        out_specs=out_specs,
        out_shape=[jax.ShapeDtypeStruct(shape, F32) for shape in shapes],
        scratch_shapes=[
            pltpu.VMEM((2 * PAD + span, 128), F32),
        ],
        compiler_params=pltpu.CompilerParams(vmem_limit_bytes=60 * MIB),
        name="finish",
    )(load, load, conv, conv_x, sums, stats, zed, y_one, weight, skip)


def local(
    low_map,
    skip_map,
    conv_first,
    gain_first,
    shift_first,
    conv_second,
    gain_second,
    shift_second,
    head_conv,
    head_bias,
    heat_weight,
    heat_bias,
    box_weight,
    box_bias,
    heat_target,
    box_target,
    obj_index,
    obj_count,
):
    batches, rows, cols = extents()
    devices = batches * rows * cols
    conv_one = conv_first.reshape(3, 192, 64)
    conv_two = conv_second.reshape(3, 192, 64)
    y_two, y_one, merged, low, stats, spot, tiles_x = rise(
        low_map,
        skip_map,
        heat_target,
        conv_one,
        conv_two,
        gain_first.reshape(1, 64),
        shift_first.reshape(1, 64),
        gain_second.reshape(1, 64),
        shift_second.reshape(1, 64),
        obj_index,
        obj_count,
    )
    heat_map, box_map, spread, load, small = heads(
        y_two,
        heat_target,
        spot,
        box_target.transpose(0, 2, 1),
        stats,
        head_conv.reshape(3, 192, 768),
        head_bias,
        heat_weight.T,
        heat_bias.reshape(1, 80),
        box_weight.transpose(0, 2, 1),
        box_bias,
        devices,
    )
    images, ext, wide, _ = spread.shape
    grad_skip, zed, load, conv, conv_x, sums, weight = fall(
        spread.reshape(images, ext * wide, 128),
        y_two,
        stats,
        load,
        small,
        tiles_x,
        y_one,
        merged,
        low,
        conv_two,
        conv_one,
    )
    grads = finish(load, conv, conv_x, sums, stats, zed, y_one, weight, grad_skip)
    return (
        heat_map,
        box_map.transpose(0, 1, 3, 2),
        grads[12],
        grads[13],
        grads[0],
        grads[1].reshape(64),
        grads[2].reshape(64),
        grads[3],
        grads[4].reshape(64),
        grads[5].reshape(64),
        grads[6],
        grads[7],
        grads[8].T,
        grads[9].reshape(80),
        grads[10].transpose(0, 2, 1),
        grads[11],
    )


def solution(mesh):
    tile = P("batch", "row", "col", None)
    return jax.shard_map(
        local,
        mesh=mesh,
        in_specs=(tile, tile)
        + (P(),) * 12
        + (tile, P("batch", None, None), P("batch", None), P("batch")),
        out_specs=(tile,) * 4 + (P(),) * 12,
        check_vma=False,
    )
```

```python
import functools

import jax
import jax.numpy as jnp
from jax import lax
from jax.experimental import pallas as pl
from jax.experimental.pallas import tpu as pltpu
from jax.sharding import PartitionSpec as P

EPSILON = 1e-05
F32 = jnp.float32
BF16 = jnp.bfloat16
KEEP = (((1,), (1,)), ((), ()))
LEFT = (((0,), (0,)), ((), ()))
MIB = 1024 * 1024


def dot(left, right):
    return jnp.dot(left, right, preferred_element_type=F32)


def dot_keep(left, right):
    return lax.dot_general(left, right, KEEP, preferred_element_type=F32)


def dot_left(left, right):
    return lax.dot_general(left, right, LEFT, preferred_element_type=F32)


def three_parts(values):
    high = values.astype(BF16)
    rest = values - high.astype(F32)
    mid = rest.astype(BF16)
    return high, mid, (rest - mid.astype(F32)).astype(BF16)


def tile_count(devices):
    return -(-230 // (2 * devices)) * 2 * devices


def heads_body(
    chunks,
    map_side,
    y_two_ref,
    target_ref,
    spot_ref,
    goal_ref,
    stat_ref,
    kernel_s,
    back_s,
    heat_w_ref,
    heat_b_ref,
    box_w_ref,
    box_b_ref,
    heat_out,
    box_out,
    spread_out,
    load_out,
    small_out,
    feat_s,
    taps_ref,
    box_s,
    goal_s,
    wide_s,
    grad_s,
    heat_grad_s,
    box_grad_s,
    heat_sum_s,
    box_sum_s,
):
    image = pl.program_id(0)
    chunk = pl.program_id(1)
    rows, breadth = target_ref.shape[1], target_ref.shape[2]
    cells = rows * breadth
    units = 256

    @pl.when(jnp.logical_and(image == 0, chunk == 0))
    def _():
        empty = jnp.zeros((2, 256), F32)
        for part in range(2):
            pieces = [empty, empty]
            pieces[part] = box_w_ref[part].astype(F32)
            box_s[part] = jnp.concatenate(pieces, axis=0).astype(BF16)
        grad_s[...] = jnp.zeros_like(grad_s)
        heat_grad_s[...] = jnp.zeros_like(heat_grad_s)
        box_grad_s[...] = jnp.zeros_like(box_grad_s)
        heat_sum_s[...] = jnp.zeros_like(heat_sum_s)
        box_sum_s[...] = jnp.zeros_like(box_sum_s)

    @pl.when(chunk == 0)
    def _():
        wide_s[...] = jnp.zeros_like(wide_s)
        ext, wide = taps_ref.shape[0], breadth + 16
        normed = (y_two_ref[0, 1 : ext + 1] - stat_ref[2:3, :]) * stat_ref[3:4, :]
        feature, _ = silu_parts(normed * stat_ref[8:9, :] + stat_ref[9:10, :])
        column = lax.broadcasted_iota(jnp.int32, (wide, 128), 0)
        keep = jnp.where(column < 8, stat_ref[12:13, :], 1.0)
        keep = jnp.where(column >= 8 + breadth, stat_ref[13:14, :], keep)
        feat_s[0:PAD, :] = jnp.zeros((PAD, 128), F32)
        feat_s[PAD : PAD + ext * wide, :] = (feature * keep).reshape(ext * wide, 128)
        feat_s[PAD + ext * wide :, :] = jnp.zeros((PAD, 128), F32)
        for line, row in ((PAD, 10), (PAD + (ext - 1) * wide, 11)):
            feat_s[line : line + wide, :] = feat_s[line : line + wide, :] * stat_ref[row : row + 1]
        pairs = tap_pairs(feat_s, PAD, ext * wide, 1.0)
        taps_ref[...] = pairs.reshape(ext, wide, 256)[:, 8 : 8 + breadth].astype(BF16)
        for place, part in enumerate(three_parts(goal_ref[0])):
            goal_s[place] = part

    first = chunk * rows
    taps = jnp.concatenate(
        [taps_ref[pl.ds(first + tap, rows)].reshape(cells, 256) for tap in range(3)], axis=1
    )
    active, slope = [], []
    for block in range(3):
        weight = kernel_s[:, :, block * units : (block + 1) * units].reshape(768, units)
        hidden = dot(taps, weight)
        turn = jnp.tanh(hidden)
        above = 1.0 + turn
        product = hidden * above
        active.append(product.astype(BF16))
        slope.append(above + product * (1.0 - turn))

    logit = dot_keep(active[0], heat_w_ref[...]) + heat_b_ref[...]
    decay = jnp.exp(-jnp.abs(logit))
    large = 1.0 / (1.0 + decay)
    small = decay * large
    above = logit >= 0.0
    chance = jnp.where(above, large, small)
    heat_out[0] = chance.reshape(rows, breadth, 80)
    target = target_ref[0].reshape(cells, 80).astype(F32)
    positive = target == 1.0
    side = jnp.where(positive, jnp.where(above, small, large), chance)
    value = jnp.where(positive, -logit, logit)
    soft = jnp.maximum(value, 0.0) + jnp.log(1.0 + decay)
    slant = side * side * (2.0 * (1.0 - side) * soft + side)
    gap = 1.0 - target
    gap = gap * gap
    weighting = jnp.where(positive, -1.0, gap * gap) * stat_ref[4:5, 0:80]
    logit_grad = weighting * slant
    logit_low = logit_grad.astype(BF16)

    box_bias = jnp.concatenate([box_b_ref[0:1, :], box_b_ref[1:2, :]], axis=1)
    boxes = dot_keep(active[1], box_s[0]) + dot_keep(active[2], box_s[1]) + box_bias
    box_out[0] = jnp.swapaxes(boxes.reshape(rows, breadth, 4), 1, 2)
    shape = (rows, breadth, 128)
    cell = (first + lax.broadcasted_iota(jnp.int32, shape, 0)) * map_side
    cell = (cell + lax.broadcasted_iota(jnp.int32, shape, 1)).reshape(cells, 128)
    chosen = (cell == spot_ref[pl.ds(image, 1), :]).astype(F32).astype(BF16)
    goals = dot_keep(chosen, goal_s[0]) + dot_keep(chosen, goal_s[1])
    goals = goals + dot_keep(chosen, goal_s[2])
    hit = dot(chosen, jnp.ones((128, 4), BF16))
    miss = boxes - goals
    lane = lax.broadcasted_iota(jnp.int32, (1, 4), 1)
    factor = jnp.where(lane < 2, 0.1, 1.0) * stat_ref[5:6, 0:4]
    box_grad = hit * factor * miss * lax.rsqrt(miss * miss + 1.0)
    box_low = box_grad.astype(BF16)

    heat_sum_s[...] += jnp.sum(logit_low.astype(F32).reshape(cells // 8, 8, 80), axis=0)
    box_sum_s[...] += jnp.sum(box_low.astype(F32).reshape(cells // 8, 8, 4), axis=0)
    heat_grad_s[...] += dot_left(logit_low, active[0])
    for part in range(2):
        box_grad_s[part] += dot_left(box_low, active[1 + part])

    back = [
        dot(logit_low, heat_w_ref[...]),
        dot(box_low, box_s[0]),
        dot(box_low, box_s[1]),
    ]
    grad_hidden = jnp.concatenate(
        [(back[block] * slope[block]).astype(BF16) for block in range(3)], axis=1
    )
    spread = []
    for tap in range(3):
        part = dot(grad_hidden, back_s[:, 256 * tap : 256 * tap + 256])
        spread.append(part.reshape(rows, breadth, 256))
    inner = slice(16, 16 + breadth)
    wide_s[pl.ds(first, 1), inner, :] += spread[0][0:1]
    wide_s[pl.ds(first + 1, 1), inner, :] += spread[0][1:2] + spread[1][0:1]
    wide_s[pl.ds(first + 2, rows - 2), inner, :] = (
        spread[0][2:] + spread[1][1:-1] + spread[2][:-2]
    )
    wide_s[pl.ds(first + rows, 1), inner, :] = spread[1][-1:] + spread[2][-2:-1]
    wide_s[pl.ds(first + rows + 1, 1), inner, :] = spread[2][-1:]
    for tap in range(3):
        grad_s[tap] += dot_left(taps[:, 256 * tap : 256 * tap + 256], grad_hidden)

    @pl.when(chunk == chunks - 1)
    def _():
        reach = breadth + 16
        centre = pltpu.roll(wide_s[:, 8 : 8 + reach, 0:128], 64, 2)
        total = wide_s[:, 9 : 9 + reach, 0:128] + centre + wide_s[:, 7 : 7 + reach, 128:256]
        lanes = lax.broadcasted_iota(jnp.int32, total.shape, 2)
        spread_out[0] = jnp.where(lanes < 64, total, pltpu.roll(total, 64, 2))

    @pl.when(jnp.logical_and(image == pl.num_programs(0) - 1, chunk == chunks - 1))
    def _():
        for column in range(6):
            span = slice(128 * column, 128 * column + 128)
            for tap in range(3):
                start = 36 * column + 12 * tap
                load_out[start : start + 12] = (
                    (0.5 * grad_s[tap, 0:192, span]).reshape(12, 16, 128).astype(BF16)
                )
            small_out[column : column + 1, :] = 0.5 * grad_s[1, 192:193, span]
        for half in range(2):
            span = slice(128 * half, 128 * half + 128)
            start = 216 + 5 * half
            load_out[start : start + 5] = heat_grad_s[:, span].reshape(5, 16, 128).astype(BF16)
            for part in range(2):
                padded = jnp.concatenate(
                    [box_grad_s[part, :, span], jnp.zeros((12, 128), F32)], axis=0
                )
                load_out[226 + 2 * part + half] = padded.astype(BF16)
        load_out[230:] = jnp.zeros((load_out.shape[0] - 230, 16, 128), BF16)
        small_out[6:8, :] = jnp.zeros((2, 128), F32)
        small_out[6:7, 0:80] = jnp.sum(heat_sum_s[...], axis=0, keepdims=True)
        small_out[7:8, 0:4] = jnp.sum(box_sum_s[...], axis=0, keepdims=True)


def heads(
    taps, target, spot, goal, stats, kernel, back, heat_w, heat_b, box_w, box_b, devices
):
    images, height, breadth, classes = target.shape
    rows = height
    chunks = height // rows
    tiles = tile_count(devices)
    whole = lambda *shape: pl.BlockSpec(shape, lambda b, c: (0,) * len(shape))
    cells = images * height * breadth
    return pl.pallas_call(
        functools.partial(heads_body, chunks, breadth * lax.axis_size("col")),
        grid=(images, chunks),
        in_specs=[
            pl.BlockSpec((1, height + 4, breadth + 16, 128), lambda b, c: (b, 0, 0, 0)),
            pl.BlockSpec((1, rows, breadth, classes), lambda b, c: (b, c, 0, 0)),
            whole(8, 128),
            pl.BlockSpec((1, 4, 128), lambda b, c: (b, 0, 0)),
            whole(24, 128),
            whole(3, 256, 768),
            whole(768, 768),
            whole(80, 256),
            whole(1, 80),
            whole(2, 2, 256),
            whole(2, 2),
        ],
        out_specs=[
            pl.BlockSpec((1, rows, breadth, classes), lambda b, c: (b, c, 0, 0)),
            pl.BlockSpec((1, rows, 4, breadth), lambda b, c: (b, c, 0, 0)),
            pl.BlockSpec((1, height + 2, breadth + 16, 128), lambda b, c: (b, 0, 0, 0)),
            whole(tiles, 16, 128),
            whole(8, 128),
        ],
        out_shape=[
            jax.ShapeDtypeStruct((images, height, breadth, classes), F32),
            jax.ShapeDtypeStruct((images, height, 4, breadth), F32),
            jax.ShapeDtypeStruct((images, height + 2, breadth + 16, 128), F32),
            jax.ShapeDtypeStruct((tiles, 16, 128), BF16),
            jax.ShapeDtypeStruct((8, 128), F32),
        ],
        scratch_shapes=[
            pltpu.VMEM((2 * PAD + (height + 2) * (breadth + 16), 128), F32),
            pltpu.VMEM((height + 2, breadth, 256), BF16),
            pltpu.VMEM((2, 4, 256), BF16),
            pltpu.VMEM((3, 4, 128), BF16),
            pltpu.VMEM((height + 2, breadth + 32, 256), F32),
            pltpu.VMEM((3, 256, 768), F32),
            pltpu.VMEM((80, 256), F32),
            pltpu.VMEM((2, 4, 256), F32),
            pltpu.VMEM((8, 80), F32),
            pltpu.VMEM((8, 4), F32),
        ],
        compiler_params=pltpu.CompilerParams(vmem_limit_bytes=60 * MIB),
        cost_estimate=pl.CostEstimate(
            flops=cells * 576 * 768 * 6, bytes_accessed=12 * MIB, transcendentals=cells * 768
        ),
        name="heads",
    )(taps, target, spot, goal, stats, kernel, back, heat_w, heat_b, box_w, box_b)


MESH = pl.DeviceIdType.MESH


def rounded_up(value, step):
    return -(-value // step) * step


def place():
    return lax.axis_index("batch"), lax.axis_index("row"), lax.axis_index("col")


def extents():
    return lax.axis_size("batch"), lax.axis_size("row"), lax.axis_size("col")


def plane_partners():
    batch, row, col = place()
    batches, _, cols = extents()
    partners = []
    for over in range(batches):
        for along in range(cols):
            if over or along:
                partners.append(
                    (lax.rem(batch + over, batches), row, lax.rem(col + along, cols))
                )
    return partners


def row_partners():
    batch, row, col = place()
    rows = lax.axis_size("row")
    return [(batch, lax.rem(row + over, rows), col) for over in range(1, rows)]


def flat():
    batches, rows, cols = extents()
    return batches * rows * cols <= 8


def all_partners():
    batch, row, col = place()
    batches, rows, cols = extents()
    partners = []
    for over in range(batches):
        for up in range(rows):
            for along in range(cols):
                if over or up or along:
                    partners.append(
                        (
                            lax.rem(batch + over, batches),
                            lax.rem(row + up, rows),
                            lax.rem(col + along, cols),
                        )
                    )
    return partners


def greet():
    barrier = pltpu.get_barrier_semaphore()
    partners = all_partners() if flat() else plane_partners() + row_partners()
    for partner in partners:
        pl.semaphore_signal(barrier, inc=1, device_id=partner, device_id_type=MESH)
    batch, row, col = place()
    _, rows, cols = extents()
    expected = len(partners)
    for up in (-1, 1):
        for along in (-1, 1):
            fits = jnp.logical_and(row + up >= 0, row + up < rows)
            fits = jnp.logical_and(fits, jnp.logical_and(col + along >= 0, col + along < cols))
            expected = expected + fits.astype(jnp.int32)

            @pl.when(fits)
            def _(up=up, along=along):
                pl.semaphore_signal(
                    barrier,
                    inc=1,
                    device_id=(batch, row + up, col + along),
                    device_id_type=MESH,
                )

    return expected


def greeted(expected):
    pl.semaphore_wait(pltpu.get_barrier_semaphore(), expected)


def remote(source, target, send, recv, device):
    return pltpu.make_async_remote_copy(
        src_ref=source,
        dst_ref=target,
        send_sem=send,
        recv_sem=recv,
        device_id=device,
        device_id_type=MESH,
    )


def start_all(copies):
    for copy in copies:
        copy.start()


def wait_all(copies):
    for copy in copies:
        copy.wait()


def slot_sum(slots):
    total = slots[0]
    for k in range(1, slots.shape[0]):
        total = total + slots[k]
    return total


class Total:
    def __init__(self, source, slots, mid, row_slots, sems):
        self.source, self.slots, self.mid = source, slots, mid
        self.row_slots, self.sems = row_slots, sems

    def send(self, source, slots, mine, partners, step):
        self.copies = [
            remote(
                source,
                slots.at[mine],
                self.sems.at[step, 0, k],
                self.sems.at[step, 1, k],
                partner,
            )
            for k, partner in enumerate(partners)
        ]
        start_all(self.copies)
        slots[mine] = source[...]

    def begin(self):
        batch, row, col = place()
        _, rows, cols = extents()
        if flat():
            mine, partners = (batch * rows + row) * cols + col, all_partners()
        else:
            mine, partners = batch * cols + col, plane_partners()
        self.send(self.source, self.slots, mine, partners, 0)

    def middle(self):
        if not flat():
            wait_all(self.copies)
            self.mid[...] = slot_sum(self.slots)
            self.send(self.mid, self.row_slots, place()[1], row_partners(), 1)

    def end(self):
        wait_all(self.copies)
        return slot_sum(self.slots if flat() else self.row_slots)


def total_scratch(lines):
    batches, rows, cols = extents()
    slots = batches * cols * (rows if flat() else 1)
    return [
        pltpu.VMEM((lines, 128), F32),
        pltpu.VMEM((slots, lines, 128), F32),
        pltpu.VMEM((lines, 128), F32),
        pltpu.VMEM((rows, lines, 128), F32),
        pltpu.SemaphoreType.DMA((2, 2, max(slots, rows) - 1)),
    ]


AROUND = ((-1, 0), (1, 0), (0, -1), (0, 1), (-1, -1), (-1, 1), (1, -1), (1, 1))


class Around:
    def __init__(self, pieces, slots, sems):
        batch, row, col = place()
        _, rows, cols = extents()

        def exists(up, along):
            fits = jnp.logical_and(row + up >= 0, row + up < rows)
            return jnp.logical_and(fits, jnp.logical_and(col + along >= 0, col + along < cols))

        self.sends = [exists(up, along) for up, along in AROUND]
        self.comes = [exists(-up, -along) for up, along in AROUND]
        self.copies = [
            remote(pieces[k], slots[k], sems.at[0, k], sems.at[1, k], (batch, row + up, col + along))
            for k, (up, along) in enumerate(AROUND)
        ]

    def start(self, which=range(8)):
        for k in which:
            pl.when(self.sends[k])(self.copies[k].start)

    def wait(self, which=range(8)):
        for k in which:
            pl.when(self.comes[k])(self.copies[k].wait_recv)
            pl.when(self.sends[k])(self.copies[k].wait_send)

    def each(self, use, which=range(8)):
        for k in which:
            pl.when(self.comes[k])(functools.partial(use, k))


def twice(values):
    return jnp.concatenate([values, values], axis=-1)


def lower_half(shape):
    return lax.broadcasted_iota(jnp.int32, shape, len(shape) - 1) < 64


def swapped(values):
    return pltpu.roll(values, 64, len(values.shape) - 1)


def widened(values):
    rows, cols = values.shape[0], values.shape[1]
    side = jnp.zeros((rows, 8, 128), F32)
    return jnp.concatenate([side, twice(values.astype(F32)), side], axis=1)


def tap_pairs(buffer, start, count, fill):
    low = lower_half((1, 128))
    first = jnp.where(low, buffer[pl.ds(start - 1, count), :], buffer[pl.ds(start, count), :])
    second = jnp.where(low, buffer[pl.ds(start + 1, count), :], fill)
    return jnp.concatenate([first, second], axis=1)


def silu_parts(values):
    logistic = 0.5 * jnp.tanh(0.5 * values) + 0.5
    return values * logistic, logistic


PAD = 16


def row_loop(total, step, body, init):
    return lax.fori_loop(0, total // step, lambda k, carry: body(k * step, carry), init)


def fold_sum(values):
    return jnp.sum(values.reshape(-1, 8, 128), axis=0)


def clear(buffer, start, rows, pitch, tops, bottoms, lefts, rights):
    _, row_at, col_at = place()
    count = rounded_up(rows, 8)

    def clear_rows(span):
        first, last = span
        size = (last - first) * pitch
        buffer[pl.ds(start + first * pitch, size), :] = jnp.zeros((size, 128), F32)

    def clear_columns(span):
        for column in range(*span):
            buffer[pl.ds(start + column, count, stride=pitch), :] = jnp.zeros((count, 128), F32)

    pl.when(row_at == 0)(lambda: clear_rows(tops))
    pl.when(row_at == lax.axis_size("row") - 1)(lambda: clear_rows(bottoms))
    pl.when(col_at == 0)(lambda: clear_columns(lefts))
    pl.when(col_at == lax.axis_size("col") - 1)(lambda: clear_columns(rights))


def stack_weight(target, source):
    for tap in range(3):
        target[256 * tap : 256 * tap + 192, :] = twice(source[tap].astype(F32)).astype(BF16)
        target[256 * tap + 192 : 256 * tap + 256, :] = jnp.zeros((64, 128), BF16)


def unpacked(packed, image, images):
    low = lower_half((1, 128))
    keep = low if image < images // 2 else jnp.logical_not(low)
    return jnp.where(keep, packed, swapped(packed))


def pack_columns(buffer, target, images, rows, pitch, first_row, first, depth):
    low = lower_half((1, 128))
    half = images // 2
    count = target.shape[1]
    for pair in range(half):
        for j in range(depth):
            parts = [
                buffer[
                    pl.ds(
                        PAD + (image * rows + first_row) * pitch + first + j, count, stride=pitch
                    ),
                    :,
                ]
                for image in (pair, pair + half)
            ]
            target[depth * pair + j] = jnp.where(low, parts[0], parts[1]).astype(target.dtype)


def pack_corner(buffer, target, images, rows, pitch, first_row, first, depth):
    low = lower_half((1, 128))
    half = images // 2
    count = target.shape[1] // 8
    for pair in range(half):
        pieces = []
        for row in range(count):
            if row < depth:
                starts = [
                    PAD + (image * rows + first_row + row) * pitch + first
                    for image in (pair, pair + half)
                ]
                pieces.append(
                    jnp.where(
                        low,
                        buffer[starts[0] : starts[0] + 8, :],
                        buffer[starts[1] : starts[1] + 8, :],
                    )
                )
            else:
                pieces.append(jnp.zeros((8, 128), F32))
        target[pair] = jnp.concatenate(pieces, axis=0).astype(target.dtype)


def unpack_columns(buffer, source, images, rows, pitch, first_row, first, depth, lines, add):
    half = images // 2
    count = rounded_up(lines, 8)
    valid = lax.broadcasted_iota(jnp.int32, (count, 128), 0) < lines
    for image in range(images):
        for j in range(depth):
            packed = source[depth * (image % half) + j].astype(F32)
            values = unpacked(packed, image, images)[:count]
            spots = pl.ds(
                PAD + (image * rows + first_row) * pitch + first + j, count, stride=pitch
            )
            if add:
                values = buffer[spots, :] + jnp.where(valid, values, 0.0)
            elif count > lines:
                values = jnp.where(valid, values, buffer[spots, :])
            buffer[spots, :] = values


def unpack_corner(buffer, source, images, rows, pitch, first_row, first, depth, add):
    half = images // 2
    valid = lax.broadcasted_iota(jnp.int32, (8, 128), 0) < depth
    for image in range(images):
        packed = unpacked(source[image % half].astype(F32), image, images)
        for row in range(depth):
            start = PAD + (image * rows + first_row + row) * pitch + first
            old = buffer[start : start + 8, :]
            values = packed[8 * row : 8 * row + 8]
            if add:
                values = old + jnp.where(valid, values, 0.0)
            else:
                values = jnp.where(valid, values, old)
            buffer[start : start + 8, :] = values


def rise_body(
    low_ref,
    skip_ref,
    target_ref,
    conv_one_ref,
    conv_two_ref,
    gain_one_ref,
    shift_one_ref,
    gain_two_ref,
    shift_two_ref,
    index_ref,
    head_ref,
    bias_ref,
    count_ref,
    y_two_out,
    y_one_out,
    merged_out,
    low_out,
    kernel_out,
    back_out,
    stat_out,
    spot_out,
    tiles_out,
    low_in,
    skip_in,
    target_in,
    conv_one_in,
    conv_two_in,
    param_in,
    index_in,
    head_in,
    bias_in,
    y_two_s,
    y_one_s,
    merged_s,
    low_s,
    kernel_s,
    back_s,
    low_x,
    skip_x,
    act_s,
    row_s,
    up_s,
    w_one,
    w_two,
    g_low,
    own_low,
    low_rows,
    skip_rows,
    low_send,
    low_recv,
    low_corner,
    skip_send,
    skip_recv,
    skip_corner,
    first_scratch,
    second_scratch,
    in_sems,
    out_sems,
    strip_sems,
):
    images, h, w, _ = low_ref.shape
    height, breadth = skip_ref.shape[1], skip_ref.shape[2]
    batch_at, row_at, col_at = place()
    batches, row_count, col_count = extents()
    pitch, wide = w + 16, breadth + 16
    low_r, y_one_r = h + 6, h + 4
    skip_r, y_two_r = height + 6, height + 4
    cells_low = float(images * batches * h * row_count * w * col_count)
    cells_high = 4.0 * cells_low

    loads = [
        pltpu.make_async_copy(source, target, in_sems.at[k])
        for k, (source, target) in enumerate(
            (
                (low_ref, low_in),
                (conv_one_ref, conv_one_in),
                (skip_ref, skip_in),
                (index_ref, index_in),
                (target_ref, target_in),
                (gain_one_ref, param_in.at[0]),
                (shift_one_ref, param_in.at[1]),
                (gain_two_ref, param_in.at[2]),
                (shift_two_ref, param_in.at[3]),
                (conv_two_ref, conv_two_in),
                (head_ref, head_in),
                (bias_ref, bias_in),
            )
        )
    ]
    expected = greet()
    for load in loads:
        load.start()
    low_around = Around(
        [low_ref.at[:, 0:3], low_ref.at[:, h - 3 : h]]
        + [low_send.at[k] for k in range(2)]
        + [low_corner.at[0, k] for k in range(4)],
        [low_rows.at[0], low_rows.at[1]]
        + [low_recv.at[k] for k in range(2)]
        + [low_corner.at[1, k] for k in range(4)],
        strip_sems.at[0],
    )
    skip_around = Around(
        [skip_ref.at[:, 0:3], skip_ref.at[:, height - 3 : height]]
        + [skip_send.at[k] for k in range(2)]
        + [skip_corner.at[0, k] for k in range(4)],
        [skip_rows.at[0], skip_rows.at[1]]
        + [skip_recv.at[k] for k in range(2)]
        + [skip_corner.at[1, k] for k in range(4)],
        strip_sems.at[1],
    )

    def place_low(b, carry):
        start = PAD + b * low_r * pitch
        low_x[pl.ds(start, 3 * pitch), :] = jnp.zeros((3 * pitch, 128), F32)
        low_x[pl.ds(start + 3 * pitch, h * pitch), :] = widened(low_in[b]).reshape(h * pitch, 128)
        low_x[pl.ds(start + (h + 3) * pitch, 3 * pitch), :] = jnp.zeros((3 * pitch, 128), F32)
        return carry

    low_x[0:PAD, :] = jnp.zeros((PAD, 128), F32)
    tail = low_x.shape[0] - PAD - images * low_r * pitch
    low_x[PAD + images * low_r * pitch :, :] = jnp.zeros((tail, 128), F32)
    loads[0].wait()
    lax.fori_loop(0, images, place_low, 0)

    def pack(buffer, sends, corners, rows, step, line, across):
        for side, first in enumerate((8, 5 + across)):
            pack_columns(buffer, sends.at[side], images, rows, line, 3, first, 3)
        for k, (up, along) in enumerate(AROUND[4:]):
            pack_corner(
                buffer,
                corners.at[0, k],
                images,
                rows,
                line,
                3 if up < 0 else step,
                8 if along < 0 else 5 + across,
                3,
            )

    def unpack(around, buffer, strips, columns, corners, rows, step, line, across):
        def use(k):
            up, along = AROUND[k]
            row = step + 3 if up < 0 else 0
            column = 8 + across if along < 0 else 5
            if k < 2:

                def body(b, carry):
                    start = PAD + (b * rows + row) * line
                    buffer[pl.ds(start, 3 * line), :] = widened(strips[k, b]).reshape(
                        3 * line, 128
                    )
                    return carry

                lax.fori_loop(0, images, body, 0)
            elif k < 4:
                unpack_columns(
                    buffer, columns.at[k - 2], images, rows, line, 3, column, 3, step, False
                )
            else:
                unpack_corner(
                    buffer, corners.at[1, k - 4], images, rows, line, row, column, 3, False
                )

        around.each(use)

    pack(low_x, low_send, low_corner, low_r, h, pitch, w)
    greeted(expected)
    low_around.start()
    skip_around.start(range(2))

    def place_skip(b, carry):
        start = PAD + b * skip_r * wide
        edge = jnp.zeros((3 * wide, 128), F32)
        skip_x[pl.ds(start, 3 * wide), :] = edge
        skip_x[pl.ds(start + 3 * wide, height * wide), :] = widened(skip_in[b]).reshape(
            height * wide, 128
        )
        skip_x[pl.ds(start + (height + 3) * wide, 3 * wide), :] = edge
        return carry

    skip_x[0:PAD, :] = jnp.zeros((PAD, 128), F32)
    skip_tail = skip_x.shape[0] - PAD - images * skip_r * wide
    skip_x[PAD + images * skip_r * wide :, :] = jnp.zeros((skip_tail, 128), F32)
    loads[2].wait()
    lax.fori_loop(0, images, place_skip, 0)
    pack(skip_x, skip_send, skip_corner, skip_r, height, wide, breadth)
    skip_around.start(range(2, 8))
    loads[1].wait()
    stack_weight(w_one, conv_one_in)
    low_around.wait()
    unpack(low_around, low_x, low_rows, low_recv, low_corner, low_r, h, pitch, w)

    def conv_one(b, sums):
        pairs = tap_pairs(low_x, PAD + b * low_r * pitch, low_r * pitch, 0.0)
        pairs = pairs.astype(BF16)
        count = y_one_r * pitch
        taps = jnp.concatenate([pairs[pitch * a : pitch * a + count] for a in range(3)], axis=1)
        value = dot(taps, w_one[...]).reshape(y_one_r, pitch, 128)
        y_one_s[b] = value
        own = value[2 : h + 2, 8 : 8 + w].reshape(h * w, 128)
        return (
            sums[0] + jnp.sum(own, axis=0, keepdims=True),
            sums[1] + jnp.sum(own * own, axis=0, keepdims=True),
        )

    def own_taps(b, sums):
        pairs = tap_pairs(low_x, PAD + (b * low_r + 2) * pitch, (h + 2) * pitch, 0.0)
        own = pairs.reshape(h + 2, pitch, 256)[:, 8 : 8 + w].astype(BF16)
        low_s[b] = own
        lines = jnp.sum(own.astype(F32), axis=1)
        return [
            sums[tap] + jnp.sum(lines[tap : tap + h], axis=0, keepdims=True) for tap in range(3)
        ]

    def count_ones(b, total):
        ones = (target_in[b].reshape(height * breadth, 80).astype(F32) == 1.0).astype(F32)
        return total + jnp.sum(ones, axis=0, keepdims=True)

    nothing = jnp.zeros((1, 128), F32)
    sums = lax.fori_loop(0, images, conv_one, (nothing, nothing))
    sum_src = first_scratch[0]
    sum_src[...] = jnp.zeros((8, 128), F32)
    sum_src[0:1, :] = sums[0]
    sum_src[1:2, :] = sums[1]
    first_total = Total(*first_scratch)
    first_total.begin()
    stores = [
        pltpu.make_async_copy(y_one_s, y_one_out, out_sems.at[0, 0]),
        pltpu.make_async_copy(low_s, low_out, out_sems.at[0, 1]),
    ]
    stores[0].start()

    loads[9].wait()
    stack_weight(w_two, conv_two_in)
    skip_around.wait()
    unpack(
        skip_around, skip_x, skip_rows, skip_recv, skip_corner, skip_r, height, wide, breadth
    )
    first_total.middle()
    for k in (3, 4):
        loads[k].wait()
    ones = lax.fori_loop(0, images, count_ones, jnp.zeros((1, 80), F32))
    base = row_at * (height * breadth * col_count) + col_at * breadth
    slot = lax.broadcasted_iota(jnp.int32, (1, 128), 1)
    objects = 0
    spot_out[...] = jnp.full((8, 128), -(2**30), jnp.int32)
    for b in range(images):
        amount = count_ref[b]
        objects = objects + amount
        spot_out[b : b + 1, :] = jnp.where(
            slot < amount, index_in[b : b + 1, :] - base, -(2**30)
        )
    leading = jnp.logical_and(row_at == 0, col_at == 0).astype(F32)
    tap_none = jnp.zeros((1, 256), F32)
    tap_sums = lax.fori_loop(0, images, own_taps, [tap_none] * 3)
    stores[1].start()
    for k in range(5, 9):
        loads[k].wait()
    totals = first_total.end()
    mean_one = totals[0:1] / cells_low
    scale_one = lax.rsqrt(totals[1:2] / cells_low - mean_one * mean_one + EPSILON)
    gain_one, shift_one = twice(param_in[0]), twice(param_in[1])
    gain_two, shift_two = twice(param_in[2]), twice(param_in[3])
    stat_out[...] = jnp.zeros((24, 128), F32)
    stat_out[0:1, :] = mean_one
    stat_out[1:2, :] = scale_one
    stat_out[6:7, :] = gain_one
    stat_out[7:8, :] = shift_one
    stat_out[8:9, :] = gain_two
    stat_out[9:10, :] = shift_two
    ends = (row_at > 0, row_at < row_count - 1, col_at > 0, col_at < col_count - 1)
    for k, inner in enumerate(ends):
        stat_out[10 + k : 11 + k, :] = jnp.full((1, 128), inner.astype(F32))

    def conv_two(b, sums):
        normed = (y_one_s[b] - mean_one) * scale_one
        value, _ = silu_parts(normed * gain_one + shift_one)
        act_s[0 : y_one_r * pitch, :] = value.astype(BF16).astype(F32).reshape(
            y_one_r * pitch, 128
        )
        clear(
            act_s, 0, y_one_r, pitch, (0, 2), (h + 2, h + 4), (6, 8), (8 + w, 10 + w)
        )
        act = act_s[0 : y_one_r * pitch, :].reshape(y_one_r, pitch, 128)
        odd = 0.75 * act[:-1] + 0.25 * act[1:]
        even = 0.75 * act[1:] + 0.25 * act[:-1]
        tall = jnp.stack([odd, even], axis=1).reshape(skip_r * pitch, 128)
        row_s[PAD : PAD + skip_r * pitch, :] = tall
        count = skip_r * pitch
        before = row_s[PAD - 1 : PAD - 1 + count, :]
        behind = row_s[PAD + 1 : PAD + 1 + count, :]
        up_s[pl.ds(0, count, stride=2), :] = 0.75 * tall + 0.25 * before
        up_s[pl.ds(1, count, stride=2), :] = 0.75 * tall + 0.25 * behind
        start = PAD + b * skip_r * wide
        whole = pl.ds(start, skip_r * wide)
        up = up_s[...].reshape(skip_r, 2 * pitch, 128)[:, 8 : 8 + wide]
        merged = up + skip_x[whole, :].reshape(skip_r, wide, 128)
        skip_x[whole, :] = merged.astype(BF16).astype(F32).reshape(skip_r * wide, 128)
        clear(
            skip_x,
            start,
            skip_r,
            wide,
            (0, 3),
            (height + 3, height + 6),
            (5, 8),
            (8 + breadth, 11 + breadth),
        )
        pairs = tap_pairs(skip_x, start, skip_r * wide, 0.0)
        merged_s[b] = pairs.reshape(skip_r, wide, 256)[2 : height + 4, 8 : 8 + breadth].astype(
            BF16
        )
        pltpu.make_async_copy(merged_s.at[b], merged_out.at[b], out_sems.at[1, b]).start()
        pairs = pairs.astype(BF16)
        count = y_two_r * wide
        taps = jnp.concatenate([pairs[wide * a : wide * a + count] for a in range(3)], axis=1)
        value = dot(taps, w_two[...]).reshape(y_two_r, wide, 128)
        y_two_s[b] = value
        pltpu.make_async_copy(y_two_s.at[b], y_two_out.at[b], out_sems.at[2, b]).start()
        own = value[2 : height + 2, 8 : 8 + breadth].reshape(height * breadth, 128)
        return (
            sums[0] + jnp.sum(own, axis=0, keepdims=True),
            sums[1] + jnp.sum(own * own, axis=0, keepdims=True),
        )

    row_s[0:PAD, :] = jnp.zeros((PAD, 128), F32)
    row_s[PAD + skip_r * pitch :, :] = jnp.zeros((PAD, 128), F32)
    sums = lax.fori_loop(0, images, conv_two, (nothing, nothing))
    sum_src = second_scratch[0]
    sum_src[...] = jnp.zeros((16, 128), F32)
    sum_src[8:9, 0:80] = ones
    sum_src[9:10, :] = jnp.full((1, 128), objects.astype(F32) * leading)
    sum_src[0:1, :] = sums[0]
    sum_src[1:2, :] = sums[1]
    for tap in range(3):
        for part in range(2):
            line = 2 + 2 * tap + part
            sum_src[line : line + 1, :] = tap_sums[tap][:, 128 * part : 128 * part + 128]
    second_total = Total(*second_scratch)
    second_total.begin()
    g_low[...] = jnp.zeros_like(g_low)
    own_low[...] = jnp.zeros_like(own_low)

    def normed_taps(b, carry):
        normed = (y_one_s[b, 2 : h + 2] - mean_one) * scale_one
        own_low[2 * w : (h + 2) * w, :] = normed[:, 8 : 8 + w].reshape(h * w, 128)
        g_low[...] += product_of_parts(
            low_s[b].reshape((h + 2) * w, 256), shifted_taps(own_low, h, w)
        )
        return carry

    lax.fori_loop(0, images, normed_taps, 0)
    tiles_out[36:] = jnp.zeros((tiles_out.shape[0] - 36, 8, 128), F32)
    fold(tiles_out, 0, g_low)
    second_total.middle()
    for k in (10, 11):
        loads[k].wait()
    for tap in range(3):
        kernel_s[tap, 0:192, :] = (0.5 * head_in[tap].astype(F32)).astype(BF16)
        kernel_s[tap, 192:256, :] = jnp.zeros((64, 768), BF16)
    parts = three_parts(0.5 * bias_in[...].reshape(1, 768))
    which = lax.broadcasted_iota(jnp.int32, (16, 768), 0)
    filled = jnp.zeros((16, 768), F32)
    for place_at in range(3):
        filled = jnp.where(which == place_at, parts[place_at].astype(F32), filled)
    kernel_s[1, 192:208, :] = filled.astype(BF16)
    for tap in range(3):
        for block in range(3):
            span = slice(256 * block, 256 * block + 256)
            back_s[span, 256 * tap : 256 * tap + 256] = (
                kernel_s[tap, :, span].astype(F32).T.astype(BF16)
            )
    stores += [
        pltpu.make_async_copy(kernel_s, kernel_out, out_sems.at[0, 2]),
        pltpu.make_async_copy(back_s, back_out, out_sems.at[0, 3]),
    ]
    for store in stores[2:]:
        store.start()
    totals = second_total.end()
    mean_two = totals[0:1] / cells_high
    scale_two = lax.rsqrt(totals[1:2] / cells_high - mean_two * mean_two + EPSILON)
    stat_out[2:3, :] = mean_two
    stat_out[3:4, :] = scale_two
    stat_out[16:22, :] = totals[2:8]
    positives = jnp.sum(totals[8:9, 0:80], axis=1, keepdims=True)
    stat_out[4:5, :] = jnp.broadcast_to(1.0 / positives, (1, 128))
    stat_out[5:6, :] = 0.5 / totals[9:10]

    for store in stores:
        store.wait()
    for b in range(images):
        pltpu.make_async_copy(merged_s.at[b], merged_out.at[b], out_sems.at[1, b]).wait()
        pltpu.make_async_copy(y_two_s.at[b], y_two_out.at[b], out_sems.at[2, b]).wait()


def rise(
    low_map,
    skip_map,
    target,
    conv_one,
    conv_two,
    gain_one,
    shift_one,
    gain_two,
    shift_two,
    index,
    head,
    bias,
    count,
):
    images, h, w, _ = low_map.shape
    _, height, breadth, _ = skip_map.shape
    pitch, wide = w + 16, breadth + 16
    low_r, skip_r = h + 6, height + 6
    half = images // 2
    vmem = pl.BlockSpec(memory_space=pltpu.VMEM)
    hbm = pl.BlockSpec(memory_space=pl.ANY)
    kept = [
        jax.ShapeDtypeStruct((images, height + 4, wide, 128), F32),
        jax.ShapeDtypeStruct((images, h + 4, pitch, 128), F32),
        jax.ShapeDtypeStruct((images, height + 2, breadth, 256), BF16),
        jax.ShapeDtypeStruct((images, h + 2, w, 256), BF16),
        jax.ShapeDtypeStruct((3, 256, 768), BF16),
        jax.ShapeDtypeStruct((768, 768), BF16),
    ]
    return pl.pallas_call(
        rise_body,
        in_specs=[hbm] * 12 + [pl.BlockSpec(memory_space=pltpu.SMEM)],
        out_specs=[hbm] * 6 + [vmem] * 3,
        out_shape=kept
        + [jax.ShapeDtypeStruct((24, 128), F32), jax.ShapeDtypeStruct((8, 128), jnp.int32)]
        + [jax.ShapeDtypeStruct((conv_tiles(36), 8, 128), F32)],
        scratch_shapes=[
            pltpu.VMEM(low_map.shape, BF16),
            pltpu.VMEM(skip_map.shape, BF16),
            pltpu.VMEM(target.shape, BF16),
            pltpu.VMEM((3, 192, 64), BF16),
            pltpu.VMEM((3, 192, 64), BF16),
            pltpu.VMEM((4, 1, 64), F32),
            pltpu.VMEM(index.shape, jnp.int32),
            pltpu.VMEM((3, 192, 768), BF16),
            pltpu.VMEM((768,), F32),
        ]
        + [pltpu.VMEM(array.shape, array.dtype) for array in kept]
        + [
            pltpu.VMEM((2 * PAD + (images * low_r + 8) * pitch, 128), F32),
            pltpu.VMEM((2 * PAD + (images * skip_r + 8) * wide, 128), F32),
            pltpu.VMEM((rounded_up(h + 4, 8) * pitch, 128), F32),
            pltpu.VMEM((2 * PAD + skip_r * pitch, 128), F32),
            pltpu.VMEM((2 * skip_r * pitch, 128), F32),
            pltpu.VMEM((768, 128), BF16),
            pltpu.VMEM((768, 128), BF16),
            pltpu.VMEM((256, 256), F32),
            pltpu.VMEM(((h + 4) * w, 128), F32),
            pltpu.VMEM((2, images, 3, w, 64), BF16),
            pltpu.VMEM((2, images, 3, breadth, 64), BF16),
            pltpu.VMEM((2, 3 * half, rounded_up(h, 16), 128), BF16),
            pltpu.VMEM((2, 3 * half, rounded_up(h, 16), 128), BF16),
            pltpu.VMEM((2, 4, half, 32, 128), BF16),
            pltpu.VMEM((2, 3 * half, rounded_up(height, 16), 128), BF16),
            pltpu.VMEM((2, 3 * half, rounded_up(height, 16), 128), BF16),
            pltpu.VMEM((2, 4, half, 32, 128), BF16),
            total_scratch(8),
            total_scratch(16),
            pltpu.SemaphoreType.DMA((12,)),
            pltpu.SemaphoreType.DMA((4, max(images, 4))),
            pltpu.SemaphoreType.DMA((2, 2, 8)),
        ],
        compiler_params=pltpu.CompilerParams(
            collective_id=1, has_side_effects=True, vmem_limit_bytes=60 * MIB
        ),
        name="rise",
    )(
        low_map,
        skip_map,
        target,
        conv_one,
        conv_two,
        gain_one,
        shift_one,
        gain_two,
        shift_two,
        index,
        head,
        bias,
        count,
    )


def levels_of(tiles):
    batch, row, col = place()
    batches, rows, cols = extents()
    pairs = 2 if cols % 2 == 0 else 1
    outer = cols // pairs
    levels = []

    def add(count, mine, device_of):
        left = (levels[-1][3] if levels else tiles) // count
        partners = []
        for over in range(1, count):
            other = lax.rem(mine + over, count)
            partners.append((other, device_of(other)))
        levels.append((count, mine, partners, left))

    low = lax.rem(col, pairs)
    add(pairs, low, lambda k: (batch, row, col - low + k))
    add(
        outer * batches,
        lax.div(col, pairs) * batches + batch,
        lambda k: (lax.rem(k, batches), row, lax.div(k, batches) * pairs + low),
    )
    add(rows, row, lambda k: (batch, k, col))
    return levels


def level_sizes(tiles):
    batches, rows, cols = extents()
    pairs = 2 if cols % 2 == 0 else 1
    sizes = []
    for count in (pairs, cols // pairs * batches, rows):
        tiles = tiles // count
        sizes.append((count, tiles))
    return sizes


class Scatter:
    def __init__(self, source, mids, slots, sems):
        self.parts = [source, *mids]
        self.slots, self.sems = slots, sems
        self.levels = levels_of(source.shape[0])

    def begin(self, level):
        _, _, partners, left = self.levels[level]
        self.copies = [
            remote(
                self.parts[level].at[pl.ds(other * left, left)],
                self.slots[level].at[k],
                self.sems.at[level, 0, k],
                self.sems.at[level, 1, k],
                device,
            )
            for k, (other, device) in enumerate(partners)
        ]
        start_all(self.copies)

    def end(self, level):
        _, mine, partners, left = self.levels[level]
        wait_all(self.copies)
        total = self.parts[level][pl.ds(mine * left, left)].astype(F32)
        for k in range(len(partners)):
            total = total + self.slots[level][k].astype(F32)
        self.parts[level + 1][...] = total.astype(BF16)


class Gather:
    def __init__(self, full, sems):
        self.full, self.sems = full, sems
        self.levels = levels_of(full.shape[0])

    def span(self, level):
        base = 0
        for _, mine, _, left in self.levels[: level + 1]:
            base = base + mine * left
        return pl.ds(base, self.levels[level][3])

    def begin(self, level):
        part = self.full.at[self.span(level)]
        self.copies = [
            remote(part, part, self.sems.at[level, 0, k], self.sems.at[level, 1, k], device)
            for k, (_, device) in enumerate(self.levels[level][2])
        ]
        start_all(self.copies)

    def end(self):
        wait_all(self.copies)


def scatter_scratch(tiles):
    sizes = level_sizes(tiles)
    return (
        tuple(pltpu.VMEM((left, 16, 128), BF16) for _, left in sizes[:-1]),
        tuple(pltpu.VMEM((count - 1, left, 16, 128), BF16) for count, left in sizes),
        level_sems(),
    )


def level_sems():
    return pltpu.SemaphoreType.DMA((3, 2, max(count for count, _ in level_sizes(1)) - 1))


class PlaneReducer:
    def __init__(self, source, slots, mid, row_slots, full, sems):
        batch, row, col = place()
        batches, rows, cols = extents()
        self.source, self.slots, self.mid = source, slots, mid
        self.row_slots, self.full, self.sems = row_slots, full, sems
        self.share = mid.shape[0]
        self.mine = batch * cols + col
        self.row = row

    def begin(self):
        _, _, cols = extents()
        self.copies = []
        for k, (batch, row, col) in enumerate(plane_partners()):
            other = batch * cols + col
            part = self.source.at[pl.ds(other * self.share, self.share)]
            self.copies.append(
                remote(
                    part, self.slots.at[k], self.sems.at[0, 0, k], self.sems.at[0, 1, k],
                    (batch, row, col),
                )
            )
        start_all(self.copies)

    def middle(self):
        wait_all(self.copies)
        total = self.source[pl.ds(self.mine * self.share, self.share)]
        for k in range(self.slots.shape[0]):
            total = total + self.slots[k]
        self.mid[...] = total
        self.copies = [
            remote(
                self.mid, self.row_slots.at[self.row], self.sems.at[1, 0, k],
                self.sems.at[1, 1, k], partner,
            )
            for k, partner in enumerate(row_partners())
        ]
        start_all(self.copies)
        self.row_slots[self.row] = total

    def last(self):
        wait_all(self.copies)
        self.full[pl.ds(self.mine * self.share, self.share)] = slot_sum(self.row_slots)
        part = self.full.at[pl.ds(self.mine * self.share, self.share)]
        self.copies = [
            remote(part, part, self.sems.at[2, 0, k], self.sems.at[2, 1, k], partner)
            for k, partner in enumerate(plane_partners())
        ]
        start_all(self.copies)

    def end(self):
        wait_all(self.copies)


def plane_scratch(tiles):
    batches, rows, cols = extents()
    planes = batches * cols
    share = tiles // planes
    most = max(planes, rows) - 1
    return [
        pltpu.VMEM((tiles, 8, 128), F32),
        pltpu.VMEM((planes - 1, share, 8, 128), F32),
        pltpu.VMEM((share, 8, 128), F32),
        pltpu.VMEM((rows, share, 8, 128), F32),
        pltpu.SemaphoreType.DMA((3, 2, most)),
    ]


def conv_tiles(tiles):
    batches, _, cols = extents()
    planes = batches * cols
    return -(-tiles // planes) * planes


def fold(target, first, grads):
    low = lower_half((1, 128))
    last = grads[0:192, 128:256]
    target[first : first + 24] = grads[0:192, 0:128].reshape(24, 8, 128)
    target[first + 24 : first + 36] = jnp.where(low, last[0:96], swapped(last[96:192])).reshape(
        12, 8, 128
    )


def unfold(source, first):
    pairs = source[first : first + 24].reshape(192, 128)
    last = source[first + 24 : first + 36].reshape(96, 128)
    return [
        pairs[:, 0:64],
        swapped(pairs)[:, 0:64],
        jnp.concatenate([last[:, 0:64], swapped(last)[:, 0:64]], axis=0),
    ]


def shifted_taps(buffer, rows, line):
    count = (rows + 2) * line
    views = [buffer[(2 - tap) * line : (2 - tap) * line + count, :] for tap in range(3)]
    low = lower_half((1, 128))
    return jnp.concatenate(
        [jnp.where(low, views[0], views[1]), jnp.where(low, views[2], 0.0)], axis=1
    )


def product_of_parts(left, right):
    high = right.astype(BF16)
    rest = (right - high.astype(F32)).astype(BF16)
    return dot_left(left, high) + dot_left(left, rest)


def stack_back(target, source):
    for tap in range(3):
        for e in range(3):
            block = source[tap, 64 * e : 64 * e + 64, :].astype(F32)
            start = 256 * tap + 64 * e
            target[start : start + 64, :] = twice(block.T).astype(BF16)
        target[256 * tap + 192 : 256 * tap + 256, :] = jnp.zeros((64, 128), BF16)


def back_pairs(buffer, start, count):
    low = lower_half((1, 128))
    first = jnp.where(low, buffer[pl.ds(start + 1, count), :], buffer[pl.ds(start, count), :])
    second = jnp.where(low, buffer[pl.ds(start - 1, count), :], 0.0)
    return jnp.concatenate([first, second], axis=1).astype(BF16)


def slope_of(values):
    logistic = 0.5 * jnp.tanh(0.5 * values) + 0.5
    return logistic * (1.0 + values * (1.0 - logistic))


def fall_body(
    spread_ref,
    y_two_ref,
    stat_ref,
    load_ref,
    small_ref,
    tiles_ref,
    y_one_ref,
    merged_ref,
    low_ref,
    conv_ref,
    conv_one_ref,
    skip_out,
    zed_out,
    load_out,
    conv_out,
    conv_x_out,
    sums_out,
    last_out,
    weight_out,
    y_two_s,
    slope_s,
    y_one_s,
    merged_s,
    low_s,
    conv_s,
    load_s,
    skip_s,
    share_s,
    grad_x,
    zed_x,
    own_s,
    own_low_s,
    pair_s,
    narrow_s,
    w_two,
    g_two,
    g_one,
    total_s,
    strip_send,
    strip_recv,
    side_send,
    side_recv,
    corners,
    zed_send,
    zed_recv,
    edge_send,
    edge_recv,
    zed_corners,
    third_scratch,
    fourth_scratch,
    load_scratch,
    conv_x_scratch,
    conv_scratch,
    gather_sems,
    in_sems,
    map_sems,
    out_sems,
    strip_sems,
    zed_sems,
):
    images, rows, wide, _ = y_two_ref.shape
    height, breadth = rows - 4, wide - 16
    h, w = height // 2, breadth // 2
    pitch, ext = w + 16, height + 2
    zed_rows = h + 2
    half = images // 2
    _, row_at, col_at = place()
    batches, row_count, col_count = extents()
    cells_high = float(images * batches * height * row_count * breadth * col_count)
    low_half = lower_half((1, 128))
    mean_one, scale_one = stat_ref[0:1, :], stat_ref[1:2, :]
    mean_two, scale_two = stat_ref[2:3, :], stat_ref[3:4, :]
    gain_one, shift_one = stat_ref[6:7, :], stat_ref[7:8, :]
    gain_two, shift_two = stat_ref[8:9, :], stat_ref[9:10, :]
    top, bottom = stat_ref[10:11, :], stat_ref[11:12, :]
    left, right = stat_ref[12:13, :], stat_ref[13:14, :]

    def spread_load(b):
        start = PAD + (b * rows + 1) * wide
        return pltpu.make_async_copy(
            spread_ref.at[b], grad_x.at[pl.ds(start, ext * wide)], map_sems.at[0, b]
        )

    def y_two_load(b):
        return pltpu.make_async_copy(y_two_ref.at[b], y_two_s.at[b], map_sems.at[1, b])

    loads = [
        pltpu.make_async_copy(source, target, in_sems.at[k])
        for k, (source, target) in enumerate(
            (
                (load_ref, load_s),
                (tiles_ref, conv_x_scratch[0]),
                (conv_ref, conv_s.at[0]),
                (conv_one_ref, conv_s.at[1]),
                (merged_ref, merged_s),
                (y_one_ref, y_one_s),
                (low_ref, low_s),
            )
        )
    ]
    for b in range(images):
        spread_load(b).start()
    for b in range(images):
        y_two_load(b).start()
    for load in loads:
        load.start()
    grad_x[0:PAD, :] = jnp.zeros((PAD, 128), F32)
    tail = PAD + images * rows * wide
    grad_x[tail:, :] = jnp.zeros((grad_x.shape[0] - tail, 128), F32)
    for b in range(images):
        for line in (0, ext + 1):
            start = PAD + (b * rows + line) * wide
            grad_x[start : start + wide, :] = jnp.zeros((wide, 128), F32)
    greeted(greet())
    for b in range(images):
        spread_load(b).wait()
    for pair in range(half):
        for side, first in enumerate((1, ext - 2)):
            parts = []
            for image in (pair, pair + half):
                start = PAD + (image * rows + first) * wide
                parts.append(grad_x[start : start + 3 * wide, :])
            strip_send[side, pair] = jnp.where(low_half, parts[0], parts[1]).astype(BF16)
    around = Around(
        [strip_send.at[k] for k in range(2)]
        + [side_send.at[k] for k in range(2)]
        + [corners.at[0, k] for k in range(4)],
        [strip_recv.at[k] for k in range(2)]
        + [side_recv.at[k] for k in range(2)]
        + [corners.at[1, k] for k in range(4)],
        strip_sems,
    )
    around.start(range(2))
    for side, first in enumerate((7, 6 + breadth)):
        pack_columns(grad_x, side_send.at[side], images, rows, wide, 1, first, 3)
    for k, (up, along) in enumerate(AROUND[4:]):
        pack_corner(
            grad_x,
            corners.at[0, k],
            images,
            rows,
            wide,
            1 if up < 0 else height,
            7 if along < 0 else 6 + breadth,
            3,
        )
    around.start(range(2, 8))
    loads[0].wait()
    load_sum = Scatter(load_s, (*load_scratch[0], share_s), load_scratch[1], load_scratch[2])
    load_sum.begin(0)

    def begin(b, sums):
        y_two_load(b).wait()
        start = PAD + b * rows * wide
        clear(
            grad_x,
            start,
            rows,
            wide,
            (1, 2),
            (ext, ext + 1),
            (7, 8),
            (8 + breadth, 9 + breadth),
        )
        normed = (y_two_s[b] - mean_two) * scale_two
        slope = slope_of(normed * gain_two + shift_two)
        slope_s[b] = slope
        part = grad_x[pl.ds(start, rows * wide), :].reshape(rows, wide, 128)
        weighted = part * slope
        return sums[0] + fold_sum(weighted), sums[1] + fold_sum(weighted * normed)

    nothing = jnp.zeros((8, 128), F32)
    sums = lax.fori_loop(0, images, begin, (nothing, nothing))
    sum_src = third_scratch[0]
    sum_src[...] = jnp.zeros((16, 128), F32)
    sum_src[0:8, :] = small_ref[...]
    sum_src[8:9, :] = jnp.sum(sums[0], axis=0, keepdims=True)
    sum_src[9:10, :] = jnp.sum(sums[1], axis=0, keepdims=True)
    third_total = Total(*third_scratch)
    third_total.begin()
    load_sum.end(0)
    load_sum.begin(1)
    loads[2].wait()
    stack_back(w_two, conv_s.at[0])
    loads[3].wait()
    stack_back(weight_out, conv_s.at[1])
    g_two[...] = jnp.zeros_like(g_two)
    g_one[...] = jnp.zeros_like(g_one)
    own_s[...] = jnp.zeros_like(own_s)
    own_low_s[...] = jnp.zeros_like(own_low_s)
    narrow_s[...] = jnp.zeros_like(narrow_s)
    zed_x[...] = jnp.zeros_like(zed_x)
    third_total.middle()
    around.wait()

    def use(k):
        up, along = AROUND[k]
        row = height + 1 if up < 0 else 0
        column = 7 + breadth if along < 0 else 6
        if k < 2:
            for image in range(images):
                values = unpacked(strip_recv[k, image % half].astype(F32), image, images)
                start = PAD + (image * rows + row) * wide
                grad_x[start : start + 3 * wide, :] += values
        elif k < 4:
            unpack_columns(
                grad_x, side_recv.at[k - 2], images, rows, wide, 1, column, 3, ext, True
            )
        else:
            unpack_corner(
                grad_x, corners.at[1, k - 4], images, rows, wide, row, column, 3, True
            )

    around.each(use)

    loads[1].wait()
    conv_x_sum = PlaneReducer(*conv_x_scratch[:4], conv_x_out, conv_x_scratch[4])
    totals = third_total.end()
    sums_out[...] = totals
    conv_x_sum.begin()
    load_sum.end(1)
    load_sum.begin(2)
    factor_two = gain_two * scale_two
    shift_part, gain_part = totals[8:9] / cells_high, totals[9:10] / cells_high
    for k in (4, 5, 6):
        loads[k].wait()
    column = lax.broadcasted_iota(jnp.int32, (wide, 128), 0)
    keep = jnp.where(column < 8, left, 1.0)
    keep = jnp.where(column >= 8 + breadth, right, keep)

    def merge(b, sums):
        start = PAD + b * rows * wide
        whole = pl.ds(start, rows * wide)
        normed = (y_two_s[b] - mean_two) * scale_two
        grad_z = grad_x[whole, :].reshape(rows, wide, 128) * slope_s[b]
        grad_y = factor_two * (grad_z - shift_part - normed * gain_part)
        grad_y = (grad_y * keep).astype(BF16).astype(F32)
        grad_x[whole, :] = grad_y.reshape(rows * wide, 128)
        for line, flag in ((0, top), (ext, bottom)):
            span = pl.ds(start + line * wide, 2 * wide)
            grad_x[span, :] = grad_x[span, :] * flag
        own_s[2 * breadth : (height + 2) * breadth, :] = grad_y[
            2 : height + 2, 8 : 8 + breadth
        ].reshape(height * breadth, 128)
        source = merged_s[b].reshape(ext * breadth, 256)
        g_two[...] += dot_left(source, shifted_taps(own_s, height, breadth).astype(BF16))
        pair_s[...] = back_pairs(grad_x, start, rows * wide)
        count = ext * wide
        taps = jnp.concatenate(
            [pair_s[wide * (2 - a) : wide * (2 - a) + count, :] for a in range(3)], axis=1
        )
        merged_grad = dot(taps, w_two[...]).reshape(ext, wide, 128)
        skip_s[b] = merged_grad[1 : height + 1, 8 : 8 + breadth, 0:64]
        pltpu.make_async_copy(skip_s.at[b], skip_out.at[b], out_sems.at[0, b]).start()
        fine = (merged_grad * keep).astype(BF16).astype(F32).reshape(h + 1, 2, wide, 128)
        even, odd = fine[:, 0], fine[:, 1]
        even = jnp.concatenate([even[0:1] * top, even[1:]], axis=0)
        odd = jnp.concatenate([odd[:-1], odd[-1:] * bottom], axis=0)
        short = 0.75 * (odd[:-1] + even[1:]) + 0.25 * (even[:-1] + odd[1:])
        side = jnp.zeros((h, 8, 128), F32)
        count = h * 2 * pitch
        narrow_s[PAD : PAD + count, :] = jnp.concatenate([side, short, side], axis=1).reshape(
            count, 128
        )
        lines = [narrow_s[pl.ds(PAD + k, count // 2, stride=2), :] for k in (-1, 0, 1, 2)]
        act_grad = 0.75 * (lines[1] + lines[2]) + 0.25 * (lines[0] + lines[3])
        act_grad = act_grad.reshape(h, pitch, 128)
        normed = (y_one_s[b, 2 : h + 2] - mean_one) * scale_one
        slope = slope_of(normed * gain_one + shift_one)
        place_at = lax.broadcasted_iota(jnp.int32, (pitch, 128), 0)
        inner = jnp.logical_and(place_at >= 8, place_at < 8 + w)
        grad_z = jnp.where(inner, act_grad * slope, 0.0)
        spot = PAD + (b * zed_rows + 1) * pitch
        zed_x[pl.ds(spot, h * pitch), :] = grad_z.reshape(h * pitch, 128)
        own_low_s[2 * w : (h + 2) * w, :] = grad_z[:, 8 : 8 + w].reshape(h * w, 128)
        g_one[...] += product_of_parts(
            low_s[b].reshape((h + 2) * w, 256), shifted_taps(own_low_s, h, w)
        )
        return sums[0] + fold_sum(grad_z), sums[1] + fold_sum(grad_z * normed)

    sums = lax.fori_loop(0, half, merge, (nothing, nothing))
    gather = Gather(load_out, gather_sems)
    load_sum.end(2)
    load_out[gather.span(2)] = share_s[...]
    gather.begin(2)
    conv_x_sum.middle()
    sums = lax.fori_loop(half, images, merge, sums)
    last_src = fourth_scratch[0]
    last_src[...] = jnp.zeros((8, 128), F32)
    last_src[0:1, :] = jnp.sum(sums[0], axis=0, keepdims=True)
    last_src[1:2, :] = jnp.sum(sums[1], axis=0, keepdims=True)
    fourth_total = Total(*fourth_scratch)
    fourth_total.begin()
    gather.end()
    gather.begin(1)
    fold(conv_scratch[0], 0, g_two)
    fold(conv_scratch[0], 36, g_one)
    if conv_out.shape[0] > 72:
        conv_scratch[0][72:] = jnp.zeros((conv_out.shape[0] - 72, 8, 128), F32)
    conv_sum = PlaneReducer(*conv_scratch[:4], conv_out, conv_scratch[4])
    conv_sum.begin()
    for pair in range(half):
        for side, line in enumerate((1, h)):
            parts = []
            for image in (pair, pair + half):
                start = PAD + (image * zed_rows + line) * pitch
                parts.append(zed_x[start : start + pitch, :])
            zed_send[side, pair] = jnp.where(low_half, parts[0], parts[1])
    for side, column in enumerate((8, 7 + w)):
        pack_columns(zed_x, edge_send.at[side], images, zed_rows, pitch, 1, column, 1)
    for k, (up, along) in enumerate(AROUND[4:]):
        pack_corner(
            zed_x,
            zed_corners.at[0, k],
            images,
            zed_rows,
            pitch,
            1 if up < 0 else h,
            8 if along < 0 else 7 + w,
            1,
        )
    zed_around = Around(
        [zed_send.at[k] for k in range(2)]
        + [edge_send.at[k] for k in range(2)]
        + [zed_corners.at[0, k] for k in range(4)],
        [zed_recv.at[k] for k in range(2)]
        + [edge_recv.at[k] for k in range(2)]
        + [zed_corners.at[1, k] for k in range(4)],
        zed_sems,
    )
    zed_around.start()
    fourth_total.middle()
    conv_x_sum.last()
    conv_sum.middle()
    zed_around.wait()

    def use_zed(k):
        up, along = AROUND[k]
        row = h + 1 if up < 0 else 0
        column = 8 + w if along < 0 else 7
        if k < 2:
            for image in range(images):
                start = PAD + (image * zed_rows + row) * pitch
                zed_x[start : start + pitch, :] = unpacked(
                    zed_recv[k, image % half], image, images
                )
        elif k < 4:
            unpack_columns(
                zed_x, edge_recv.at[k - 2], images, zed_rows, pitch, 1, column, 1, h, False
            )
        else:
            unpack_corner(
                zed_x, zed_corners.at[1, k - 4], images, zed_rows, pitch, row, column, 1, False
            )

    zed_around.each(use_zed)

    def zed_store(b):
        return pltpu.make_async_copy(
            zed_x.at[pl.ds(PAD + b * zed_rows * pitch, zed_rows * pitch)],
            zed_out.at[b],
            out_sems.at[1, b],
        )

    for b in range(images):
        zed_store(b).start()
    last_out[...] = fourth_total.end()
    conv_sum.last()
    gather.end()
    gather.begin(0)
    conv_x_sum.end()
    conv_sum.end()
    gather.end()
    for b in range(images):
        zed_store(b).wait()
        pltpu.make_async_copy(skip_s.at[b], skip_out.at[b], out_sems.at[0, b]).wait()


def fall(
    spread, y_two, stats, load, small, tiles_x, y_one, merged, low, conv_two, conv_one
):
    images, rows, wide, _ = y_two.shape
    height, breadth = rows - 4, wide - 16
    h, w = height // 2, breadth // 2
    pitch, ext, zed_rows = w + 16, height + 2, h + 2
    half = images // 2
    tiles, parts_x, parts = load.shape[0], tiles_x.shape[0], conv_tiles(72)
    vmem = pl.BlockSpec(memory_space=pltpu.VMEM)
    hbm = pl.BlockSpec(memory_space=pl.ANY)
    lines, low_lines = rounded_up(ext, 16), rounded_up(h, 8)
    return pl.pallas_call(
        fall_body,
        in_specs=[hbm] * 2 + [vmem, hbm, vmem] + [hbm] * 6,
        out_specs=[hbm] * 2 + [vmem] * 6,
        out_shape=[
            jax.ShapeDtypeStruct((images, height, breadth, 64), F32),
            jax.ShapeDtypeStruct((images, zed_rows * pitch, 128), F32),
            jax.ShapeDtypeStruct((tiles, 16, 128), BF16),
            jax.ShapeDtypeStruct((parts, 8, 128), F32),
            jax.ShapeDtypeStruct((parts_x, 8, 128), F32),
            jax.ShapeDtypeStruct((16, 128), F32),
            jax.ShapeDtypeStruct((8, 128), F32),
            jax.ShapeDtypeStruct((768, 128), BF16),
        ],
        scratch_shapes=[
            pltpu.VMEM(y_two.shape, F32),
            pltpu.VMEM(y_two.shape, F32),
            pltpu.VMEM(y_one.shape, F32),
            pltpu.VMEM(merged.shape, BF16),
            pltpu.VMEM(low.shape, BF16),
            pltpu.VMEM((2, 3, 192, 64), BF16),
            pltpu.VMEM(load.shape, BF16),
            pltpu.VMEM((images, height, breadth, 64), F32),
            pltpu.VMEM((level_sizes(tiles)[-1][1], 16, 128), BF16),
            pltpu.VMEM((2 * PAD + (images * rows + lines - ext) * wide, 128), F32),
            pltpu.VMEM((2 * PAD + (images * zed_rows + 8) * pitch, 128), F32),
            pltpu.VMEM(((height + 4) * breadth, 128), F32),
            pltpu.VMEM(((h + 4) * w, 128), F32),
            pltpu.VMEM((rows * wide, 256), BF16),
            pltpu.VMEM((2 * PAD + h * 2 * pitch, 128), F32),
            pltpu.VMEM((768, 128), BF16),
            pltpu.VMEM((256, 256), F32),
            pltpu.VMEM((256, 256), F32),
            pltpu.VMEM((2, 8, 128), F32),
            pltpu.VMEM((2, half, 3 * wide, 128), BF16),
            pltpu.VMEM((2, half, 3 * wide, 128), BF16),
            pltpu.VMEM((2, 3 * half, lines, 128), BF16),
            pltpu.VMEM((2, 3 * half, lines, 128), BF16),
            pltpu.VMEM((2, 4, half, 32, 128), BF16),
            pltpu.VMEM((2, half, pitch, 128), F32),
            pltpu.VMEM((2, half, pitch, 128), F32),
            pltpu.VMEM((2, half, low_lines, 128), F32),
            pltpu.VMEM((2, half, low_lines, 128), F32),
            pltpu.VMEM((2, 4, half, 8, 128), F32),
            total_scratch(16),
            total_scratch(8),
            scatter_scratch(tiles),
            plane_scratch(parts_x),
            plane_scratch(parts),
            level_sems(),
            pltpu.SemaphoreType.DMA((7,)),
            pltpu.SemaphoreType.DMA((2, images)),
            pltpu.SemaphoreType.DMA((2, images)),
            pltpu.SemaphoreType.DMA((2, 8)),
            pltpu.SemaphoreType.DMA((2, 8)),
        ],
        compiler_params=pltpu.CompilerParams(
            collective_id=2, has_side_effects=True, vmem_limit_bytes=60 * MIB
        ),
        name="fall",
    )(spread, y_two, stats, load, small, tiles_x, y_one, merged, low, conv_two, conv_one)


def finish_body(
    cells_low,
    load_ref,
    rest_ref,
    conv_ref,
    conv_x_ref,
    sums_ref,
    last_ref,
    stat_ref,
    zed_ref,
    y_one_ref,
    weight_ref,
    skip_ref,
    conv_one_out,
    gain_one_out,
    shift_one_out,
    conv_two_out,
    gain_two_out,
    shift_two_out,
    head_out,
    head_b_out,
    heat_w_out,
    heat_b_out,
    box_w_out,
    box_b_out,
    low_out,
    skip_out,
    zed_x,
):
    step = pl.program_id(0)
    each, h, w, _ = low_out.shape
    pitch = w + 16
    rows = h + 2
    factor = stat_ref[6:7, :] * stat_ref[1:2, :]
    shift_low, gain_low = last_ref[0:1, :] / cells_low, last_ref[1:2, :] / cells_low
    skip_out[...] = skip_ref[...]
    for column in range(head_out.shape[3] // 128):
        block = load_ref[36 * column : 36 * column + 36].astype(F32)
        head_out[:, :, :, 128 * column : 128 * column + 128] = block.reshape(3, 3, 64, 128)

    @pl.when(step == 0)
    def _():
        zed_x[0:PAD, :] = jnp.zeros((PAD, 128), F32)
        zed_x[PAD + rows * pitch :, :] = jnp.zeros((PAD, 128), F32)
        spread = stat_ref[16:24, :].T
        ones = unfold(conv_ref, 36)
        normed = unfold(conv_x_ref, 0)
        for tap, part in enumerate(unfold(conv_ref, 0)):
            conv_two_out[tap] = part.reshape(3, 64, 64)
            count = jnp.concatenate(
                [spread[:, 2 * tap : 2 * tap + 1], spread[0:64, 2 * tap + 1 : 2 * tap + 2]], axis=0
            )
            value = ones[tap] - count * shift_low[:, 0:64] - normed[tap] * gain_low[:, 0:64]
            conv_one_out[tap] = (value * factor[:, 0:64]).reshape(3, 64, 64)
        for column in range(6):
            span = slice(128 * column, 128 * column + 128)
            head_b_out[span] = sums_ref[column : column + 1, :].reshape(128)
        for part in range(2):
            span = slice(128 * part, 128 * part + 128)
            heat_w_out[:, span] = rest_ref[5 * part : 5 * part + 5].astype(F32).reshape(80, 128)
            for box in range(2):
                block = rest_ref[10 + 2 * box + part].astype(F32)
                box_w_out[box, :, span] = block[2 * box : 2 * box + 2, :]
            box_b_out[part : part + 1, :] = sums_ref[7:8, 2 * part : 2 * part + 2]
        heat_b_out[...] = sums_ref[6:7, 0:80]
        shift_two_out[...] = sums_ref[8:9, 0:64]
        gain_two_out[...] = sums_ref[9:10, 0:64]
        shift_one_out[...] = last_ref[0:1, 0:64]
        gain_one_out[...] = last_ref[1:2, 0:64]

    for b in range(each):
        normed = (y_one_ref[b, 1 : h + 3] - stat_ref[0:1, :]) * stat_ref[1:2, :]
        grad_z = zed_ref[b].reshape(rows, pitch, 128)
        grad_y = factor * (grad_z - shift_low - normed * gain_low)
        column = lax.broadcasted_iota(jnp.int32, (pitch, 128), 0)
        keep = jnp.where(column < 8, stat_ref[12:13, :], 1.0)
        keep = jnp.where(column >= 8 + w, stat_ref[13:14, :], keep)
        grad_y = (grad_y * keep).astype(BF16).astype(F32)
        zed_x[PAD : PAD + rows * pitch, :] = grad_y.reshape(rows * pitch, 128)
        for line, row in ((0, 10), (rows - 1, 11)):
            span = slice(PAD + line * pitch, PAD + (line + 1) * pitch)
            zed_x[span, :] = zed_x[span, :] * stat_ref[row : row + 1, :]
        pairs = back_pairs(zed_x, PAD, rows * pitch)
        count = h * pitch
        taps = jnp.concatenate(
            [pairs[pitch * (2 - a) : pitch * (2 - a) + count] for a in range(3)], axis=1
        )
        grad = dot(taps, weight_ref[...]).reshape(h, pitch, 128)
        low_out[b] = grad[:, 8 : 8 + w, 0:64]


def finish(load, conv, conv_x, sums, last, stats, zed, y_one, weight, skip):
    images, y_rows, pitch, _ = y_one.shape
    h, w = y_rows - 4, pitch - 16
    batches, row_count, col_count = extents()
    cells = float(images * batches * h * row_count * w * col_count)
    span = zed.shape[1]
    steps = 2
    each = images // steps
    shapes = [
        (3, 3, 64, 64),
        (1, 64),
        (1, 64),
        (3, 3, 64, 64),
        (1, 64),
        (1, 64),
        (3, 3, 64, 768),
        (768,),
        (80, 256),
        (1, 80),
        (2, 2, 256),
        (2, 2),
        (images, h, w, 64),
        skip.shape,
    ]
    whole = lambda shape: pl.BlockSpec(shape, lambda c: (0,) * len(shape))
    part = lambda shape: pl.BlockSpec(shape, lambda c: (c,) + (0,) * (len(shape) - 1))
    out_specs = [whole(shape) for shape in shapes]
    out_specs[6] = pl.BlockSpec((3, 3, 64, 768 // steps), lambda c: (0, 0, 0, c))
    out_specs[12] = part((each, h, w, 64))
    out_specs[13] = part((each,) + skip.shape[1:])
    return pl.pallas_call(
        functools.partial(finish_body, cells),
        grid=(steps,),
        in_specs=[
            part((216 // steps, 16, 128)),
            pl.BlockSpec((36, 16, 128), lambda c: (6, 0, 0)),
        ]
        + [whole(array.shape) for array in (conv, conv_x, sums, last, stats)]
        + [
            part((each, span, 128)),
            part((each, y_rows, pitch, 128)),
            whole(weight.shape),
            part((each,) + skip.shape[1:]),
        ],
        out_specs=out_specs,
        out_shape=[jax.ShapeDtypeStruct(shape, F32) for shape in shapes],
        scratch_shapes=[
            pltpu.VMEM((2 * PAD + span, 128), F32),
        ],
        compiler_params=pltpu.CompilerParams(vmem_limit_bytes=60 * MIB),
        name="finish",
    )(load, load, conv, conv_x, sums, last, stats, zed, y_one, weight, skip)


def local(
    low_map,
    skip_map,
    conv_first,
    gain_first,
    shift_first,
    conv_second,
    gain_second,
    shift_second,
    head_conv,
    head_bias,
    heat_weight,
    heat_bias,
    box_weight,
    box_bias,
    heat_target,
    box_target,
    obj_index,
    obj_count,
):
    batches, rows, cols = extents()
    devices = batches * rows * cols
    conv_one = conv_first.reshape(3, 192, 64)
    conv_two = conv_second.reshape(3, 192, 64)
    y_two, y_one, merged, low, kernel, back, stats, spot, tiles_x = rise(
        low_map,
        skip_map,
        heat_target,
        conv_one,
        conv_two,
        gain_first.reshape(1, 64),
        shift_first.reshape(1, 64),
        gain_second.reshape(1, 64),
        shift_second.reshape(1, 64),
        obj_index,
        head_conv.reshape(3, 192, 768),
        head_bias,
        obj_count,
    )
    heat_map, box_map, spread, load, small = heads(
        y_two,
        heat_target,
        spot,
        box_target.transpose(0, 2, 1),
        stats,
        kernel,
        back,
        heat_weight.T,
        heat_bias.reshape(1, 80),
        box_weight.transpose(0, 2, 1),
        box_bias,
        devices,
    )
    images, ext, wide, _ = spread.shape
    grad_skip, zed, load, conv, conv_x, sums, last, weight = fall(
        spread.reshape(images, ext * wide, 128),
        y_two,
        stats,
        load,
        small,
        tiles_x,
        y_one,
        merged,
        low,
        conv_two,
        conv_one,
    )
    grads = finish(load, conv, conv_x, sums, last, stats, zed, y_one, weight, grad_skip)
    return (
        heat_map,
        box_map.transpose(0, 1, 3, 2),
        grads[12],
        grads[13],
        grads[0],
        grads[1].reshape(64),
        grads[2].reshape(64),
        grads[3],
        grads[4].reshape(64),
        grads[5].reshape(64),
        grads[6],
        grads[7],
        grads[8].T,
        grads[9].reshape(80),
        grads[10].transpose(0, 2, 1),
        grads[11],
    )


def solution(mesh):
    tile = P("batch", "row", "col", None)
    return jax.shard_map(
        local,
        mesh=mesh,
        in_specs=(tile, tile)
        + (P(),) * 12
        + (tile, P("batch", None, None), P("batch", None), P("batch")),
        out_specs=(tile,) * 4 + (P(),) * 12,
        check_vma=False,
    )
```

```python
import functools

import jax
import jax.numpy as jnp
from jax import lax
from jax.experimental import pallas as pl
from jax.experimental.pallas import tpu as pltpu
from jax.sharding import PartitionSpec as P

EPSILON = 1e-05
F32 = jnp.float32
BF16 = jnp.bfloat16
KEEP = (((1,), (1,)), ((), ()))
LEFT = (((0,), (0,)), ((), ()))
MIB = 1024 * 1024


def dot(left, right):
    return jnp.dot(left, right, preferred_element_type=F32)


def dot_keep(left, right):
    return lax.dot_general(left, right, KEEP, preferred_element_type=F32)


def dot_left(left, right):
    return lax.dot_general(left, right, LEFT, preferred_element_type=F32)


def three_parts(values):
    high = values.astype(BF16)
    rest = values - high.astype(F32)
    mid = rest.astype(BF16)
    return high, mid, (rest - mid.astype(F32)).astype(BF16)


def tile_count(devices):
    return -(-230 // (2 * devices)) * 2 * devices


def heads_body(
    chunks,
    map_side,
    y_two_ref,
    target_ref,
    spot_ref,
    goal_ref,
    stat_ref,
    kernel_s,
    back_s,
    heat_w_ref,
    heat_b_ref,
    box_w_ref,
    box_b_ref,
    heat_out,
    box_out,
    spread_out,
    load_out,
    small_out,
    feat_s,
    taps_ref,
    box_s,
    goal_s,
    wide_s,
    grad_s,
    heat_grad_s,
    box_grad_s,
    heat_sum_s,
    box_sum_s,
):
    image = pl.program_id(0)
    chunk = pl.program_id(1)
    rows, breadth = target_ref.shape[1], target_ref.shape[2]
    cells = rows * breadth
    units = 256

    @pl.when(jnp.logical_and(image == 0, chunk == 0))
    def _():
        empty = jnp.zeros((2, 256), F32)
        for part in range(2):
            pieces = [empty, empty]
            pieces[part] = box_w_ref[part].astype(F32)
            box_s[part] = jnp.concatenate(pieces, axis=0).astype(BF16)
        grad_s[...] = jnp.zeros_like(grad_s)
        heat_grad_s[...] = jnp.zeros_like(heat_grad_s)
        box_grad_s[...] = jnp.zeros_like(box_grad_s)
        heat_sum_s[...] = jnp.zeros_like(heat_sum_s)
        box_sum_s[...] = jnp.zeros_like(box_sum_s)

    @pl.when(chunk == 0)
    def _():
        wide_s[...] = jnp.zeros_like(wide_s)
        ext, wide = taps_ref.shape[0], breadth + 16
        normed = (y_two_ref[0, 1 : ext + 1] - stat_ref[2:3, :]) * stat_ref[3:4, :]
        feature, _ = silu_parts(normed * stat_ref[8:9, :] + stat_ref[9:10, :])
        column = lax.broadcasted_iota(jnp.int32, (wide, 128), 0)
        keep = jnp.where(column < 8, stat_ref[12:13, :], 1.0)
        keep = jnp.where(column >= 8 + breadth, stat_ref[13:14, :], keep)
        feat_s[0:PAD, :] = jnp.zeros((PAD, 128), F32)
        feat_s[PAD : PAD + ext * wide, :] = (feature * keep).reshape(ext * wide, 128)
        feat_s[PAD + ext * wide :, :] = jnp.zeros((PAD, 128), F32)
        for line, row in ((PAD, 10), (PAD + (ext - 1) * wide, 11)):
            feat_s[line : line + wide, :] = feat_s[line : line + wide, :] * stat_ref[row : row + 1]
        pairs = tap_pairs(feat_s, PAD, ext * wide, 1.0)
        taps_ref[...] = pairs.reshape(ext, wide, 256)[:, 8 : 8 + breadth].astype(BF16)
        for place, part in enumerate(three_parts(goal_ref[0])):
            goal_s[place] = part

    taps = jnp.concatenate(
        [taps_ref[tap : tap + rows].reshape(cells, 256) for tap in range(3)], axis=1
    )
    active, slope = {}, {}

    def forward(block):
        weight = kernel_s[:, :, block * units : (block + 1) * units].reshape(768, units)
        hidden = dot(taps, weight)
        turn = jnp.tanh(hidden)
        above = 1.0 + turn
        product = hidden * above
        active[block] = product.astype(BF16)
        slope[block] = above + product * (1.0 - turn)

    forward(1)
    forward(2)
    box_bias = jnp.concatenate([box_b_ref[0:1, :], box_b_ref[1:2, :]], axis=1)
    boxes = dot_keep(active[1], box_s[0]) + dot_keep(active[2], box_s[1]) + box_bias
    forward(0)
    box_out[0] = jnp.swapaxes(boxes.reshape(rows, breadth, 4), 1, 2)
    shape = (rows, breadth, 128)
    cell = lax.broadcasted_iota(jnp.int32, shape, 0) * map_side
    cell = (cell + lax.broadcasted_iota(jnp.int32, shape, 1)).reshape(cells, 128)
    chosen = (cell == spot_ref[pl.ds(image, 1), :]).astype(F32).astype(BF16)
    goals = dot_keep(chosen, goal_s[0]) + dot_keep(chosen, goal_s[1])
    goals = goals + dot_keep(chosen, goal_s[2])
    hit = dot(chosen, jnp.ones((128, 4), BF16))
    miss = boxes - goals
    lane = lax.broadcasted_iota(jnp.int32, (1, 4), 1)
    factor = jnp.where(lane < 2, 0.1, 1.0) * stat_ref[5:6, 0:4]
    box_low = (hit * factor * miss * lax.rsqrt(miss * miss + 1.0)).astype(BF16)
    box_sum_s[...] += jnp.sum(box_low.astype(F32).reshape(cells // 8, 8, 4), axis=0)
    hidden_low = {}
    for part in range(2):
        box_grad_s[part] += dot_left(box_low, active[1 + part])
        back = dot(box_low, box_s[part])
        hidden_low[1 + part] = (back * slope[1 + part]).astype(BF16)
    boxes_low = jnp.concatenate([hidden_low[1], hidden_low[2]], axis=1)
    logits = dot_keep(active[0], heat_w_ref[...]) + heat_b_ref[...]
    piece_rows = rows // 4
    piece_cells = piece_rows * breadth

    def focal(piece):
        lines = slice(piece_rows * piece, piece_rows * piece + piece_rows)
        logit = logits[piece_cells * piece : piece_cells * piece + piece_cells]
        decay = jnp.exp(-jnp.abs(logit))
        large = 1.0 / (1.0 + decay)
        small = decay * large
        above = logit >= 0.0
        chance = jnp.where(above, large, small)
        heat_out[0, lines] = chance.reshape(piece_rows, breadth, 80)
        target = target_ref[0, lines].reshape(piece_cells, 80).astype(F32)
        positive = target == 1.0
        side = jnp.where(positive, jnp.where(above, small, large), chance)
        value = jnp.where(positive, -logit, logit)
        soft = jnp.maximum(value, 0.0) + jnp.log(1.0 + decay)
        slant = side * side * (2.0 * (1.0 - side) * soft + side)
        gap = 1.0 - target
        gap = gap * gap
        weighting = jnp.where(positive, -1.0, gap * gap) * stat_ref[4:5, 0:80]
        return (weighting * slant).astype(BF16)

    turned = [taps[:, 256 * tap : 256 * tap + 256].T for tap in range(3)]
    pieces = []
    for tap in range(3):
        grad_s[tap, :, 256:768] += dot(turned[tap], boxes_low)
        if tap < 2:
            pieces += [focal(2 * tap), focal(2 * tap + 1)]
    logit_low = jnp.concatenate(pieces, axis=0)
    heat_sum_s[...] += jnp.sum(logit_low.astype(F32).reshape(cells // 8, 8, 80), axis=0)
    heat_grad_s[...] += dot_left(logit_low, active[0])
    hidden_low[0] = (dot(logit_low, heat_w_ref[...]) * slope[0]).astype(BF16)
    grad_hidden = jnp.concatenate([hidden_low[0], boxes_low], axis=1)
    spread = []
    for tap in range(3):
        part = dot(grad_hidden, back_s[:, 256 * tap : 256 * tap + 256])
        spread.append(part.reshape(rows, breadth, 256))
    inner = slice(16, 16 + breadth)
    wide_s[0:1, inner, :] = spread[0][0:1]
    wide_s[1:2, inner, :] = spread[0][1:2] + spread[1][0:1]
    wide_s[2:rows, inner, :] = spread[0][2:] + spread[1][1:-1] + spread[2][:-2]
    wide_s[rows : rows + 1, inner, :] = spread[1][-1:] + spread[2][-2:-1]
    wide_s[rows + 1 : rows + 2, inner, :] = spread[2][-1:]
    reach, ends = breadth + 16, [(rows + 2) * k // 3 for k in range(4)]
    for tap in range(3):
        grad_s[tap, :, 0:256] += dot(turned[tap], hidden_low[0])
        lines = slice(ends[tap], ends[tap + 1])
        centre = pltpu.roll(wide_s[lines, 8 : 8 + reach, 0:128], 64, 2)
        total = wide_s[lines, 9 : 9 + reach, 0:128] + centre
        total = total + wide_s[lines, 7 : 7 + reach, 128:256]
        lanes = lax.broadcasted_iota(jnp.int32, total.shape, 2)
        spread_out[0, lines] = jnp.where(lanes < 64, total, pltpu.roll(total, 64, 2))

    @pl.when(jnp.logical_and(image == pl.num_programs(0) - 1, chunk == chunks - 1))
    def _():
        for column in range(6):
            span = slice(128 * column, 128 * column + 128)
            for tap in range(3):
                start = 36 * column + 12 * tap
                load_out[start : start + 12] = (
                    (0.5 * grad_s[tap, 0:192, span]).reshape(12, 16, 128).astype(BF16)
                )
            small_out[column : column + 1, :] = 0.5 * grad_s[1, 192:193, span]
        for half in range(2):
            span = slice(128 * half, 128 * half + 128)
            start = 216 + 5 * half
            load_out[start : start + 5] = heat_grad_s[:, span].reshape(5, 16, 128).astype(BF16)
            for part in range(2):
                padded = jnp.concatenate(
                    [box_grad_s[part, :, span], jnp.zeros((12, 128), F32)], axis=0
                )
                load_out[226 + 2 * part + half] = padded.astype(BF16)
        load_out[230:] = jnp.zeros((load_out.shape[0] - 230, 16, 128), BF16)
        small_out[6:8, :] = jnp.zeros((2, 128), F32)
        small_out[6:7, 0:80] = jnp.sum(heat_sum_s[...], axis=0, keepdims=True)
        small_out[7:8, 0:4] = jnp.sum(box_sum_s[...], axis=0, keepdims=True)


def heads(
    taps, target, spot, goal, stats, kernel, back, heat_w, heat_b, box_w, box_b, devices
):
    images, height, breadth, classes = target.shape
    rows = height
    chunks = height // rows
    tiles = tile_count(devices)
    whole = lambda *shape: pl.BlockSpec(shape, lambda b, c: (0,) * len(shape))
    cells = images * height * breadth
    return pl.pallas_call(
        functools.partial(heads_body, chunks, breadth * lax.axis_size("col")),
        grid=(images, chunks),
        in_specs=[
            pl.BlockSpec((1, height + 4, breadth + 16, 128), lambda b, c: (b, 0, 0, 0)),
            pl.BlockSpec((1, rows, breadth, classes), lambda b, c: (b, c, 0, 0)),
            whole(8, 128),
            pl.BlockSpec((1, 4, 128), lambda b, c: (b, 0, 0)),
            whole(24, 128),
            whole(3, 256, 768),
            whole(768, 768),
            whole(80, 256),
            whole(1, 80),
            whole(2, 2, 256),
            whole(2, 2),
        ],
        out_specs=[
            pl.BlockSpec((1, rows, breadth, classes), lambda b, c: (b, c, 0, 0)),
            pl.BlockSpec((1, rows, 4, breadth), lambda b, c: (b, c, 0, 0)),
            pl.BlockSpec((1, height + 2, breadth + 16, 128), lambda b, c: (b, 0, 0, 0)),
            whole(tiles, 16, 128),
            whole(8, 128),
        ],
        out_shape=[
            jax.ShapeDtypeStruct((images, height, breadth, classes), F32),
            jax.ShapeDtypeStruct((images, height, 4, breadth), F32),
            jax.ShapeDtypeStruct((images, height + 2, breadth + 16, 128), F32),
            jax.ShapeDtypeStruct((tiles, 16, 128), BF16),
            jax.ShapeDtypeStruct((8, 128), F32),
        ],
        scratch_shapes=[
            pltpu.VMEM((2 * PAD + (height + 2) * (breadth + 16), 128), F32),
            pltpu.VMEM((height + 2, breadth, 256), BF16),
            pltpu.VMEM((2, 4, 256), BF16),
            pltpu.VMEM((3, 4, 128), BF16),
            pltpu.VMEM((height + 2, breadth + 32, 256), F32),
            pltpu.VMEM((3, 256, 768), F32),
            pltpu.VMEM((80, 256), F32),
            pltpu.VMEM((2, 4, 256), F32),
            pltpu.VMEM((8, 80), F32),
            pltpu.VMEM((8, 4), F32),
        ],
        compiler_params=pltpu.CompilerParams(vmem_limit_bytes=60 * MIB),
        cost_estimate=pl.CostEstimate(
            flops=cells * 576 * 768 * 6, bytes_accessed=12 * MIB, transcendentals=cells * 768
        ),
        name="heads",
    )(taps, target, spot, goal, stats, kernel, back, heat_w, heat_b, box_w, box_b)


MESH = pl.DeviceIdType.MESH


def rounded_up(value, step):
    return -(-value // step) * step


def place():
    return lax.axis_index("batch"), lax.axis_index("row"), lax.axis_index("col")


def extents():
    return lax.axis_size("batch"), lax.axis_size("row"), lax.axis_size("col")


def plane_partners():
    batch, row, col = place()
    batches, _, cols = extents()
    partners = []
    for over in range(batches):
        for along in range(cols):
            if over or along:
                partners.append(
                    (lax.rem(batch + over, batches), row, lax.rem(col + along, cols))
                )
    return partners


def row_partners():
    batch, row, col = place()
    rows = lax.axis_size("row")
    return [(batch, lax.rem(row + over, rows), col) for over in range(1, rows)]


def flat():
    batches, rows, cols = extents()
    return batches * rows * cols <= 8


def all_partners():
    batch, row, col = place()
    batches, rows, cols = extents()
    partners = []
    for over in range(batches):
        for up in range(rows):
            for along in range(cols):
                if over or up or along:
                    partners.append(
                        (
                            lax.rem(batch + over, batches),
                            lax.rem(row + up, rows),
                            lax.rem(col + along, cols),
                        )
                    )
    return partners


def greet():
    barrier = pltpu.get_barrier_semaphore()
    partners = all_partners() if flat() else plane_partners() + row_partners()
    for partner in partners:
        pl.semaphore_signal(barrier, inc=1, device_id=partner, device_id_type=MESH)
    batch, row, col = place()
    _, rows, cols = extents()
    expected = len(partners)
    for up in (-1, 1):
        for along in (-1, 1):
            fits = jnp.logical_and(row + up >= 0, row + up < rows)
            fits = jnp.logical_and(fits, jnp.logical_and(col + along >= 0, col + along < cols))
            expected = expected + fits.astype(jnp.int32)

            @pl.when(fits)
            def _(up=up, along=along):
                pl.semaphore_signal(
                    barrier,
                    inc=1,
                    device_id=(batch, row + up, col + along),
                    device_id_type=MESH,
                )

    return expected


def greeted(expected):
    pl.semaphore_wait(pltpu.get_barrier_semaphore(), expected)


def remote(source, target, send, recv, device):
    return pltpu.make_async_remote_copy(
        src_ref=source,
        dst_ref=target,
        send_sem=send,
        recv_sem=recv,
        device_id=device,
        device_id_type=MESH,
    )


def start_all(copies):
    for copy in copies:
        copy.start()


def wait_all(copies):
    for copy in copies:
        copy.wait()


def slot_sum(slots):
    total = slots[0]
    for k in range(1, slots.shape[0]):
        total = total + slots[k]
    return total


class Total:
    def __init__(self, source, slots, mid, row_slots, sems):
        self.source, self.slots, self.mid = source, slots, mid
        self.row_slots, self.sems = row_slots, sems

    def send(self, source, slots, mine, partners, step):
        self.copies = [
            remote(
                source,
                slots.at[mine],
                self.sems.at[step, 0, k],
                self.sems.at[step, 1, k],
                partner,
            )
            for k, partner in enumerate(partners)
        ]
        start_all(self.copies)
        slots[mine] = source[...]

    def begin(self):
        batch, row, col = place()
        _, rows, cols = extents()
        if flat():
            mine, partners = (batch * rows + row) * cols + col, all_partners()
        else:
            mine, partners = batch * cols + col, plane_partners()
        self.send(self.source, self.slots, mine, partners, 0)

    def middle(self):
        if not flat():
            wait_all(self.copies)
            self.mid[...] = slot_sum(self.slots)
            self.send(self.mid, self.row_slots, place()[1], row_partners(), 1)

    def end(self):
        wait_all(self.copies)
        return slot_sum(self.slots if flat() else self.row_slots)


def total_scratch(lines):
    batches, rows, cols = extents()
    slots = batches * cols * (rows if flat() else 1)
    return [
        pltpu.VMEM((lines, 128), F32),
        pltpu.VMEM((slots, lines, 128), F32),
        pltpu.VMEM((lines, 128), F32),
        pltpu.VMEM((rows, lines, 128), F32),
        pltpu.SemaphoreType.DMA((2, 2, max(slots, rows) - 1)),
    ]


AROUND = ((-1, 0), (1, 0), (0, -1), (0, 1), (-1, -1), (-1, 1), (1, -1), (1, 1))


class Around:
    def __init__(self, pieces, slots, sems):
        batch, row, col = place()
        _, rows, cols = extents()

        def exists(up, along):
            fits = jnp.logical_and(row + up >= 0, row + up < rows)
            return jnp.logical_and(fits, jnp.logical_and(col + along >= 0, col + along < cols))

        self.sends = [exists(up, along) for up, along in AROUND]
        self.comes = [exists(-up, -along) for up, along in AROUND]
        self.copies = [
            remote(pieces[k], slots[k], sems.at[0, k], sems.at[1, k], (batch, row + up, col + along))
            for k, (up, along) in enumerate(AROUND)
        ]

    def start(self, which=range(8)):
        for k in which:
            pl.when(self.sends[k])(self.copies[k].start)

    def wait(self, which=range(8)):
        for k in which:
            pl.when(self.comes[k])(self.copies[k].wait_recv)
            pl.when(self.sends[k])(self.copies[k].wait_send)

    def each(self, use, which=range(8)):
        for k in which:
            pl.when(self.comes[k])(functools.partial(use, k))


def twice(values):
    return jnp.concatenate([values, values], axis=-1)


def lower_half(shape):
    return lax.broadcasted_iota(jnp.int32, shape, len(shape) - 1) < 64


def swapped(values):
    return pltpu.roll(values, 64, len(values.shape) - 1)


def widened(values):
    rows, cols = values.shape[0], values.shape[1]
    side = jnp.zeros((rows, 8, 128), F32)
    return jnp.concatenate([side, twice(values.astype(F32)), side], axis=1)


def tap_pairs(buffer, start, count, fill):
    low = lower_half((1, 128))
    first = jnp.where(low, buffer[pl.ds(start - 1, count), :], buffer[pl.ds(start, count), :])
    second = jnp.where(low, buffer[pl.ds(start + 1, count), :], fill)
    return jnp.concatenate([first, second], axis=1)


def silu_parts(values):
    logistic = 0.5 * jnp.tanh(0.5 * values) + 0.5
    return values * logistic, logistic


PAD = 16


def row_loop(total, step, body, init):
    return lax.fori_loop(0, total // step, lambda k, carry: body(k * step, carry), init)


def fold_sum(values):
    return jnp.sum(values.reshape(-1, 8, 128), axis=0)


def clear(buffer, start, rows, pitch, tops, bottoms, lefts, rights):
    _, row_at, col_at = place()
    count = rounded_up(rows, 8)

    def clear_rows(span):
        first, last = span
        size = (last - first) * pitch
        buffer[pl.ds(start + first * pitch, size), :] = jnp.zeros((size, 128), F32)

    def clear_columns(span):
        for column in range(*span):
            buffer[pl.ds(start + column, count, stride=pitch), :] = jnp.zeros((count, 128), F32)

    pl.when(row_at == 0)(lambda: clear_rows(tops))
    pl.when(row_at == lax.axis_size("row") - 1)(lambda: clear_rows(bottoms))
    pl.when(col_at == 0)(lambda: clear_columns(lefts))
    pl.when(col_at == lax.axis_size("col") - 1)(lambda: clear_columns(rights))


def stack_weight(target, source):
    for tap in range(3):
        target[256 * tap : 256 * tap + 192, :] = twice(source[tap].astype(F32)).astype(BF16)
        target[256 * tap + 192 : 256 * tap + 256, :] = jnp.zeros((64, 128), BF16)


def unpacked(packed, image, images):
    low = lower_half((1, 128))
    keep = low if image < images // 2 else jnp.logical_not(low)
    return jnp.where(keep, packed, swapped(packed))


def pack_columns(buffer, target, images, rows, pitch, first_row, first, depth):
    low = lower_half((1, 128))
    half = images // 2
    count = target.shape[1]
    for pair in range(half):
        for j in range(depth):
            parts = [
                buffer[
                    pl.ds(
                        PAD + (image * rows + first_row) * pitch + first + j, count, stride=pitch
                    ),
                    :,
                ]
                for image in (pair, pair + half)
            ]
            target[depth * pair + j] = jnp.where(low, parts[0], parts[1]).astype(target.dtype)


def pack_corner(buffer, target, images, rows, pitch, first_row, first, depth):
    low = lower_half((1, 128))
    half = images // 2
    count = target.shape[1] // 8
    for pair in range(half):
        pieces = []
        for row in range(count):
            if row < depth:
                starts = [
                    PAD + (image * rows + first_row + row) * pitch + first
                    for image in (pair, pair + half)
                ]
                pieces.append(
                    jnp.where(
                        low,
                        buffer[starts[0] : starts[0] + 8, :],
                        buffer[starts[1] : starts[1] + 8, :],
                    )
                )
            else:
                pieces.append(jnp.zeros((8, 128), F32))
        target[pair] = jnp.concatenate(pieces, axis=0).astype(target.dtype)


def unpack_columns(buffer, source, images, rows, pitch, first_row, first, depth, lines, add):
    half = images // 2
    count = rounded_up(lines, 8)
    valid = lax.broadcasted_iota(jnp.int32, (count, 128), 0) < lines
    for image in range(images):
        for j in range(depth):
            packed = source[depth * (image % half) + j].astype(F32)
            values = unpacked(packed, image, images)[:count]
            spots = pl.ds(
                PAD + (image * rows + first_row) * pitch + first + j, count, stride=pitch
            )
            if add:
                values = buffer[spots, :] + jnp.where(valid, values, 0.0)
            elif count > lines:
                values = jnp.where(valid, values, buffer[spots, :])
            buffer[spots, :] = values


def unpack_corner(buffer, source, images, rows, pitch, first_row, first, depth, add):
    half = images // 2
    valid = lax.broadcasted_iota(jnp.int32, (8, 128), 0) < depth
    for image in range(images):
        packed = unpacked(source[image % half].astype(F32), image, images)
        for row in range(depth):
            start = PAD + (image * rows + first_row + row) * pitch + first
            old = buffer[start : start + 8, :]
            values = packed[8 * row : 8 * row + 8]
            if add:
                values = old + jnp.where(valid, values, 0.0)
            else:
                values = jnp.where(valid, values, old)
            buffer[start : start + 8, :] = values


def rise_body(
    low_ref,
    skip_ref,
    target_ref,
    conv_one_ref,
    conv_two_ref,
    gain_one_ref,
    shift_one_ref,
    gain_two_ref,
    shift_two_ref,
    index_ref,
    head_ref,
    bias_ref,
    count_ref,
    y_two_out,
    y_one_out,
    merged_out,
    low_out,
    kernel_out,
    back_out,
    stat_out,
    spot_out,
    tiles_out,
    low_in,
    skip_in,
    target_in,
    conv_one_in,
    conv_two_in,
    param_in,
    index_in,
    head_in,
    bias_in,
    y_two_s,
    y_one_s,
    merged_s,
    low_s,
    kernel_s,
    back_s,
    low_x,
    skip_x,
    act_s,
    row_s,
    up_s,
    w_one,
    w_two,
    g_low,
    own_low,
    low_rows,
    skip_rows,
    low_send,
    low_recv,
    low_corner,
    skip_send,
    skip_recv,
    skip_corner,
    first_scratch,
    second_scratch,
    in_sems,
    out_sems,
    strip_sems,
):
    images, h, w, _ = low_ref.shape
    height, breadth = skip_ref.shape[1], skip_ref.shape[2]
    batch_at, row_at, col_at = place()
    batches, row_count, col_count = extents()
    pitch, wide = w + 16, breadth + 16
    low_r, y_one_r = h + 6, h + 4
    skip_r, y_two_r = height + 6, height + 4
    cells_low = float(images * batches * h * row_count * w * col_count)
    cells_high = 4.0 * cells_low

    loads = [
        pltpu.make_async_copy(source, target, in_sems.at[k])
        for k, (source, target) in enumerate(
            (
                (low_ref, low_in),
                (conv_one_ref, conv_one_in),
                (skip_ref, skip_in),
                (index_ref, index_in),
                (target_ref, target_in),
                (gain_one_ref, param_in.at[0]),
                (shift_one_ref, param_in.at[1]),
                (gain_two_ref, param_in.at[2]),
                (shift_two_ref, param_in.at[3]),
                (conv_two_ref, conv_two_in),
                (head_ref, head_in),
                (bias_ref, bias_in),
            )
        )
    ]
    expected = greet()
    for load in loads:
        load.start()
    low_around = Around(
        [low_ref.at[:, 0:3], low_ref.at[:, h - 3 : h]]
        + [low_send.at[k] for k in range(2)]
        + [low_corner.at[0, k] for k in range(4)],
        [low_rows.at[0], low_rows.at[1]]
        + [low_recv.at[k] for k in range(2)]
        + [low_corner.at[1, k] for k in range(4)],
        strip_sems.at[0],
    )
    skip_around = Around(
        [skip_ref.at[:, 0:3], skip_ref.at[:, height - 3 : height]]
        + [skip_send.at[k] for k in range(2)]
        + [skip_corner.at[0, k] for k in range(4)],
        [skip_rows.at[0], skip_rows.at[1]]
        + [skip_recv.at[k] for k in range(2)]
        + [skip_corner.at[1, k] for k in range(4)],
        strip_sems.at[1],
    )

    def place_low(b, carry):
        start = PAD + b * low_r * pitch
        low_x[pl.ds(start, 3 * pitch), :] = jnp.zeros((3 * pitch, 128), F32)
        low_x[pl.ds(start + 3 * pitch, h * pitch), :] = widened(low_in[b]).reshape(h * pitch, 128)
        low_x[pl.ds(start + (h + 3) * pitch, 3 * pitch), :] = jnp.zeros((3 * pitch, 128), F32)
        return carry

    low_x[0:PAD, :] = jnp.zeros((PAD, 128), F32)
    tail = low_x.shape[0] - PAD - images * low_r * pitch
    low_x[PAD + images * low_r * pitch :, :] = jnp.zeros((tail, 128), F32)
    loads[0].wait()
    lax.fori_loop(0, images, place_low, 0)

    def pack(buffer, sends, corners, rows, step, line, across):
        for side, first in enumerate((8, 5 + across)):
            pack_columns(buffer, sends.at[side], images, rows, line, 3, first, 3)
        for k, (up, along) in enumerate(AROUND[4:]):
            pack_corner(
                buffer,
                corners.at[0, k],
                images,
                rows,
                line,
                3 if up < 0 else step,
                8 if along < 0 else 5 + across,
                3,
            )

    def unpack(around, buffer, strips, columns, corners, rows, step, line, across):
        def use(k):
            up, along = AROUND[k]
            row = step + 3 if up < 0 else 0
            column = 8 + across if along < 0 else 5
            if k < 2:

                def body(b, carry):
                    start = PAD + (b * rows + row) * line
                    buffer[pl.ds(start, 3 * line), :] = widened(strips[k, b]).reshape(
                        3 * line, 128
                    )
                    return carry

                lax.fori_loop(0, images, body, 0)
            elif k < 4:
                unpack_columns(
                    buffer, columns.at[k - 2], images, rows, line, 3, column, 3, step, False
                )
            else:
                unpack_corner(
                    buffer, corners.at[1, k - 4], images, rows, line, row, column, 3, False
                )

        around.each(use)

    pack(low_x, low_send, low_corner, low_r, h, pitch, w)
    greeted(expected)
    low_around.start()
    skip_around.start(range(2))

    def place_skip(b, carry):
        start = PAD + b * skip_r * wide
        edge = jnp.zeros((3 * wide, 128), F32)
        skip_x[pl.ds(start, 3 * wide), :] = edge
        skip_x[pl.ds(start + 3 * wide, height * wide), :] = widened(skip_in[b]).reshape(
            height * wide, 128
        )
        skip_x[pl.ds(start + (height + 3) * wide, 3 * wide), :] = edge
        return carry

    skip_x[0:PAD, :] = jnp.zeros((PAD, 128), F32)
    skip_tail = skip_x.shape[0] - PAD - images * skip_r * wide
    skip_x[PAD + images * skip_r * wide :, :] = jnp.zeros((skip_tail, 128), F32)
    loads[2].wait()
    lax.fori_loop(0, images, place_skip, 0)
    pack(skip_x, skip_send, skip_corner, skip_r, height, wide, breadth)
    skip_around.start(range(2, 8))
    loads[1].wait()
    stack_weight(w_one, conv_one_in)
    low_around.wait()
    unpack(low_around, low_x, low_rows, low_recv, low_corner, low_r, h, pitch, w)

    def conv_one(b, sums):
        pairs = tap_pairs(low_x, PAD + b * low_r * pitch, low_r * pitch, 0.0)
        pairs = pairs.astype(BF16)
        count = y_one_r * pitch
        taps = jnp.concatenate([pairs[pitch * a : pitch * a + count] for a in range(3)], axis=1)
        value = dot(taps, w_one[...]).reshape(y_one_r, pitch, 128)
        y_one_s[b] = value
        own = value[2 : h + 2, 8 : 8 + w].reshape(h * w, 128)
        return (
            sums[0] + jnp.sum(own, axis=0, keepdims=True),
            sums[1] + jnp.sum(own * own, axis=0, keepdims=True),
        )

    def own_taps(b, sums):
        pairs = tap_pairs(low_x, PAD + (b * low_r + 2) * pitch, (h + 2) * pitch, 0.0)
        own = pairs.reshape(h + 2, pitch, 256)[:, 8 : 8 + w].astype(BF16)
        low_s[b] = own
        lines = jnp.sum(own.astype(F32), axis=1)
        return [
            sums[tap] + jnp.sum(lines[tap : tap + h], axis=0, keepdims=True) for tap in range(3)
        ]

    def count_ones(b, total):
        ones = (target_in[b].reshape(height * breadth, 80).astype(F32) == 1.0).astype(F32)
        return total + jnp.sum(ones, axis=0, keepdims=True)

    nothing = jnp.zeros((1, 128), F32)
    sums = lax.fori_loop(0, images, conv_one, (nothing, nothing))
    sum_src = first_scratch[0]
    sum_src[...] = jnp.zeros((8, 128), F32)
    sum_src[0:1, :] = sums[0]
    sum_src[1:2, :] = sums[1]
    first_total = Total(*first_scratch)
    first_total.begin()
    stores = [
        pltpu.make_async_copy(y_one_s, y_one_out, out_sems.at[0, 0]),
        pltpu.make_async_copy(low_s, low_out, out_sems.at[0, 1]),
    ]
    stores[0].start()

    loads[9].wait()
    stack_weight(w_two, conv_two_in)
    skip_around.wait()
    unpack(
        skip_around, skip_x, skip_rows, skip_recv, skip_corner, skip_r, height, wide, breadth
    )
    first_total.middle()
    for k in (3, 4):
        loads[k].wait()
    ones = lax.fori_loop(0, images, count_ones, jnp.zeros((1, 80), F32))
    base = row_at * (height * breadth * col_count) + col_at * breadth
    slot = lax.broadcasted_iota(jnp.int32, (1, 128), 1)
    objects = 0
    spot_out[...] = jnp.full((8, 128), -(2**30), jnp.int32)
    for b in range(images):
        amount = count_ref[b]
        objects = objects + amount
        spot_out[b : b + 1, :] = jnp.where(
            slot < amount, index_in[b : b + 1, :] - base, -(2**30)
        )
    leading = jnp.logical_and(row_at == 0, col_at == 0).astype(F32)
    tap_none = jnp.zeros((1, 256), F32)
    tap_sums = lax.fori_loop(0, images, own_taps, [tap_none] * 3)
    stores[1].start()
    for k in range(5, 9):
        loads[k].wait()
    totals = first_total.end()
    mean_one = totals[0:1] / cells_low
    scale_one = lax.rsqrt(totals[1:2] / cells_low - mean_one * mean_one + EPSILON)
    gain_one, shift_one = twice(param_in[0]), twice(param_in[1])
    gain_two, shift_two = twice(param_in[2]), twice(param_in[3])
    stat_out[...] = jnp.zeros((24, 128), F32)
    stat_out[0:1, :] = mean_one
    stat_out[1:2, :] = scale_one
    stat_out[6:7, :] = gain_one
    stat_out[7:8, :] = shift_one
    stat_out[8:9, :] = gain_two
    stat_out[9:10, :] = shift_two
    ends = (row_at > 0, row_at < row_count - 1, col_at > 0, col_at < col_count - 1)
    for k, inner in enumerate(ends):
        stat_out[10 + k : 11 + k, :] = jnp.full((1, 128), inner.astype(F32))

    def conv_two(b, sums):
        normed = (y_one_s[b] - mean_one) * scale_one
        value, _ = silu_parts(normed * gain_one + shift_one)
        act_s[0 : y_one_r * pitch, :] = value.astype(BF16).astype(F32).reshape(
            y_one_r * pitch, 128
        )
        clear(
            act_s, 0, y_one_r, pitch, (0, 2), (h + 2, h + 4), (6, 8), (8 + w, 10 + w)
        )
        act = act_s[0 : y_one_r * pitch, :].reshape(y_one_r, pitch, 128)
        odd = 0.75 * act[:-1] + 0.25 * act[1:]
        even = 0.75 * act[1:] + 0.25 * act[:-1]
        tall = jnp.stack([odd, even], axis=1).reshape(skip_r * pitch, 128)
        row_s[PAD : PAD + skip_r * pitch, :] = tall
        count = skip_r * pitch
        before = row_s[PAD - 1 : PAD - 1 + count, :]
        behind = row_s[PAD + 1 : PAD + 1 + count, :]
        up_s[pl.ds(0, count, stride=2), :] = 0.75 * tall + 0.25 * before
        up_s[pl.ds(1, count, stride=2), :] = 0.75 * tall + 0.25 * behind
        start = PAD + b * skip_r * wide
        whole = pl.ds(start, skip_r * wide)
        up = up_s[...].reshape(skip_r, 2 * pitch, 128)[:, 8 : 8 + wide]
        merged = up + skip_x[whole, :].reshape(skip_r, wide, 128)
        skip_x[whole, :] = merged.astype(BF16).astype(F32).reshape(skip_r * wide, 128)
        clear(
            skip_x,
            start,
            skip_r,
            wide,
            (0, 3),
            (height + 3, height + 6),
            (5, 8),
            (8 + breadth, 11 + breadth),
        )
        pairs = tap_pairs(skip_x, start, skip_r * wide, 0.0)
        merged_s[b] = pairs.reshape(skip_r, wide, 256)[2 : height + 4, 8 : 8 + breadth].astype(
            BF16
        )
        pltpu.make_async_copy(merged_s.at[b], merged_out.at[b], out_sems.at[1, b]).start()
        pairs = pairs.astype(BF16)
        count = y_two_r * wide
        taps = jnp.concatenate([pairs[wide * a : wide * a + count] for a in range(3)], axis=1)
        value = dot(taps, w_two[...]).reshape(y_two_r, wide, 128)
        y_two_s[b] = value
        pltpu.make_async_copy(y_two_s.at[b], y_two_out.at[b], out_sems.at[2, b]).start()
        own = value[2 : height + 2, 8 : 8 + breadth].reshape(height * breadth, 128)
        return (
            sums[0] + jnp.sum(own, axis=0, keepdims=True),
            sums[1] + jnp.sum(own * own, axis=0, keepdims=True),
        )

    row_s[0:PAD, :] = jnp.zeros((PAD, 128), F32)
    row_s[PAD + skip_r * pitch :, :] = jnp.zeros((PAD, 128), F32)
    sums = lax.fori_loop(0, images, conv_two, (nothing, nothing))
    sum_src = second_scratch[0]
    sum_src[...] = jnp.zeros((16, 128), F32)
    sum_src[8:9, 0:80] = ones
    sum_src[9:10, :] = jnp.full((1, 128), objects.astype(F32) * leading)
    sum_src[0:1, :] = sums[0]
    sum_src[1:2, :] = sums[1]
    for tap in range(3):
        for part in range(2):
            line = 2 + 2 * tap + part
            sum_src[line : line + 1, :] = tap_sums[tap][:, 128 * part : 128 * part + 128]
    second_total = Total(*second_scratch)
    second_total.begin()
    g_low[...] = jnp.zeros_like(g_low)
    own_low[...] = jnp.zeros_like(own_low)

    def normed_taps(b, carry):
        normed = (y_one_s[b, 2 : h + 2] - mean_one) * scale_one
        own_low[2 * w : (h + 2) * w, :] = normed[:, 8 : 8 + w].reshape(h * w, 128)
        g_low[...] += product_of_parts(
            low_s[b].reshape((h + 2) * w, 256), shifted_taps(own_low, h, w)
        )
        return carry

    lax.fori_loop(0, images, normed_taps, 0)
    tiles_out[36:] = jnp.zeros((tiles_out.shape[0] - 36, 8, 128), F32)
    fold(tiles_out, 0, g_low)
    second_total.middle()
    for k in (10, 11):
        loads[k].wait()
    for tap in range(3):
        kernel_s[tap, 0:192, :] = (0.5 * head_in[tap].astype(F32)).astype(BF16)
        kernel_s[tap, 192:256, :] = jnp.zeros((64, 768), BF16)
    parts = three_parts(0.5 * bias_in[...].reshape(1, 768))
    which = lax.broadcasted_iota(jnp.int32, (16, 768), 0)
    filled = jnp.zeros((16, 768), F32)
    for place_at in range(3):
        filled = jnp.where(which == place_at, parts[place_at].astype(F32), filled)
    kernel_s[1, 192:208, :] = filled.astype(BF16)
    for tap in range(3):
        for block in range(3):
            span = slice(256 * block, 256 * block + 256)
            back_s[span, 256 * tap : 256 * tap + 256] = (
                kernel_s[tap, :, span].astype(F32).T.astype(BF16)
            )
    stores += [
        pltpu.make_async_copy(kernel_s, kernel_out, out_sems.at[0, 2]),
        pltpu.make_async_copy(back_s, back_out, out_sems.at[0, 3]),
    ]
    for store in stores[2:]:
        store.start()
    totals = second_total.end()
    mean_two = totals[0:1] / cells_high
    scale_two = lax.rsqrt(totals[1:2] / cells_high - mean_two * mean_two + EPSILON)
    stat_out[2:3, :] = mean_two
    stat_out[3:4, :] = scale_two
    stat_out[16:22, :] = totals[2:8]
    positives = jnp.sum(totals[8:9, 0:80], axis=1, keepdims=True)
    stat_out[4:5, :] = jnp.broadcast_to(1.0 / positives, (1, 128))
    stat_out[5:6, :] = 0.5 / totals[9:10]

    for store in stores:
        store.wait()
    for b in range(images):
        pltpu.make_async_copy(merged_s.at[b], merged_out.at[b], out_sems.at[1, b]).wait()
        pltpu.make_async_copy(y_two_s.at[b], y_two_out.at[b], out_sems.at[2, b]).wait()


def rise(
    low_map,
    skip_map,
    target,
    conv_one,
    conv_two,
    gain_one,
    shift_one,
    gain_two,
    shift_two,
    index,
    head,
    bias,
    count,
):
    images, h, w, _ = low_map.shape
    _, height, breadth, _ = skip_map.shape
    pitch, wide = w + 16, breadth + 16
    low_r, skip_r = h + 6, height + 6
    half = images // 2
    vmem = pl.BlockSpec(memory_space=pltpu.VMEM)
    hbm = pl.BlockSpec(memory_space=pl.ANY)
    kept = [
        jax.ShapeDtypeStruct((images, height + 4, wide, 128), F32),
        jax.ShapeDtypeStruct((images, h + 4, pitch, 128), F32),
        jax.ShapeDtypeStruct((images, height + 2, breadth, 256), BF16),
        jax.ShapeDtypeStruct((images, h + 2, w, 256), BF16),
        jax.ShapeDtypeStruct((3, 256, 768), BF16),
        jax.ShapeDtypeStruct((768, 768), BF16),
    ]
    return pl.pallas_call(
        rise_body,
        in_specs=[hbm] * 12 + [pl.BlockSpec(memory_space=pltpu.SMEM)],
        out_specs=[hbm] * 6 + [vmem] * 3,
        out_shape=kept
        + [jax.ShapeDtypeStruct((24, 128), F32), jax.ShapeDtypeStruct((8, 128), jnp.int32)]
        + [jax.ShapeDtypeStruct((conv_tiles(36), 8, 128), F32)],
        scratch_shapes=[
            pltpu.VMEM(low_map.shape, BF16),
            pltpu.VMEM(skip_map.shape, BF16),
            pltpu.VMEM(target.shape, BF16),
            pltpu.VMEM((3, 192, 64), BF16),
            pltpu.VMEM((3, 192, 64), BF16),
            pltpu.VMEM((4, 1, 64), F32),
            pltpu.VMEM(index.shape, jnp.int32),
            pltpu.VMEM((3, 192, 768), BF16),
            pltpu.VMEM((768,), F32),
        ]
        + [pltpu.VMEM(array.shape, array.dtype) for array in kept]
        + [
            pltpu.VMEM((2 * PAD + (images * low_r + 8) * pitch, 128), F32),
            pltpu.VMEM((2 * PAD + (images * skip_r + 8) * wide, 128), F32),
            pltpu.VMEM((rounded_up(h + 4, 8) * pitch, 128), F32),
            pltpu.VMEM((2 * PAD + skip_r * pitch, 128), F32),
            pltpu.VMEM((2 * skip_r * pitch, 128), F32),
            pltpu.VMEM((768, 128), BF16),
            pltpu.VMEM((768, 128), BF16),
            pltpu.VMEM((256, 256), F32),
            pltpu.VMEM(((h + 4) * w, 128), F32),
            pltpu.VMEM((2, images, 3, w, 64), BF16),
            pltpu.VMEM((2, images, 3, breadth, 64), BF16),
            pltpu.VMEM((2, 3 * half, rounded_up(h, 16), 128), BF16),
            pltpu.VMEM((2, 3 * half, rounded_up(h, 16), 128), BF16),
            pltpu.VMEM((2, 4, half, 32, 128), BF16),
            pltpu.VMEM((2, 3 * half, rounded_up(height, 16), 128), BF16),
            pltpu.VMEM((2, 3 * half, rounded_up(height, 16), 128), BF16),
            pltpu.VMEM((2, 4, half, 32, 128), BF16),
            total_scratch(8),
            total_scratch(16),
            pltpu.SemaphoreType.DMA((12,)),
            pltpu.SemaphoreType.DMA((4, max(images, 4))),
            pltpu.SemaphoreType.DMA((2, 2, 8)),
        ],
        compiler_params=pltpu.CompilerParams(
            collective_id=1, has_side_effects=True, vmem_limit_bytes=60 * MIB
        ),
        name="rise",
    )(
        low_map,
        skip_map,
        target,
        conv_one,
        conv_two,
        gain_one,
        shift_one,
        gain_two,
        shift_two,
        index,
        head,
        bias,
        count,
    )


def levels_of(tiles):
    batch, row, col = place()
    batches, rows, cols = extents()
    pairs = 2 if cols % 2 == 0 else 1
    outer = cols // pairs
    levels = []

    def add(count, mine, device_of):
        left = (levels[-1][3] if levels else tiles) // count
        partners = []
        for over in range(1, count):
            other = lax.rem(mine + over, count)
            partners.append((other, device_of(other)))
        levels.append((count, mine, partners, left))

    low = lax.rem(col, pairs)
    add(pairs, low, lambda k: (batch, row, col - low + k))
    add(
        outer * batches,
        lax.div(col, pairs) * batches + batch,
        lambda k: (lax.rem(k, batches), row, lax.div(k, batches) * pairs + low),
    )
    add(rows, row, lambda k: (batch, k, col))
    return levels


def level_sizes(tiles):
    batches, rows, cols = extents()
    pairs = 2 if cols % 2 == 0 else 1
    sizes = []
    for count in (pairs, cols // pairs * batches, rows):
        tiles = tiles // count
        sizes.append((count, tiles))
    return sizes


class Scatter:
    def __init__(self, source, mids, slots, sems):
        self.parts = [source, *mids]
        self.slots, self.sems = slots, sems
        self.levels = levels_of(source.shape[0])

    def begin(self, level):
        _, _, partners, left = self.levels[level]
        self.copies = [
            remote(
                self.parts[level].at[pl.ds(other * left, left)],
                self.slots[level].at[k],
                self.sems.at[level, 0, k],
                self.sems.at[level, 1, k],
                device,
            )
            for k, (other, device) in enumerate(partners)
        ]
        start_all(self.copies)

    def end(self, level):
        _, mine, partners, left = self.levels[level]
        wait_all(self.copies)
        total = self.parts[level][pl.ds(mine * left, left)].astype(F32)
        for k in range(len(partners)):
            total = total + self.slots[level][k].astype(F32)
        self.parts[level + 1][...] = total.astype(BF16)


class Gather:
    def __init__(self, full, sems):
        self.full, self.sems = full, sems
        self.levels = levels_of(full.shape[0])

    def span(self, level):
        base = 0
        for _, mine, _, left in self.levels[: level + 1]:
            base = base + mine * left
        return pl.ds(base, self.levels[level][3])

    def begin(self, level):
        part = self.full.at[self.span(level)]
        self.copies = [
            remote(part, part, self.sems.at[level, 0, k], self.sems.at[level, 1, k], device)
            for k, (_, device) in enumerate(self.levels[level][2])
        ]
        start_all(self.copies)

    def end(self):
        wait_all(self.copies)


def scatter_scratch(tiles):
    sizes = level_sizes(tiles)
    return (
        tuple(pltpu.VMEM((left, 16, 128), BF16) for _, left in sizes[:-1]),
        tuple(pltpu.VMEM((count - 1, left, 16, 128), BF16) for count, left in sizes),
        level_sems(),
    )


def level_sems():
    return pltpu.SemaphoreType.DMA((3, 2, max(count for count, _ in level_sizes(1)) - 1))


class PlaneReducer:
    def __init__(self, source, slots, mid, row_slots, full, sems):
        batch, row, col = place()
        batches, rows, cols = extents()
        self.source, self.slots, self.mid = source, slots, mid
        self.row_slots, self.full, self.sems = row_slots, full, sems
        self.share = mid.shape[0]
        self.mine = batch * cols + col
        self.row = row

    def begin(self):
        _, _, cols = extents()
        self.copies = []
        for k, (batch, row, col) in enumerate(plane_partners()):
            other = batch * cols + col
            part = self.source.at[pl.ds(other * self.share, self.share)]
            self.copies.append(
                remote(
                    part, self.slots.at[k], self.sems.at[0, 0, k], self.sems.at[0, 1, k],
                    (batch, row, col),
                )
            )
        start_all(self.copies)

    def middle(self):
        wait_all(self.copies)
        total = self.source[pl.ds(self.mine * self.share, self.share)]
        for k in range(self.slots.shape[0]):
            total = total + self.slots[k]
        self.mid[...] = total
        self.copies = [
            remote(
                self.mid, self.row_slots.at[self.row], self.sems.at[1, 0, k],
                self.sems.at[1, 1, k], partner,
            )
            for k, partner in enumerate(row_partners())
        ]
        start_all(self.copies)
        self.row_slots[self.row] = total

    def last(self):
        wait_all(self.copies)
        self.full[pl.ds(self.mine * self.share, self.share)] = slot_sum(self.row_slots)
        part = self.full.at[pl.ds(self.mine * self.share, self.share)]
        self.copies = [
            remote(part, part, self.sems.at[2, 0, k], self.sems.at[2, 1, k], partner)
            for k, partner in enumerate(plane_partners())
        ]
        start_all(self.copies)

    def end(self):
        wait_all(self.copies)


def plane_scratch(tiles):
    batches, rows, cols = extents()
    planes = batches * cols
    share = tiles // planes
    most = max(planes, rows) - 1
    return [
        pltpu.VMEM((tiles, 8, 128), F32),
        pltpu.VMEM((planes - 1, share, 8, 128), F32),
        pltpu.VMEM((share, 8, 128), F32),
        pltpu.VMEM((rows, share, 8, 128), F32),
        pltpu.SemaphoreType.DMA((3, 2, most)),
    ]


def conv_tiles(tiles):
    batches, _, cols = extents()
    planes = batches * cols
    return -(-tiles // planes) * planes


def fold(target, first, grads):
    low = lower_half((1, 128))
    last = grads[0:192, 128:256]
    target[first : first + 24] = grads[0:192, 0:128].reshape(24, 8, 128)
    target[first + 24 : first + 36] = jnp.where(low, last[0:96], swapped(last[96:192])).reshape(
        12, 8, 128
    )


def unfold(source, first):
    pairs = source[first : first + 24].reshape(192, 128)
    last = source[first + 24 : first + 36].reshape(96, 128)
    return [
        pairs[:, 0:64],
        swapped(pairs)[:, 0:64],
        jnp.concatenate([last[:, 0:64], swapped(last)[:, 0:64]], axis=0),
    ]


def shifted_taps(buffer, rows, line):
    count = (rows + 2) * line
    views = [buffer[(2 - tap) * line : (2 - tap) * line + count, :] for tap in range(3)]
    low = lower_half((1, 128))
    return jnp.concatenate(
        [jnp.where(low, views[0], views[1]), jnp.where(low, views[2], 0.0)], axis=1
    )


def product_of_parts(left, right):
    high = right.astype(BF16)
    rest = (right - high.astype(F32)).astype(BF16)
    return dot_left(left, high) + dot_left(left, rest)


def stack_back(target, source):
    for tap in range(3):
        for e in range(3):
            block = source[tap, 64 * e : 64 * e + 64, :].astype(F32)
            start = 256 * tap + 64 * e
            target[start : start + 64, :] = twice(block.T).astype(BF16)
        target[256 * tap + 192 : 256 * tap + 256, :] = jnp.zeros((64, 128), BF16)


def back_pairs(buffer, start, count):
    low = lower_half((1, 128))
    first = jnp.where(low, buffer[pl.ds(start + 1, count), :], buffer[pl.ds(start, count), :])
    second = jnp.where(low, buffer[pl.ds(start - 1, count), :], 0.0)
    return jnp.concatenate([first, second], axis=1).astype(BF16)


def slope_of(values):
    logistic = 0.5 * jnp.tanh(0.5 * values) + 0.5
    return logistic * (1.0 + values * (1.0 - logistic))


def fall_body(
    spread_ref,
    y_two_ref,
    stat_ref,
    load_ref,
    small_ref,
    tiles_ref,
    y_one_ref,
    merged_ref,
    low_ref,
    conv_ref,
    conv_one_ref,
    skip_out,
    zed_out,
    load_out,
    conv_out,
    conv_x_out,
    sums_out,
    last_out,
    weight_out,
    y_two_s,
    slope_s,
    y_one_s,
    merged_s,
    low_s,
    conv_s,
    load_s,
    skip_s,
    share_s,
    grad_x,
    zed_x,
    own_s,
    own_low_s,
    pair_s,
    narrow_s,
    w_two,
    g_two,
    g_one,
    total_s,
    strip_send,
    strip_recv,
    side_send,
    side_recv,
    corners,
    zed_send,
    zed_recv,
    edge_send,
    edge_recv,
    zed_corners,
    third_scratch,
    fourth_scratch,
    load_scratch,
    conv_x_scratch,
    conv_scratch,
    gather_sems,
    in_sems,
    map_sems,
    out_sems,
    strip_sems,
    zed_sems,
):
    images, rows, wide, _ = y_two_ref.shape
    height, breadth = rows - 4, wide - 16
    h, w = height // 2, breadth // 2
    pitch, ext = w + 16, height + 2
    zed_rows = h + 2
    half = images // 2
    _, row_at, col_at = place()
    batches, row_count, col_count = extents()
    cells_high = float(images * batches * height * row_count * breadth * col_count)
    low_half = lower_half((1, 128))
    mean_one, scale_one = stat_ref[0:1, :], stat_ref[1:2, :]
    mean_two, scale_two = stat_ref[2:3, :], stat_ref[3:4, :]
    gain_one, shift_one = stat_ref[6:7, :], stat_ref[7:8, :]
    gain_two, shift_two = stat_ref[8:9, :], stat_ref[9:10, :]
    top, bottom = stat_ref[10:11, :], stat_ref[11:12, :]
    left, right = stat_ref[12:13, :], stat_ref[13:14, :]

    def spread_load(b):
        start = PAD + (b * rows + 1) * wide
        return pltpu.make_async_copy(
            spread_ref.at[b], grad_x.at[pl.ds(start, ext * wide)], map_sems.at[0, b]
        )

    def y_two_load(b):
        return pltpu.make_async_copy(y_two_ref.at[b], y_two_s.at[b], map_sems.at[1, b])

    loads = [
        pltpu.make_async_copy(source, target, in_sems.at[k])
        for k, (source, target) in enumerate(
            (
                (load_ref, load_s),
                (tiles_ref, conv_x_scratch[0]),
                (conv_ref, conv_s.at[0]),
                (conv_one_ref, conv_s.at[1]),
                (merged_ref, merged_s),
                (y_one_ref, y_one_s),
                (low_ref, low_s),
            )
        )
    ]
    for b in range(images):
        spread_load(b).start()
    for b in range(images):
        y_two_load(b).start()
    for load in loads:
        load.start()
    grad_x[0:PAD, :] = jnp.zeros((PAD, 128), F32)
    tail = PAD + images * rows * wide
    grad_x[tail:, :] = jnp.zeros((grad_x.shape[0] - tail, 128), F32)
    for b in range(images):
        for line in (0, ext + 1):
            start = PAD + (b * rows + line) * wide
            grad_x[start : start + wide, :] = jnp.zeros((wide, 128), F32)
    greeted(greet())
    for b in range(images):
        spread_load(b).wait()
    for pair in range(half):
        for side, first in enumerate((1, ext - 2)):
            parts = []
            for image in (pair, pair + half):
                start = PAD + (image * rows + first) * wide
                parts.append(grad_x[start : start + 3 * wide, :])
            strip_send[side, pair] = jnp.where(low_half, parts[0], parts[1]).astype(BF16)
    around = Around(
        [strip_send.at[k] for k in range(2)]
        + [side_send.at[k] for k in range(2)]
        + [corners.at[0, k] for k in range(4)],
        [strip_recv.at[k] for k in range(2)]
        + [side_recv.at[k] for k in range(2)]
        + [corners.at[1, k] for k in range(4)],
        strip_sems,
    )
    around.start(range(2))
    for side, first in enumerate((7, 6 + breadth)):
        pack_columns(grad_x, side_send.at[side], images, rows, wide, 1, first, 3)
    for k, (up, along) in enumerate(AROUND[4:]):
        pack_corner(
            grad_x,
            corners.at[0, k],
            images,
            rows,
            wide,
            1 if up < 0 else height,
            7 if along < 0 else 6 + breadth,
            3,
        )
    around.start(range(2, 8))
    loads[0].wait()
    load_sum = Scatter(load_s, (*load_scratch[0], share_s), load_scratch[1], load_scratch[2])
    load_sum.begin(0)

    def begin(b, sums):
        y_two_load(b).wait()
        start = PAD + b * rows * wide
        clear(
            grad_x,
            start,
            rows,
            wide,
            (1, 2),
            (ext, ext + 1),
            (7, 8),
            (8 + breadth, 9 + breadth),
        )
        normed = (y_two_s[b] - mean_two) * scale_two
        slope = slope_of(normed * gain_two + shift_two)
        slope_s[b] = slope
        part = grad_x[pl.ds(start, rows * wide), :].reshape(rows, wide, 128)
        weighted = part * slope
        return sums[0] + fold_sum(weighted), sums[1] + fold_sum(weighted * normed)

    nothing = jnp.zeros((8, 128), F32)
    sums = lax.fori_loop(0, images, begin, (nothing, nothing))
    sum_src = third_scratch[0]
    sum_src[...] = jnp.zeros((16, 128), F32)
    sum_src[0:8, :] = small_ref[...]
    sum_src[8:9, :] = jnp.sum(sums[0], axis=0, keepdims=True)
    sum_src[9:10, :] = jnp.sum(sums[1], axis=0, keepdims=True)
    third_total = Total(*third_scratch)
    third_total.begin()
    load_sum.end(0)
    load_sum.begin(1)
    loads[2].wait()
    stack_back(w_two, conv_s.at[0])
    loads[3].wait()
    stack_back(weight_out, conv_s.at[1])
    g_two[...] = jnp.zeros_like(g_two)
    g_one[...] = jnp.zeros_like(g_one)
    own_s[...] = jnp.zeros_like(own_s)
    own_low_s[...] = jnp.zeros_like(own_low_s)
    narrow_s[...] = jnp.zeros_like(narrow_s)
    zed_x[...] = jnp.zeros_like(zed_x)
    third_total.middle()
    around.wait()

    def use(k):
        up, along = AROUND[k]
        row = height + 1 if up < 0 else 0
        column = 7 + breadth if along < 0 else 6
        if k < 2:
            for image in range(images):
                values = unpacked(strip_recv[k, image % half].astype(F32), image, images)
                start = PAD + (image * rows + row) * wide
                grad_x[start : start + 3 * wide, :] += values
        elif k < 4:
            unpack_columns(
                grad_x, side_recv.at[k - 2], images, rows, wide, 1, column, 3, ext, True
            )
        else:
            unpack_corner(
                grad_x, corners.at[1, k - 4], images, rows, wide, row, column, 3, True
            )

    around.each(use)

    loads[1].wait()
    conv_x_sum = PlaneReducer(*conv_x_scratch[:4], conv_x_out, conv_x_scratch[4])
    totals = third_total.end()
    sums_out[...] = totals
    conv_x_sum.begin()
    load_sum.end(1)
    load_sum.begin(2)
    factor_two = gain_two * scale_two
    shift_part, gain_part = totals[8:9] / cells_high, totals[9:10] / cells_high
    for k in (4, 5, 6):
        loads[k].wait()
    column = lax.broadcasted_iota(jnp.int32, (wide, 128), 0)
    keep = jnp.where(column < 8, left, 1.0)
    keep = jnp.where(column >= 8 + breadth, right, keep)

    def merge(b, sums):
        start = PAD + b * rows * wide
        whole = pl.ds(start, rows * wide)
        normed = (y_two_s[b] - mean_two) * scale_two
        grad_z = grad_x[whole, :].reshape(rows, wide, 128) * slope_s[b]
        grad_y = factor_two * (grad_z - shift_part - normed * gain_part)
        grad_y = (grad_y * keep).astype(BF16).astype(F32)
        grad_x[whole, :] = grad_y.reshape(rows * wide, 128)
        for line, flag in ((0, top), (ext, bottom)):
            span = pl.ds(start + line * wide, 2 * wide)
            grad_x[span, :] = grad_x[span, :] * flag
        own_s[2 * breadth : (height + 2) * breadth, :] = grad_y[
            2 : height + 2, 8 : 8 + breadth
        ].reshape(height * breadth, 128)
        source = merged_s[b].reshape(ext * breadth, 256)
        g_two[...] += dot_left(source, shifted_taps(own_s, height, breadth).astype(BF16))
        pair_s[...] = back_pairs(grad_x, start, rows * wide)
        count = ext * wide
        taps = jnp.concatenate(
            [pair_s[wide * (2 - a) : wide * (2 - a) + count, :] for a in range(3)], axis=1
        )
        merged_grad = dot(taps, w_two[...]).reshape(ext, wide, 128)
        skip_s[b] = merged_grad[1 : height + 1, 8 : 8 + breadth, 0:64]
        pltpu.make_async_copy(skip_s.at[b], skip_out.at[b], out_sems.at[0, b]).start()
        fine = (merged_grad * keep).astype(BF16).astype(F32).reshape(h + 1, 2, wide, 128)
        even, odd = fine[:, 0], fine[:, 1]
        even = jnp.concatenate([even[0:1] * top, even[1:]], axis=0)
        odd = jnp.concatenate([odd[:-1], odd[-1:] * bottom], axis=0)
        short = 0.75 * (odd[:-1] + even[1:]) + 0.25 * (even[:-1] + odd[1:])
        side = jnp.zeros((h, 8, 128), F32)
        count = h * 2 * pitch
        narrow_s[PAD : PAD + count, :] = jnp.concatenate([side, short, side], axis=1).reshape(
            count, 128
        )
        lines = [narrow_s[pl.ds(PAD + k, count // 2, stride=2), :] for k in (-1, 0, 1, 2)]
        act_grad = 0.75 * (lines[1] + lines[2]) + 0.25 * (lines[0] + lines[3])
        act_grad = act_grad.reshape(h, pitch, 128)
        normed = (y_one_s[b, 2 : h + 2] - mean_one) * scale_one
        slope = slope_of(normed * gain_one + shift_one)
        place_at = lax.broadcasted_iota(jnp.int32, (pitch, 128), 0)
        inner = jnp.logical_and(place_at >= 8, place_at < 8 + w)
        grad_z = jnp.where(inner, act_grad * slope, 0.0)
        spot = PAD + (b * zed_rows + 1) * pitch
        zed_x[pl.ds(spot, h * pitch), :] = grad_z.reshape(h * pitch, 128)
        own_low_s[2 * w : (h + 2) * w, :] = grad_z[:, 8 : 8 + w].reshape(h * w, 128)
        g_one[...] += product_of_parts(
            low_s[b].reshape((h + 2) * w, 256), shifted_taps(own_low_s, h, w)
        )
        return sums[0] + fold_sum(grad_z), sums[1] + fold_sum(grad_z * normed)

    sums = lax.fori_loop(0, half, merge, (nothing, nothing))
    gather = Gather(load_out, gather_sems)
    load_sum.end(2)
    load_out[gather.span(2)] = share_s[...]
    gather.begin(2)
    conv_x_sum.middle()
    sums = lax.fori_loop(half, images, merge, sums)
    last_src = fourth_scratch[0]
    last_src[...] = jnp.zeros((8, 128), F32)
    last_src[0:1, :] = jnp.sum(sums[0], axis=0, keepdims=True)
    last_src[1:2, :] = jnp.sum(sums[1], axis=0, keepdims=True)
    fourth_total = Total(*fourth_scratch)
    fourth_total.begin()
    gather.end()
    gather.begin(1)
    fold(conv_scratch[0], 0, g_two)
    fold(conv_scratch[0], 36, g_one)
    if conv_out.shape[0] > 72:
        conv_scratch[0][72:] = jnp.zeros((conv_out.shape[0] - 72, 8, 128), F32)
    conv_sum = PlaneReducer(*conv_scratch[:4], conv_out, conv_scratch[4])
    conv_sum.begin()
    for pair in range(half):
        for side, line in enumerate((1, h)):
            parts = []
            for image in (pair, pair + half):
                start = PAD + (image * zed_rows + line) * pitch
                parts.append(zed_x[start : start + pitch, :])
            zed_send[side, pair] = jnp.where(low_half, parts[0], parts[1])
    for side, column in enumerate((8, 7 + w)):
        pack_columns(zed_x, edge_send.at[side], images, zed_rows, pitch, 1, column, 1)
    for k, (up, along) in enumerate(AROUND[4:]):
        pack_corner(
            zed_x,
            zed_corners.at[0, k],
            images,
            zed_rows,
            pitch,
            1 if up < 0 else h,
            8 if along < 0 else 7 + w,
            1,
        )
    zed_around = Around(
        [zed_send.at[k] for k in range(2)]
        + [edge_send.at[k] for k in range(2)]
        + [zed_corners.at[0, k] for k in range(4)],
        [zed_recv.at[k] for k in range(2)]
        + [edge_recv.at[k] for k in range(2)]
        + [zed_corners.at[1, k] for k in range(4)],
        zed_sems,
    )
    zed_around.start()
    fourth_total.middle()
    conv_x_sum.last()
    conv_sum.middle()
    zed_around.wait()

    def use_zed(k):
        up, along = AROUND[k]
        row = h + 1 if up < 0 else 0
        column = 8 + w if along < 0 else 7
        if k < 2:
            for image in range(images):
                start = PAD + (image * zed_rows + row) * pitch
                zed_x[start : start + pitch, :] = unpacked(
                    zed_recv[k, image % half], image, images
                )
        elif k < 4:
            unpack_columns(
                zed_x, edge_recv.at[k - 2], images, zed_rows, pitch, 1, column, 1, h, False
            )
        else:
            unpack_corner(
                zed_x, zed_corners.at[1, k - 4], images, zed_rows, pitch, row, column, 1, False
            )

    zed_around.each(use_zed)

    def zed_store(b):
        return pltpu.make_async_copy(
            zed_x.at[pl.ds(PAD + b * zed_rows * pitch, zed_rows * pitch)],
            zed_out.at[b],
            out_sems.at[1, b],
        )

    for b in range(images):
        zed_store(b).start()
    last_out[...] = fourth_total.end()
    conv_sum.last()
    gather.end()
    gather.begin(0)
    conv_x_sum.end()
    conv_sum.end()
    gather.end()
    for b in range(images):
        zed_store(b).wait()
        pltpu.make_async_copy(skip_s.at[b], skip_out.at[b], out_sems.at[0, b]).wait()


def fall(
    spread, y_two, stats, load, small, tiles_x, y_one, merged, low, conv_two, conv_one
):
    images, rows, wide, _ = y_two.shape
    height, breadth = rows - 4, wide - 16
    h, w = height // 2, breadth // 2
    pitch, ext, zed_rows = w + 16, height + 2, h + 2
    half = images // 2
    tiles, parts_x, parts = load.shape[0], tiles_x.shape[0], conv_tiles(72)
    vmem = pl.BlockSpec(memory_space=pltpu.VMEM)
    hbm = pl.BlockSpec(memory_space=pl.ANY)
    lines, low_lines = rounded_up(ext, 16), rounded_up(h, 8)
    return pl.pallas_call(
        fall_body,
        in_specs=[hbm] * 2 + [vmem, hbm, vmem] + [hbm] * 6,
        out_specs=[hbm] * 2 + [vmem] * 6,
        out_shape=[
            jax.ShapeDtypeStruct((images, height, breadth, 64), F32),
            jax.ShapeDtypeStruct((images, zed_rows * pitch, 128), F32),
            jax.ShapeDtypeStruct((tiles, 16, 128), BF16),
            jax.ShapeDtypeStruct((parts, 8, 128), F32),
            jax.ShapeDtypeStruct((parts_x, 8, 128), F32),
            jax.ShapeDtypeStruct((16, 128), F32),
            jax.ShapeDtypeStruct((8, 128), F32),
            jax.ShapeDtypeStruct((768, 128), BF16),
        ],
        scratch_shapes=[
            pltpu.VMEM(y_two.shape, F32),
            pltpu.VMEM(y_two.shape, F32),
            pltpu.VMEM(y_one.shape, F32),
            pltpu.VMEM(merged.shape, BF16),
            pltpu.VMEM(low.shape, BF16),
            pltpu.VMEM((2, 3, 192, 64), BF16),
            pltpu.VMEM(load.shape, BF16),
            pltpu.VMEM((images, height, breadth, 64), F32),
            pltpu.VMEM((level_sizes(tiles)[-1][1], 16, 128), BF16),
            pltpu.VMEM((2 * PAD + (images * rows + lines - ext) * wide, 128), F32),
            pltpu.VMEM((2 * PAD + (images * zed_rows + 8) * pitch, 128), F32),
            pltpu.VMEM(((height + 4) * breadth, 128), F32),
            pltpu.VMEM(((h + 4) * w, 128), F32),
            pltpu.VMEM((rows * wide, 256), BF16),
            pltpu.VMEM((2 * PAD + h * 2 * pitch, 128), F32),
            pltpu.VMEM((768, 128), BF16),
            pltpu.VMEM((256, 256), F32),
            pltpu.VMEM((256, 256), F32),
            pltpu.VMEM((2, 8, 128), F32),
            pltpu.VMEM((2, half, 3 * wide, 128), BF16),
            pltpu.VMEM((2, half, 3 * wide, 128), BF16),
            pltpu.VMEM((2, 3 * half, lines, 128), BF16),
            pltpu.VMEM((2, 3 * half, lines, 128), BF16),
            pltpu.VMEM((2, 4, half, 32, 128), BF16),
            pltpu.VMEM((2, half, pitch, 128), F32),
            pltpu.VMEM((2, half, pitch, 128), F32),
            pltpu.VMEM((2, half, low_lines, 128), F32),
            pltpu.VMEM((2, half, low_lines, 128), F32),
            pltpu.VMEM((2, 4, half, 8, 128), F32),
            total_scratch(16),
            total_scratch(8),
            scatter_scratch(tiles),
            plane_scratch(parts_x),
            plane_scratch(parts),
            level_sems(),
            pltpu.SemaphoreType.DMA((7,)),
            pltpu.SemaphoreType.DMA((2, images)),
            pltpu.SemaphoreType.DMA((2, images)),
            pltpu.SemaphoreType.DMA((2, 8)),
            pltpu.SemaphoreType.DMA((2, 8)),
        ],
        compiler_params=pltpu.CompilerParams(
            collective_id=2, has_side_effects=True, vmem_limit_bytes=60 * MIB
        ),
        name="fall",
    )(spread, y_two, stats, load, small, tiles_x, y_one, merged, low, conv_two, conv_one)


def finish_body(
    cells_low,
    load_ref,
    rest_ref,
    conv_ref,
    conv_x_ref,
    sums_ref,
    last_ref,
    stat_ref,
    zed_ref,
    y_one_ref,
    weight_ref,
    skip_ref,
    conv_one_out,
    gain_one_out,
    shift_one_out,
    conv_two_out,
    gain_two_out,
    shift_two_out,
    head_out,
    head_b_out,
    heat_w_out,
    heat_b_out,
    box_w_out,
    box_b_out,
    low_out,
    skip_out,
    zed_x,
):
    step = pl.program_id(0)
    each, h, w, _ = low_out.shape
    pitch = w + 16
    rows = h + 2
    factor = stat_ref[6:7, :] * stat_ref[1:2, :]
    shift_low, gain_low = last_ref[0:1, :] / cells_low, last_ref[1:2, :] / cells_low
    skip_out[...] = skip_ref[...]
    for column in range(head_out.shape[3] // 128):
        block = load_ref[36 * column : 36 * column + 36].astype(F32)
        head_out[:, :, :, 128 * column : 128 * column + 128] = block.reshape(3, 3, 64, 128)

    @pl.when(step == 0)
    def _():
        zed_x[0:PAD, :] = jnp.zeros((PAD, 128), F32)
        zed_x[PAD + rows * pitch :, :] = jnp.zeros((PAD, 128), F32)
        spread = stat_ref[16:24, :].T
        ones = unfold(conv_ref, 36)
        normed = unfold(conv_x_ref, 0)
        for tap, part in enumerate(unfold(conv_ref, 0)):
            conv_two_out[tap] = part.reshape(3, 64, 64)
            count = jnp.concatenate(
                [spread[:, 2 * tap : 2 * tap + 1], spread[0:64, 2 * tap + 1 : 2 * tap + 2]], axis=0
            )
            value = ones[tap] - count * shift_low[:, 0:64] - normed[tap] * gain_low[:, 0:64]
            conv_one_out[tap] = (value * factor[:, 0:64]).reshape(3, 64, 64)
        for column in range(6):
            span = slice(128 * column, 128 * column + 128)
            head_b_out[span] = sums_ref[column : column + 1, :].reshape(128)
        for part in range(2):
            span = slice(128 * part, 128 * part + 128)
            heat_w_out[:, span] = rest_ref[5 * part : 5 * part + 5].astype(F32).reshape(80, 128)
            for box in range(2):
                block = rest_ref[10 + 2 * box + part].astype(F32)
                box_w_out[box, :, span] = block[2 * box : 2 * box + 2, :]
            box_b_out[part : part + 1, :] = sums_ref[7:8, 2 * part : 2 * part + 2]
        heat_b_out[...] = sums_ref[6:7, 0:80]
        shift_two_out[...] = sums_ref[8:9, 0:64]
        gain_two_out[...] = sums_ref[9:10, 0:64]
        shift_one_out[...] = last_ref[0:1, 0:64]
        gain_one_out[...] = last_ref[1:2, 0:64]

    for b in range(each):
        normed = (y_one_ref[b, 1 : h + 3] - stat_ref[0:1, :]) * stat_ref[1:2, :]
        grad_z = zed_ref[b].reshape(rows, pitch, 128)
        grad_y = factor * (grad_z - shift_low - normed * gain_low)
        column = lax.broadcasted_iota(jnp.int32, (pitch, 128), 0)
        keep = jnp.where(column < 8, stat_ref[12:13, :], 1.0)
        keep = jnp.where(column >= 8 + w, stat_ref[13:14, :], keep)
        grad_y = (grad_y * keep).astype(BF16).astype(F32)
        zed_x[PAD : PAD + rows * pitch, :] = grad_y.reshape(rows * pitch, 128)
        for line, row in ((0, 10), (rows - 1, 11)):
            span = slice(PAD + line * pitch, PAD + (line + 1) * pitch)
            zed_x[span, :] = zed_x[span, :] * stat_ref[row : row + 1, :]
        pairs = back_pairs(zed_x, PAD, rows * pitch)
        count = h * pitch
        taps = jnp.concatenate(
            [pairs[pitch * (2 - a) : pitch * (2 - a) + count] for a in range(3)], axis=1
        )
        grad = dot(taps, weight_ref[...]).reshape(h, pitch, 128)
        low_out[b] = grad[:, 8 : 8 + w, 0:64]


def finish(load, conv, conv_x, sums, last, stats, zed, y_one, weight, skip):
    images, y_rows, pitch, _ = y_one.shape
    h, w = y_rows - 4, pitch - 16
    batches, row_count, col_count = extents()
    cells = float(images * batches * h * row_count * w * col_count)
    span = zed.shape[1]
    steps = 2
    each = images // steps
    shapes = [
        (3, 3, 64, 64),
        (1, 64),
        (1, 64),
        (3, 3, 64, 64),
        (1, 64),
        (1, 64),
        (3, 3, 64, 768),
        (768,),
        (80, 256),
        (1, 80),
        (2, 2, 256),
        (2, 2),
        (images, h, w, 64),
        skip.shape,
    ]
    whole = lambda shape: pl.BlockSpec(shape, lambda c: (0,) * len(shape))
    part = lambda shape: pl.BlockSpec(shape, lambda c: (c,) + (0,) * (len(shape) - 1))
    out_specs = [whole(shape) for shape in shapes]
    out_specs[6] = pl.BlockSpec((3, 3, 64, 768 // steps), lambda c: (0, 0, 0, c))
    out_specs[12] = part((each, h, w, 64))
    out_specs[13] = part((each,) + skip.shape[1:])
    return pl.pallas_call(
        functools.partial(finish_body, cells),
        grid=(steps,),
        in_specs=[
            part((216 // steps, 16, 128)),
            pl.BlockSpec((36, 16, 128), lambda c: (6, 0, 0)),
        ]
        + [whole(array.shape) for array in (conv, conv_x, sums, last, stats)]
        + [
            part((each, span, 128)),
            part((each, y_rows, pitch, 128)),
            whole(weight.shape),
            part((each,) + skip.shape[1:]),
        ],
        out_specs=out_specs,
        out_shape=[jax.ShapeDtypeStruct(shape, F32) for shape in shapes],
        scratch_shapes=[
            pltpu.VMEM((2 * PAD + span, 128), F32),
        ],
        compiler_params=pltpu.CompilerParams(vmem_limit_bytes=60 * MIB),
        name="finish",
    )(load, load, conv, conv_x, sums, last, stats, zed, y_one, weight, skip)


def local(
    low_map,
    skip_map,
    conv_first,
    gain_first,
    shift_first,
    conv_second,
    gain_second,
    shift_second,
    head_conv,
    head_bias,
    heat_weight,
    heat_bias,
    box_weight,
    box_bias,
    heat_target,
    box_target,
    obj_index,
    obj_count,
):
    batches, rows, cols = extents()
    devices = batches * rows * cols
    conv_one = conv_first.reshape(3, 192, 64)
    conv_two = conv_second.reshape(3, 192, 64)
    y_two, y_one, merged, low, kernel, back, stats, spot, tiles_x = rise(
        low_map,
        skip_map,
        heat_target,
        conv_one,
        conv_two,
        gain_first.reshape(1, 64),
        shift_first.reshape(1, 64),
        gain_second.reshape(1, 64),
        shift_second.reshape(1, 64),
        obj_index,
        head_conv.reshape(3, 192, 768),
        head_bias,
        obj_count,
    )
    heat_map, box_map, spread, load, small = heads(
        y_two,
        heat_target,
        spot,
        box_target.transpose(0, 2, 1),
        stats,
        kernel,
        back,
        heat_weight.T,
        heat_bias.reshape(1, 80),
        box_weight.transpose(0, 2, 1),
        box_bias,
        devices,
    )
    images, ext, wide, _ = spread.shape
    grad_skip, zed, load, conv, conv_x, sums, last, weight = fall(
        spread.reshape(images, ext * wide, 128),
        y_two,
        stats,
        load,
        small,
        tiles_x,
        y_one,
        merged,
        low,
        conv_two,
        conv_one,
    )
    grads = finish(load, conv, conv_x, sums, last, stats, zed, y_one, weight, grad_skip)
    return (
        heat_map,
        box_map.transpose(0, 1, 3, 2),
        grads[12],
        grads[13],
        grads[0],
        grads[1].reshape(64),
        grads[2].reshape(64),
        grads[3],
        grads[4].reshape(64),
        grads[5].reshape(64),
        grads[6],
        grads[7],
        grads[8].T,
        grads[9].reshape(80),
        grads[10].transpose(0, 2, 1),
        grads[11],
    )


def solution(mesh):
    tile = P("batch", "row", "col", None)
    return jax.shard_map(
        local,
        mesh=mesh,
        in_specs=(tile, tile)
        + (P(),) * 12
        + (tile, P("batch", None, None), P("batch", None), P("batch")),
        out_specs=(tile,) * 4 + (P(),) * 12,
        check_vma=False,
    )
```

```python
import functools

import jax
import jax.numpy as jnp
from jax import lax
from jax.experimental import pallas as pl
from jax.experimental.pallas import tpu as pltpu
from jax.sharding import PartitionSpec as P

EPSILON = 1e-05
F32 = jnp.float32
BF16 = jnp.bfloat16
KEEP = (((1,), (1,)), ((), ()))
LEFT = (((0,), (0,)), ((), ()))
MIB = 1024 * 1024


def dot(left, right):
    return jnp.dot(left, right, preferred_element_type=F32)


def dot_keep(left, right):
    return lax.dot_general(left, right, KEEP, preferred_element_type=F32)


def dot_left(left, right):
    return lax.dot_general(left, right, LEFT, preferred_element_type=F32)


def three_parts(values):
    high = values.astype(BF16)
    rest = values - high.astype(F32)
    mid = rest.astype(BF16)
    return high, mid, (rest - mid.astype(F32)).astype(BF16)


def tile_count(devices):
    return -(-230 // (2 * devices)) * 2 * devices


def heads_body(
    chunks,
    map_side,
    y_two_ref,
    target_ref,
    spot_ref,
    goal_ref,
    stat_ref,
    kernel_s,
    back_s,
    heat_w_ref,
    heat_b_ref,
    box_w_ref,
    box_b_ref,
    heat_out,
    box_out,
    spread_out,
    load_out,
    small_out,
    feat_s,
    taps_ref,
    box_s,
    goal_s,
    wide_s,
    grad_s,
    heat_grad_s,
    box_grad_s,
    heat_sum_s,
    box_sum_s,
):
    image = pl.program_id(0)
    chunk = pl.program_id(1)
    rows, breadth = target_ref.shape[1], target_ref.shape[2]
    cells = rows * breadth
    units = 256

    @pl.when(jnp.logical_and(image == 0, chunk == 0))
    def _():
        empty = jnp.zeros((2, 256), F32)
        for part in range(2):
            pieces = [empty, empty]
            pieces[part] = box_w_ref[part].astype(F32)
            box_s[part] = jnp.concatenate(pieces, axis=0).astype(BF16)
        grad_s[...] = jnp.zeros_like(grad_s)
        heat_grad_s[...] = jnp.zeros_like(heat_grad_s)
        box_grad_s[...] = jnp.zeros_like(box_grad_s)
        heat_sum_s[...] = jnp.zeros_like(heat_sum_s)
        box_sum_s[...] = jnp.zeros_like(box_sum_s)

    @pl.when(chunk == 0)
    def _():
        wide_s[...] = jnp.zeros_like(wide_s)
        ext, wide = taps_ref.shape[0], breadth + 16
        normed = (y_two_ref[0, 1 : ext + 1] - stat_ref[2:3, :]) * stat_ref[3:4, :]
        feature, _ = silu_parts(normed * stat_ref[8:9, :] + stat_ref[9:10, :])
        column = lax.broadcasted_iota(jnp.int32, (wide, 128), 0)
        keep = jnp.where(column < 8, stat_ref[12:13, :], 1.0)
        keep = jnp.where(column >= 8 + breadth, stat_ref[13:14, :], keep)
        feat_s[0:PAD, :] = jnp.zeros((PAD, 128), F32)
        feat_s[PAD : PAD + ext * wide, :] = (feature * keep).reshape(ext * wide, 128)
        feat_s[PAD + ext * wide :, :] = jnp.zeros((PAD, 128), F32)
        for line, row in ((PAD, 10), (PAD + (ext - 1) * wide, 11)):
            feat_s[line : line + wide, :] = feat_s[line : line + wide, :] * stat_ref[row : row + 1]
        pairs = tap_pairs(feat_s, PAD, ext * wide, 1.0)
        taps_ref[...] = pairs.reshape(ext, wide, 256)[:, 8 : 8 + breadth].astype(BF16)
        for place, part in enumerate(three_parts(goal_ref[0])):
            goal_s[place] = part

    first = chunk * rows
    taps = jnp.concatenate(
        [taps_ref[pl.ds(first + tap, rows)].reshape(cells, 256) for tap in range(3)], axis=1
    )
    active, slope = [], []
    for block in range(3):
        weight = kernel_s[:, :, block * units : (block + 1) * units].reshape(768, units)
        hidden = dot(taps, weight)
        turn = jnp.tanh(hidden)
        above = 1.0 + turn
        product = hidden * above
        active.append(product.astype(BF16))
        slope.append(above + product * (1.0 - turn))

    logit = dot_keep(active[0], heat_w_ref[...]) + heat_b_ref[...]
    decay = jnp.exp(-jnp.abs(logit))
    large = 1.0 / (1.0 + decay)
    small = decay * large
    above = logit >= 0.0
    chance = jnp.where(above, large, small)
    heat_out[0] = chance.reshape(rows, breadth, 80)
    target = target_ref[0].reshape(cells, 80).astype(F32)
    positive = target == 1.0
    side = jnp.where(positive, jnp.where(above, small, large), chance)
    value = jnp.where(positive, -logit, logit)
    soft = jnp.maximum(value, 0.0) + jnp.log(1.0 + decay)
    slant = side * side * (2.0 * (1.0 - side) * soft + side)
    gap = 1.0 - target
    gap = gap * gap
    weighting = jnp.where(positive, -1.0, gap * gap) * stat_ref[4:5, 0:80]
    logit_grad = weighting * slant
    logit_low = logit_grad.astype(BF16)

    box_bias = jnp.concatenate([box_b_ref[0:1, :], box_b_ref[1:2, :]], axis=1)
    boxes = dot_keep(active[1], box_s[0]) + dot_keep(active[2], box_s[1]) + box_bias
    box_out[0] = jnp.swapaxes(boxes.reshape(rows, breadth, 4), 1, 2)
    shape = (rows, breadth, 128)
    cell = (first + lax.broadcasted_iota(jnp.int32, shape, 0)) * map_side
    cell = (cell + lax.broadcasted_iota(jnp.int32, shape, 1)).reshape(cells, 128)
    chosen = (cell == spot_ref[pl.ds(image, 1), :]).astype(F32).astype(BF16)
    twofold = jnp.concatenate([chosen, chosen], axis=1)
    goals = dot_keep(twofold, jnp.concatenate([goal_s[0], goal_s[1]], axis=1))
    ends = jnp.concatenate([goal_s[2].astype(F32), jnp.ones((4, 128), F32)], axis=0)
    both = dot_keep(chosen, ends.astype(BF16))
    goals, hit = goals + both[:, 0:4], both[:, 4:8]
    miss = boxes - goals
    lane = lax.broadcasted_iota(jnp.int32, (1, 4), 1)
    factor = jnp.where(lane < 2, 0.1, 1.0) * stat_ref[5:6, 0:4]
    box_grad = hit * factor * miss * lax.rsqrt(miss * miss + 1.0)
    box_low = box_grad.astype(BF16)

    heat_sum_s[...] += jnp.sum(logit_low.astype(F32).reshape(cells // 8, 8, 80), axis=0)
    box_sum_s[...] += jnp.sum(box_low.astype(F32).reshape(cells // 8, 8, 4), axis=0)
    heat_grad_s[...] += dot_left(logit_low, active[0])
    for part in range(2):
        box_grad_s[part] += dot_left(box_low, active[1 + part])

    back = [
        dot(logit_low, heat_w_ref[...]),
        dot(box_low, box_s[0]),
        dot(box_low, box_s[1]),
    ]
    grad_hidden = jnp.concatenate(
        [(back[block] * slope[block]).astype(BF16) for block in range(3)], axis=1
    )
    spread = []
    for tap in range(3):
        part = dot(grad_hidden, back_s[:, 256 * tap : 256 * tap + 256])
        spread.append(part.reshape(rows, breadth, 256))
    inner = slice(16, 16 + breadth)
    wide_s[pl.ds(first, 1), inner, :] += spread[0][0:1]
    wide_s[pl.ds(first + 1, 1), inner, :] += spread[0][1:2] + spread[1][0:1]
    wide_s[pl.ds(first + 2, rows - 2), inner, :] = (
        spread[0][2:] + spread[1][1:-1] + spread[2][:-2]
    )
    wide_s[pl.ds(first + rows, 1), inner, :] = spread[1][-1:] + spread[2][-2:-1]
    wide_s[pl.ds(first + rows + 1, 1), inner, :] = spread[2][-1:]
    for tap in range(3):
        grad_s[tap] += dot_left(taps[:, 256 * tap : 256 * tap + 256], grad_hidden)

    @pl.when(chunk == chunks - 1)
    def _():
        reach = breadth + 16
        centre = pltpu.roll(wide_s[:, 8 : 8 + reach, 0:128], 64, 2)
        total = wide_s[:, 9 : 9 + reach, 0:128] + centre + wide_s[:, 7 : 7 + reach, 128:256]
        lanes = lax.broadcasted_iota(jnp.int32, total.shape, 2)
        spread_out[0] = jnp.where(lanes < 64, total, pltpu.roll(total, 64, 2))

    @pl.when(jnp.logical_and(image == pl.num_programs(0) - 1, chunk == chunks - 1))
    def _():
        for column in range(6):
            span = slice(128 * column, 128 * column + 128)
            for tap in range(3):
                start = 36 * column + 12 * tap
                load_out[start : start + 12] = (
                    (0.5 * grad_s[tap, 0:192, span]).reshape(12, 16, 128).astype(BF16)
                )
            small_out[column : column + 1, :] = 0.5 * grad_s[1, 192:193, span]
        for half in range(2):
            span = slice(128 * half, 128 * half + 128)
            start = 216 + 5 * half
            load_out[start : start + 5] = heat_grad_s[:, span].reshape(5, 16, 128).astype(BF16)
            for part in range(2):
                padded = jnp.concatenate(
                    [box_grad_s[part, :, span], jnp.zeros((12, 128), F32)], axis=0
                )
                load_out[226 + 2 * part + half] = padded.astype(BF16)
        load_out[230:] = jnp.zeros((load_out.shape[0] - 230, 16, 128), BF16)
        small_out[6:8, :] = jnp.zeros((2, 128), F32)
        small_out[6:7, 0:80] = jnp.sum(heat_sum_s[...], axis=0, keepdims=True)
        small_out[7:8, 0:4] = jnp.sum(box_sum_s[...], axis=0, keepdims=True)


def heads(
    taps, target, spot, goal, stats, kernel, back, heat_w, heat_b, box_w, box_b, devices
):
    images, height, breadth, classes = target.shape
    rows = height
    chunks = height // rows
    tiles = tile_count(devices)
    whole = lambda *shape: pl.BlockSpec(shape, lambda b, c: (0,) * len(shape))
    cells = images * height * breadth
    return pl.pallas_call(
        functools.partial(heads_body, chunks, breadth * lax.axis_size("col")),
        grid=(images, chunks),
        in_specs=[
            pl.BlockSpec((1, height + 4, breadth + 16, 128), lambda b, c: (b, 0, 0, 0)),
            pl.BlockSpec((1, rows, breadth, classes), lambda b, c: (b, c, 0, 0)),
            whole(8, 128),
            pl.BlockSpec((1, 4, 128), lambda b, c: (b, 0, 0)),
            whole(24, 128),
            whole(3, 256, 768),
            whole(768, 768),
            whole(80, 256),
            whole(1, 80),
            whole(2, 2, 256),
            whole(2, 2),
        ],
        out_specs=[
            pl.BlockSpec((1, rows, breadth, classes), lambda b, c: (b, c, 0, 0)),
            pl.BlockSpec((1, rows, 4, breadth), lambda b, c: (b, c, 0, 0)),
            pl.BlockSpec((1, height + 2, breadth + 16, 128), lambda b, c: (b, 0, 0, 0)),
            whole(tiles, 16, 128),
            whole(8, 128),
        ],
        out_shape=[
            jax.ShapeDtypeStruct((images, height, breadth, classes), F32),
            jax.ShapeDtypeStruct((images, height, 4, breadth), F32),
            jax.ShapeDtypeStruct((images, height + 2, breadth + 16, 128), F32),
            jax.ShapeDtypeStruct((tiles, 16, 128), BF16),
            jax.ShapeDtypeStruct((8, 128), F32),
        ],
        scratch_shapes=[
            pltpu.VMEM((2 * PAD + (height + 2) * (breadth + 16), 128), F32),
            pltpu.VMEM((height + 2, breadth, 256), BF16),
            pltpu.VMEM((2, 4, 256), BF16),
            pltpu.VMEM((3, 4, 128), BF16),
            pltpu.VMEM((height + 2, breadth + 32, 256), F32),
            pltpu.VMEM((3, 256, 768), F32),
            pltpu.VMEM((80, 256), F32),
            pltpu.VMEM((2, 4, 256), F32),
            pltpu.VMEM((8, 80), F32),
            pltpu.VMEM((8, 4), F32),
        ],
        compiler_params=pltpu.CompilerParams(vmem_limit_bytes=60 * MIB),
        cost_estimate=pl.CostEstimate(
            flops=cells * 576 * 768 * 6, bytes_accessed=12 * MIB, transcendentals=cells * 768
        ),
        name="heads",
    )(taps, target, spot, goal, stats, kernel, back, heat_w, heat_b, box_w, box_b)


MESH = pl.DeviceIdType.MESH


def rounded_up(value, step):
    return -(-value // step) * step


def place():
    return lax.axis_index("batch"), lax.axis_index("row"), lax.axis_index("col")


def extents():
    return lax.axis_size("batch"), lax.axis_size("row"), lax.axis_size("col")


def plane_partners():
    batch, row, col = place()
    batches, _, cols = extents()
    partners = []
    for over in range(batches):
        for along in range(cols):
            if over or along:
                partners.append(
                    (lax.rem(batch + over, batches), row, lax.rem(col + along, cols))
                )
    return partners


def row_partners():
    batch, row, col = place()
    rows = lax.axis_size("row")
    return [(batch, lax.rem(row + over, rows), col) for over in range(1, rows)]


def flat():
    batches, rows, cols = extents()
    return batches * rows * cols <= 8


def all_partners():
    batch, row, col = place()
    batches, rows, cols = extents()
    partners = []
    for over in range(batches):
        for up in range(rows):
            for along in range(cols):
                if over or up or along:
                    partners.append(
                        (
                            lax.rem(batch + over, batches),
                            lax.rem(row + up, rows),
                            lax.rem(col + along, cols),
                        )
                    )
    return partners


def greet():
    barrier = pltpu.get_barrier_semaphore()
    partners = all_partners() if flat() else plane_partners() + row_partners()
    for partner in partners:
        pl.semaphore_signal(barrier, inc=1, device_id=partner, device_id_type=MESH)
    batch, row, col = place()
    _, rows, cols = extents()
    expected = len(partners)
    for up in (-1, 1):
        for along in (-1, 1):
            fits = jnp.logical_and(row + up >= 0, row + up < rows)
            fits = jnp.logical_and(fits, jnp.logical_and(col + along >= 0, col + along < cols))
            expected = expected + fits.astype(jnp.int32)

            @pl.when(fits)
            def _(up=up, along=along):
                pl.semaphore_signal(
                    barrier,
                    inc=1,
                    device_id=(batch, row + up, col + along),
                    device_id_type=MESH,
                )

    return expected


def greeted(expected):
    pl.semaphore_wait(pltpu.get_barrier_semaphore(), expected)


def remote(source, target, send, recv, device):
    return pltpu.make_async_remote_copy(
        src_ref=source,
        dst_ref=target,
        send_sem=send,
        recv_sem=recv,
        device_id=device,
        device_id_type=MESH,
    )


def start_all(copies):
    for copy in copies:
        copy.start()


def wait_all(copies):
    for copy in copies:
        copy.wait()


def slot_sum(slots):
    total = slots[0]
    for k in range(1, slots.shape[0]):
        total = total + slots[k]
    return total


class Total:
    def __init__(self, source, slots, mid, row_slots, sems):
        self.source, self.slots, self.mid = source, slots, mid
        self.row_slots, self.sems = row_slots, sems

    def send(self, source, slots, mine, partners, step):
        self.copies = [
            remote(
                source,
                slots.at[mine],
                self.sems.at[step, 0, k],
                self.sems.at[step, 1, k],
                partner,
            )
            for k, partner in enumerate(partners)
        ]
        start_all(self.copies)
        slots[mine] = source[...]

    def begin(self):
        batch, row, col = place()
        _, rows, cols = extents()
        if flat():
            mine, partners = (batch * rows + row) * cols + col, all_partners()
        else:
            mine, partners = batch * cols + col, plane_partners()
        self.send(self.source, self.slots, mine, partners, 0)

    def middle(self):
        if not flat():
            wait_all(self.copies)
            self.mid[...] = slot_sum(self.slots)
            self.send(self.mid, self.row_slots, place()[1], row_partners(), 1)

    def end(self):
        wait_all(self.copies)
        return slot_sum(self.slots if flat() else self.row_slots)


def total_scratch(lines):
    batches, rows, cols = extents()
    slots = batches * cols * (rows if flat() else 1)
    return [
        pltpu.VMEM((lines, 128), F32),
        pltpu.VMEM((slots, lines, 128), F32),
        pltpu.VMEM((lines, 128), F32),
        pltpu.VMEM((rows, lines, 128), F32),
        pltpu.SemaphoreType.DMA((2, 2, max(slots, rows) - 1)),
    ]


AROUND = ((-1, 0), (1, 0), (0, -1), (0, 1), (-1, -1), (-1, 1), (1, -1), (1, 1))


class Around:
    def __init__(self, pieces, slots, sems):
        batch, row, col = place()
        _, rows, cols = extents()

        def exists(up, along):
            fits = jnp.logical_and(row + up >= 0, row + up < rows)
            return jnp.logical_and(fits, jnp.logical_and(col + along >= 0, col + along < cols))

        self.sends = [exists(up, along) for up, along in AROUND]
        self.comes = [exists(-up, -along) for up, along in AROUND]
        self.copies = [
            remote(pieces[k], slots[k], sems.at[0, k], sems.at[1, k], (batch, row + up, col + along))
            for k, (up, along) in enumerate(AROUND)
        ]

    def start(self, which=range(8)):
        for k in which:
            pl.when(self.sends[k])(self.copies[k].start)

    def wait(self, which=range(8)):
        for k in which:
            pl.when(self.comes[k])(self.copies[k].wait_recv)
            pl.when(self.sends[k])(self.copies[k].wait_send)

    def each(self, use, which=range(8)):
        for k in which:
            pl.when(self.comes[k])(functools.partial(use, k))


def twice(values):
    return jnp.concatenate([values, values], axis=-1)


def lower_half(shape):
    return lax.broadcasted_iota(jnp.int32, shape, len(shape) - 1) < 64


def swapped(values):
    return pltpu.roll(values, 64, len(values.shape) - 1)


def widened(values):
    rows, cols = values.shape[0], values.shape[1]
    side = jnp.zeros((rows, 8, 128), F32)
    return jnp.concatenate([side, twice(values.astype(F32)), side], axis=1)


def tap_pairs(buffer, start, count, fill):
    low = lower_half((1, 128))
    first = jnp.where(low, buffer[pl.ds(start - 1, count), :], buffer[pl.ds(start, count), :])
    second = jnp.where(low, buffer[pl.ds(start + 1, count), :], fill)
    return jnp.concatenate([first, second], axis=1)


def silu_parts(values):
    logistic = 0.5 * jnp.tanh(0.5 * values) + 0.5
    return values * logistic, logistic


PAD = 16


def row_loop(total, step, body, init):
    return lax.fori_loop(0, total // step, lambda k, carry: body(k * step, carry), init)


def fold_sum(values):
    return jnp.sum(values.reshape(-1, 8, 128), axis=0)


def clear(buffer, start, rows, pitch, tops, bottoms, lefts, rights):
    _, row_at, col_at = place()
    count = rounded_up(rows, 8)

    def clear_rows(span):
        first, last = span
        size = (last - first) * pitch
        buffer[pl.ds(start + first * pitch, size), :] = jnp.zeros((size, 128), F32)

    def clear_columns(span):
        for column in range(*span):
            buffer[pl.ds(start + column, count, stride=pitch), :] = jnp.zeros((count, 128), F32)

    pl.when(row_at == 0)(lambda: clear_rows(tops))
    pl.when(row_at == lax.axis_size("row") - 1)(lambda: clear_rows(bottoms))
    pl.when(col_at == 0)(lambda: clear_columns(lefts))
    pl.when(col_at == lax.axis_size("col") - 1)(lambda: clear_columns(rights))


def stack_weight(target, source):
    for tap in range(3):
        target[256 * tap : 256 * tap + 192, :] = twice(source[tap].astype(F32)).astype(BF16)
        target[256 * tap + 192 : 256 * tap + 256, :] = jnp.zeros((64, 128), BF16)


def unpacked(packed, image, images):
    low = lower_half((1, 128))
    keep = low if image < images // 2 else jnp.logical_not(low)
    return jnp.where(keep, packed, swapped(packed))


def pack_columns(buffer, target, images, rows, pitch, first_row, first, depth):
    low = lower_half((1, 128))
    half = images // 2
    count = target.shape[1]
    for pair in range(half):
        for j in range(depth):
            parts = [
                buffer[
                    pl.ds(
                        PAD + (image * rows + first_row) * pitch + first + j, count, stride=pitch
                    ),
                    :,
                ]
                for image in (pair, pair + half)
            ]
            target[depth * pair + j] = jnp.where(low, parts[0], parts[1]).astype(target.dtype)


def pack_corner(buffer, target, images, rows, pitch, first_row, first, depth):
    low = lower_half((1, 128))
    half = images // 2
    count = target.shape[1] // 8
    for pair in range(half):
        pieces = []
        for row in range(count):
            if row < depth:
                starts = [
                    PAD + (image * rows + first_row + row) * pitch + first
                    for image in (pair, pair + half)
                ]
                pieces.append(
                    jnp.where(
                        low,
                        buffer[starts[0] : starts[0] + 8, :],
                        buffer[starts[1] : starts[1] + 8, :],
                    )
                )
            else:
                pieces.append(jnp.zeros((8, 128), F32))
        target[pair] = jnp.concatenate(pieces, axis=0).astype(target.dtype)


def unpack_columns(buffer, source, images, rows, pitch, first_row, first, depth, lines, add):
    half = images // 2
    count = rounded_up(lines, 8)
    valid = lax.broadcasted_iota(jnp.int32, (count, 128), 0) < lines
    for image in range(images):
        for j in range(depth):
            packed = source[depth * (image % half) + j].astype(F32)
            values = unpacked(packed, image, images)[:count]
            spots = pl.ds(
                PAD + (image * rows + first_row) * pitch + first + j, count, stride=pitch
            )
            if add:
                values = buffer[spots, :] + jnp.where(valid, values, 0.0)
            elif count > lines:
                values = jnp.where(valid, values, buffer[spots, :])
            buffer[spots, :] = values


def unpack_corner(buffer, source, images, rows, pitch, first_row, first, depth, add):
    half = images // 2
    valid = lax.broadcasted_iota(jnp.int32, (8, 128), 0) < depth
    for image in range(images):
        packed = unpacked(source[image % half].astype(F32), image, images)
        for row in range(depth):
            start = PAD + (image * rows + first_row + row) * pitch + first
            old = buffer[start : start + 8, :]
            values = packed[8 * row : 8 * row + 8]
            if add:
                values = old + jnp.where(valid, values, 0.0)
            else:
                values = jnp.where(valid, values, old)
            buffer[start : start + 8, :] = values


def rise_body(
    low_ref,
    skip_ref,
    target_ref,
    conv_one_ref,
    conv_two_ref,
    gain_one_ref,
    shift_one_ref,
    gain_two_ref,
    shift_two_ref,
    index_ref,
    head_ref,
    bias_ref,
    count_ref,
    y_two_out,
    y_one_out,
    merged_out,
    low_out,
    kernel_out,
    back_out,
    stat_out,
    spot_out,
    tiles_out,
    low_in,
    skip_in,
    target_in,
    conv_one_in,
    conv_two_in,
    param_in,
    index_in,
    head_in,
    bias_in,
    y_two_s,
    y_one_s,
    merged_s,
    low_s,
    kernel_s,
    back_s,
    low_x,
    skip_x,
    act_s,
    row_s,
    up_s,
    w_one,
    w_two,
    g_low,
    own_low,
    low_rows,
    skip_rows,
    low_send,
    low_recv,
    low_corner,
    skip_send,
    skip_recv,
    skip_corner,
    first_scratch,
    second_scratch,
    in_sems,
    out_sems,
    strip_sems,
):
    images, h, w, _ = low_ref.shape
    height, breadth = skip_ref.shape[1], skip_ref.shape[2]
    batch_at, row_at, col_at = place()
    batches, row_count, col_count = extents()
    pitch, wide = w + 16, breadth + 16
    low_r, y_one_r = h + 6, h + 4
    skip_r, y_two_r = height + 6, height + 4
    cells_low = float(images * batches * h * row_count * w * col_count)
    cells_high = 4.0 * cells_low

    loads = [
        pltpu.make_async_copy(source, target, in_sems.at[k])
        for k, (source, target) in enumerate(
            (
                (low_ref, low_in),
                (conv_one_ref, conv_one_in),
                (skip_ref, skip_in),
                (index_ref, index_in),
                (target_ref, target_in),
                (gain_one_ref, param_in.at[0]),
                (shift_one_ref, param_in.at[1]),
                (gain_two_ref, param_in.at[2]),
                (shift_two_ref, param_in.at[3]),
                (conv_two_ref, conv_two_in),
                (head_ref, head_in),
                (bias_ref, bias_in),
            )
        )
    ]
    expected = greet()
    for load in loads:
        load.start()
    low_around = Around(
        [low_ref.at[:, 0:3], low_ref.at[:, h - 3 : h]]
        + [low_send.at[k] for k in range(2)]
        + [low_corner.at[0, k] for k in range(4)],
        [low_rows.at[0], low_rows.at[1]]
        + [low_recv.at[k] for k in range(2)]
        + [low_corner.at[1, k] for k in range(4)],
        strip_sems.at[0],
    )
    skip_around = Around(
        [skip_ref.at[:, 0:3], skip_ref.at[:, height - 3 : height]]
        + [skip_send.at[k] for k in range(2)]
        + [skip_corner.at[0, k] for k in range(4)],
        [skip_rows.at[0], skip_rows.at[1]]
        + [skip_recv.at[k] for k in range(2)]
        + [skip_corner.at[1, k] for k in range(4)],
        strip_sems.at[1],
    )

    def place_low(b, carry):
        start = PAD + b * low_r * pitch
        low_x[pl.ds(start, 3 * pitch), :] = jnp.zeros((3 * pitch, 128), F32)
        low_x[pl.ds(start + 3 * pitch, h * pitch), :] = widened(low_in[b]).reshape(h * pitch, 128)
        low_x[pl.ds(start + (h + 3) * pitch, 3 * pitch), :] = jnp.zeros((3 * pitch, 128), F32)
        return carry

    low_x[0:PAD, :] = jnp.zeros((PAD, 128), F32)
    tail = low_x.shape[0] - PAD - images * low_r * pitch
    low_x[PAD + images * low_r * pitch :, :] = jnp.zeros((tail, 128), F32)
    loads[0].wait()
    lax.fori_loop(0, images, place_low, 0)

    def pack(buffer, sends, corners, rows, step, line, across):
        for side, first in enumerate((8, 5 + across)):
            pack_columns(buffer, sends.at[side], images, rows, line, 3, first, 3)
        for k, (up, along) in enumerate(AROUND[4:]):
            pack_corner(
                buffer,
                corners.at[0, k],
                images,
                rows,
                line,
                3 if up < 0 else step,
                8 if along < 0 else 5 + across,
                3,
            )

    def unpack(around, buffer, strips, columns, corners, rows, step, line, across):
        def use(k):
            up, along = AROUND[k]
            row = step + 3 if up < 0 else 0
            column = 8 + across if along < 0 else 5
            if k < 2:

                def body(b, carry):
                    start = PAD + (b * rows + row) * line
                    buffer[pl.ds(start, 3 * line), :] = widened(strips[k, b]).reshape(
                        3 * line, 128
                    )
                    return carry

                lax.fori_loop(0, images, body, 0)
            elif k < 4:
                unpack_columns(
                    buffer, columns.at[k - 2], images, rows, line, 3, column, 3, step, False
                )
            else:
                unpack_corner(
                    buffer, corners.at[1, k - 4], images, rows, line, row, column, 3, False
                )

        around.each(use)

    pack(low_x, low_send, low_corner, low_r, h, pitch, w)
    greeted(expected)
    low_around.start()
    skip_around.start(range(2))

    def place_skip(b, carry):
        start = PAD + b * skip_r * wide
        edge = jnp.zeros((3 * wide, 128), F32)
        skip_x[pl.ds(start, 3 * wide), :] = edge
        skip_x[pl.ds(start + 3 * wide, height * wide), :] = widened(skip_in[b]).reshape(
            height * wide, 128
        )
        skip_x[pl.ds(start + (height + 3) * wide, 3 * wide), :] = edge
        return carry

    skip_x[0:PAD, :] = jnp.zeros((PAD, 128), F32)
    skip_tail = skip_x.shape[0] - PAD - images * skip_r * wide
    skip_x[PAD + images * skip_r * wide :, :] = jnp.zeros((skip_tail, 128), F32)
    loads[2].wait()
    lax.fori_loop(0, images, place_skip, 0)
    pack(skip_x, skip_send, skip_corner, skip_r, height, wide, breadth)
    skip_around.start(range(2, 8))
    loads[1].wait()
    stack_weight(w_one, conv_one_in)
    low_around.wait()
    unpack(low_around, low_x, low_rows, low_recv, low_corner, low_r, h, pitch, w)

    def conv_one(b, sums):
        pairs = tap_pairs(low_x, PAD + b * low_r * pitch, low_r * pitch, 0.0)
        pairs = pairs.astype(BF16)
        count = y_one_r * pitch
        taps = jnp.concatenate([pairs[pitch * a : pitch * a + count] for a in range(3)], axis=1)
        value = dot(taps, w_one[...]).reshape(y_one_r, pitch, 128)
        y_one_s[b] = value
        own = value[2 : h + 2, 8 : 8 + w].reshape(h * w, 128)
        return (
            sums[0] + jnp.sum(own, axis=0, keepdims=True),
            sums[1] + jnp.sum(own * own, axis=0, keepdims=True),
        )

    def own_taps(b, sums):
        pairs = tap_pairs(low_x, PAD + (b * low_r + 2) * pitch, (h + 2) * pitch, 0.0)
        own = pairs.reshape(h + 2, pitch, 256)[:, 8 : 8 + w].astype(BF16)
        low_s[b] = own
        lines = jnp.sum(own.astype(F32), axis=1)
        return [
            sums[tap] + jnp.sum(lines[tap : tap + h], axis=0, keepdims=True) for tap in range(3)
        ]

    def count_ones(b, total):
        ones = (target_in[b].reshape(height * breadth, 80).astype(F32) == 1.0).astype(F32)
        return total + jnp.sum(ones, axis=0, keepdims=True)

    nothing = jnp.zeros((1, 128), F32)
    sums = lax.fori_loop(0, images, conv_one, (nothing, nothing))
    sum_src = first_scratch[0]
    sum_src[...] = jnp.zeros((8, 128), F32)
    sum_src[0:1, :] = sums[0]
    sum_src[1:2, :] = sums[1]
    first_total = Total(*first_scratch)
    first_total.begin()
    stores = [
        pltpu.make_async_copy(y_one_s, y_one_out, out_sems.at[0, 0]),
        pltpu.make_async_copy(low_s, low_out, out_sems.at[0, 1]),
    ]
    stores[0].start()

    loads[9].wait()
    stack_weight(w_two, conv_two_in)
    skip_around.wait()
    unpack(
        skip_around, skip_x, skip_rows, skip_recv, skip_corner, skip_r, height, wide, breadth
    )
    first_total.middle()
    for k in (3, 4):
        loads[k].wait()
    ones = lax.fori_loop(0, images, count_ones, jnp.zeros((1, 80), F32))
    base = row_at * (height * breadth * col_count) + col_at * breadth
    slot = lax.broadcasted_iota(jnp.int32, (1, 128), 1)
    objects = 0
    spot_out[...] = jnp.full((8, 128), -(2**30), jnp.int32)
    for b in range(images):
        amount = count_ref[b]
        objects = objects + amount
        spot_out[b : b + 1, :] = jnp.where(
            slot < amount, index_in[b : b + 1, :] - base, -(2**30)
        )
    leading = jnp.logical_and(row_at == 0, col_at == 0).astype(F32)
    tap_none = jnp.zeros((1, 256), F32)
    tap_sums = lax.fori_loop(0, images, own_taps, [tap_none] * 3)
    stores[1].start()
    for k in range(5, 9):
        loads[k].wait()
    totals = first_total.end()
    mean_one = totals[0:1] / cells_low
    scale_one = lax.rsqrt(totals[1:2] / cells_low - mean_one * mean_one + EPSILON)
    gain_one, shift_one = twice(param_in[0]), twice(param_in[1])
    gain_two, shift_two = twice(param_in[2]), twice(param_in[3])
    stat_out[...] = jnp.zeros((24, 128), F32)
    stat_out[0:1, :] = mean_one
    stat_out[1:2, :] = scale_one
    stat_out[6:7, :] = gain_one
    stat_out[7:8, :] = shift_one
    stat_out[8:9, :] = gain_two
    stat_out[9:10, :] = shift_two
    ends = (row_at > 0, row_at < row_count - 1, col_at > 0, col_at < col_count - 1)
    for k, inner in enumerate(ends):
        stat_out[10 + k : 11 + k, :] = jnp.full((1, 128), inner.astype(F32))

    def conv_two(b, sums):
        normed = (y_one_s[b] - mean_one) * scale_one
        value, _ = silu_parts(normed * gain_one + shift_one)
        act_s[0 : y_one_r * pitch, :] = value.astype(BF16).astype(F32).reshape(
            y_one_r * pitch, 128
        )
        clear(
            act_s, 0, y_one_r, pitch, (0, 2), (h + 2, h + 4), (6, 8), (8 + w, 10 + w)
        )
        act = act_s[0 : y_one_r * pitch, :].reshape(y_one_r, pitch, 128)
        odd = 0.75 * act[:-1] + 0.25 * act[1:]
        even = 0.75 * act[1:] + 0.25 * act[:-1]
        tall = jnp.stack([odd, even], axis=1).reshape(skip_r * pitch, 128)
        row_s[PAD : PAD + skip_r * pitch, :] = tall
        count = skip_r * pitch
        before = row_s[PAD - 1 : PAD - 1 + count, :]
        behind = row_s[PAD + 1 : PAD + 1 + count, :]
        up_s[pl.ds(0, count, stride=2), :] = 0.75 * tall + 0.25 * before
        up_s[pl.ds(1, count, stride=2), :] = 0.75 * tall + 0.25 * behind
        start = PAD + b * skip_r * wide
        whole = pl.ds(start, skip_r * wide)
        up = up_s[...].reshape(skip_r, 2 * pitch, 128)[:, 8 : 8 + wide]
        merged = up + skip_x[whole, :].reshape(skip_r, wide, 128)
        skip_x[whole, :] = merged.astype(BF16).astype(F32).reshape(skip_r * wide, 128)
        clear(
            skip_x,
            start,
            skip_r,
            wide,
            (0, 3),
            (height + 3, height + 6),
            (5, 8),
            (8 + breadth, 11 + breadth),
        )
        pairs = tap_pairs(skip_x, start, skip_r * wide, 0.0)
        merged_s[b] = pairs.reshape(skip_r, wide, 256)[2 : height + 4, 8 : 8 + breadth].astype(
            BF16
        )
        pltpu.make_async_copy(merged_s.at[b], merged_out.at[b], out_sems.at[1, b]).start()
        pairs = pairs.astype(BF16)
        count = y_two_r * wide
        taps = jnp.concatenate([pairs[wide * a : wide * a + count] for a in range(3)], axis=1)
        value = dot(taps, w_two[...]).reshape(y_two_r, wide, 128)
        y_two_s[b] = value
        pltpu.make_async_copy(y_two_s.at[b], y_two_out.at[b], out_sems.at[2, b]).start()
        own = value[2 : height + 2, 8 : 8 + breadth].reshape(height * breadth, 128)
        return (
            sums[0] + jnp.sum(own, axis=0, keepdims=True),
            sums[1] + jnp.sum(own * own, axis=0, keepdims=True),
        )

    row_s[0:PAD, :] = jnp.zeros((PAD, 128), F32)
    row_s[PAD + skip_r * pitch :, :] = jnp.zeros((PAD, 128), F32)
    sums = lax.fori_loop(0, images, conv_two, (nothing, nothing))
    sum_src = second_scratch[0]
    sum_src[...] = jnp.zeros((16, 128), F32)
    sum_src[8:9, 0:80] = ones
    sum_src[9:10, :] = jnp.full((1, 128), objects.astype(F32) * leading)
    sum_src[0:1, :] = sums[0]
    sum_src[1:2, :] = sums[1]
    for tap in range(3):
        for part in range(2):
            line = 2 + 2 * tap + part
            sum_src[line : line + 1, :] = tap_sums[tap][:, 128 * part : 128 * part + 128]
    second_total = Total(*second_scratch)
    second_total.begin()
    g_low[...] = jnp.zeros_like(g_low)
    own_low[...] = jnp.zeros_like(own_low)

    def normed_taps(b, carry):
        normed = (y_one_s[b, 2 : h + 2] - mean_one) * scale_one
        own_low[2 * w : (h + 2) * w, :] = normed[:, 8 : 8 + w].reshape(h * w, 128)
        g_low[...] += product_of_parts(
            low_s[b].reshape((h + 2) * w, 256), shifted_taps(own_low, h, w)
        )
        return carry

    lax.fori_loop(0, images, normed_taps, 0)
    tiles_out[36:] = jnp.zeros((tiles_out.shape[0] - 36, 8, 128), F32)
    fold(tiles_out, 0, g_low)
    second_total.middle()
    for k in (10, 11):
        loads[k].wait()
    for tap in range(3):
        kernel_s[tap, 0:192, :] = (0.5 * head_in[tap].astype(F32)).astype(BF16)
        kernel_s[tap, 192:256, :] = jnp.zeros((64, 768), BF16)
    parts = three_parts(0.5 * bias_in[...].reshape(1, 768))
    which = lax.broadcasted_iota(jnp.int32, (16, 768), 0)
    filled = jnp.zeros((16, 768), F32)
    for place_at in range(3):
        filled = jnp.where(which == place_at, parts[place_at].astype(F32), filled)
    kernel_s[1, 192:208, :] = filled.astype(BF16)
    for tap in range(3):
        for block in range(3):
            span = slice(256 * block, 256 * block + 256)
            back_s[span, 256 * tap : 256 * tap + 256] = (
                kernel_s[tap, :, span].astype(F32).T.astype(BF16)
            )
    stores += [
        pltpu.make_async_copy(kernel_s, kernel_out, out_sems.at[0, 2]),
        pltpu.make_async_copy(back_s, back_out, out_sems.at[0, 3]),
    ]
    for store in stores[2:]:
        store.start()
    totals = second_total.end()
    mean_two = totals[0:1] / cells_high
    scale_two = lax.rsqrt(totals[1:2] / cells_high - mean_two * mean_two + EPSILON)
    stat_out[2:3, :] = mean_two
    stat_out[3:4, :] = scale_two
    stat_out[16:22, :] = totals[2:8]
    positives = jnp.sum(totals[8:9, 0:80], axis=1, keepdims=True)
    stat_out[4:5, :] = jnp.broadcast_to(1.0 / positives, (1, 128))
    stat_out[5:6, :] = 0.5 / totals[9:10]

    for store in stores:
        store.wait()
    for b in range(images):
        pltpu.make_async_copy(merged_s.at[b], merged_out.at[b], out_sems.at[1, b]).wait()
        pltpu.make_async_copy(y_two_s.at[b], y_two_out.at[b], out_sems.at[2, b]).wait()


def rise(
    low_map,
    skip_map,
    target,
    conv_one,
    conv_two,
    gain_one,
    shift_one,
    gain_two,
    shift_two,
    index,
    head,
    bias,
    count,
):
    images, h, w, _ = low_map.shape
    _, height, breadth, _ = skip_map.shape
    pitch, wide = w + 16, breadth + 16
    low_r, skip_r = h + 6, height + 6
    half = images // 2
    vmem = pl.BlockSpec(memory_space=pltpu.VMEM)
    hbm = pl.BlockSpec(memory_space=pl.ANY)
    kept = [
        jax.ShapeDtypeStruct((images, height + 4, wide, 128), F32),
        jax.ShapeDtypeStruct((images, h + 4, pitch, 128), F32),
        jax.ShapeDtypeStruct((images, height + 2, breadth, 256), BF16),
        jax.ShapeDtypeStruct((images, h + 2, w, 256), BF16),
        jax.ShapeDtypeStruct((3, 256, 768), BF16),
        jax.ShapeDtypeStruct((768, 768), BF16),
    ]
    return pl.pallas_call(
        rise_body,
        in_specs=[hbm] * 12 + [pl.BlockSpec(memory_space=pltpu.SMEM)],
        out_specs=[hbm] * 6 + [vmem] * 3,
        out_shape=kept
        + [jax.ShapeDtypeStruct((24, 128), F32), jax.ShapeDtypeStruct((8, 128), jnp.int32)]
        + [jax.ShapeDtypeStruct((conv_tiles(36), 8, 128), F32)],
        scratch_shapes=[
            pltpu.VMEM(low_map.shape, BF16),
            pltpu.VMEM(skip_map.shape, BF16),
            pltpu.VMEM(target.shape, BF16),
            pltpu.VMEM((3, 192, 64), BF16),
            pltpu.VMEM((3, 192, 64), BF16),
            pltpu.VMEM((4, 1, 64), F32),
            pltpu.VMEM(index.shape, jnp.int32),
            pltpu.VMEM((3, 192, 768), BF16),
            pltpu.VMEM((768,), F32),
        ]
        + [pltpu.VMEM(array.shape, array.dtype) for array in kept]
        + [
            pltpu.VMEM((2 * PAD + (images * low_r + 8) * pitch, 128), F32),
            pltpu.VMEM((2 * PAD + (images * skip_r + 8) * wide, 128), F32),
            pltpu.VMEM((rounded_up(h + 4, 8) * pitch, 128), F32),
            pltpu.VMEM((2 * PAD + skip_r * pitch, 128), F32),
            pltpu.VMEM((2 * skip_r * pitch, 128), F32),
            pltpu.VMEM((768, 128), BF16),
            pltpu.VMEM((768, 128), BF16),
            pltpu.VMEM((256, 256), F32),
            pltpu.VMEM(((h + 4) * w, 128), F32),
            pltpu.VMEM((2, images, 3, w, 64), BF16),
            pltpu.VMEM((2, images, 3, breadth, 64), BF16),
            pltpu.VMEM((2, 3 * half, rounded_up(h, 16), 128), BF16),
            pltpu.VMEM((2, 3 * half, rounded_up(h, 16), 128), BF16),
            pltpu.VMEM((2, 4, half, 32, 128), BF16),
            pltpu.VMEM((2, 3 * half, rounded_up(height, 16), 128), BF16),
            pltpu.VMEM((2, 3 * half, rounded_up(height, 16), 128), BF16),
            pltpu.VMEM((2, 4, half, 32, 128), BF16),
            total_scratch(8),
            total_scratch(16),
            pltpu.SemaphoreType.DMA((12,)),
            pltpu.SemaphoreType.DMA((4, max(images, 4))),
            pltpu.SemaphoreType.DMA((2, 2, 8)),
        ],
        compiler_params=pltpu.CompilerParams(
            collective_id=1, has_side_effects=True, vmem_limit_bytes=60 * MIB
        ),
        name="rise",
    )(
        low_map,
        skip_map,
        target,
        conv_one,
        conv_two,
        gain_one,
        shift_one,
        gain_two,
        shift_two,
        index,
        head,
        bias,
        count,
    )


def levels_of(tiles):
    batch, row, col = place()
    batches, rows, cols = extents()
    pairs = 2 if cols % 2 == 0 else 1
    outer = cols // pairs
    levels = []

    def add(count, mine, device_of):
        left = (levels[-1][3] if levels else tiles) // count
        partners = []
        for over in range(1, count):
            other = lax.rem(mine + over, count)
            partners.append((other, device_of(other)))
        levels.append((count, mine, partners, left))

    low = lax.rem(col, pairs)
    add(pairs, low, lambda k: (batch, row, col - low + k))
    add(
        outer * batches,
        lax.div(col, pairs) * batches + batch,
        lambda k: (lax.rem(k, batches), row, lax.div(k, batches) * pairs + low),
    )
    add(rows, row, lambda k: (batch, k, col))
    return levels


def level_sizes(tiles):
    batches, rows, cols = extents()
    pairs = 2 if cols % 2 == 0 else 1
    sizes = []
    for count in (pairs, cols // pairs * batches, rows):
        tiles = tiles // count
        sizes.append((count, tiles))
    return sizes


class Scatter:
    def __init__(self, source, mids, slots, sems):
        self.parts = [source, *mids]
        self.slots, self.sems = slots, sems
        self.levels = levels_of(source.shape[0])

    def begin(self, level):
        _, _, partners, left = self.levels[level]
        self.copies = [
            remote(
                self.parts[level].at[pl.ds(other * left, left)],
                self.slots[level].at[k],
                self.sems.at[level, 0, k],
                self.sems.at[level, 1, k],
                device,
            )
            for k, (other, device) in enumerate(partners)
        ]
        start_all(self.copies)

    def end(self, level):
        _, mine, partners, left = self.levels[level]
        wait_all(self.copies)
        total = self.parts[level][pl.ds(mine * left, left)].astype(F32)
        for k in range(len(partners)):
            total = total + self.slots[level][k].astype(F32)
        self.parts[level + 1][...] = total.astype(BF16)


class Gather:
    def __init__(self, full, sems):
        self.full, self.sems = full, sems
        self.levels = levels_of(full.shape[0])

    def span(self, level):
        base = 0
        for _, mine, _, left in self.levels[: level + 1]:
            base = base + mine * left
        return pl.ds(base, self.levels[level][3])

    def begin(self, level):
        part = self.full.at[self.span(level)]
        self.copies = [
            remote(part, part, self.sems.at[level, 0, k], self.sems.at[level, 1, k], device)
            for k, (_, device) in enumerate(self.levels[level][2])
        ]
        start_all(self.copies)

    def end(self):
        wait_all(self.copies)


def scatter_scratch(tiles):
    sizes = level_sizes(tiles)
    return (
        tuple(pltpu.VMEM((left, 16, 128), BF16) for _, left in sizes[:-1]),
        tuple(pltpu.VMEM((count - 1, left, 16, 128), BF16) for count, left in sizes),
        level_sems(),
    )


def level_sems():
    return pltpu.SemaphoreType.DMA((3, 2, max(count for count, _ in level_sizes(1)) - 1))


class PlaneReducer:
    def __init__(self, source, slots, mid, row_slots, full, sems):
        batch, row, col = place()
        batches, rows, cols = extents()
        self.source, self.slots, self.mid = source, slots, mid
        self.row_slots, self.full, self.sems = row_slots, full, sems
        self.share = mid.shape[0]
        self.mine = batch * cols + col
        self.row = row

    def begin(self):
        _, _, cols = extents()
        self.copies = []
        for k, (batch, row, col) in enumerate(plane_partners()):
            other = batch * cols + col
            part = self.source.at[pl.ds(other * self.share, self.share)]
            self.copies.append(
                remote(
                    part, self.slots.at[k], self.sems.at[0, 0, k], self.sems.at[0, 1, k],
                    (batch, row, col),
                )
            )
        start_all(self.copies)

    def middle(self):
        wait_all(self.copies)
        total = self.source[pl.ds(self.mine * self.share, self.share)]
        for k in range(self.slots.shape[0]):
            total = total + self.slots[k]
        self.mid[...] = total
        self.copies = [
            remote(
                self.mid, self.row_slots.at[self.row], self.sems.at[1, 0, k],
                self.sems.at[1, 1, k], partner,
            )
            for k, partner in enumerate(row_partners())
        ]
        start_all(self.copies)
        self.row_slots[self.row] = total

    def last(self):
        wait_all(self.copies)
        self.full[pl.ds(self.mine * self.share, self.share)] = slot_sum(self.row_slots)
        part = self.full.at[pl.ds(self.mine * self.share, self.share)]
        self.copies = [
            remote(part, part, self.sems.at[2, 0, k], self.sems.at[2, 1, k], partner)
            for k, partner in enumerate(plane_partners())
        ]
        start_all(self.copies)

    def end(self):
        wait_all(self.copies)


def plane_scratch(tiles):
    batches, rows, cols = extents()
    planes = batches * cols
    share = tiles // planes
    most = max(planes, rows) - 1
    return [
        pltpu.VMEM((tiles, 8, 128), F32),
        pltpu.VMEM((planes - 1, share, 8, 128), F32),
        pltpu.VMEM((share, 8, 128), F32),
        pltpu.VMEM((rows, share, 8, 128), F32),
        pltpu.SemaphoreType.DMA((3, 2, most)),
    ]


def conv_tiles(tiles):
    batches, _, cols = extents()
    planes = batches * cols
    return -(-tiles // planes) * planes


def fold(target, first, grads):
    low = lower_half((1, 128))
    last = grads[0:192, 128:256]
    target[first : first + 24] = grads[0:192, 0:128].reshape(24, 8, 128)
    target[first + 24 : first + 36] = jnp.where(low, last[0:96], swapped(last[96:192])).reshape(
        12, 8, 128
    )


def unfold(source, first):
    pairs = source[first : first + 24].reshape(192, 128)
    last = source[first + 24 : first + 36].reshape(96, 128)
    return [
        pairs[:, 0:64],
        swapped(pairs)[:, 0:64],
        jnp.concatenate([last[:, 0:64], swapped(last)[:, 0:64]], axis=0),
    ]


def shifted_taps(buffer, rows, line):
    count = (rows + 2) * line
    views = [buffer[(2 - tap) * line : (2 - tap) * line + count, :] for tap in range(3)]
    low = lower_half((1, 128))
    return jnp.concatenate(
        [jnp.where(low, views[0], views[1]), jnp.where(low, views[2], 0.0)], axis=1
    )


def product_of_parts(left, right):
    high = right.astype(BF16)
    rest = (right - high.astype(F32)).astype(BF16)
    return dot_left(left, high) + dot_left(left, rest)


def stack_back(target, source):
    for tap in range(3):
        for e in range(3):
            block = source[tap, 64 * e : 64 * e + 64, :].astype(F32)
            start = 256 * tap + 64 * e
            target[start : start + 64, :] = twice(block.T).astype(BF16)
        target[256 * tap + 192 : 256 * tap + 256, :] = jnp.zeros((64, 128), BF16)


def back_pairs(buffer, start, count):
    low = lower_half((1, 128))
    first = jnp.where(low, buffer[pl.ds(start + 1, count), :], buffer[pl.ds(start, count), :])
    second = jnp.where(low, buffer[pl.ds(start - 1, count), :], 0.0)
    return jnp.concatenate([first, second], axis=1).astype(BF16)


def slope_of(values):
    logistic = 0.5 * jnp.tanh(0.5 * values) + 0.5
    return logistic * (1.0 + values * (1.0 - logistic))


def fall_body(
    spread_ref,
    y_two_ref,
    stat_ref,
    load_ref,
    small_ref,
    tiles_ref,
    y_one_ref,
    merged_ref,
    low_ref,
    conv_ref,
    conv_one_ref,
    skip_out,
    zed_out,
    load_out,
    conv_out,
    conv_x_out,
    sums_out,
    last_out,
    weight_out,
    y_two_s,
    slope_s,
    y_one_s,
    merged_s,
    low_s,
    conv_s,
    load_s,
    skip_s,
    share_s,
    grad_x,
    zed_x,
    own_s,
    own_low_s,
    pair_s,
    narrow_s,
    w_two,
    g_two,
    g_one,
    total_s,
    strip_send,
    strip_recv,
    side_send,
    side_recv,
    corners,
    zed_send,
    zed_recv,
    edge_send,
    edge_recv,
    zed_corners,
    third_scratch,
    fourth_scratch,
    load_scratch,
    conv_x_scratch,
    conv_scratch,
    gather_sems,
    in_sems,
    map_sems,
    out_sems,
    strip_sems,
    zed_sems,
):
    images, rows, wide, _ = y_two_ref.shape
    height, breadth = rows - 4, wide - 16
    h, w = height // 2, breadth // 2
    pitch, ext = w + 16, height + 2
    zed_rows = h + 2
    half = images // 2
    _, row_at, col_at = place()
    batches, row_count, col_count = extents()
    cells_high = float(images * batches * height * row_count * breadth * col_count)
    low_half = lower_half((1, 128))
    mean_one, scale_one = stat_ref[0:1, :], stat_ref[1:2, :]
    mean_two, scale_two = stat_ref[2:3, :], stat_ref[3:4, :]
    gain_one, shift_one = stat_ref[6:7, :], stat_ref[7:8, :]
    gain_two, shift_two = stat_ref[8:9, :], stat_ref[9:10, :]
    top, bottom = stat_ref[10:11, :], stat_ref[11:12, :]
    left, right = stat_ref[12:13, :], stat_ref[13:14, :]

    def spread_load(b):
        start = PAD + (b * rows + 1) * wide
        return pltpu.make_async_copy(
            spread_ref.at[b], grad_x.at[pl.ds(start, ext * wide)], map_sems.at[0, b]
        )

    def y_two_load(b):
        return pltpu.make_async_copy(y_two_ref.at[b], y_two_s.at[b], map_sems.at[1, b])

    loads = [
        pltpu.make_async_copy(source, target, in_sems.at[k])
        for k, (source, target) in enumerate(
            (
                (load_ref, load_s),
                (tiles_ref, conv_x_scratch[0]),
                (conv_ref, conv_s.at[0]),
                (conv_one_ref, conv_s.at[1]),
                (merged_ref, merged_s),
                (y_one_ref, y_one_s),
                (low_ref, low_s),
            )
        )
    ]
    for b in range(images):
        spread_load(b).start()
    for b in range(images):
        y_two_load(b).start()
    for load in loads:
        load.start()
    grad_x[0:PAD, :] = jnp.zeros((PAD, 128), F32)
    tail = PAD + images * rows * wide
    grad_x[tail:, :] = jnp.zeros((grad_x.shape[0] - tail, 128), F32)
    for b in range(images):
        for line in (0, ext + 1):
            start = PAD + (b * rows + line) * wide
            grad_x[start : start + wide, :] = jnp.zeros((wide, 128), F32)
    greeted(greet())
    for b in range(images):
        spread_load(b).wait()
    for pair in range(half):
        for side, first in enumerate((1, ext - 2)):
            parts = []
            for image in (pair, pair + half):
                start = PAD + (image * rows + first) * wide
                parts.append(grad_x[start : start + 3 * wide, :])
            strip_send[side, pair] = jnp.where(low_half, parts[0], parts[1]).astype(BF16)
    around = Around(
        [strip_send.at[k] for k in range(2)]
        + [side_send.at[k] for k in range(2)]
        + [corners.at[0, k] for k in range(4)],
        [strip_recv.at[k] for k in range(2)]
        + [side_recv.at[k] for k in range(2)]
        + [corners.at[1, k] for k in range(4)],
        strip_sems,
    )
    around.start(range(2))
    for side, first in enumerate((7, 6 + breadth)):
        pack_columns(grad_x, side_send.at[side], images, rows, wide, 1, first, 3)
    for k, (up, along) in enumerate(AROUND[4:]):
        pack_corner(
            grad_x,
            corners.at[0, k],
            images,
            rows,
            wide,
            1 if up < 0 else height,
            7 if along < 0 else 6 + breadth,
            3,
        )
    around.start(range(2, 8))
    loads[0].wait()
    load_sum = Scatter(load_s, (*load_scratch[0], share_s), load_scratch[1], load_scratch[2])
    load_sum.begin(0)

    def begin(b, sums):
        y_two_load(b).wait()
        start = PAD + b * rows * wide
        clear(
            grad_x,
            start,
            rows,
            wide,
            (1, 2),
            (ext, ext + 1),
            (7, 8),
            (8 + breadth, 9 + breadth),
        )
        normed = (y_two_s[b] - mean_two) * scale_two
        slope = slope_of(normed * gain_two + shift_two)
        slope_s[b] = slope
        part = grad_x[pl.ds(start, rows * wide), :].reshape(rows, wide, 128)
        weighted = part * slope
        return sums[0] + fold_sum(weighted), sums[1] + fold_sum(weighted * normed)

    nothing = jnp.zeros((8, 128), F32)
    sums = lax.fori_loop(0, images, begin, (nothing, nothing))
    sum_src = third_scratch[0]
    sum_src[...] = jnp.zeros((16, 128), F32)
    sum_src[0:8, :] = small_ref[...]
    sum_src[8:9, :] = jnp.sum(sums[0], axis=0, keepdims=True)
    sum_src[9:10, :] = jnp.sum(sums[1], axis=0, keepdims=True)
    third_total = Total(*third_scratch)
    third_total.begin()
    load_sum.end(0)
    load_sum.begin(1)
    loads[2].wait()
    stack_back(w_two, conv_s.at[0])
    loads[3].wait()
    stack_back(weight_out, conv_s.at[1])
    g_two[...] = jnp.zeros_like(g_two)
    g_one[...] = jnp.zeros_like(g_one)
    own_s[...] = jnp.zeros_like(own_s)
    own_low_s[...] = jnp.zeros_like(own_low_s)
    narrow_s[...] = jnp.zeros_like(narrow_s)
    zed_x[...] = jnp.zeros_like(zed_x)
    third_total.middle()
    around.wait()

    def use(k):
        up, along = AROUND[k]
        row = height + 1 if up < 0 else 0
        column = 7 + breadth if along < 0 else 6
        if k < 2:
            for image in range(images):
                values = unpacked(strip_recv[k, image % half].astype(F32), image, images)
                start = PAD + (image * rows + row) * wide
                grad_x[start : start + 3 * wide, :] += values
        elif k < 4:
            unpack_columns(
                grad_x, side_recv.at[k - 2], images, rows, wide, 1, column, 3, ext, True
            )
        else:
            unpack_corner(
                grad_x, corners.at[1, k - 4], images, rows, wide, row, column, 3, True
            )

    around.each(use)

    loads[1].wait()
    conv_x_sum = PlaneReducer(*conv_x_scratch[:4], conv_x_out, conv_x_scratch[4])
    totals = third_total.end()
    sums_out[...] = totals
    conv_x_sum.begin()
    load_sum.end(1)
    load_sum.begin(2)
    factor_two = gain_two * scale_two
    shift_part, gain_part = totals[8:9] / cells_high, totals[9:10] / cells_high
    for k in (4, 5, 6):
        loads[k].wait()
    column = lax.broadcasted_iota(jnp.int32, (wide, 128), 0)
    keep = jnp.where(column < 8, left, 1.0)
    keep = jnp.where(column >= 8 + breadth, right, keep)

    def merge(b, sums):
        start = PAD + b * rows * wide
        whole = pl.ds(start, rows * wide)
        normed = (y_two_s[b] - mean_two) * scale_two
        grad_z = grad_x[whole, :].reshape(rows, wide, 128) * slope_s[b]
        grad_y = factor_two * (grad_z - shift_part - normed * gain_part)
        grad_y = (grad_y * keep).astype(BF16).astype(F32)
        grad_x[whole, :] = grad_y.reshape(rows * wide, 128)
        for line, flag in ((0, top), (ext, bottom)):
            span = pl.ds(start + line * wide, 2 * wide)
            grad_x[span, :] = grad_x[span, :] * flag
        own_s[2 * breadth : (height + 2) * breadth, :] = grad_y[
            2 : height + 2, 8 : 8 + breadth
        ].reshape(height * breadth, 128)
        source = merged_s[b].reshape(ext * breadth, 256)
        g_two[...] += dot_left(source, shifted_taps(own_s, height, breadth).astype(BF16))
        pair_s[...] = back_pairs(grad_x, start, rows * wide)
        count = ext * wide
        taps = jnp.concatenate(
            [pair_s[wide * (2 - a) : wide * (2 - a) + count, :] for a in range(3)], axis=1
        )
        merged_grad = dot(taps, w_two[...]).reshape(ext, wide, 128)
        skip_s[b] = merged_grad[1 : height + 1, 8 : 8 + breadth, 0:64]
        pltpu.make_async_copy(skip_s.at[b], skip_out.at[b], out_sems.at[0, b]).start()
        fine = (merged_grad * keep).astype(BF16).astype(F32).reshape(h + 1, 2, wide, 128)
        even, odd = fine[:, 0], fine[:, 1]
        even = jnp.concatenate([even[0:1] * top, even[1:]], axis=0)
        odd = jnp.concatenate([odd[:-1], odd[-1:] * bottom], axis=0)
        short = 0.75 * (odd[:-1] + even[1:]) + 0.25 * (even[:-1] + odd[1:])
        side = jnp.zeros((h, 8, 128), F32)
        count = h * 2 * pitch
        narrow_s[PAD : PAD + count, :] = jnp.concatenate([side, short, side], axis=1).reshape(
            count, 128
        )
        lines = [narrow_s[pl.ds(PAD + k, count // 2, stride=2), :] for k in (-1, 0, 1, 2)]
        act_grad = 0.75 * (lines[1] + lines[2]) + 0.25 * (lines[0] + lines[3])
        act_grad = act_grad.reshape(h, pitch, 128)
        normed = (y_one_s[b, 2 : h + 2] - mean_one) * scale_one
        slope = slope_of(normed * gain_one + shift_one)
        place_at = lax.broadcasted_iota(jnp.int32, (pitch, 128), 0)
        inner = jnp.logical_and(place_at >= 8, place_at < 8 + w)
        grad_z = jnp.where(inner, act_grad * slope, 0.0)
        spot = PAD + (b * zed_rows + 1) * pitch
        zed_x[pl.ds(spot, h * pitch), :] = grad_z.reshape(h * pitch, 128)
        own_low_s[2 * w : (h + 2) * w, :] = grad_z[:, 8 : 8 + w].reshape(h * w, 128)
        g_one[...] += product_of_parts(
            low_s[b].reshape((h + 2) * w, 256), shifted_taps(own_low_s, h, w)
        )
        return sums[0] + fold_sum(grad_z), sums[1] + fold_sum(grad_z * normed)

    sums = lax.fori_loop(0, half, merge, (nothing, nothing))
    gather = Gather(load_out, gather_sems)
    load_sum.end(2)
    load_out[gather.span(2)] = share_s[...]
    gather.begin(2)
    conv_x_sum.middle()
    sums = lax.fori_loop(half, images, merge, sums)
    last_src = fourth_scratch[0]
    last_src[...] = jnp.zeros((8, 128), F32)
    last_src[0:1, :] = jnp.sum(sums[0], axis=0, keepdims=True)
    last_src[1:2, :] = jnp.sum(sums[1], axis=0, keepdims=True)
    fourth_total = Total(*fourth_scratch)
    fourth_total.begin()
    gather.end()
    gather.begin(1)
    fold(conv_scratch[0], 0, g_two)
    fold(conv_scratch[0], 36, g_one)
    if conv_out.shape[0] > 72:
        conv_scratch[0][72:] = jnp.zeros((conv_out.shape[0] - 72, 8, 128), F32)
    conv_sum = PlaneReducer(*conv_scratch[:4], conv_out, conv_scratch[4])
    conv_sum.begin()
    for pair in range(half):
        for side, line in enumerate((1, h)):
            parts = []
            for image in (pair, pair + half):
                start = PAD + (image * zed_rows + line) * pitch
                parts.append(zed_x[start : start + pitch, :])
            zed_send[side, pair] = jnp.where(low_half, parts[0], parts[1])
    for side, column in enumerate((8, 7 + w)):
        pack_columns(zed_x, edge_send.at[side], images, zed_rows, pitch, 1, column, 1)
    for k, (up, along) in enumerate(AROUND[4:]):
        pack_corner(
            zed_x,
            zed_corners.at[0, k],
            images,
            zed_rows,
            pitch,
            1 if up < 0 else h,
            8 if along < 0 else 7 + w,
            1,
        )
    zed_around = Around(
        [zed_send.at[k] for k in range(2)]
        + [edge_send.at[k] for k in range(2)]
        + [zed_corners.at[0, k] for k in range(4)],
        [zed_recv.at[k] for k in range(2)]
        + [edge_recv.at[k] for k in range(2)]
        + [zed_corners.at[1, k] for k in range(4)],
        zed_sems,
    )
    zed_around.start()
    fourth_total.middle()
    conv_x_sum.last()
    conv_sum.middle()
    zed_around.wait()

    def use_zed(k):
        up, along = AROUND[k]
        row = h + 1 if up < 0 else 0
        column = 8 + w if along < 0 else 7
        if k < 2:
            for image in range(images):
                start = PAD + (image * zed_rows + row) * pitch
                zed_x[start : start + pitch, :] = unpacked(
                    zed_recv[k, image % half], image, images
                )
        elif k < 4:
            unpack_columns(
                zed_x, edge_recv.at[k - 2], images, zed_rows, pitch, 1, column, 1, h, False
            )
        else:
            unpack_corner(
                zed_x, zed_corners.at[1, k - 4], images, zed_rows, pitch, row, column, 1, False
            )

    zed_around.each(use_zed)

    def zed_store(b):
        return pltpu.make_async_copy(
            zed_x.at[pl.ds(PAD + b * zed_rows * pitch, zed_rows * pitch)],
            zed_out.at[b],
            out_sems.at[1, b],
        )

    for b in range(images):
        zed_store(b).start()
    last_out[...] = fourth_total.end()
    conv_sum.last()
    gather.end()
    gather.begin(0)
    conv_x_sum.end()
    conv_sum.end()
    gather.end()
    for b in range(images):
        zed_store(b).wait()
        pltpu.make_async_copy(skip_s.at[b], skip_out.at[b], out_sems.at[0, b]).wait()


def fall(
    spread, y_two, stats, load, small, tiles_x, y_one, merged, low, conv_two, conv_one
):
    images, rows, wide, _ = y_two.shape
    height, breadth = rows - 4, wide - 16
    h, w = height // 2, breadth // 2
    pitch, ext, zed_rows = w + 16, height + 2, h + 2
    half = images // 2
    tiles, parts_x, parts = load.shape[0], tiles_x.shape[0], conv_tiles(72)
    vmem = pl.BlockSpec(memory_space=pltpu.VMEM)
    hbm = pl.BlockSpec(memory_space=pl.ANY)
    lines, low_lines = rounded_up(ext, 16), rounded_up(h, 8)
    return pl.pallas_call(
        fall_body,
        in_specs=[hbm] * 2 + [vmem, hbm, vmem] + [hbm] * 6,
        out_specs=[hbm] * 2 + [vmem] * 6,
        out_shape=[
            jax.ShapeDtypeStruct((images, height, breadth, 64), F32),
            jax.ShapeDtypeStruct((images, zed_rows * pitch, 128), F32),
            jax.ShapeDtypeStruct((tiles, 16, 128), BF16),
            jax.ShapeDtypeStruct((parts, 8, 128), F32),
            jax.ShapeDtypeStruct((parts_x, 8, 128), F32),
            jax.ShapeDtypeStruct((16, 128), F32),
            jax.ShapeDtypeStruct((8, 128), F32),
            jax.ShapeDtypeStruct((768, 128), BF16),
        ],
        scratch_shapes=[
            pltpu.VMEM(y_two.shape, F32),
            pltpu.VMEM(y_two.shape, F32),
            pltpu.VMEM(y_one.shape, F32),
            pltpu.VMEM(merged.shape, BF16),
            pltpu.VMEM(low.shape, BF16),
            pltpu.VMEM((2, 3, 192, 64), BF16),
            pltpu.VMEM(load.shape, BF16),
            pltpu.VMEM((images, height, breadth, 64), F32),
            pltpu.VMEM((level_sizes(tiles)[-1][1], 16, 128), BF16),
            pltpu.VMEM((2 * PAD + (images * rows + lines - ext) * wide, 128), F32),
            pltpu.VMEM((2 * PAD + (images * zed_rows + 8) * pitch, 128), F32),
            pltpu.VMEM(((height + 4) * breadth, 128), F32),
            pltpu.VMEM(((h + 4) * w, 128), F32),
            pltpu.VMEM((rows * wide, 256), BF16),
            pltpu.VMEM((2 * PAD + h * 2 * pitch, 128), F32),
            pltpu.VMEM((768, 128), BF16),
            pltpu.VMEM((256, 256), F32),
            pltpu.VMEM((256, 256), F32),
            pltpu.VMEM((2, 8, 128), F32),
            pltpu.VMEM((2, half, 3 * wide, 128), BF16),
            pltpu.VMEM((2, half, 3 * wide, 128), BF16),
            pltpu.VMEM((2, 3 * half, lines, 128), BF16),
            pltpu.VMEM((2, 3 * half, lines, 128), BF16),
            pltpu.VMEM((2, 4, half, 32, 128), BF16),
            pltpu.VMEM((2, half, pitch, 128), F32),
            pltpu.VMEM((2, half, pitch, 128), F32),
            pltpu.VMEM((2, half, low_lines, 128), F32),
            pltpu.VMEM((2, half, low_lines, 128), F32),
            pltpu.VMEM((2, 4, half, 8, 128), F32),
            total_scratch(16),
            total_scratch(8),
            scatter_scratch(tiles),
            plane_scratch(parts_x),
            plane_scratch(parts),
            level_sems(),
            pltpu.SemaphoreType.DMA((7,)),
            pltpu.SemaphoreType.DMA((2, images)),
            pltpu.SemaphoreType.DMA((2, images)),
            pltpu.SemaphoreType.DMA((2, 8)),
            pltpu.SemaphoreType.DMA((2, 8)),
        ],
        compiler_params=pltpu.CompilerParams(
            collective_id=2, has_side_effects=True, vmem_limit_bytes=60 * MIB
        ),
        name="fall",
    )(spread, y_two, stats, load, small, tiles_x, y_one, merged, low, conv_two, conv_one)


def finish_body(
    cells_low,
    load_ref,
    rest_ref,
    conv_ref,
    conv_x_ref,
    sums_ref,
    last_ref,
    stat_ref,
    zed_ref,
    y_one_ref,
    weight_ref,
    skip_ref,
    conv_one_out,
    gain_one_out,
    shift_one_out,
    conv_two_out,
    gain_two_out,
    shift_two_out,
    head_out,
    head_b_out,
    heat_w_out,
    heat_b_out,
    box_w_out,
    box_b_out,
    low_out,
    skip_out,
    zed_x,
):
    step = pl.program_id(0)
    each, h, w, _ = low_out.shape
    pitch = w + 16
    rows = h + 2
    factor = stat_ref[6:7, :] * stat_ref[1:2, :]
    shift_low, gain_low = last_ref[0:1, :] / cells_low, last_ref[1:2, :] / cells_low
    skip_out[...] = skip_ref[...]
    for column in range(head_out.shape[3] // 128):
        block = load_ref[36 * column : 36 * column + 36].astype(F32)
        head_out[:, :, :, 128 * column : 128 * column + 128] = block.reshape(3, 3, 64, 128)

    @pl.when(step == 0)
    def _():
        zed_x[0:PAD, :] = jnp.zeros((PAD, 128), F32)
        zed_x[PAD + rows * pitch :, :] = jnp.zeros((PAD, 128), F32)
        spread = stat_ref[16:24, :].T
        ones = unfold(conv_ref, 36)
        normed = unfold(conv_x_ref, 0)
        for tap, part in enumerate(unfold(conv_ref, 0)):
            conv_two_out[tap] = part.reshape(3, 64, 64)
            count = jnp.concatenate(
                [spread[:, 2 * tap : 2 * tap + 1], spread[0:64, 2 * tap + 1 : 2 * tap + 2]], axis=0
            )
            value = ones[tap] - count * shift_low[:, 0:64] - normed[tap] * gain_low[:, 0:64]
            conv_one_out[tap] = (value * factor[:, 0:64]).reshape(3, 64, 64)
        for column in range(6):
            span = slice(128 * column, 128 * column + 128)
            head_b_out[span] = sums_ref[column : column + 1, :].reshape(128)
        for part in range(2):
            span = slice(128 * part, 128 * part + 128)
            heat_w_out[:, span] = rest_ref[5 * part : 5 * part + 5].astype(F32).reshape(80, 128)
            for box in range(2):
                block = rest_ref[10 + 2 * box + part].astype(F32)
                box_w_out[box, :, span] = block[2 * box : 2 * box + 2, :]
            box_b_out[part : part + 1, :] = sums_ref[7:8, 2 * part : 2 * part + 2]
        heat_b_out[...] = sums_ref[6:7, 0:80]
        shift_two_out[...] = sums_ref[8:9, 0:64]
        gain_two_out[...] = sums_ref[9:10, 0:64]
        shift_one_out[...] = last_ref[0:1, 0:64]
        gain_one_out[...] = last_ref[1:2, 0:64]

    for b in range(each):
        normed = (y_one_ref[b, 1 : h + 3] - stat_ref[0:1, :]) * stat_ref[1:2, :]
        grad_z = zed_ref[b].reshape(rows, pitch, 128)
        grad_y = factor * (grad_z - shift_low - normed * gain_low)
        column = lax.broadcasted_iota(jnp.int32, (pitch, 128), 0)
        keep = jnp.where(column < 8, stat_ref[12:13, :], 1.0)
        keep = jnp.where(column >= 8 + w, stat_ref[13:14, :], keep)
        grad_y = (grad_y * keep).astype(BF16).astype(F32)
        zed_x[PAD : PAD + rows * pitch, :] = grad_y.reshape(rows * pitch, 128)
        for line, row in ((0, 10), (rows - 1, 11)):
            span = slice(PAD + line * pitch, PAD + (line + 1) * pitch)
            zed_x[span, :] = zed_x[span, :] * stat_ref[row : row + 1, :]
        pairs = back_pairs(zed_x, PAD, rows * pitch)
        count = h * pitch
        taps = jnp.concatenate(
            [pairs[pitch * (2 - a) : pitch * (2 - a) + count] for a in range(3)], axis=1
        )
        grad = dot(taps, weight_ref[...]).reshape(h, pitch, 128)
        low_out[b] = grad[:, 8 : 8 + w, 0:64]


def finish(load, conv, conv_x, sums, last, stats, zed, y_one, weight, skip):
    images, y_rows, pitch, _ = y_one.shape
    h, w = y_rows - 4, pitch - 16
    batches, row_count, col_count = extents()
    cells = float(images * batches * h * row_count * w * col_count)
    span = zed.shape[1]
    steps = 2
    each = images // steps
    shapes = [
        (3, 3, 64, 64),
        (1, 64),
        (1, 64),
        (3, 3, 64, 64),
        (1, 64),
        (1, 64),
        (3, 3, 64, 768),
        (768,),
        (80, 256),
        (1, 80),
        (2, 2, 256),
        (2, 2),
        (images, h, w, 64),
        skip.shape,
    ]
    whole = lambda shape: pl.BlockSpec(shape, lambda c: (0,) * len(shape))
    part = lambda shape: pl.BlockSpec(shape, lambda c: (c,) + (0,) * (len(shape) - 1))
    out_specs = [whole(shape) for shape in shapes]
    out_specs[6] = pl.BlockSpec((3, 3, 64, 768 // steps), lambda c: (0, 0, 0, c))
    out_specs[12] = part((each, h, w, 64))
    out_specs[13] = part((each,) + skip.shape[1:])
    return pl.pallas_call(
        functools.partial(finish_body, cells),
        grid=(steps,),
        in_specs=[
            part((216 // steps, 16, 128)),
            pl.BlockSpec((36, 16, 128), lambda c: (6, 0, 0)),
        ]
        + [whole(array.shape) for array in (conv, conv_x, sums, last, stats)]
        + [
            part((each, span, 128)),
            part((each, y_rows, pitch, 128)),
            whole(weight.shape),
            part((each,) + skip.shape[1:]),
        ],
        out_specs=out_specs,
        out_shape=[jax.ShapeDtypeStruct(shape, F32) for shape in shapes],
        scratch_shapes=[
            pltpu.VMEM((2 * PAD + span, 128), F32),
        ],
        compiler_params=pltpu.CompilerParams(vmem_limit_bytes=60 * MIB),
        name="finish",
    )(load, load, conv, conv_x, sums, last, stats, zed, y_one, weight, skip)


def local(
    low_map,
    skip_map,
    conv_first,
    gain_first,
    shift_first,
    conv_second,
    gain_second,
    shift_second,
    head_conv,
    head_bias,
    heat_weight,
    heat_bias,
    box_weight,
    box_bias,
    heat_target,
    box_target,
    obj_index,
    obj_count,
):
    batches, rows, cols = extents()
    devices = batches * rows * cols
    conv_one = conv_first.reshape(3, 192, 64)
    conv_two = conv_second.reshape(3, 192, 64)
    y_two, y_one, merged, low, kernel, back, stats, spot, tiles_x = rise(
        low_map,
        skip_map,
        heat_target,
        conv_one,
        conv_two,
        gain_first.reshape(1, 64),
        shift_first.reshape(1, 64),
        gain_second.reshape(1, 64),
        shift_second.reshape(1, 64),
        obj_index,
        head_conv.reshape(3, 192, 768),
        head_bias,
        obj_count,
    )
    heat_map, box_map, spread, load, small = heads(
        y_two,
        heat_target,
        spot,
        box_target.transpose(0, 2, 1),
        stats,
        kernel,
        back,
        heat_weight.T,
        heat_bias.reshape(1, 80),
        box_weight.transpose(0, 2, 1),
        box_bias,
        devices,
    )
    images, ext, wide, _ = spread.shape
    grad_skip, zed, load, conv, conv_x, sums, last, weight = fall(
        spread.reshape(images, ext * wide, 128),
        y_two,
        stats,
        load,
        small,
        tiles_x,
        y_one,
        merged,
        low,
        conv_two,
        conv_one,
    )
    grads = finish(load, conv, conv_x, sums, last, stats, zed, y_one, weight, grad_skip)
    return (
        heat_map,
        box_map.transpose(0, 1, 3, 2),
        grads[12],
        grads[13],
        grads[0],
        grads[1].reshape(64),
        grads[2].reshape(64),
        grads[3],
        grads[4].reshape(64),
        grads[5].reshape(64),
        grads[6],
        grads[7],
        grads[8].T,
        grads[9].reshape(80),
        grads[10].transpose(0, 2, 1),
        grads[11],
    )


def solution(mesh):
    tile = P("batch", "row", "col", None)
    return jax.shard_map(
        local,
        mesh=mesh,
        in_specs=(tile, tile)
        + (P(),) * 12
        + (tile, P("batch", None, None), P("batch", None), P("batch")),
        out_specs=(tile,) * 4 + (P(),) * 12,
        check_vma=False,
    )
```
